32 devices in a mesh: ctx: 8 (over z, x), fsdp: 4 (over y, core).
Axes of the slice: x: 2, y: 2, z: 4, core: 2. Of those that a mesh axis runs over, the one named last changes fastest.
Arguments:
- layer_input: bfloat16 [4, 8192, 512], P('fsdp', 'ctx'), may hold values from -6 to 6
- doc_lengths: int32 [4, 8], P('fsdp'), may hold values from 1 to 7168, as said below
- ln1_gain: bfloat16 [512], P('fsdp'), may hold values from 0.099609375 to 1.8984375
- ln1_bias: bfloat16 [512], P('fsdp'), may hold values from -1.75 to 1.75
- qkv_weight: bfloat16 [512, 1536], P('fsdp'), may hold values from -0.375 to 0.375
- query_bias: bfloat16 [512], P('fsdp'), may hold values from -3 to 3
- value_bias: bfloat16 [512], P('fsdp'), may hold values from -3 to 3
- out_weight: bfloat16 [512, 512], P('fsdp'), may hold values from -1 to 1
- out_bias: bfloat16 [512], P('fsdp'), may hold values from -1.75 to 1.75
- ln2_gain: bfloat16 [512], P('fsdp'), may hold values from 0.099609375 to 1.8984375
- ln2_bias: bfloat16 [512], P('fsdp'), may hold values from -1.75 to 1.75
- up_weight: bfloat16 [512, 2048], P('fsdp'), may hold values from -0.25 to 0.25
- up_bias: bfloat16 [2048], P('fsdp'), may hold values from -1.75 to 1.75
- down_weight: bfloat16 [2048, 512], P('fsdp'), may hold values from -0.1875 to 0.1875
- down_bias: bfloat16 [512], P('fsdp'), may hold values from -1.75 to 1.75
- cotangent: bfloat16 [4, 8192, 512], P('fsdp', 'ctx'), may hold values from -8 to 8
Outputs:
- output: bfloat16 [4, 8192, 512], P('fsdp', 'ctx')
- input_grad: float32 [4, 8192, 512], P('fsdp', 'ctx')
- ln1_gain_grad: float32 [512], P('fsdp')
- ln1_bias_grad: float32 [512], P('fsdp')
- qkv_weight_grad: float32 [512, 1536], P('fsdp')
- query_bias_grad: float32 [512], P('fsdp')
- value_bias_grad: float32 [512], P('fsdp')
- out_weight_grad: float32 [512, 512], P('fsdp')
- out_bias_grad: float32 [512], P('fsdp')
- ln2_gain_grad: float32 [512], P('fsdp')
- ln2_bias_grad: float32 [512], P('fsdp')
- up_weight_grad: float32 [512, 2048], P('fsdp')
- up_bias_grad: float32 [2048], P('fsdp')
- down_weight_grad: float32 [2048, 512], P('fsdp')
- down_bias_grad: float32 [512], P('fsdp')
The draws below stay inside these ranges and needn't reach their ends.
Inputs may be any that keep to these rules, and one draw needn't show every extreme that they name: `doc_lengths`: each row gives the lengths of a stream's 8 documents in order; they sum to 8192; exactly one document has 7168 tokens, neither first nor last, so that it begins among the first 1024 tokens and ends among the last 1024; the others together hold 1024 tokens.
All inputs are finite; a program needn't handle non-finite values.
Results may differ from the reference program's by a relative error of at most 0.011.
The reference program's roundings to bfloat16 on the way count: a program that leaves them out, or rounds other values in their place, can miss the bound.
Values may be sent and summed in bfloat16 or wider, within the bound.
No kernel may reach another device: no remote copies, remote signals or barrier semaphores. Data moves between devices by JAX's collectives and lax.ppermute only.
A program may use at most 192 MiB of HBM per device.

```python
import math
from functools import partial
import jax
import jax.numpy as jnp
from jax import lax

D = 512
ATTENTION_HEADS = 8
HEAD_FEATURES = 64
FF = 2048
BLOCK = 16
LEVELS = 10
TOK_DEV = 1024
DOC_COUNT = 8
STREAMS = 4
TOKENS = 8192
DOCMAX = 7168


def draw_doc_lengths(key, part):
    key = jax.random.fold_in(key, 11)

    def one_stream(stream_key):
        cut_key, place_key = jax.random.split(stream_key)
        picked = jax.random.permutation(cut_key, TOK_DEV - 1)[:DOC_COUNT - 2].astype(jnp.int32) + 1
        cuts = jnp.sort(picked)
        edges = jnp.concatenate([jnp.zeros((1,), jnp.int32), cuts, jnp.full((1,), TOK_DEV, jnp.int32)])
        shorts = edges[1:] - edges[:-1]
        place = jax.random.randint(place_key, (), 1, DOC_COUNT - 1).astype(jnp.int32)
        slots = jnp.arange(DOC_COUNT, dtype=jnp.int32)
        before = shorts[jnp.clip(slots, 0, DOC_COUNT - 2)]
        after = shorts[jnp.clip(slots - 1, 0, DOC_COUNT - 2)]
        longest = jnp.full((DOC_COUNT,), DOCMAX, jnp.int32)
        return jnp.where(slots < place, before, jnp.where(slots == place, longest, after))
    stream_keys = jax.random.split(key, STREAMS)
    return jax.vmap(one_stream)(stream_keys).astype(jnp.int32)


def strengthened(entries, key, source, target, shards_of, factor):
    owner, partner = [(jnp.arange(entries.shape[dim]) // (entries.shape[dim] // shards_of)).reshape([-1 if axis == dim else 1 for axis in range(entries.ndim)]) for dim in (source, target)]
    chosen = jax.random.permutation(key, shards_of)[partner]
    strong = (owner == chosen) | (owner == (partner + shards_of // 2) % shards_of)
    return jnp.where(strong, factor * entries, entries)


def shard_levels(rng, shape, pieces, least, top_value):
    level = 1.0
    for axis_at, shards_of in pieces:
        draws = jax.random.uniform(jax.random.fold_in(jax.random.fold_in(rng, 6), axis_at), (shards_of,), jnp.float32, least / len(pieces), top_value / len(pieces))
        level = level * jnp.repeat(jnp.exp(draws), shape[axis_at] // shards_of).reshape((-1,) + (1,) * (len(shape) - 1 - axis_at))
    return level


def normal_values(rng, extent, spread, bound, cuts=(), kind=jnp.bfloat16):
    factor_of = shard_levels(rng, extent, cuts, -0.22, 0.18) if cuts else 1.0
    drawn = jax.random.normal(rng, extent, jnp.float32) * spread * factor_of
    return jnp.minimum(jnp.maximum(drawn, -bound), bound).astype(kind)


def bell_draw_with(own_key, extent, scale, bound, pieces, heavy, kind=jnp.bfloat16):
    entries = scale * jax.random.normal(own_key, extent, jnp.float32)
    if pieces:
        entries = entries * shard_levels(own_key, extent, pieces, -0.22, 0.18)
    return jnp.clip(strengthened(entries, jax.random.fold_in(own_key, 3), *heavy), -bound, bound).astype(kind)


def setup_inputs(seed: int = 0) -> dict:
    key_list = jax.random.split(jax.random.key(seed), 17)
    return {
        "layer_input": normal_values(key_list[0], (STREAMS, TOKENS, D), 1.0, 6.0, ((0, 4), (1, 8))),
        "doc_lengths": draw_doc_lengths(jax.random.fold_in(key_list[16], 71), 0),
        "ln1_gain": jnp.clip(1.0 + 0.18 * jax.random.normal(key_list[2], (D,), jnp.float32), 0.099609375, 1.8984375).astype(jnp.bfloat16),
        "ln1_bias": normal_values(key_list[3], (D,), 0.3, 1.75, ((0, 4),)),
        "qkv_weight": normal_values(key_list[4], (D, 3 * D), (D // 2) ** -0.5, 0.375, ((0, 4),)),
        "query_bias": normal_values(key_list[5], (D,), 0.5, 3.0, ((0, 4),)),
        "value_bias": normal_values(key_list[6], (D,), 0.5, 3.0, ((0, 4),)),
        "out_weight": normal_values(key_list[7], (D, D), (D // 16) ** -0.5, 1.0, ((0, 4),)),
        "out_bias": normal_values(key_list[8], (D,), 0.3, 1.75, ((0, 4),)),
        "ln2_gain": jnp.clip(1.0 + 0.18 * jax.random.normal(key_list[9], (D,), jnp.float32), 0.099609375, 1.8984375).astype(jnp.bfloat16),
        "ln2_bias": normal_values(key_list[10], (D,), 0.3, 1.75, ((0, 4),)),
        "up_weight": normal_values(key_list[11], (D, FF), D ** -0.5, 0.25, ((0, 4),)),
        "up_bias": normal_values(key_list[12], (FF,), 0.3, 1.75, ((0, 4),)),
        "down_weight": normal_values(key_list[13], (FF, D), (FF // 2) ** -0.5, 0.1875, ((0, 4),)),
        "down_bias": normal_values(key_list[14], (D,), 0.3, 1.75, ((0, 4),)),
        "cotangent": bell_draw_with(key_list[15], (STREAMS, TOKENS, D), 1.0, 8.0, ((0, 4), (1, 8)), (1, 2, 8, 2.0)),
    }


@jax.custom_vjp
def low(v):
    return lax.optimization_barrier(v.astype(jnp.bfloat16)).astype(jnp.float32)

@jax.custom_vjp
def low_back(v):
    return v

def low_keep(v):
    return (low(v), None)

def low_pass(kept, grad):
    return (grad,)

def back_keep(v):
    return (v, None)

def back_low(kept, grad):
    return (low(grad),)
low.defvjp(low_keep, low_pass)
low_back.defvjp(back_keep, back_low)
highest = lax.Precision.HIGHEST
norm_epsilon = 1e-05
masked_score = -1e+30

def layer_norm(values, norm_gain, norm_bias):
    row_mean = lax.optimization_barrier(jnp.mean(values, axis=-1, keepdims=True))
    centred = values - row_mean
    variance = lax.optimization_barrier(jnp.mean(centred * centred, axis=-1, keepdims=True))
    return centred * lax.rsqrt(variance + norm_epsilon) * norm_gain + norm_bias

def doc_index(positions, starts):
    return lax.optimization_barrier(jnp.sum((starts[None, :] <= positions[:, None]).astype(jnp.int32), axis=1)) - 1

def allowed(query_pos, key_first, key_level, key_span, starts, total):
    block_span = BLOCK * key_span[None, :]
    parent_span = jnp.maximum(block_span // 2, 1)
    query_col = query_pos[:, None]
    first_row = key_first[None, :]
    block_gap = jnp.abs(first_row // block_span - query_col // block_span)
    parent_gap = jnp.abs(first_row // parent_span - query_col // parent_span)
    level_ok = jnp.where(key_level[None, :] == 0, block_gap <= 1, (block_gap == 1) & (parent_gap > 1))
    inside = (key_first >= 0) & (key_first < total)
    first_doc = doc_index(key_first, starts)
    last_doc = doc_index(key_first + key_span - 1, starts)
    key_doc = jnp.where(inside & (first_doc == last_doc), first_doc, -2)
    query_doc = doc_index(query_pos, starts)
    return level_ok & (key_doc[None, :] == query_doc[:, None])

def pair_mean(rows):
    paired = rows.reshape(rows.shape[0] // 2, 2, rows.shape[1])
    return 0.5 * (paired[:, 0] + paired[:, 1])

def stream_attention(queries, keys, values, starts):
    key_levels = [keys]
    value_levels = [values]
    for level_num in range(1, LEVELS):
        key_levels.append(low(pair_mean(key_levels[-1])))
        value_levels.append(low(pair_mean(value_levels[-1])))
    block_row_span = min(512, TOKENS)
    margin = 2 * BLOCK
    padded_keys = [jnp.pad(level_keys, ((margin, margin), (0, 0))) for level_keys in key_levels]
    padded_values = [jnp.pad(level_values, ((margin, margin), (0, 0))) for level_values in value_levels]
    score_scale = 1.0 / math.sqrt(HEAD_FEATURES)

    def one_block(block_start):
        query_row_block = lax.dynamic_slice_in_dim(queries, block_start, block_row_span, 0)
        key_parts, value_parts, first_parts, level_parts, span_parts = ([], [], [], [], [])
        for level_num in range(LEVELS):
            level_span = 2 ** level_num
            level_count = block_row_span // level_span + 2 * margin
            level_start = block_start // level_span
            key_parts.append(lax.dynamic_slice_in_dim(padded_keys[level_num], level_start, level_count, 0))
            value_parts.append(lax.dynamic_slice_in_dim(padded_values[level_num], level_start, level_count, 0))
            first_parts.append((level_start - margin + jnp.arange(level_count, dtype=jnp.int32)) * level_span)
            level_parts.append(jnp.full((level_count,), level_num, jnp.int32))
            span_parts.append(jnp.full((level_count,), level_span, jnp.int32))
        key_row_block = jnp.concatenate(key_parts, axis=0)
        value_row_block = jnp.concatenate(value_parts, axis=0)
        key_first = jnp.concatenate(first_parts)
        key_level = jnp.concatenate(level_parts)
        key_span = jnp.concatenate(span_parts)
        query_pos = block_start + jnp.arange(block_row_span, dtype=jnp.int32)
        mask = allowed(query_pos, key_first, key_level, key_span, starts, TOKENS)
        level_weight = key_level.astype(jnp.float32) * math.log(2.0)
        key_total_count = key_row_block.shape[0]
        attention_scores = jnp.einsum('cse,jse->scj', query_row_block.reshape(block_row_span, ATTENTION_HEADS, HEAD_FEATURES), key_row_block.reshape(key_total_count, ATTENTION_HEADS, HEAD_FEATURES), precision=highest) * score_scale
        attention_scores = jnp.where(mask[None], low_back(attention_scores) + level_weight[None, None, :], masked_score)
        attention_probabilities = jax.nn.softmax(attention_scores, axis=-1)
        attended_output = jnp.einsum('fao,ofx->afx', low(attention_probabilities), value_row_block.reshape(key_total_count, ATTENTION_HEADS, HEAD_FEATURES), precision=highest)
        return attended_output.reshape(block_row_span, D)
    block_starts = jnp.arange(TOKENS // block_row_span, dtype=jnp.int32) * block_row_span
    results = lax.map(jax.checkpoint(one_block), block_starts)
    return results.reshape(TOKENS, D)

def forward(input_all, gain_first, shift_first, qkv_weight, query_bias, value_bias, out_weight, out_bias, gain_second, shift_second, up_weight, up_bias, down_weight, down_bias, starts_all):
    rows = input_all.reshape(STREAMS * TOKENS, D)
    normed_first = low(layer_norm(rows, gain_first, shift_first))
    bias_row = jnp.concatenate([query_bias, jnp.zeros_like(query_bias), value_bias])
    qkv = low(low_back(jnp.dot(normed_first, qkv_weight, precision=highest) + bias_row))
    attended_parts = []
    for stream_num in range(STREAMS):
        stream_rows = qkv[stream_num * TOKENS:(stream_num + 1) * TOKENS]
        attended_parts.append(stream_attention(stream_rows[:, :D], stream_rows[:, D:2 * D], stream_rows[:, 2 * D:], starts_all[stream_num]))
    attended_output = low(low_back(jnp.concatenate(attended_parts, axis=0)))
    projected = low_back(jnp.dot(attended_output, out_weight, precision=highest) + out_bias)
    middle = rows + projected
    normed_second = low(layer_norm(middle, gain_second, shift_second))
    pre = low_back(jnp.dot(normed_second, up_weight, precision=highest) + up_bias)
    hidden = low(jax.nn.gelu(pre, approximate=False))
    lowered = low_back(jnp.dot(hidden, down_weight, precision=highest) + down_bias)
    return (middle + lowered).reshape(STREAMS, TOKENS, D)

def reference(layer_input, doc_lengths, ln1_gain, ln1_bias, qkv_weight, query_bias, value_bias, out_weight, out_bias, ln2_gain, ln2_bias, up_weight, up_bias, down_weight, down_bias, cotangent):
    starts_all = (jnp.cumsum(doc_lengths, axis=1) - doc_lengths).astype(jnp.int32)
    inputs = tuple((operand.astype(jnp.float32) for operand in (layer_input, ln1_gain, ln1_bias, qkv_weight, query_bias, value_bias, out_weight, out_bias, ln2_gain, ln2_bias, up_weight, up_bias, down_weight, down_bias)))
    result, pullback = jax.vjp(partial(forward, starts_all=starts_all), *inputs)
    grads = pullback(cotangent.astype(jnp.float32))
    return (result.astype(jnp.bfloat16), grads[0], grads[1], grads[2], grads[3], grads[4], grads[5], grads[6], grads[7], grads[8], grads[9], grads[10], grads[11], grads[12], grads[13])
```

```python
from functools import partial
import math

import jax
import jax.numpy as jnp
from jax import lax
from jax.experimental import pallas as pl
from jax.experimental.pallas import tpu as pltpu
from jax.sharding import PartitionSpec as P

HEADS = 8
BLOCK = 16
LEVELS = 10
NEAR = 4
LOCAL = 7
CHUNK = 128
WIDTH = 512
PAIRS = HEADS // 2
MASKED = -1e30
EPSILON = 1e-05
VMEM_LIMIT = 56 * 1024 * 1024

f32 = jnp.float32
bf16 = jnp.bfloat16


def level_rows(rows, level):
    return rows // 2**level


def far_levels(total):
    return [l for l in range(LOCAL, LEVELS) if total // (BLOCK * 2**l) >= 2]


def extended_offsets(rows, far):
    offsets, cursor = [], 0
    for level in range(LOCAL):
        offsets.append(cursor)
        cursor += level_rows(rows, level) + 2 * BLOCK
    for _ in far:
        offsets.append(cursor)
        cursor += 2 * BLOCK
    return offsets, cursor


def slot_layout(far):
    parts = [(level, CHUNK // 2**level + 2 * BLOCK) for level in range(NEAR)]
    parts += [(level, BLOCK) for level in list(range(NEAR, LOCAL)) + far for _ in range(2)]
    return parts, sum(count for _, count in parts)


def slot_sources(rows, far, chunk):
    offsets, _ = extended_offsets(rows, far)
    sources = []
    for level in range(NEAR):
        sources.append((offsets[level] + chunk * (CHUNK // 2**level), CHUNK // 2**level + 2 * BLOCK))
    for level in range(NEAR, LOCAL):
        block = chunk // (BLOCK * 2**level // CHUNK)
        sources.append((offsets[level] + block * BLOCK, BLOCK))
        sources.append((offsets[level] + block * BLOCK + 2 * BLOCK, BLOCK))
    for at in range(len(far)):
        sources.append((offsets[LOCAL + at], BLOCK))
        sources.append((offsets[LOCAL + at] + BLOCK, BLOCK))
    return sources


def count_starts(positions, starts):
    total = jnp.zeros(positions.shape, jnp.int32)
    for at in range(starts.shape[0]):
        total = total + (starts[at] <= positions).astype(jnp.int32)
    return total - 1


def score_bias(rows, total, offset, starts, far):
    chunks = rows // CHUNK
    bases = offset + CHUNK * jnp.arange(chunks, dtype=jnp.int32)
    firsts, spans, levels = [], [], []
    for level in range(NEAR):
        span = 2**level
        count = CHUNK // span + 2 * BLOCK
        firsts.append(bases[:, None] + (jnp.arange(count, dtype=jnp.int32)[None, :] - BLOCK) * span)
        spans += [span] * count
        levels += [level] * count
    for level in list(range(NEAR, LOCAL)) + far:
        span = 2**level
        block = bases // (BLOCK * span)
        for side in (-1, 1):
            firsts.append(
                (block[:, None] + side) * (BLOCK * span)
                + jnp.arange(BLOCK, dtype=jnp.int32)[None, :] * span
            )
            spans += [span] * BLOCK
            levels += [level] * BLOCK
    first = jnp.concatenate(firsts, axis=1)
    span = jnp.array(spans, jnp.int32)[None, :]
    level = jnp.array(levels, jnp.int32)[None, :]
    inside = (first >= 0) & (first < total)
    first_doc = count_starts(first, starts)
    last_doc = count_starts(first + span - 1, starts)
    key_doc = jnp.where(inside & (first_doc == last_doc), first_doc, -2)
    query = bases[:, None] + jnp.arange(CHUNK, dtype=jnp.int32)[None, :]
    query_doc = count_starts(query, starts)
    shift = level + 4
    parent = jnp.maximum(shift - 1, 0)
    first3, shift3, parent3, query3 = (
        first[:, :, None],
        shift[:, :, None],
        parent[:, :, None],
        query[:, None, :],
    )
    gap = jnp.abs((first3 >> shift3) - (query3 >> shift3))
    parent_gap = jnp.abs((first3 >> parent3) - (query3 >> parent3))
    seen = jnp.where(level[:, :, None] == 0, gap <= 1, (gap == 1) & (parent_gap > 1))
    seen = seen & (key_doc[:, :, None] == query_doc[:, None, :])
    return jnp.where(seen, level[:, :, None].astype(f32) * math.log(2.0), MASKED)


def dot_nt(left, right):
    return lax.dot_general(left, right, (((1,), (1,)), ((), ())), preferred_element_type=f32)


def dot_tn(left, right):
    return lax.dot_general(left, right, (((0,), (0,)), ((), ())), preferred_element_type=f32)


def dot_nn(left, right):
    return jnp.dot(left, right, preferred_element_type=f32)


def pool_matrix(count):
    row = lax.broadcasted_iota(jnp.int32, (count // 2, count), 0)
    column = lax.broadcasted_iota(jnp.int32, (count // 2, count), 1)
    return jnp.where((column >> 1) == row, 0.5, 0.0).astype(bf16)


def spread_matrix(count):
    row = lax.broadcasted_iota(jnp.int32, (2 * count, count), 0)
    column = lax.broadcasted_iota(jnp.int32, (2 * count, count), 1)
    return jnp.where((row >> 1) == column, 0.5, 0.0).astype(bf16)


def spread(values):
    count = values.shape[0]
    tile = min(count, 128)
    matrix = spread_matrix(tile)
    high = values.astype(bf16)
    low = (values - high.astype(f32)).astype(bf16)
    parts = [
        dot_nn(matrix, high[at : at + tile]) + dot_nn(matrix, low[at : at + tile])
        for at in range(0, count, tile)
    ]
    return parts[0] if len(parts) == 1 else jnp.concatenate(parts, axis=0)


def norm_rows(values):
    mean = jnp.mean(values, axis=-1, keepdims=True)
    centred = values - mean
    variance = jnp.mean(centred * centred, axis=-1, keepdims=True)
    inverse = lax.rsqrt(variance + EPSILON)
    return centred * inverse, inverse


def norm_back(grad_out, scaled, inverse, gain):
    grad_scaled = grad_out * gain
    first = jnp.mean(grad_scaled, axis=-1, keepdims=True)
    second = jnp.mean(grad_scaled * scaled, axis=-1, keepdims=True)
    return inverse * (grad_scaled - first - scaled * second)


def split_heads(pair):
    lane = lax.broadcasted_iota(jnp.int32, pair.shape, 1)
    zero = jnp.zeros_like(pair)
    return jnp.concatenate([jnp.where(lane < 64, pair, zero), jnp.where(lane < 64, zero, pair)], axis=0)


def join_heads(stacked):
    rows = stacked.shape[0] // 2
    lane = lax.broadcasted_iota(jnp.int32, (rows, stacked.shape[1]), 1)
    return jnp.where(lane < 64, stacked[:rows], stacked[rows:])


def qkv_kernel(rows, x_ref, w_ref, bias_ref, gain_ref, shift_ref, normed_ref, q_ref, *level_refs):
    tail_ref, head_ref = level_refs[LOCAL], level_refs[LOCAL + 1]
    level_refs = level_refs[:LOCAL]
    tile = 256

    def body(at, _):
        start = pl.multiple_of(at * tile, tile)
        scaled, _ = norm_rows(x_ref[pl.ds(start, tile), :].astype(f32))
        normed = (scaled * gain_ref[...] + shift_ref[...]).astype(bf16)
        normed_ref[pl.ds(start, tile), :] = normed
        qkv = (dot_nn(normed, w_ref[...]) + bias_ref[...]).astype(bf16)
        q_ref[pl.ds(start, tile), :] = qkv[:, :WIDTH] * jnp.asarray(0.125, bf16)
        current = qkv[:, WIDTH:]
        level_refs[0][pl.ds(start, tile), :] = current
        for level in range(1, 5):
            count = tile // 2**level
            current = dot_nn(pool_matrix(2 * count), current).astype(bf16)
            level_refs[level][pl.ds(pl.multiple_of(at * count, count), count), :] = current
        return 0

    lax.fori_loop(0, rows // tile, body, 0)
    for level in range(5, LOCAL):
        below = level_refs[level - 1][...]
        level_refs[level][...] = dot_nn(pool_matrix(below.shape[0]), below).astype(bf16)
    for level in range(LOCAL):
        count = level_rows(rows, level)
        tail_ref[BLOCK * level : BLOCK * (level + 1), :] = level_refs[level][count - BLOCK :, :]
        head_ref[BLOCK * level : BLOCK * (level + 1), :] = level_refs[level][:BLOCK, :]


def vmem_specs(count):
    return [pl.BlockSpec(memory_space=pltpu.VMEM)] * count


def qkv_call(rows, x, weight, bias, gain, shift):
    shapes = [(rows, WIDTH), (rows, WIDTH)]
    shapes += [(level_rows(rows, level), 2 * WIDTH) for level in range(LOCAL)]
    shapes += [(BLOCK * LOCAL, 2 * WIDTH)] * 2
    return pl.pallas_call(
        partial(qkv_kernel, rows),
        out_shape=[jax.ShapeDtypeStruct(s, bf16) for s in shapes],
        in_specs=vmem_specs(5),
        out_specs=vmem_specs(len(shapes)),
        compiler_params=pltpu.CompilerParams(vmem_limit_bytes=VMEM_LIMIT),
        cost_estimate=pl.CostEstimate(flops=2 * rows * WIDTH * 3 * WIDTH, bytes_accessed=10 << 20, transcendentals=0),
        name="qkv_levels",
    )(x, weight, bias, gain, shift)


def assemble(rows, devices, far, here, level_refs, left_ref, right_ref, base_ref, ext_ref, far_ref):
    offsets, _ = extended_offsets(rows, far)
    for level in range(LOCAL):
        at, count = offsets[level], level_rows(rows, level)
        ext_ref[at : at + BLOCK, :] = left_ref[BLOCK * level : BLOCK * (level + 1), :]
        ext_ref[at + BLOCK : at + BLOCK + count, :] = level_refs[level][...]
        ext_ref[at + BLOCK + count : at + 2 * BLOCK + count, :] = right_ref[
            BLOCK * level : BLOCK * (level + 1), :
        ]
    current = base_ref[...]
    for index, level in enumerate(far):
        current = dot_nn(pool_matrix(current.shape[0]), current).astype(bf16)
        count = current.shape[0]
        far_ref[0:count, :] = current
        block = here >> (level - 6)
        last = count // BLOCK - 1
        for side, neighbour in enumerate((block - 1, block + 1)):
            start = pl.multiple_of(jnp.clip(neighbour, 0, last) * BLOCK, BLOCK)
            at = offsets[LOCAL + index] + side * BLOCK
            ext_ref[at : at + BLOCK, :] = far_ref[pl.ds(start, BLOCK), :]


def load_slots(rows, far, chunk, ext_ref, slots_ref):
    at = 0
    for start, count in slot_sources(rows, far, chunk):
        if not isinstance(start, int):
            start = pl.multiple_of(start, BLOCK)
        slots_ref[at : at + count, :] = ext_ref[pl.ds(start, count), :]
        at += count


def attend_kernel(rows, devices, far, here_ref, q_ref, bias_ref, *refs):
    level_refs, refs = refs[:LOCAL], refs[LOCAL:]
    left_ref, right_ref, base_ref, out_ref, log_ref, ext_ref, far_ref, slots_ref = refs
    chunk = pl.program_id(0)

    @pl.when(chunk == 0)
    def _():
        assemble(rows, devices, far, here_ref[0], level_refs, left_ref, right_ref, base_ref, ext_ref, far_ref)

    load_slots(rows, far, chunk, ext_ref, slots_ref)
    bias = bias_ref[0]
    bias = jnp.concatenate([bias, bias], axis=1)
    for pair in range(PAIRS):
        lanes = slice(128 * pair, 128 * (pair + 1))
        values = slots_ref[:, WIDTH + 128 * pair : WIDTH + 128 * (pair + 1)]
        scores = dot_nt(slots_ref[:, lanes], split_heads(q_ref[:, lanes])) + bias
        top = jnp.max(scores, axis=0, keepdims=True)
        exponent = jnp.exp(scores - top)
        total = jnp.sum(exponent, axis=0, keepdims=True)
        probs = (exponent * (1.0 / total)).astype(bf16)
        out_ref[:, lanes] = join_heads(dot_tn(probs, values)).astype(bf16)
        log_ref[0, pair : pair + 1, :] = top + jnp.log(total)


def attend_call(rows, devices, far, here, q, bias, levels, left, right, base):
    chunks = rows // CHUNK
    _, entries = extended_offsets(rows, far)
    _, slots = slot_layout(far)
    return pl.pallas_call(
        partial(attend_kernel, rows, devices, far),
        grid=(chunks,),
        out_shape=[
            jax.ShapeDtypeStruct((rows, WIDTH), bf16),
            jax.ShapeDtypeStruct((chunks, 8, 2 * CHUNK), f32),
        ],
        in_specs=[
            pl.BlockSpec(memory_space=pltpu.SMEM),
            pl.BlockSpec((CHUNK, WIDTH), lambda i: (i, 0)),
            pl.BlockSpec((1, slots, CHUNK), lambda i: (i, 0, 0)),
        ]
        + vmem_specs(LOCAL + 3),
        out_specs=[
            pl.BlockSpec((CHUNK, WIDTH), lambda i: (i, 0)),
            pl.BlockSpec((1, 8, 2 * CHUNK), lambda i: (i, 0, 0)),
        ],
        scratch_shapes=[
            pltpu.VMEM((entries, 2 * WIDTH), bf16),
            pltpu.VMEM((8 * devices, 2 * WIDTH), bf16),
            pltpu.VMEM((slots, 2 * WIDTH), bf16),
        ],
        compiler_params=pltpu.CompilerParams(vmem_limit_bytes=VMEM_LIMIT),
        cost_estimate=pl.CostEstimate(flops=16 << 30, bytes_accessed=12 << 20, transcendentals=4 << 20),
        name="attend",
    )(here, q, bias, *levels, left, right, base)


def attend_back_kernel(rows, devices, far, here_ref, q_ref, grad_ref, bias_ref, log_ref, *refs):
    level_refs, refs = refs[:LOCAL], refs[LOCAL:]
    left_ref, right_ref, base_ref, refs = refs[0], refs[1], refs[2], refs[3:]
    dq_ref, local_ref, to_left_ref, to_right_ref, to_far_ref = refs[:5]
    ext_ref, far_ref, slots_ref, acc_ref, tree_ref = refs[5:]
    chunk = pl.program_id(0)
    offsets, _ = extended_offsets(rows, far)

    @pl.when(chunk == 0)
    def _():
        assemble(rows, devices, far, here_ref[0], level_refs, left_ref, right_ref, base_ref, ext_ref, far_ref)
        acc_ref[...] = jnp.zeros_like(acc_ref)

    load_slots(rows, far, chunk, ext_ref, slots_ref)
    bias = bias_ref[0]
    bias = jnp.concatenate([bias, bias], axis=1)
    sources = slot_sources(rows, far, chunk)
    for pair in range(PAIRS):
        lanes = slice(128 * pair, 128 * (pair + 1))
        value_lanes = slice(WIDTH + 128 * pair, WIDTH + 128 * (pair + 1))
        keys, values = slots_ref[:, lanes], slots_ref[:, value_lanes]
        queries, grads = split_heads(q_ref[:, lanes]), split_heads(grad_ref[:, lanes])
        probs = jnp.exp(dot_nt(keys, queries) + bias - log_ref[0, pair : pair + 1, :])
        grad_probs = dot_nt(values, grads)
        delta = jnp.sum(probs * grad_probs, axis=0, keepdims=True)
        grad_scores = (probs * (grad_probs - delta)).astype(bf16)
        dq_ref[:, lanes] = (join_heads(dot_tn(grad_scores, keys)) * 0.125).astype(bf16)
        grad_keys = dot_nn(grad_scores, queries)
        grad_values = dot_nn(probs.astype(bf16), grads)
        at = 0
        for start, count in sources:
            if not isinstance(start, int):
                start = pl.multiple_of(start, BLOCK)
            acc_ref[pl.ds(start, count), lanes] += grad_keys[at : at + count]
            acc_ref[pl.ds(start, count), value_lanes] += grad_values[at : at + count]
            at += count

    @pl.when(chunk == pl.num_programs(0) - 1)
    def _():
        for level in range(LOCAL):
            at, count = offsets[level], level_rows(rows, level)
            to_left_ref[BLOCK * level : BLOCK * (level + 1), :] = acc_ref[at : at + BLOCK, :].astype(bf16)
            to_right_ref[BLOCK * level : BLOCK * (level + 1), :] = acc_ref[
                at + BLOCK + count : at + 2 * BLOCK + count, :
            ].astype(bf16)
        for level in range(LOCAL - 1, 0, -1):
            at, count = offsets[level] + BLOCK, level_rows(rows, level)
            below = offsets[level - 1] + BLOCK
            tile = min(count, 128)
            for row in range(0, count, tile):
                carry = spread(acc_ref[at + row : at + row + tile, :])
                target = slice(below + 2 * row, below + 2 * (row + tile))
                total = acc_ref[target, :] + carry
                if level == 1:
                    local_ref[2 * row : 2 * (row + tile), :] = total
                else:
                    acc_ref[target, :] = total
        carry = None
        for index in range(len(far) - 1, -1, -1):
            level = far[index]
            count = 8 * devices // 2 ** (level - LOCAL)
            tree_ref[0:count, :] = jnp.zeros((count, 2 * WIDTH), f32) if carry is None else spread(carry)
            block = here_ref[0] >> (level - 6)
            last = count // BLOCK - 1
            for side, neighbour in enumerate((block - 1, block + 1)):
                start = pl.multiple_of(jnp.clip(neighbour, 0, last) * BLOCK, BLOCK)
                at = offsets[LOCAL + index] + side * BLOCK
                tree_ref[pl.ds(start, BLOCK), :] += acc_ref[at : at + BLOCK, :]
            carry = tree_ref[0:count, :]
        to_far_ref[...] = carry


def attend_back_call(rows, devices, far, here, q, grads, bias, logs, levels, left, right, base):
    chunks = rows // CHUNK
    _, entries = extended_offsets(rows, far)
    _, slots = slot_layout(far)
    edge = (BLOCK * LOCAL, 2 * WIDTH)
    return pl.pallas_call(
        partial(attend_back_kernel, rows, devices, far),
        grid=(chunks,),
        out_shape=[
            jax.ShapeDtypeStruct((rows, WIDTH), bf16),
            jax.ShapeDtypeStruct((rows, 2 * WIDTH), f32),
            jax.ShapeDtypeStruct(edge, bf16),
            jax.ShapeDtypeStruct(edge, bf16),
            jax.ShapeDtypeStruct((8 * devices, 2 * WIDTH), f32),
        ],
        in_specs=[
            pl.BlockSpec(memory_space=pltpu.SMEM),
            pl.BlockSpec((CHUNK, WIDTH), lambda i: (i, 0)),
            pl.BlockSpec((CHUNK, WIDTH), lambda i: (i, 0)),
            pl.BlockSpec((1, slots, CHUNK), lambda i: (i, 0, 0)),
            pl.BlockSpec((1, 8, 2 * CHUNK), lambda i: (i, 0, 0)),
        ]
        + vmem_specs(LOCAL + 3),
        out_specs=[pl.BlockSpec((CHUNK, WIDTH), lambda i: (i, 0))] + vmem_specs(4),
        scratch_shapes=[
            pltpu.VMEM((entries, 2 * WIDTH), bf16),
            pltpu.VMEM((8 * devices, 2 * WIDTH), bf16),
            pltpu.VMEM((slots, 2 * WIDTH), bf16),
            pltpu.VMEM((entries, 2 * WIDTH), f32),
            pltpu.VMEM((8 * devices, 2 * WIDTH), f32),
        ],
        compiler_params=pltpu.CompilerParams(vmem_limit_bytes=VMEM_LIMIT),
        cost_estimate=pl.CostEstimate(flops=40 << 30, bytes_accessed=24 << 20, transcendentals=4 << 20),
        name="attend_back",
    )(here, q, grads, bias, logs, *levels, left, right, base)


def normal_parts(values):
    size = jnp.abs(values)
    bell = jnp.exp(-0.5 * values * values)
    t = 1.0 / (1.0 + (0.3275911 / math.sqrt(2.0)) * size)
    poly = t * (
        0.5 * 0.254829592
        + t * (0.5 * -0.284496736 + t * (0.5 * 1.421413741 + t * (0.5 * -1.453152027 + t * (0.5 * 1.061405429))))
    )
    tail = poly * bell
    return jnp.where(values < 0, tail, 1.0 - tail), bell * (1.0 / math.sqrt(2.0 * math.pi))


def feed_kernel(
    hidden_width,
    x_ref,
    attended_ref,
    cot_ref,
    out_w_ref,
    up_w_ref,
    down_w_ref,
    vec_ref,
    up_bias_ref,
    y_ref,
    grad_middle_ref,
    grad_attended_ref,
    weights_ref,
    vec_grad_ref,
    up_bias_grad_ref,
    down_acc,
    up_acc,
    out_acc,
):
    step = pl.program_id(0)

    @pl.when(step == 0)
    def _():
        down_acc[...] = jnp.zeros_like(down_acc)
        up_acc[...] = jnp.zeros_like(up_acc)
        out_acc[...] = jnp.zeros_like(out_acc)
        vec_grad_ref[...] = jnp.zeros_like(vec_grad_ref)
        up_bias_grad_ref[...] = jnp.zeros_like(up_bias_grad_ref)

    out_bias, gain, shift, down_bias = (vec_ref[at : at + 1, :] for at in range(4))
    attended = attended_ref[...]
    middle = x_ref[...].astype(f32) + dot_nn(attended, out_w_ref[...]) + out_bias
    scaled, inverse = norm_rows(middle)
    normed = (scaled * gain + shift).astype(bf16)
    cot = cot_ref[...]
    wide = cot.astype(f32)
    lowered = jnp.zeros_like(middle)
    grad_normed = jnp.zeros_like(middle)
    part = 512
    for at in range(0, hidden_width, part):
        columns = slice(at, at + part)
        pre = dot_nn(normed, up_w_ref[:, columns]) + up_bias_ref[:, columns]
        phi, bell = normal_parts(pre)
        hidden = (pre * phi).astype(bf16)
        lowered += dot_nn(hidden, down_w_ref[columns, :])
        grad_hidden = dot_nt(cot, down_w_ref[columns, :])
        grad_pre_wide = grad_hidden * (phi + pre * bell)
        grad_pre = grad_pre_wide.astype(bf16)
        up_bias_grad_ref[:, columns] += jnp.sum(grad_pre.astype(f32), axis=0, keepdims=True)
        grad_normed += dot_nt(grad_pre, up_w_ref[:, columns])
        down_acc[columns, :] += dot_tn(hidden, cot)
        up_acc[:, columns] += dot_tn(normed, grad_pre)
    y_ref[...] = (middle + lowered + down_bias).astype(bf16)
    grad_middle = wide + norm_back(grad_normed, scaled, inverse, gain)
    grad_middle_ref[...] = grad_middle
    grad_proj = grad_middle.astype(bf16)
    grad_attended_ref[...] = dot_nt(grad_proj, out_w_ref[...]).astype(bf16)
    out_acc[...] += dot_tn(attended, grad_proj)
    vec_grad_ref[0:1, :] += jnp.sum(grad_proj.astype(f32), axis=0, keepdims=True)
    vec_grad_ref[1:2, :] += jnp.sum(grad_normed * scaled, axis=0, keepdims=True)
    vec_grad_ref[2:3, :] += jnp.sum(grad_normed, axis=0, keepdims=True)
    vec_grad_ref[3:4, :] += jnp.sum(wide, axis=0, keepdims=True)

    @pl.when(step == pl.num_programs(0) - 1)
    def _():
        owners = weights_ref.shape[0]
        wide_rows, rows = hidden_width // owners, WIDTH // owners
        for owner in range(owners):
            weights_ref[owner, 0:wide_rows, :] = down_acc[owner * wide_rows : (owner + 1) * wide_rows, :].astype(bf16)
            for block in range(hidden_width // WIDTH):
                at = wide_rows + block * rows
                weights_ref[owner, at : at + rows, :] = up_acc[
                    owner * rows : (owner + 1) * rows, block * WIDTH : (block + 1) * WIDTH
                ].astype(bf16)
            at = 2 * wide_rows
            weights_ref[owner, at : at + rows, :] = out_acc[owner * rows : (owner + 1) * rows, :].astype(bf16)


def feed_call(owners, x, attended, cot, out_w, up_w, down_w, vectors, up_bias):
    rows, hidden_width = x.shape[0], up_w.shape[1]
    tile = 256
    row_spec = pl.BlockSpec((tile, WIDTH), lambda i: (i, 0))
    packed = 2 * (hidden_width // owners) + WIDTH // owners
    return pl.pallas_call(
        partial(feed_kernel, hidden_width),
        grid=(rows // tile,),
        out_shape=[
            jax.ShapeDtypeStruct((rows, WIDTH), bf16),
            jax.ShapeDtypeStruct((rows, WIDTH), f32),
            jax.ShapeDtypeStruct((rows, WIDTH), bf16),
            jax.ShapeDtypeStruct((owners, packed, WIDTH), bf16),
            jax.ShapeDtypeStruct((8, WIDTH), f32),
            jax.ShapeDtypeStruct((1, hidden_width), f32),
        ],
        in_specs=[row_spec, row_spec, row_spec] + vmem_specs(5),
        out_specs=[row_spec, row_spec, row_spec] + vmem_specs(3),
        scratch_shapes=[
            pltpu.VMEM((hidden_width, WIDTH), f32),
            pltpu.VMEM((WIDTH, hidden_width), f32),
            pltpu.VMEM((WIDTH, WIDTH), f32),
        ],
        compiler_params=pltpu.CompilerParams(vmem_limit_bytes=VMEM_LIMIT),
        cost_estimate=pl.CostEstimate(flops=15 << 30, bytes_accessed=20 << 20, transcendentals=4 << 20),
        name="feed_forward",
    )(x, attended, cot, out_w, up_w, down_w, vectors, up_bias)


def project_back_kernel(
    rows,
    x_ref,
    normed_ref,
    dq_ref,
    local_ref,
    grad_middle_ref,
    from_right_ref,
    from_left_ref,
    base_ref,
    w_ref,
    gain_ref,
    input_grad_ref,
    weights_ref,
    vec_grad_ref,
    tree_ref,
    acc_ref,
):
    carry = spread(base_ref[...])
    for level in range(LOCAL - 1, -1, -1):
        count = level_rows(rows, level)
        edge = slice(BLOCK * level, BLOCK * (level + 1))
        if level == LOCAL - 1:
            tree_ref[0:count, :] = carry
        tree_ref[0:BLOCK, :] += from_left_ref[edge, :].astype(f32)
        tree_ref[count - BLOCK : count, :] += from_right_ref[edge, :].astype(f32)
        if level:
            tile = min(count, 128)
            for row in range(count - tile, -1, -tile):
                tree_ref[2 * row : 2 * (row + tile), :] = spread(tree_ref[row : row + tile, :])
    acc_ref[...] = jnp.zeros_like(acc_ref)
    vec_grad_ref[...] = jnp.zeros_like(vec_grad_ref)
    tile = 256

    def body(at, _):
        span = pl.ds(pl.multiple_of(at * tile, tile), tile)
        scaled, inverse = norm_rows(x_ref[span, :].astype(f32))
        normed = normed_ref[span, :]
        dkv = (local_ref[span, :] + tree_ref[span, :]).astype(bf16)
        dq = dq_ref[span, :]
        acc_ref[:, :WIDTH] += dot_tn(normed, dq)
        acc_ref[:, WIDTH:] += dot_tn(normed, dkv)
        grad = dot_nt(dq, w_ref[:, :WIDTH]) + dot_nt(dkv, w_ref[:, WIDTH:])
        input_grad_ref[span, :] = grad_middle_ref[span, :] + norm_back(grad, scaled, inverse, gain_ref[...])
        vec_grad_ref[0:1, :] += jnp.sum(grad * scaled, axis=0, keepdims=True)
        vec_grad_ref[1:2, :] += jnp.sum(grad, axis=0, keepdims=True)
        vec_grad_ref[2:3, :] += jnp.sum(dq.astype(f32), axis=0, keepdims=True)
        vec_grad_ref[3:4, :] += jnp.sum(dkv[:, WIDTH:].astype(f32), axis=0, keepdims=True)
        return 0

    lax.fori_loop(0, rows // tile, body, 0)
    owners = weights_ref.shape[0]
    part = WIDTH // owners
    for owner in range(owners):
        for block in range(3):
            weights_ref[owner, block * part : (block + 1) * part, :] = acc_ref[
                owner * part : (owner + 1) * part, block * WIDTH : (block + 1) * WIDTH
            ].astype(bf16)


def project_back_call(owners, x, normed, dq, local, grad_middle, from_right, from_left, base, weight, gain):
    rows = x.shape[0]
    return pl.pallas_call(
        partial(project_back_kernel, rows),
        out_shape=[
            jax.ShapeDtypeStruct((rows, WIDTH), f32),
            jax.ShapeDtypeStruct((owners, 3 * WIDTH // owners, WIDTH), bf16),
            jax.ShapeDtypeStruct((8, WIDTH), f32),
        ],
        in_specs=vmem_specs(10),
        out_specs=vmem_specs(3),
        scratch_shapes=[pltpu.VMEM((rows, 2 * WIDTH), f32), pltpu.VMEM((WIDTH, 3 * WIDTH), f32)],
        compiler_params=pltpu.CompilerParams(vmem_limit_bytes=VMEM_LIMIT),
        cost_estimate=pl.CostEstimate(flops=4 << 30, bytes_accessed=20 << 20, transcendentals=0),
        name="project_back",
    )(x, normed, dq, local, grad_middle, from_right, from_left, base, weight, gain)


def shifted(block, axis, distance):
    devices = range(lax.axis_size(axis))
    route = [(i - distance, i) for i in devices if i - distance in devices]
    return lax.ppermute(block, axis, route)


def swap(block, axis, bit):
    return lax.ppermute(block, axis, [(i, i ^ bit) for i in range(lax.axis_size(axis))])


def add_low(left, right):
    return (left.astype(f32) + right.astype(f32)).astype(bf16)


def scatter_step(parts, axis, bit):
    mine = (lax.axis_index(axis) // bit) % 2
    keep = lax.dynamic_index_in_dim(parts, mine, 0, keepdims=False)
    send = lax.dynamic_index_in_dim(parts, 1 - mine, 0, keepdims=False)
    return add_low(keep, swap(send, axis, bit))


def gather_step(part, axis, bit):
    mine = (lax.axis_index(axis) // bit) % 2
    other = swap(part, axis, bit)
    first = jnp.where(mine == 0, part, other)
    second = jnp.where(mine == 0, other, part)
    return jnp.concatenate([first, second], axis=0)


def gather_ctx(block, axis):
    bit = 1
    while bit < lax.axis_size(axis):
        block = gather_step(block, axis, bit)
        bit *= 2
    return block


def scatter_ctx(block, axis):
    bit = lax.axis_size(axis) // 2
    while bit >= 1:
        block = scatter_step(block.reshape(2, block.shape[0] // 2, *block.shape[1:]), axis, bit)
        bit //= 2
    return block


def reduce_weights(parts):
    owners = parts.shape[0]
    shape = parts.shape[1:]
    current = parts.reshape(owners // 2, 2, *shape).transpose(1, 0, 2, 3)
    current = scatter_step(current, "fsdp", 1)
    bit = 2
    while bit < owners:
        current = current.reshape(-1, 2, *shape).transpose(1, 0, 2, 3)
        current = scatter_step(current, "fsdp", bit)
        bit *= 2
    current = current.reshape(shape)
    bit = 1
    bits = []
    while bit < lax.axis_size("ctx"):
        current = scatter_step(current.reshape(2, current.shape[0] // 2, shape[1]), "ctx", bit)
        bits.append(bit)
        bit *= 2
    for bit in reversed(bits):
        current = gather_step(current, "ctx", bit)
    return current.astype(f32)


def shards(
    layer_input,
    doc_lengths,
    ln1_gain,
    ln1_bias,
    qkv_weight,
    query_bias,
    value_bias,
    out_weight,
    out_bias,
    ln2_gain,
    ln2_bias,
    up_weight,
    up_bias,
    down_weight,
    down_bias,
    cotangent,
):
    owners = lax.axis_size("fsdp")
    devices = lax.axis_size("ctx")
    x, cot = layer_input[0], cotangent[0]
    rows = x.shape[0]
    total = rows * devices
    far = far_levels(total)
    here = lax.axis_index("ctx")
    part = WIDTH // owners

    small = jnp.concatenate(
        [ln1_gain, ln1_bias, query_bias, value_bias, out_bias, ln2_gain, ln2_bias, down_bias, up_bias]
    )
    gathered = lax.all_gather(small, "fsdp", axis=0, tiled=False)
    vectors = [gathered[:, at * part : (at + 1) * part].reshape(1, WIDTH).astype(f32) for at in range(8)]
    up_shift = gathered[:, 8 * part :].reshape(1, -1).astype(f32)
    gain_first, shift_first, query_shift, value_shift = vectors[:4]
    feed_vectors = jnp.concatenate(vectors[4:] + [jnp.zeros((4, WIDTH), f32)], axis=0)
    qkv_shift = jnp.concatenate([query_shift, jnp.zeros_like(query_shift), value_shift], axis=1)

    qkv_full = lax.all_gather(qkv_weight, "fsdp", axis=0, tiled=True)
    out_full = lax.all_gather(out_weight, "fsdp", axis=0, tiled=True)
    up_full = lax.all_gather(up_weight, "fsdp", axis=0, tiled=True)
    down_full = lax.all_gather(down_weight, "fsdp", axis=0, tiled=True)

    starts = jnp.cumsum(doc_lengths[0]) - doc_lengths[0]
    bias = score_bias(rows, total, here * rows, starts, far)

    normed, queries, *levels = qkv_call(rows, x, qkv_full, qkv_shift, gain_first, shift_first)
    levels, tail, head = levels[:LOCAL], levels[LOCAL], levels[LOCAL + 1]
    left = shifted(tail, "ctx", 1)
    right = shifted(head, "ctx", -1)
    base = gather_ctx(levels[LOCAL - 1], "ctx")

    here_array = here.reshape(1).astype(jnp.int32)
    attended, logs = attend_call(rows, devices, far, here_array, queries, bias, levels, left, right, base)
    output, grad_middle, grad_attended, feed_grads, vec_grads, up_bias_grad = feed_call(
        owners, x, attended, cot, out_full, up_full, down_full, feed_vectors, up_shift
    )
    extra = jnp.zeros((owners, 32, WIDTH), bf16)
    extra = extra.at[:, 0, :].set(vec_grads[:4].reshape(4, owners, part).transpose(1, 0, 2).reshape(owners, -1).astype(bf16))
    extra = extra.at[:, 1, :].set(up_bias_grad.reshape(owners, -1).astype(bf16))
    feed_sum = reduce_weights(jnp.concatenate([feed_grads, extra], axis=1))

    dq, local, to_left, to_right, to_far = attend_back_call(
        rows, devices, far, here_array, queries, grad_attended, bias, logs, levels, left, right, base
    )
    back_right = shifted(to_left, "ctx", -1)
    back_left = shifted(to_right, "ctx", 1)
    back_far = scatter_ctx(to_far, "ctx").astype(f32)
    input_grad, qkv_grads, first_grads = project_back_call(
        owners, x, normed, dq, local, grad_middle, back_right, back_left, back_far, qkv_full, gain_first
    )
    extra = jnp.zeros((owners, 32, WIDTH), bf16)
    extra = extra.at[:, 0, :].set(first_grads[:4].reshape(4, owners, part).transpose(1, 0, 2).reshape(owners, -1).astype(bf16))
    qkv_sum = reduce_weights(jnp.concatenate([qkv_grads, extra], axis=1))

    wide = up_weight.shape[1]
    wide_rows = wide // owners
    down_grad = feed_sum[:wide_rows]
    up_grad = jnp.concatenate(
        [feed_sum[wide_rows + at * part : wide_rows + (at + 1) * part] for at in range(wide // WIDTH)], axis=1
    )
    out_grad = feed_sum[2 * wide_rows : 2 * wide_rows + part]
    feed_row = feed_sum[2 * wide_rows + part]
    up_row = feed_sum[2 * wide_rows + part + 1]
    qkv_grad = jnp.concatenate([qkv_sum[at * part : (at + 1) * part] for at in range(3)], axis=1)
    first_row = qkv_sum[3 * part]
    pick = lambda row, at: row[at * part : (at + 1) * part]
    return (
        output[None],
        input_grad[None],
        pick(first_row, 0),
        pick(first_row, 1),
        qkv_grad,
        pick(first_row, 2),
        pick(first_row, 3),
        out_grad,
        pick(feed_row, 0),
        pick(feed_row, 1),
        pick(feed_row, 2),
        up_grad,
        up_row,
        down_grad,
        pick(feed_row, 3),
    )


def solution(mesh):
    row, vector = P("fsdp", None), P("fsdp")
    tokens = P("fsdp", "ctx", None)
    return jax.shard_map(
        shards,
        mesh=mesh,
        in_specs=(
            tokens,
            row,
            vector,
            vector,
            row,
            vector,
            vector,
            row,
            vector,
            vector,
            vector,
            row,
            vector,
            row,
            vector,
            tokens,
        ),
        out_specs=(
            tokens,
            tokens,
            vector,
            vector,
            row,
            vector,
            vector,
            row,
            vector,
            vector,
            vector,
            row,
            vector,
            row,
            vector,
        ),
        check_vma=False,
    )
```

```python
from functools import partial
import math

import jax
import jax.numpy as jnp
from jax import lax
from jax.experimental import pallas as pl
from jax.experimental.pallas import tpu as pltpu
from jax.sharding import PartitionSpec as P

HEADS = 8
BLOCK = 16
LEVELS = 10
NEAR = 4
LOCAL = 7
CHUNK = 128
WIDTH = 512
PAIRS = HEADS // 2
ENTRY = 3 * WIDTH
SMALL = 16
MASKED = -1e30
EPSILON = 1e-05
VMEM_LIMIT = 56 * 1024 * 1024

f32 = jnp.float32
bf16 = jnp.bfloat16


def level_rows(rows, level):
    return rows // 2**level


def far_levels(total):
    return [l for l in range(LOCAL, LEVELS) if total // (BLOCK * 2**l) >= 2]


def extended_offsets(rows, far):
    offsets, cursor = [], 0
    for level in range(LOCAL):
        offsets.append(cursor)
        cursor += level_rows(rows, level) + 2 * BLOCK
    for _ in far:
        offsets.append(cursor)
        cursor += 2 * BLOCK
    return offsets, cursor


def slot_layout(far):
    parts = [(level, CHUNK // 2**level + 2 * BLOCK) for level in range(NEAR)]
    parts += [(level, BLOCK) for level in list(range(NEAR, LOCAL)) + far for _ in range(2)]
    return parts, sum(count for _, count in parts)


def slot_sources(rows, far, chunk):
    offsets, _ = extended_offsets(rows, far)
    sources = []
    for level in range(NEAR):
        sources.append((offsets[level] + chunk * (CHUNK // 2**level), CHUNK // 2**level + 2 * BLOCK))
    for level in range(NEAR, LOCAL):
        block = chunk // (BLOCK * 2**level // CHUNK)
        sources.append((offsets[level] + block * BLOCK, BLOCK))
        sources.append((offsets[level] + block * BLOCK + 2 * BLOCK, BLOCK))
    for at in range(len(far)):
        sources.append((offsets[LOCAL + at], BLOCK))
        sources.append((offsets[LOCAL + at] + BLOCK, BLOCK))
    return sources


def count_starts(positions, starts):
    total = jnp.full(positions.shape, -1, jnp.int32)
    for start in starts:
        total = total + (start <= positions).astype(jnp.int32)
    return total


def mask_kernel(rows, total, far, here_ref, lengths_ref, bias_ref):
    starts, start = [], jnp.int32(0)
    for at in range(lengths_ref.shape[1]):
        starts.append(start)
        start = start + lengths_ref[0, at]
    base = here_ref[0] * rows + pl.program_id(0) * CHUNK
    query = base + lax.broadcasted_iota(jnp.int32, (1, CHUNK), 1)
    query_doc = count_starts(query, starts)

    def part(at, count, first_row, level):
        span = 2**level
        shift = level + 4
        first = first_row + span * lax.broadcasted_iota(jnp.int32, (count, CHUNK), 0)
        gap = jnp.abs((first >> shift) - (query >> shift))
        if level == 0:
            seen = gap <= 1
        else:
            seen = (gap == 1) & (jnp.abs((first >> (shift - 1)) - (query >> (shift - 1))) > 1)
        doc = count_starts(first, starts)
        seen = seen & (first >= 0) & (first < total) & (doc == query_doc)
        if level:
            seen = seen & (count_starts(first + (span - 1), starts) == doc)
        bias_ref[0, at : at + count, :] = jnp.where(seen, level * math.log(2.0), MASKED)

    at = 0
    for level in range(NEAR):
        count = CHUNK // 2**level + 2 * BLOCK
        part(at, count, base - BLOCK * 2**level, level)
        at += count
    for level in list(range(NEAR, LOCAL)) + far:
        block = base >> (level + 4)
        for side in (-1, 1):
            part(at, BLOCK, (block + side) * (BLOCK * 2**level), level)
            at += BLOCK


def mask_call(rows, total, far, meta, lengths):
    chunks = rows // CHUNK
    _, slots = slot_layout(far)
    return pl.pallas_call(
        partial(mask_kernel, rows, total, far),
        grid=(chunks,),
        out_shape=jax.ShapeDtypeStruct((chunks, slots, CHUNK), f32),
        in_specs=[pl.BlockSpec(memory_space=pltpu.SMEM)] * 2,
        out_specs=pl.BlockSpec((1, slots, CHUNK), lambda i: (i, 0, 0)),
        cost_estimate=pl.CostEstimate(flops=4 << 30, bytes_accessed=3 << 20, transcendentals=0),
        name="mask",
    )(meta, lengths)


def dot_nt(left, right):
    return lax.dot_general(left, right, (((1,), (1,)), ((), ())), preferred_element_type=f32)


def dot_tn(left, right):
    return lax.dot_general(left, right, (((0,), (0,)), ((), ())), preferred_element_type=f32)


def dot_nn(left, right):
    return jnp.dot(left, right, preferred_element_type=f32)


def pool_matrix(count):
    row = lax.broadcasted_iota(jnp.int32, (count // 2, count), 0)
    column = lax.broadcasted_iota(jnp.int32, (count // 2, count), 1)
    return jnp.where((column >> 1) == row, 0.5, 0.0).astype(bf16)


def spread_matrix(count):
    row = lax.broadcasted_iota(jnp.int32, (2 * count, count), 0)
    column = lax.broadcasted_iota(jnp.int32, (2 * count, count), 1)
    return jnp.where((row >> 1) == column, 0.5, 0.0).astype(bf16)


def spread(values):
    count = values.shape[0]
    tile = min(count, 128)
    matrix = spread_matrix(tile)
    high = values.astype(bf16)
    low = (values - high.astype(f32)).astype(bf16)
    parts = [
        dot_nn(matrix, high[at : at + tile]) + dot_nn(matrix, low[at : at + tile])
        for at in range(0, count, tile)
    ]
    return parts[0] if len(parts) == 1 else jnp.concatenate(parts, axis=0)


def norm_rows(values):
    mean = jnp.mean(values, axis=-1, keepdims=True)
    centred = values - mean
    variance = jnp.mean(centred * centred, axis=-1, keepdims=True)
    inverse = lax.rsqrt(variance + EPSILON)
    return centred * inverse, inverse


def norm_back(grad_out, scaled, inverse, gain):
    grad_scaled = grad_out * gain
    first = jnp.mean(grad_scaled, axis=-1, keepdims=True)
    second = jnp.mean(grad_scaled * scaled, axis=-1, keepdims=True)
    return inverse * (grad_scaled - first - scaled * second)


def split_heads(pair):
    lane = lax.broadcasted_iota(jnp.int32, pair.shape, 1)
    zero = jnp.zeros_like(pair)
    return jnp.concatenate([jnp.where(lane < 64, pair, zero), jnp.where(lane < 64, zero, pair)], axis=0)


def join_heads(stacked):
    rows = stacked.shape[0] // 2
    lane = lax.broadcasted_iota(jnp.int32, (rows, stacked.shape[1]), 1)
    return jnp.where(lane < 64, stacked[:rows], stacked[rows:])


def pack_kernel(w_ref, *refs):
    out_ref = refs[-1]
    part = w_ref.shape[0]
    out_ref[0:part, :] = w_ref[...]
    row = jnp.concatenate([ref[...].reshape(1, -1) for ref in refs[:-1]], axis=1)
    out_ref[part : part + SMALL, :] = jnp.broadcast_to(row.astype(f32), (SMALL, row.shape[1])).astype(bf16)


def pack_call(weight, vectors):
    return pl.pallas_call(
        pack_kernel,
        out_shape=jax.ShapeDtypeStruct((weight.shape[0] + SMALL, weight.shape[1]), bf16),
        in_specs=vmem_specs(1 + len(vectors)),
        out_specs=vmem_specs(1)[0],
        name="pack",
    )(weight, *vectors)


def vmem_specs(count):
    return [pl.BlockSpec(memory_space=pltpu.VMEM)] * count


def qkv_kernel(rows, owners, meta_ref, x_ref, *refs):
    shard_refs, refs = refs[:owners], refs[owners:]
    w_ref, vec_ref, up_bias_ref, q_ref = refs[:4]
    kv_refs, scaled_refs = refs[4 : 4 + LOCAL], refs[4 + LOCAL : 4 + 2 * LOCAL]
    tail_ref, head_ref = refs[4 + 2 * LOCAL : 6 + 2 * LOCAL]
    keep_ref = refs[6 + 2 * LOCAL]
    part = WIDTH // owners
    step = pl.program_id(0)

    @pl.when(step == 0)
    def _():
        for at, ref in enumerate(shard_refs):
            owner = meta_ref[1 + at]
            w_ref[pl.ds(pl.multiple_of(owner * part, part), part), :] = ref[0:part, :]
            row = ref[part : part + 1, :].astype(f32)
            for vector in range(8):
                vec_ref[vector : vector + 1, pl.ds(pl.multiple_of(owner * part, part), part)] = row[
                    :, vector * part : (vector + 1) * part
                ]
            wide = row.shape[1] - 8 * part
            up_bias_ref[:, pl.ds(pl.multiple_of(owner * wide, wide), wide)] = row[:, 8 * part :]

    tile = x_ref.shape[0]
    scaled, _ = norm_rows(x_ref[...].astype(f32))
    normed = (scaled * vec_ref[0:1, :] + vec_ref[1:2, :]).astype(bf16)
    queries = (dot_nn(normed, w_ref[:, :WIDTH]) + vec_ref[2:3, :]).astype(bf16)
    q_ref[...] = queries * jnp.asarray(0.125, bf16)
    keys = dot_nn(normed, w_ref[:, WIDTH : 2 * WIDTH]).astype(bf16)
    values = (dot_nn(normed, w_ref[:, 2 * WIDTH :]) + vec_ref[3:4, :]).astype(bf16)
    current = jnp.concatenate([keys, values, scaled.astype(bf16)], axis=1)

    def edges(level, block):
        @pl.when(step == 0)
        def _():
            head_ref[BLOCK * level : BLOCK * (level + 1), :] = block[:BLOCK]

        @pl.when(step == pl.num_programs(0) - 1)
        def _():
            tail_ref[BLOCK * level : BLOCK * (level + 1), :] = block[block.shape[0] - BLOCK :]

    for level in range(5):
        if level:
            current = dot_nn(pool_matrix(current.shape[0]), current).astype(bf16)
        kv_refs[level][...] = current[:, : 2 * WIDTH]
        scaled_refs[level][...] = current[:, 2 * WIDTH :]
        edges(level, current)
    count = tile // 16
    keep_ref[pl.ds(pl.multiple_of(step * count, count), count), :] = current

    @pl.when(step == pl.num_programs(0) - 1)
    def _():
        current = keep_ref[...]
        for level in range(5, LOCAL):
            current = dot_nn(pool_matrix(current.shape[0]), current).astype(bf16)
            kv_refs[level][...] = current[:, : 2 * WIDTH]
            scaled_refs[level][...] = current[:, 2 * WIDTH :]
            tail_ref[BLOCK * level : BLOCK * (level + 1), :] = current[current.shape[0] - BLOCK :]
            head_ref[BLOCK * level : BLOCK * (level + 1), :] = current[:BLOCK]


def qkv_call(rows, hidden_width, meta, x, pieces):
    owners = len(pieces)
    tile = 256

    def tiled(count, width):
        return pl.BlockSpec((count, width), lambda i: (i, 0))

    def leveled(width):
        shapes, specs = [], []
        for level in range(LOCAL):
            shapes.append(jax.ShapeDtypeStruct((level_rows(rows, level), width), bf16))
            specs.append(tiled(tile // 2**level, width) if level < 5 else vmem_specs(1)[0])
        return shapes, specs

    kv_shapes, kv_specs = leveled(2 * WIDTH)
    scaled_shapes, scaled_specs = leveled(WIDTH)
    edge = jax.ShapeDtypeStruct((BLOCK * LOCAL, ENTRY), bf16)
    outs = pl.pallas_call(
        partial(qkv_kernel, rows, owners),
        grid=(rows // tile,),
        out_shape=[
            jax.ShapeDtypeStruct((WIDTH, 3 * WIDTH), bf16),
            jax.ShapeDtypeStruct((8, WIDTH), f32),
            jax.ShapeDtypeStruct((1, hidden_width), f32),
            jax.ShapeDtypeStruct((rows, WIDTH), bf16),
        ]
        + kv_shapes
        + scaled_shapes
        + [edge, edge],
        in_specs=[pl.BlockSpec(memory_space=pltpu.SMEM), tiled(tile, WIDTH)] + vmem_specs(owners),
        out_specs=vmem_specs(3) + [tiled(tile, WIDTH)] + kv_specs + scaled_specs + vmem_specs(2),
        scratch_shapes=[pltpu.VMEM((level_rows(rows, 4), ENTRY), bf16)],
        compiler_params=pltpu.CompilerParams(vmem_limit_bytes=VMEM_LIMIT),
        cost_estimate=pl.CostEstimate(flops=9 << 30, bytes_accessed=12 << 20, transcendentals=0),
        name="qkv_levels",
    )(meta, x, *pieces)
    weight, vectors, up_bias, queries = outs[:4]
    return weight, vectors, up_bias, queries, outs[4 : 4 + LOCAL], outs[4 + LOCAL : 4 + 2 * LOCAL], outs[-2], outs[-1]


def far_level(entries):
    return dot_nn(pool_matrix(entries.shape[0]), entries).astype(bf16)


def assemble(rows, far, here, columns, level_refs, left_ref, right_ref, base_ref, ext_ref, far_ref):
    offsets, _ = extended_offsets(rows, far)
    for inner, outer, target, width in columns:
        lanes, edge_lanes = slice(target, target + width), slice(outer, outer + width)
        for level in range(LOCAL):
            at, count = offsets[level], level_rows(rows, level)
            edge = slice(BLOCK * level, BLOCK * (level + 1))
            ext_ref[at : at + BLOCK, lanes] = left_ref[edge, edge_lanes]
            ext_ref[at + BLOCK : at + BLOCK + count, lanes] = level_refs[level][:, inner : inner + width]
            ext_ref[at + BLOCK + count : at + 2 * BLOCK + count, lanes] = right_ref[edge, edge_lanes]
        current = base_ref[:, edge_lanes]
        for index, level in enumerate(far):
            current = far_level(current)
            count = current.shape[0]
            far_ref[0:count, 0:width] = current
            for side, start in enumerate(far_starts(here, level, count)):
                at = offsets[LOCAL + index] + side * BLOCK
                ext_ref[at : at + BLOCK, lanes] = far_ref[pl.ds(start, BLOCK), 0:width]


def far_starts(here, level, count):
    block = here >> (level - 6)
    last = count // BLOCK - 1
    return [pl.multiple_of(jnp.clip(at, 0, last) * BLOCK, BLOCK) for at in (block - 1, block + 1)]


def load_slots(rows, far, chunk, ext_ref, slots_ref):
    at = 0
    for start, count in slot_sources(rows, far, chunk):
        if not isinstance(start, int):
            start = pl.multiple_of(start, BLOCK)
        slots_ref[at : at + count, :] = ext_ref[pl.ds(start, count), :]
        at += count


def attend_kernel(rows, far, meta_ref, q_ref, bias_ref, *refs):
    level_refs, refs = refs[:LOCAL], refs[LOCAL:]
    left_ref, right_ref, base_ref, out_ref, log_ref, ext_ref, far_ref, slots_ref = refs
    chunk = pl.program_id(0)

    @pl.when(chunk == 0)
    def _():
        columns = [(0, 0, 0, 2 * WIDTH)]
        assemble(rows, far, meta_ref[0], columns, level_refs, left_ref, right_ref, base_ref, ext_ref, far_ref)

    load_slots(rows, far, chunk, ext_ref, slots_ref)
    bias = bias_ref[0]
    bias = jnp.concatenate([bias, bias], axis=1)
    for pair in range(PAIRS):
        lanes = slice(128 * pair, 128 * (pair + 1))
        values = slots_ref[:, WIDTH + 128 * pair : WIDTH + 128 * (pair + 1)]
        scores = dot_nt(slots_ref[:, lanes], split_heads(q_ref[:, lanes])) + bias
        top = jnp.max(scores, axis=0, keepdims=True)
        exponent = jnp.exp(scores - top)
        total = jnp.sum(exponent, axis=0, keepdims=True)
        probs = (exponent * (1.0 / total)).astype(bf16)
        out_ref[:, lanes] = join_heads(dot_tn(probs, values)).astype(bf16)
        log_ref[0, pair : pair + 1, :] = top + jnp.log(total)


def attend_call(rows, devices, far, meta, q, bias, levels, left, right, base):
    chunks = rows // CHUNK
    _, entries = extended_offsets(rows, far)
    _, slots = slot_layout(far)
    return pl.pallas_call(
        partial(attend_kernel, rows, far),
        grid=(chunks,),
        out_shape=[
            jax.ShapeDtypeStruct((rows, WIDTH), bf16),
            jax.ShapeDtypeStruct((chunks, 8, 2 * CHUNK), f32),
        ],
        in_specs=[
            pl.BlockSpec(memory_space=pltpu.SMEM),
            pl.BlockSpec((CHUNK, WIDTH), lambda i: (i, 0)),
            pl.BlockSpec((1, slots, CHUNK), lambda i: (i, 0, 0)),
        ]
        + vmem_specs(LOCAL + 3),
        out_specs=[
            pl.BlockSpec((CHUNK, WIDTH), lambda i: (i, 0)),
            pl.BlockSpec((1, 8, 2 * CHUNK), lambda i: (i, 0, 0)),
        ],
        scratch_shapes=[
            pltpu.VMEM((entries, 2 * WIDTH), bf16),
            pltpu.VMEM((8 * devices, 2 * WIDTH), bf16),
            pltpu.VMEM((slots, 2 * WIDTH), bf16),
        ],
        compiler_params=pltpu.CompilerParams(vmem_limit_bytes=VMEM_LIMIT),
        cost_estimate=pl.CostEstimate(flops=20 << 30, bytes_accessed=12 << 20, transcendentals=4 << 20),
        name="attend",
    )(meta, q, bias, *levels, left, right, base)


def column_sum(values):
    return jnp.sum(values, axis=0, keepdims=True)


def matrix_row(left, right):
    total = None
    for a in two_parts(left):
        for b in two_parts(right):
            term = dot_nt(a, b)
            total = term if total is None else total + term
    return total[0:1]


def two_parts(values):
    if values.dtype == bf16:
        return [values]
    high = values.astype(bf16)
    return [high, (values - high.astype(f32)).astype(bf16)]


def attend_back_kernel(rows, far, first, count_pairs, combine, *refs):
    refs = list(refs)
    take = lambda count: [refs.pop(0) for _ in range(count)]
    meta_ref, q_ref, grad_ref, bias_ref, log_ref = take(5)
    level_refs, scaled_refs = take(LOCAL), take(LOCAL)
    left_ref, right_ref, base_ref, w_ref, vec_ref = take(5)
    if combine:
        before_left, before_right, before_far, before_weights, before_vec = take(5)
    dq_ref, local_ref, to_left_ref, to_right_ref, to_far_ref, weights_ref = take(6)
    vec_grad_ref = None if combine else take(1)[0]
    ext_ref, far_ref, slots_ref, acc_ref, tree_ref, scaled_ref, dq_keep_ref = take(7)
    chunk = pl.program_id(0)
    offsets, entries = extended_offsets(rows, far)
    half = 128 * count_pairs
    lane = 128 * first

    @pl.when(chunk == 0)
    def _():
        columns = [(lane, lane, 0, half), (WIDTH + lane, WIDTH + lane, half, half)]
        common = (left_ref, right_ref, base_ref)
        assemble(rows, far, meta_ref[0], columns, level_refs, *common, ext_ref, far_ref)
        assemble(rows, far, meta_ref[0], [(0, 2 * WIDTH, 0, WIDTH)], scaled_refs, *common, scaled_ref, far_ref)
        acc_ref[...] = jnp.zeros_like(acc_ref)

    load_slots(rows, far, chunk, ext_ref, slots_ref)
    bias = bias_ref[0]
    bias = jnp.concatenate([bias, bias], axis=1)
    sources = slot_sources(rows, far, chunk)
    for pair in range(count_pairs):
        lanes = slice(128 * pair, 128 * (pair + 1))
        value_lanes = slice(half + 128 * pair, half + 128 * (pair + 1))
        keys, values = slots_ref[:, lanes], slots_ref[:, value_lanes]
        queries, grads = split_heads(q_ref[:, lanes]), split_heads(grad_ref[:, lanes])
        logs = log_ref[0, first + pair : first + pair + 1, :]
        probs = jnp.exp(dot_nt(keys, queries) + bias - logs)
        grad_probs = dot_nt(values, grads)
        delta = jnp.sum(probs * grad_probs, axis=0, keepdims=True)
        grad_scores = (probs * (grad_probs - delta)).astype(bf16)
        dq = (join_heads(dot_tn(grad_scores, keys)) * 0.125).astype(bf16)
        dq_ref[:, lanes] = dq
        dq_keep_ref[pl.ds(pl.multiple_of(chunk * CHUNK, CHUNK), CHUNK), lanes] = dq
        grad_keys = dot_nn(grad_scores, queries)
        grad_values = dot_nn(probs.astype(bf16), grads)
        at = 0
        for start, count in sources:
            if not isinstance(start, int):
                start = pl.multiple_of(start, BLOCK)
            acc_ref[pl.ds(start, count), lanes] += grad_keys[at : at + count]
            acc_ref[pl.ds(start, count), value_lanes] += grad_values[at : at + count]
            at += count

    @pl.when(chunk == pl.num_programs(0) - 1)
    def _():
        dq = dq_keep_ref[...]
        sums = [column_sum(dq.astype(f32)), column_sum(acc_ref[:, :half]), column_sum(acc_ref[:, half:])]
        parts = [
            dot_tn(scaled_refs[0][...], dq),
            dot_tn(scaled_ref[...], acc_ref[:, :half].astype(bf16)),
            dot_tn(scaled_ref[...], acc_ref[:, half:].astype(bf16)),
        ]
        first_row = lax.broadcasted_iota(jnp.int32, (16, 1), 0) == 0
        ones = jnp.where(first_row, jnp.ones((16, half), f32), 0.0).astype(bf16)
        as_column = lambda row: dot_tn(jnp.where(first_row, row, 0.0).astype(bf16), ones)
        gain, shift = as_column(vec_ref[0:1, :]), as_column(vec_ref[1:2, :])
        gain_grad, shift_grad = jnp.zeros((1, WIDTH), f32), jnp.zeros((1, WIDTH), f32)
        owners = weights_ref.shape[0]
        part = WIDTH // owners
        for block in range(3):
            weight = w_ref[:, block * WIDTH + lane : block * WIDTH + lane + half]
            wide = weight.astype(f32)
            gain_grad += matrix_row(jnp.ones((16, half), bf16), wide * parts[block])
            shift_grad += matrix_row(jnp.broadcast_to(sums[block], (16, half)), weight)
            grad = (gain * parts[block] + shift * sums[block]).astype(bf16)
            for owner in range(owners):
                weights_ref[owner, block * part : (block + 1) * part, lane * combine : lane * combine + half] = grad[
                    owner * part : (owner + 1) * part
                ]
        if combine:
            for owner in range(owners):
                weights_ref[owner, 0 : 3 * part, 0:lane] = before_weights[owner, 0 : 3 * part, :]
            extend = lambda row, at: jnp.concatenate([before_vec[at : at + 1, 0:lane], row], axis=1)
            rows_out = [
                before_vec[0:1, :] + gain_grad,
                before_vec[1:2, :] + shift_grad,
                extend(sums[0], 2),
                extend(sums[2], 3),
            ]
            extra = weights_ref.shape[1] - 3 * part
            top_row = lax.broadcasted_iota(jnp.int32, (extra, 1), 0) == 0
            for owner in range(owners):
                row = jnp.concatenate([r[:, owner * part : (owner + 1) * part] for r in rows_out], axis=1)
                weights_ref[owner, 3 * part :, :] = jnp.where(top_row, row, 0.0).astype(bf16)
        else:
            vec_grad_ref[...] = jnp.zeros_like(vec_grad_ref)
            vec_grad_ref[0:1, :] = gain_grad
            vec_grad_ref[1:2, :] = shift_grad
            vec_grad_ref[2:3, 0:half] = sums[0]
            vec_grad_ref[3:4, 0:half] = sums[2]

        def put(target, values, before):
            if combine:
                target[:, 0:lane] = before[:, 0:lane]
                target[:, WIDTH : WIDTH + lane] = before[:, lane:]
                target[:, lane : lane + half] = values[:, :half].astype(bf16)
                target[:, WIDTH + lane : WIDTH + lane + half] = values[:, half:].astype(bf16)
            else:
                target[...] = values.astype(bf16)

        lefts, rights = [], []
        for level in range(LOCAL):
            at, count = offsets[level], level_rows(rows, level)
            lefts.append(acc_ref[at : at + BLOCK, :])
            rights.append(acc_ref[at + BLOCK + count : at + 2 * BLOCK + count, :])
        put(to_left_ref, jnp.concatenate(lefts, axis=0), before_left if combine else None)
        put(to_right_ref, jnp.concatenate(rights, axis=0), before_right if combine else None)
        carry = None
        for index in range(len(far) - 1, -1, -1):
            level = far[index]
            count = base_ref.shape[0] // 2 ** (level - LOCAL + 1)
            tree_ref[0:count, :] = jnp.zeros((count, 2 * half), f32) if carry is None else spread(carry)
            for side, start in enumerate(far_starts(meta_ref[0], level, count)):
                at = offsets[LOCAL + index] + side * BLOCK
                tree_ref[pl.ds(start, BLOCK), :] += acc_ref[at : at + BLOCK, :]
            carry = tree_ref[0:count, :]
        put(to_far_ref, carry, before_far if combine else None)
        for level in range(LOCAL - 1, 0, -1):
            at, count = offsets[level] + BLOCK, level_rows(rows, level)
            below = offsets[level - 1] + BLOCK
            tile = min(count, 128)
            for row in range(0, count, tile):
                carry = spread(acc_ref[at + row : at + row + tile, :])
                target = slice(below + 2 * row, below + 2 * (row + tile))
                total = acc_ref[target, :] + carry
                if level == 1:
                    local_ref[2 * row : 2 * (row + tile), :] = total
                else:
                    acc_ref[target, :] = total


def attend_back_call(rows, devices, far, owners, first, count_pairs, before, meta, q, grads, bias, logs, levels, scaled, left, right, base, weight, vectors):
    chunks = rows // CHUNK
    _, entries = extended_offsets(rows, far)
    _, slots = slot_layout(far)
    combine = before is not None
    half = 128 * count_pairs
    side = 2 * WIDTH if combine else 2 * half
    part = WIDTH // owners
    lanes = first // count_pairs
    outs = [
        jax.ShapeDtypeStruct((rows, half), bf16),
        jax.ShapeDtypeStruct((rows, 2 * half), f32),
        jax.ShapeDtypeStruct((BLOCK * LOCAL, side), bf16),
        jax.ShapeDtypeStruct((BLOCK * LOCAL, side), bf16),
        jax.ShapeDtypeStruct((8 * devices, side), bf16),
        jax.ShapeDtypeStruct((owners, 3 * part + 64, WIDTH) if combine else (owners, 3 * part, half), bf16),
    ]
    if not combine:
        outs.append(jax.ShapeDtypeStruct((8, WIDTH), f32))
    return pl.pallas_call(
        partial(attend_back_kernel, rows, far, first, count_pairs, combine),
        grid=(chunks,),
        out_shape=outs,
        in_specs=[
            pl.BlockSpec(memory_space=pltpu.SMEM),
            pl.BlockSpec((CHUNK, half), lambda i: (i, lanes)),
            pl.BlockSpec((CHUNK, half), lambda i: (i, lanes)),
            pl.BlockSpec((1, slots, CHUNK), lambda i: (i, 0, 0)),
            pl.BlockSpec((1, 8, 2 * CHUNK), lambda i: (i, 0, 0)),
        ]
        + vmem_specs(2 * LOCAL + 5 + (5 if combine else 0)),
        out_specs=[pl.BlockSpec((CHUNK, half), lambda i: (i, 0))] + vmem_specs(len(outs) - 1),
        scratch_shapes=[
            pltpu.VMEM((entries, 2 * half), bf16),
            pltpu.VMEM((8 * devices, WIDTH), bf16),
            pltpu.VMEM((slots, 2 * half), bf16),
            pltpu.VMEM((entries, 2 * half), f32),
            pltpu.VMEM((8 * devices, 2 * half), f32),
            pltpu.VMEM((entries, WIDTH), bf16),
            pltpu.VMEM((rows, half), bf16),
        ],
        compiler_params=pltpu.CompilerParams(vmem_limit_bytes=VMEM_LIMIT),
        cost_estimate=pl.CostEstimate(flops=(40 << 30) * count_pairs // PAIRS, bytes_accessed=12 << 20, transcendentals=4 << 20),
        name="attend_back",
    )(meta, q, grads, bias, logs, *levels, *scaled, left, right, base, weight, vectors, *(before or []))


def normal_parts(values):
    size = jnp.abs(values)
    bell = jnp.exp(-0.5 * values * values)
    t = 1.0 / (1.0 + (0.3275911 / math.sqrt(2.0)) * size)
    poly = t * (
        0.5 * 0.254829592
        + t * (0.5 * -0.284496736 + t * (0.5 * 1.421413741 + t * (0.5 * -1.453152027 + t * (0.5 * 1.061405429))))
    )
    tail = poly * bell
    return jnp.where(values < 0, tail, 1.0 - tail), bell * (1.0 / math.sqrt(2.0 * math.pi))


def feed_kernel(
    hidden_width,
    x_ref,
    attended_ref,
    cot_ref,
    rest_ref,
    up_w_ref,
    vec_ref,
    up_bias_ref,
    y_ref,
    grad_middle_ref,
    grad_attended_ref,
    weights_ref,
    out_w_ref,
    vec_grad_ref,
    up_bias_grad_ref,
    down_acc,
    up_acc,
    out_acc,
):
    step = pl.program_id(0)
    owners = rest_ref.shape[0]
    rows = WIDTH // owners
    wide_rows = hidden_width // owners

    @pl.when(step == 0)
    def _():
        for owner in range(owners):
            out_w_ref[owner * rows : (owner + 1) * rows, :] = rest_ref[owner, wide_rows:, :]
        down_acc[...] = jnp.zeros_like(down_acc)
        up_acc[...] = jnp.zeros_like(up_acc)
        out_acc[...] = jnp.zeros_like(out_acc)
        vec_grad_ref[...] = jnp.zeros_like(vec_grad_ref)
        up_bias_grad_ref[...] = jnp.zeros_like(up_bias_grad_ref)

    out_bias, gain, shift, down_bias = (vec_ref[4 + at : 5 + at, :] for at in range(4))
    attended = attended_ref[...]
    middle = x_ref[...].astype(f32) + dot_nn(attended, out_w_ref[...]) + out_bias
    scaled, inverse = norm_rows(middle)
    normed = (scaled * gain + shift).astype(bf16)
    cot = cot_ref[...]
    wide = cot.astype(f32)
    lowered = jnp.zeros_like(middle)
    grad_normed = jnp.zeros_like(middle)
    for owner in range(owners):
        columns = slice(owner * wide_rows, (owner + 1) * wide_rows)
        down = rest_ref[owner, 0:wide_rows, :]
        pre = dot_nn(normed, up_w_ref[:, columns]) + up_bias_ref[:, columns]
        phi, bell = normal_parts(pre)
        hidden = (pre * phi).astype(bf16)
        lowered += dot_nn(hidden, down)
        grad_pre = (dot_nt(cot, down) * (phi + pre * bell)).astype(bf16)
        up_bias_grad_ref[:, columns] += column_sum(grad_pre.astype(f32))
        grad_normed += dot_nt(grad_pre, up_w_ref[:, columns])
        down_acc[columns, :] += dot_tn(hidden, cot)
        up_acc[:, columns] += dot_tn(normed, grad_pre)
    y_ref[...] = (middle + lowered + down_bias).astype(bf16)
    grad_middle = wide + norm_back(grad_normed, scaled, inverse, gain)
    grad_middle_ref[...] = grad_middle
    grad_proj = grad_middle.astype(bf16)
    grad_attended_ref[...] = dot_nt(grad_proj, out_w_ref[...]).astype(bf16)
    out_acc[...] += dot_tn(attended, grad_proj)
    vec_grad_ref[0:1, :] += column_sum(grad_proj.astype(f32))
    vec_grad_ref[1:2, :] += column_sum(grad_normed * scaled)
    vec_grad_ref[2:3, :] += column_sum(grad_normed)
    vec_grad_ref[3:4, :] += column_sum(wide)

    @pl.when(step == pl.num_programs(0) - 1)
    def _():
        extra = weights_ref.shape[1] - 2 * wide_rows - rows
        row_at = lax.broadcasted_iota(jnp.int32, (extra, 1), 0)
        for owner in range(owners):
            wide_span, span = slice(owner * wide_rows, (owner + 1) * wide_rows), slice(owner * rows, (owner + 1) * rows)
            weights_ref[owner, 0:wide_rows, :] = down_acc[wide_span, :].astype(bf16)
            at = wide_rows
            for block in range(hidden_width // WIDTH):
                weights_ref[owner, at : at + rows, :] = up_acc[span, block * WIDTH : (block + 1) * WIDTH].astype(bf16)
                at += rows
            weights_ref[owner, at : at + rows, :] = out_acc[span, :].astype(bf16)
            first = jnp.concatenate([vec_grad_ref[i : i + 1, span] for i in range(4)], axis=1)
            second = up_bias_grad_ref[:, wide_span]
            weights_ref[owner, at + rows :, :] = jnp.where(
                row_at == 0, first, jnp.where(row_at == 1, second, 0.0)
            ).astype(bf16)


def feed_call(owners, x, attended, cot, rest, up_w, vectors, up_bias):
    rows, hidden_width = x.shape[0], up_w.shape[1]
    tile = 256
    row_spec = pl.BlockSpec((tile, WIDTH), lambda i: (i, 0))
    packed = 2 * (hidden_width // owners) + WIDTH // owners + 64
    return pl.pallas_call(
        partial(feed_kernel, hidden_width),
        grid=(rows // tile,),
        out_shape=[
            jax.ShapeDtypeStruct((rows, WIDTH), bf16),
            jax.ShapeDtypeStruct((rows, WIDTH), f32),
            jax.ShapeDtypeStruct((rows, WIDTH), bf16),
            jax.ShapeDtypeStruct((owners, packed, WIDTH), bf16),
        ],
        in_specs=[row_spec, row_spec, row_spec] + vmem_specs(4),
        out_specs=[row_spec, row_spec, row_spec] + vmem_specs(1),
        scratch_shapes=[
            pltpu.VMEM((WIDTH, WIDTH), bf16),
            pltpu.VMEM((8, WIDTH), f32),
            pltpu.VMEM((1, hidden_width), f32),
            pltpu.VMEM((hidden_width, WIDTH), f32),
            pltpu.VMEM((WIDTH, hidden_width), f32),
            pltpu.VMEM((WIDTH, WIDTH), f32),
        ],
        compiler_params=pltpu.CompilerParams(vmem_limit_bytes=VMEM_LIMIT),
        cost_estimate=pl.CostEstimate(flops=32 << 30, bytes_accessed=20 << 20, transcendentals=4 << 20),
        name="feed_forward",
    )(x, attended, cot, rest, up_w, vectors, up_bias)


def input_grad_kernel(
    x_ref,
    dq_refs,
    local_refs,
    grad_middle_ref,
    from_right_ref,
    from_left_ref,
    base_ref,
    w_ref,
    vec_ref,
    out_ref,
    tree_ref,
):
    rows = tree_ref.shape[0]
    step = pl.program_id(0)
    tile = x_ref.shape[0]

    @pl.when(step == 0)
    def _():
        carry = spread(base_ref[...].astype(f32))
        for level in range(LOCAL - 1, -1, -1):
            count = level_rows(rows, level)
            edge = slice(BLOCK * level, BLOCK * (level + 1))
            if level == LOCAL - 1:
                tree_ref[0:count, :] = carry
            tree_ref[0:BLOCK, :] += from_left_ref[edge, :].astype(f32)
            tree_ref[count - BLOCK : count, :] += from_right_ref[edge, :].astype(f32)
            if level:
                part = min(count, 128)
                for row in range(count - part, -1, -part):
                    tree_ref[2 * row : 2 * (row + part), :] = spread(tree_ref[row : row + part, :])

    span = pl.ds(pl.multiple_of(step * tile, tile), tile)
    scaled, inverse = norm_rows(x_ref[...].astype(f32))
    grad = jnp.zeros((tile, WIDTH), f32)
    half = dq_refs[0].shape[1]
    for index, (dq_ref, local_ref) in enumerate(zip(dq_refs, local_refs)):
        lane = index * half
        grad += dot_nt(dq_ref[...], w_ref[:, lane : lane + half])
        for block in range(2):
            column = block * WIDTH + lane
            dkv = (local_ref[:, block * half : (block + 1) * half] + tree_ref[span, column : column + half]).astype(bf16)
            grad += dot_nt(dkv, w_ref[:, WIDTH + column : WIDTH + column + half])
    out_ref[...] = grad_middle_ref[...] + norm_back(grad, scaled, inverse, vec_ref[0:1, :])


def input_grad_call(x, dqs, locals_, grad_middle, from_right, from_left, base, weight, vectors):
    rows = x.shape[0]
    tile = 256
    count = len(dqs)
    tiled = lambda width: pl.BlockSpec((tile, width), lambda i: (i, 0))

    def kernel(x_ref, *refs):
        input_grad_kernel(x_ref, refs[:count], refs[count : 2 * count], *refs[2 * count :])

    return pl.pallas_call(
        kernel,
        grid=(rows // tile,),
        out_shape=jax.ShapeDtypeStruct((rows, WIDTH), f32),
        in_specs=[tiled(WIDTH)]
        + [tiled(d.shape[1]) for d in dqs]
        + [tiled(d.shape[1]) for d in locals_]
        + [tiled(WIDTH)]
        + vmem_specs(5),
        out_specs=tiled(WIDTH),
        scratch_shapes=[pltpu.VMEM((rows, 2 * WIDTH), f32)],
        compiler_params=pltpu.CompilerParams(vmem_limit_bytes=VMEM_LIMIT),
        cost_estimate=pl.CostEstimate(flops=8 << 30, bytes_accessed=14 << 20, transcendentals=0),
        name="input_grad",
    )(x, *dqs, *locals_, grad_middle, from_right, from_left, base, weight, vectors)


def shifted(block, axis, distance):
    devices = range(lax.axis_size(axis))
    route = [(i - distance, i) for i in devices if i - distance in devices]
    return lax.ppermute(block, axis, route)


def swap(block, axis, bit):
    return lax.ppermute(block, axis, [(i, i ^ bit) for i in range(lax.axis_size(axis))])


def add_low(left, right):
    return (left.astype(f32) + right.astype(f32)).astype(bf16)


def scatter_step(parts, axis, bit):
    mine = (lax.axis_index(axis) // bit) % 2
    keep = lax.dynamic_index_in_dim(parts, mine, 0, keepdims=False)
    send = lax.dynamic_index_in_dim(parts, 1 - mine, 0, keepdims=False)
    return add_low(keep, swap(send, axis, bit))


def gather_step(part, axis, bit, rows_axis=0):
    mine = (lax.axis_index(axis) // bit) % 2
    other = swap(part, axis, bit)
    first = jnp.where(mine == 0, part, other)
    second = jnp.where(mine == 0, other, part)
    return jnp.concatenate([first, second], axis=rows_axis)


def together(*values):
    return lax.optimization_barrier(values)


def bits_of(axis):
    size = lax.axis_size(axis)
    return [1 << at for at in range(size.bit_length() - 1)]


class Reduction:
    def __init__(self, parts):
        self.shape = parts.shape[1:]
        self.value = parts
        self.done = []
        self.todo = [self.low, self.cross_one, self.cross_two]
        self.todo += [partial(self.scatter, bit) for bit in bits_of("ctx")[1:]]
        self.todo += [partial(self.gather, bit) for bit in reversed(bits_of("ctx")[1:])]
        self.todo += [self.last]

    def step(self, count=1):
        for _ in range(count):
            if self.todo:
                self.todo.pop(0)()
        return self

    def after(self, *others):
        tied = together(self.value, *others)
        self.value = tied[0]
        return tied[1:]

    def low(self):
        owners = self.value.shape[0]
        self.value = scatter_step(self.value.reshape(owners // 2, 2, *self.shape).transpose(1, 0, 2, 3), "fsdp", 1)

    def over_owners(self, current):
        for bit in bits_of("fsdp")[1:]:
            current = current.reshape(-1, 2, *current.shape[1:]).transpose(1, 0, 2, 3)
            current = scatter_step(current, "fsdp", bit)
        return current.reshape(current.shape[1:])

    def over_ctx(self, current):
        outer, rows, width = current.shape
        return scatter_step(current.reshape(outer, 2, rows // 2, width).transpose(1, 0, 2, 3), "ctx", 1)

    def cross_one(self):
        half = self.shape[0] // 2
        one, two = self.value[:, :half], self.value[:, half:]
        self.value = (self.over_owners(one)[None], self.over_ctx(two))

    def cross_two(self):
        one, two = self.value
        self.value = jnp.concatenate([self.over_ctx(one)[0], self.over_owners(two)], axis=0)

    def scatter(self, bit):
        rows, width = self.value.shape
        self.value = scatter_step(self.value.reshape(2, rows // 2, width), "ctx", bit)

    def gather(self, bit):
        self.value = gather_step(self.value, "ctx", bit)

    def last(self):
        rows, width = self.value.shape
        both = gather_step(self.value.reshape(2, 1, rows // 2, width), "ctx", 1, 1)
        self.value = both.reshape(2 * rows, width)


def shards(
    layer_input,
    doc_lengths,
    ln1_gain,
    ln1_bias,
    qkv_weight,
    query_bias,
    value_bias,
    out_weight,
    out_bias,
    ln2_gain,
    ln2_bias,
    up_weight,
    up_bias,
    down_weight,
    down_bias,
    cotangent,
):
    owners = lax.axis_size("fsdp")
    devices = lax.axis_size("ctx")
    x, cot = layer_input[0], cotangent[0]
    rows = x.shape[0]
    total = rows * devices
    far = far_levels(total)
    here, owner = lax.axis_index("ctx"), lax.axis_index("fsdp")
    part = WIDTH // owners
    hidden_width = up_weight.shape[1]
    meta = jnp.stack([here] + [owner ^ at for at in range(owners)]).astype(jnp.int32)

    vectors = [ln1_gain, ln1_bias, query_bias, value_bias, out_bias, ln2_gain, ln2_bias, down_bias, up_bias]
    pieces = {0: pack_call(qkv_weight, vectors)}
    for bit in reversed(bits_of("fsdp")):
        for at in list(pieces):
            pieces[at ^ bit] = swap(pieces[at], "fsdp", bit)
    rest_shard = jnp.concatenate([down_weight, out_weight], axis=0)
    tied = together(up_weight, rest_shard, *(pieces[at] for at in range(owners)))
    pieces = tied[2:]
    rest = lax.all_gather(tied[1], "fsdp", axis=0, tiled=False)
    up_full = lax.all_gather(tied[0], "fsdp", axis=0, tiled=True)

    bias = mask_call(rows, total, far, meta, doc_lengths)
    qkv_full, vec, up_shift, queries, levels, scaled, tail, head = qkv_call(rows, hidden_width, meta, x, pieces)
    left = shifted(tail, "ctx", 1)
    right = shifted(head, "ctx", -1)
    base = tail[BLOCK * (LOCAL - 1) :]
    for at, bit in enumerate(bits_of("ctx")):
        base = gather_step(base, "ctx", bit)
        if at == 0:
            base, left, right = together(base, left, right)

    attended, logs = attend_call(rows, devices, far, meta, queries, bias, levels, left, right, base)
    output, grad_middle, grad_attended, feed_grads = feed_call(
        owners, x, attended, cot, rest, up_full, vec, up_shift
    )
    feed = Reduction(feed_grads).step()
    back = partial(attend_back_call, rows, devices, far, owners)
    count = PAIRS // 2
    common = (bias, logs, levels, scaled, left, right, base, qkv_full, vec)
    (grad_attended,) = feed.after(grad_attended)
    dq_one, local_one, *before = back(0, count, None, meta, queries, grad_attended, *common)
    feed.step()
    tied = together(*feed.value, *before)
    feed.value, before = tied[:2], tied[2:]
    dq_two, local_two, to_left, to_right, to_far, qkv_grads = back(
        count, count, before, meta, queries, grad_attended, *common
    )
    feed.step()
    first = Reduction(qkv_grads)

    back_right = shifted(to_left, "ctx", -1)
    back_left = shifted(to_right, "ctx", 1)
    back_far = to_far
    for at, bit in enumerate(reversed(bits_of("ctx"))):
        back_far = scatter_step(back_far.reshape(2, -1, 2 * WIDTH), "ctx", bit)
        if at == 0:
            back_far, back_right, back_left = together(back_far, back_right, back_left)
    input_grad = input_grad_call(
        x, [dq_one, dq_two], [local_one, local_two], grad_middle, back_right, back_left, back_far, qkv_full, vec
    )
    while feed.todo or first.todo:
        first.step()
        feed.step()
    feed_sum, qkv_sum = feed.value.astype(f32), first.value.astype(f32)

    wide_rows = hidden_width // owners
    down_grad = feed_sum[:wide_rows]
    up_grad = jnp.concatenate(
        [feed_sum[wide_rows + at * part : wide_rows + (at + 1) * part] for at in range(hidden_width // WIDTH)], axis=1
    )
    out_grad = feed_sum[2 * wide_rows : 2 * wide_rows + part]
    feed_row = feed_sum[2 * wide_rows + part]
    up_row = feed_sum[2 * wide_rows + part + 1]
    qkv_grad = jnp.concatenate([qkv_sum[at * part : (at + 1) * part] for at in range(3)], axis=1)
    first_row = qkv_sum[3 * part]
    pick = lambda row, at: row[at * part : (at + 1) * part]
    return (
        output[None],
        input_grad[None],
        pick(first_row, 0),
        pick(first_row, 1),
        qkv_grad,
        pick(first_row, 2),
        pick(first_row, 3),
        out_grad,
        pick(feed_row, 0),
        pick(feed_row, 1),
        pick(feed_row, 2),
        up_grad,
        up_row,
        down_grad,
        pick(feed_row, 3),
    )


def solution(mesh):
    row, vector = P("fsdp", None), P("fsdp")
    tokens = P("fsdp", "ctx", None)
    return jax.shard_map(
        shards,
        mesh=mesh,
        in_specs=(
            tokens,
            row,
            vector,
            vector,
            row,
            vector,
            vector,
            row,
            vector,
            vector,
            vector,
            row,
            vector,
            row,
            vector,
            tokens,
        ),
        out_specs=(
            tokens,
            tokens,
            vector,
            vector,
            row,
            vector,
            vector,
            row,
            vector,
            vector,
            vector,
            row,
            vector,
            row,
            vector,
        ),
        check_vma=False,
    )
```

```python
from functools import partial
import math

import jax
import jax.numpy as jnp
from jax import lax
from jax.experimental import pallas as pl
from jax.experimental.pallas import tpu as pltpu
from jax.sharding import PartitionSpec as P

HEADS = 8
BLOCK = 16
LEVELS = 10
NEAR = 4
LOCAL = 7
CHUNK = 128
WIDTH = 512
PAIRS = HEADS // 2
ENTRY = 3 * WIDTH
SMALL = 16
MASKED = -1e30
EPSILON = 1e-05
VMEM_LIMIT = 56 * 1024 * 1024

f32 = jnp.float32
bf16 = jnp.bfloat16


def level_rows(rows, level):
    return rows // 2**level


def far_levels(total):
    return [l for l in range(LOCAL, LEVELS) if total // (BLOCK * 2**l) >= 2]


def extended_offsets(rows, far):
    offsets, cursor = [], 0
    for level in range(LOCAL):
        offsets.append(cursor)
        cursor += level_rows(rows, level) + 2 * BLOCK
    for _ in far:
        offsets.append(cursor)
        cursor += 2 * BLOCK
    return offsets, cursor


def slot_layout(far):
    parts = [(level, CHUNK // 2**level + 2 * BLOCK) for level in range(NEAR)]
    parts += [(level, BLOCK) for level in list(range(NEAR, LOCAL)) + far for _ in range(2)]
    return parts, sum(count for _, count in parts)


def slot_sources(rows, far, chunk):
    offsets, _ = extended_offsets(rows, far)
    sources = []
    for level in range(NEAR):
        sources.append((offsets[level] + chunk * (CHUNK // 2**level), CHUNK // 2**level + 2 * BLOCK))
    for level in range(NEAR, LOCAL):
        block = chunk // (BLOCK * 2**level // CHUNK)
        sources.append((offsets[level] + block * BLOCK, BLOCK))
        sources.append((offsets[level] + block * BLOCK + 2 * BLOCK, BLOCK))
    for at in range(len(far)):
        sources.append((offsets[LOCAL + at], BLOCK))
        sources.append((offsets[LOCAL + at] + BLOCK, BLOCK))
    return sources


def mask_kernel(rows, total, far, here_ref, lengths_ref, bias_ref):
    base = here_ref[0] * rows + pl.program_id(0) * CHUNK
    query = base + lax.broadcasted_iota(jnp.int32, (1, CHUNK), 1)
    first_token = jnp.zeros((1, CHUNK), jnp.int32)
    end_token = jnp.full((1, CHUNK), total, jnp.int32)
    start = jnp.int32(0)
    for at in range(lengths_ref.shape[1]):
        first_token = jnp.where(start <= query, start, first_token)
        start = start + lengths_ref[0, at]
        end_token = jnp.where(start > query, jnp.minimum(end_token, start), end_token)

    def part(at, count, first_row, level):
        span = 2**level
        shift = level + 4
        first = first_row + span * lax.broadcasted_iota(jnp.int32, (count, CHUNK), 0)
        gap = jnp.abs((first >> shift) - (query >> shift))
        if level == 0:
            seen = gap <= 1
        else:
            seen = (gap == 1) & (jnp.abs((first >> (shift - 1)) - (query >> (shift - 1))) > 1)
        seen = seen & (first >= first_token) & (first + (span - 1) < end_token)
        bias_ref[0, at : at + count, :] = jnp.where(seen, level * math.log(2.0), MASKED)

    at = 0
    for level in range(NEAR):
        count = CHUNK // 2**level + 2 * BLOCK
        part(at, count, base - BLOCK * 2**level, level)
        at += count
    for level in list(range(NEAR, LOCAL)) + far:
        block = base >> (level + 4)
        for side in (-1, 1):
            part(at, BLOCK, (block + side) * (BLOCK * 2**level), level)
            at += BLOCK


def mask_call(rows, total, far, meta, lengths):
    chunks = rows // CHUNK
    _, slots = slot_layout(far)
    return pl.pallas_call(
        partial(mask_kernel, rows, total, far),
        grid=(chunks,),
        out_shape=jax.ShapeDtypeStruct((chunks, slots, CHUNK), f32),
        in_specs=[pl.BlockSpec(memory_space=pltpu.SMEM)] * 2,
        out_specs=pl.BlockSpec((1, slots, CHUNK), lambda i: (i, 0, 0)),
        cost_estimate=pl.CostEstimate(flops=4 << 30, bytes_accessed=3 << 20, transcendentals=0),
        name="mask",
    )(meta, lengths)


def dot_nt(left, right):
    return lax.dot_general(left, right, (((1,), (1,)), ((), ())), preferred_element_type=f32)


def dot_tn(left, right):
    return lax.dot_general(left, right, (((0,), (0,)), ((), ())), preferred_element_type=f32)


def dot_nn(left, right):
    return jnp.dot(left, right, preferred_element_type=f32)


def pool_matrix(count):
    row = lax.broadcasted_iota(jnp.int32, (count // 2, count), 0)
    column = lax.broadcasted_iota(jnp.int32, (count // 2, count), 1)
    return jnp.where((column >> 1) == row, 0.5, 0.0).astype(bf16)


def spread_matrix(count):
    row = lax.broadcasted_iota(jnp.int32, (2 * count, count), 0)
    column = lax.broadcasted_iota(jnp.int32, (2 * count, count), 1)
    return jnp.where((row >> 1) == column, 0.5, 0.0).astype(bf16)


def spread(values):
    count = values.shape[0]
    tile = min(count, 128)
    matrix = spread_matrix(tile)
    high = values.astype(bf16)
    low = (values - high.astype(f32)).astype(bf16)
    parts = [
        dot_nn(matrix, high[at : at + tile]) + dot_nn(matrix, low[at : at + tile])
        for at in range(0, count, tile)
    ]
    return parts[0] if len(parts) == 1 else jnp.concatenate(parts, axis=0)


def norm_rows(values):
    mean = jnp.mean(values, axis=-1, keepdims=True)
    centred = values - mean
    variance = jnp.mean(centred * centred, axis=-1, keepdims=True)
    inverse = lax.rsqrt(variance + EPSILON)
    return centred * inverse, inverse


def norm_back(grad_out, scaled, inverse, gain):
    grad_scaled = grad_out * gain
    first = jnp.mean(grad_scaled, axis=-1, keepdims=True)
    second = jnp.mean(grad_scaled * scaled, axis=-1, keepdims=True)
    return inverse * (grad_scaled - first - scaled * second)


def split_heads(pair):
    lane = lax.broadcasted_iota(jnp.int32, pair.shape, 1)
    zero = jnp.zeros_like(pair)
    return jnp.concatenate([jnp.where(lane < 64, pair, zero), jnp.where(lane < 64, zero, pair)], axis=0)


def join_heads(stacked):
    rows = stacked.shape[0] // 2
    lane = lax.broadcasted_iota(jnp.int32, (rows, stacked.shape[1]), 1)
    return jnp.where(lane < 64, stacked[:rows], stacked[rows:])


def pack_kernel(w_ref, *refs):
    out_ref = refs[-1]
    part = w_ref.shape[0]
    out_ref[0:part, :] = w_ref[...]
    row = jnp.concatenate([ref[...].reshape(1, -1) for ref in refs[:-1]], axis=1)
    out_ref[part : part + SMALL, :] = jnp.broadcast_to(row.astype(f32), (SMALL, row.shape[1])).astype(bf16)


def pack_call(weight, vectors):
    return pl.pallas_call(
        pack_kernel,
        out_shape=jax.ShapeDtypeStruct((weight.shape[0] + SMALL, weight.shape[1]), bf16),
        in_specs=vmem_specs(1 + len(vectors)),
        out_specs=vmem_specs(1)[0],
        name="pack",
    )(weight, *vectors)


def pack_rest_kernel(down_ref, up_ref, out_w_ref, one_ref, two_ref):
    rows = up_ref.shape[0]
    blocks = up_ref.shape[1] // WIDTH
    for block in range(blocks - 1):
        one_ref[block * rows : (block + 1) * rows, :] = up_ref[:, block * WIDTH : (block + 1) * WIDTH]
    two_ref[0:rows, :] = up_ref[:, (blocks - 1) * WIDTH :]
    two_ref[rows : 2 * rows, :] = out_w_ref[...]
    two_ref[2 * rows :, :] = down_ref[...]


def pack_rest_call(down, up, out_w):
    rows, blocks = up.shape[0], up.shape[1] // WIDTH
    return pl.pallas_call(
        pack_rest_kernel,
        out_shape=[
            jax.ShapeDtypeStruct(((blocks - 1) * rows, WIDTH), bf16),
            jax.ShapeDtypeStruct((2 * rows + down.shape[0], WIDTH), bf16),
        ],
        in_specs=vmem_specs(3),
        out_specs=vmem_specs(2),
        name="pack_rest",
    )(down, up, out_w)


def vmem_specs(count):
    return [pl.BlockSpec(memory_space=pltpu.VMEM)] * count


def qkv_kernel(rows, owners, meta_ref, x_ref, *refs):
    shard_refs, refs = refs[:owners], refs[owners + 1 :]
    w_ref, vec_ref, up_bias_ref, q_ref = refs[:4]
    kv_refs, scaled_refs = refs[4 : 4 + LOCAL], refs[4 + LOCAL : 4 + 2 * LOCAL]
    tail_ref, head_ref, top_ref, keep_ref = refs[4 + 2 * LOCAL :]
    part = WIDTH // owners
    step = pl.program_id(0)

    @pl.when(step == 0)
    def _():
        for at, ref in enumerate(shard_refs):
            owner = meta_ref[1 + at]
            w_ref[pl.ds(pl.multiple_of(owner * part, part), part), :] = ref[0:part, :]
            row = ref[part : part + 1, :].astype(f32)
            for vector in range(8):
                vec_ref[vector : vector + 1, pl.ds(pl.multiple_of(owner * part, part), part)] = row[
                    :, vector * part : (vector + 1) * part
                ]
            wide = row.shape[1] - 8 * part
            up_bias_ref[:, pl.ds(pl.multiple_of(owner * wide, wide), wide)] = row[:, 8 * part :]

    tile = x_ref.shape[0]
    scaled, _ = norm_rows(x_ref[...].astype(f32))
    normed = (scaled * vec_ref[0:1, :] + vec_ref[1:2, :]).astype(bf16)
    queries = (dot_nn(normed, w_ref[:, :WIDTH]) + vec_ref[2:3, :]).astype(bf16)
    q_ref[...] = queries * jnp.asarray(0.125, bf16)
    keys = dot_nn(normed, w_ref[:, WIDTH : 2 * WIDTH]).astype(bf16)
    values = (dot_nn(normed, w_ref[:, 2 * WIDTH :]) + vec_ref[3:4, :]).astype(bf16)
    current = jnp.concatenate([keys, values, scaled.astype(bf16)], axis=1)

    def edges(level, block):
        @pl.when(step == 0)
        def _():
            head_ref[BLOCK * level : BLOCK * (level + 1), :] = block[:BLOCK]

        @pl.when(step == pl.num_programs(0) - 1)
        def _():
            tail_ref[BLOCK * level : BLOCK * (level + 1), :] = block[block.shape[0] - BLOCK :]

    for level in range(5):
        if level:
            current = dot_nn(pool_matrix(current.shape[0]), current).astype(bf16)
        kv_refs[level][...] = current[:, : 2 * WIDTH]
        scaled_refs[level][...] = current[:, 2 * WIDTH :]
        edges(level, current)
    count = tile // 16
    keep_ref[pl.ds(pl.multiple_of(step * count, count), count), :] = current

    @pl.when(step == pl.num_programs(0) - 1)
    def _():
        current = keep_ref[...]
        for level in range(5, LOCAL):
            current = dot_nn(pool_matrix(current.shape[0]), current).astype(bf16)
            kv_refs[level][...] = current[:, : 2 * WIDTH]
            scaled_refs[level][...] = current[:, 2 * WIDTH :]
            tail_ref[BLOCK * level : BLOCK * (level + 1), :] = current[current.shape[0] - BLOCK :]
            head_ref[BLOCK * level : BLOCK * (level + 1), :] = current[:BLOCK]
        top_ref[...] = current


def qkv_call(rows, hidden_width, meta, x, pieces, earlier):
    owners = len(pieces)
    tile = 256

    def tiled(count, width):
        return pl.BlockSpec((count, width), lambda i: (i, 0))

    def leveled(width):
        shapes, specs = [], []
        for level in range(LOCAL):
            shapes.append(jax.ShapeDtypeStruct((level_rows(rows, level), width), bf16))
            specs.append(tiled(tile // 2**level, width) if level < 5 else vmem_specs(1)[0])
        return shapes, specs

    kv_shapes, kv_specs = leveled(2 * WIDTH)
    scaled_shapes, scaled_specs = leveled(WIDTH)
    edge = jax.ShapeDtypeStruct((BLOCK * LOCAL, ENTRY), bf16)
    outs = pl.pallas_call(
        partial(qkv_kernel, rows, owners),
        grid=(rows // tile,),
        out_shape=[
            jax.ShapeDtypeStruct((WIDTH, 3 * WIDTH), bf16),
            jax.ShapeDtypeStruct((8, WIDTH), f32),
            jax.ShapeDtypeStruct((1, hidden_width), f32),
            jax.ShapeDtypeStruct((rows, WIDTH), bf16),
        ]
        + kv_shapes
        + scaled_shapes
        + [edge, edge, jax.ShapeDtypeStruct((BLOCK, ENTRY), bf16)],
        in_specs=[pl.BlockSpec(memory_space=pltpu.SMEM), tiled(tile, WIDTH)]
        + vmem_specs(owners)
        + [pl.BlockSpec(memory_space=pl.ANY)],
        out_specs=vmem_specs(3) + [tiled(tile, WIDTH)] + kv_specs + scaled_specs + vmem_specs(3),
        scratch_shapes=[pltpu.VMEM((level_rows(rows, 4), ENTRY), bf16)],
        compiler_params=pltpu.CompilerParams(vmem_limit_bytes=VMEM_LIMIT),
        cost_estimate=pl.CostEstimate(flops=9 << 30, bytes_accessed=12 << 20, transcendentals=0),
        name="qkv_levels",
    )(meta, x, *pieces, earlier)
    return outs


def far_level(entries):
    return dot_nn(pool_matrix(entries.shape[0]), entries).astype(bf16)


def assemble(rows, far, here, columns, level_refs, left_ref, right_ref, base_ref, ext_ref, far_ref):
    offsets, _ = extended_offsets(rows, far)
    for inner, outer, target, width in columns:
        lanes, edge_lanes = slice(target, target + width), slice(outer, outer + width)
        for level in range(LOCAL):
            at, count = offsets[level], level_rows(rows, level)
            edge = slice(BLOCK * level, BLOCK * (level + 1))
            ext_ref[at : at + BLOCK, lanes] = left_ref[edge, edge_lanes]
            ext_ref[at + BLOCK : at + BLOCK + count, lanes] = level_refs[level][:, inner : inner + width]
            ext_ref[at + BLOCK + count : at + 2 * BLOCK + count, lanes] = right_ref[edge, edge_lanes]
        current = base_ref[:, edge_lanes]
        for index, level in enumerate(far):
            current = far_level(current)
            count = current.shape[0]
            far_ref[0:count, 0:width] = current
            for side, start in enumerate(far_starts(here, level, count)):
                at = offsets[LOCAL + index] + side * BLOCK
                ext_ref[at : at + BLOCK, lanes] = far_ref[pl.ds(start, BLOCK), 0:width]


def far_starts(here, level, count):
    block = here >> (level - 6)
    last = count // BLOCK - 1
    return [pl.multiple_of(jnp.clip(at, 0, last) * BLOCK, BLOCK) for at in (block - 1, block + 1)]


def load_slots(rows, far, chunk, ext_ref, slots_ref):
    at = 0
    for start, count in slot_sources(rows, far, chunk):
        if not isinstance(start, int):
            start = pl.multiple_of(start, BLOCK)
        slots_ref[at : at + count, :] = ext_ref[pl.ds(start, count), :]
        at += count


def attend_kernel(rows, far, meta_ref, q_ref, bias_ref, *refs):
    level_refs, refs = refs[:LOCAL], refs[LOCAL:]
    left_ref, right_ref, base_ref, out_ref, log_ref, ext_ref, far_ref, slots_ref = refs
    chunk = pl.program_id(0)

    @pl.when(chunk == 0)
    def _():
        columns = [(0, 0, 0, 2 * WIDTH)]
        assemble(rows, far, meta_ref[0], columns, level_refs, left_ref, right_ref, base_ref, ext_ref, far_ref)

    load_slots(rows, far, chunk, ext_ref, slots_ref)
    bias = bias_ref[0]
    bias = jnp.concatenate([bias, bias], axis=1)
    for pair in range(PAIRS):
        lanes = slice(128 * pair, 128 * (pair + 1))
        values = slots_ref[:, WIDTH + 128 * pair : WIDTH + 128 * (pair + 1)]
        scores = dot_nt(slots_ref[:, lanes], split_heads(q_ref[:, lanes])) + bias
        top = jnp.max(scores, axis=0, keepdims=True)
        exponent = jnp.exp(scores - top)
        total = jnp.sum(exponent, axis=0, keepdims=True)
        probs = (exponent * (1.0 / total)).astype(bf16)
        out_ref[:, lanes] = join_heads(dot_tn(probs, values)).astype(bf16)
        log_ref[0, pair : pair + 1, :] = top + jnp.log(total)


def attend_call(rows, devices, far, meta, q, bias, levels, left, right, base):
    chunks = rows // CHUNK
    _, entries = extended_offsets(rows, far)
    _, slots = slot_layout(far)
    return pl.pallas_call(
        partial(attend_kernel, rows, far),
        grid=(chunks,),
        out_shape=[
            jax.ShapeDtypeStruct((rows, WIDTH), bf16),
            jax.ShapeDtypeStruct((chunks, 8, 2 * CHUNK), f32),
        ],
        in_specs=[
            pl.BlockSpec(memory_space=pltpu.SMEM),
            pl.BlockSpec((CHUNK, WIDTH), lambda i: (i, 0)),
            pl.BlockSpec((1, slots, CHUNK), lambda i: (i, 0, 0)),
        ]
        + vmem_specs(LOCAL + 3),
        out_specs=[
            pl.BlockSpec((CHUNK, WIDTH), lambda i: (i, 0)),
            pl.BlockSpec((1, 8, 2 * CHUNK), lambda i: (i, 0, 0)),
        ],
        scratch_shapes=[
            pltpu.VMEM((entries, 2 * WIDTH), bf16),
            pltpu.VMEM((8 * devices, 2 * WIDTH), bf16),
            pltpu.VMEM((slots, 2 * WIDTH), bf16),
        ],
        compiler_params=pltpu.CompilerParams(vmem_limit_bytes=VMEM_LIMIT),
        cost_estimate=pl.CostEstimate(flops=20 << 30, bytes_accessed=12 << 20, transcendentals=4 << 20),
        name="attend",
    )(meta, q, bias, *levels, left, right, base)


def column_sum(values):
    return jnp.sum(values, axis=0, keepdims=True)


def matrix_row(left, right):
    total = None
    for a in two_parts(left):
        for b in two_parts(right):
            term = dot_nt(a, b)
            total = term if total is None else total + term
    return total[0:1]


def two_parts(values):
    if values.dtype == bf16:
        return [values]
    high = values.astype(bf16)
    return [high, (values - high.astype(f32)).astype(bf16)]


def choose(flag, zero, one):
    return jnp.where(flag == 0, zero, one), jnp.where(flag == 0, one, zero)


def choose_groups(flag, folded):
    groups = folded.reshape(-1, 2, 8, folded.shape[1])
    return [part.reshape(-1, folded.shape[1]) for part in choose(flag, groups[:, 0], groups[:, 1])]


def attend_back_kernel(rows, far, *refs):
    refs = list(refs)
    take = lambda count: [refs.pop(0) for _ in range(count)]
    meta_ref, q_ref, grad_ref, bias_ref, log_ref = take(5)
    level_refs, scaled_refs = take(LOCAL), take(LOCAL)
    left_ref, right_ref, base_ref, w_ref, vec_ref = take(5)
    dq_ref, local_ref, to_left_ref, to_right_ref, far_keep_ref, far_send_ref, keep_ref, send_ref = take(8)
    ext_ref, far_ref, slots_ref, acc_ref, tree_ref, scaled_ref, dq_keep_ref = take(7)
    chunk = pl.program_id(0)
    offsets, entries = extended_offsets(rows, far)

    @pl.when(chunk == 0)
    def _():
        common = (left_ref, right_ref, base_ref)
        assemble(rows, far, meta_ref[0], [(0, 0, 0, 2 * WIDTH)], level_refs, *common, ext_ref, far_ref)
        assemble(rows, far, meta_ref[0], [(0, 2 * WIDTH, 0, WIDTH)], scaled_refs, *common, scaled_ref, far_ref)
        acc_ref[...] = jnp.zeros_like(acc_ref)

    load_slots(rows, far, chunk, ext_ref, slots_ref)
    bias = bias_ref[0]
    bias = jnp.concatenate([bias, bias], axis=1)
    sources = slot_sources(rows, far, chunk)
    for pair in range(PAIRS):
        lanes = slice(128 * pair, 128 * (pair + 1))
        value_lanes = slice(WIDTH + 128 * pair, WIDTH + 128 * (pair + 1))
        keys, values = slots_ref[:, lanes], slots_ref[:, value_lanes]
        queries, grads = split_heads(q_ref[:, lanes]), split_heads(grad_ref[:, lanes])
        probs = jnp.exp(dot_nt(keys, queries) + bias - log_ref[0, pair : pair + 1, :])
        grad_probs = dot_nt(values, grads)
        delta = jnp.sum(probs * grad_probs, axis=0, keepdims=True)
        grad_scores = (probs * (grad_probs - delta)).astype(bf16)
        dq = (join_heads(dot_tn(grad_scores, keys)) * 0.125).astype(bf16)
        dq_ref[:, lanes] = dq
        dq_keep_ref[pl.ds(pl.multiple_of(chunk * CHUNK, CHUNK), CHUNK), lanes] = dq
        grad_keys = dot_nn(grad_scores, queries)
        grad_values = dot_nn(probs.astype(bf16), grads)
        at = 0
        for start, count in sources:
            if not isinstance(start, int):
                start = pl.multiple_of(start, BLOCK)
            acc_ref[pl.ds(start, count), lanes] += grad_keys[at : at + count]
            acc_ref[pl.ds(start, count), value_lanes] += grad_values[at : at + count]
            at += count

    @pl.when(chunk == pl.num_programs(0) - 1)
    def _():
        dq = dq_keep_ref[...]
        sums = [column_sum(dq.astype(f32)), column_sum(acc_ref[:, :WIDTH]), column_sum(acc_ref[:, WIDTH:])]
        both = dot_tn(scaled_ref[...], acc_ref[...].astype(bf16))
        parts = [dot_tn(scaled_refs[0][...], dq), both[:, :WIDTH], both[:, WIDTH:]]
        first_row = lax.broadcasted_iota(jnp.int32, (16, 1), 0) == 0
        ones = jnp.where(first_row, jnp.ones((16, WIDTH), f32), 0.0).astype(bf16)
        as_column = lambda row: dot_tn(jnp.where(first_row, row, 0.0).astype(bf16), ones)
        gain, shift = as_column(vec_ref[0:1, :]), as_column(vec_ref[1:2, :])
        gain_grad, shift_grad = jnp.zeros((1, WIDTH), f32), jnp.zeros((1, WIDTH), f32)
        owners = 2 * keep_ref.shape[0]
        part = WIDTH // owners
        low_bit = meta_ref[1] & 1
        for block in range(3):
            weight = w_ref[:, block * WIDTH : (block + 1) * WIDTH]
            gain_grad += matrix_row(jnp.ones((16, WIDTH), bf16), weight.astype(f32) * parts[block])
            shift_grad += matrix_row(jnp.broadcast_to(sums[block], (16, WIDTH)), weight)
            grad = gain * parts[block] + shift * sums[block]
            for high in range(owners // 2):
                at = 2 * high * part
                mine, other = choose(low_bit, grad[at : at + part], grad[at + part : at + 2 * part])
                keep_ref[high, block * part : (block + 1) * part, :] = mine.astype(bf16)
                send_ref[high, block * part : (block + 1) * part, :] = other.astype(bf16)
        extra = keep_ref.shape[1] - 3 * part
        top_row = lax.broadcasted_iota(jnp.int32, (extra, 1), 0) == 0
        vectors = [gain_grad, shift_grad, sums[0], sums[2]]
        owner_row = lambda owner: jnp.concatenate([v[:, owner * part : (owner + 1) * part] for v in vectors], axis=1)
        for high in range(owners // 2):
            mine, other = choose(low_bit, owner_row(2 * high), owner_row(2 * high + 1))
            keep_ref[high, 3 * part :, :] = jnp.where(top_row, mine, 0.0).astype(bf16)
            send_ref[high, 3 * part :, :] = jnp.where(top_row, other, 0.0).astype(bf16)

        for level in range(LOCAL):
            at, count = offsets[level], level_rows(rows, level)
            edge = slice(BLOCK * level, BLOCK * (level + 1))
            to_left_ref[edge, :] = acc_ref[at : at + BLOCK, :].astype(bf16)
            to_right_ref[edge, :] = acc_ref[at + BLOCK + count : at + 2 * BLOCK + count, :].astype(bf16)
        carry = None
        for index in range(len(far) - 1, -1, -1):
            level = far[index]
            count = base_ref.shape[0] // 2 ** (level - LOCAL + 1)
            tree_ref[0:count, :] = jnp.zeros((count, 2 * WIDTH), f32) if carry is None else spread(carry)
            for side, start in enumerate(far_starts(meta_ref[0], level, count)):
                at = offsets[LOCAL + index] + side * BLOCK
                tree_ref[pl.ds(start, BLOCK), :] += acc_ref[at : at + BLOCK, :]
            carry = tree_ref[0:count, :]
        mine, other = choose_groups(meta_ref[0] & 1, jnp.concatenate([carry[:, :WIDTH], carry[:, WIDTH:]], axis=0))
        far_keep_ref[...] = mine.astype(bf16)
        far_send_ref[...] = other.astype(bf16)
        for level in range(LOCAL - 1, 0, -1):
            at, count = offsets[level] + BLOCK, level_rows(rows, level)
            below = offsets[level - 1] + BLOCK
            tile = min(count, 128)
            for row in range(0, count, tile):
                carry = spread(acc_ref[at + row : at + row + tile, :])
                target = slice(below + 2 * row, below + 2 * (row + tile))
                total = acc_ref[target, :] + carry
                if level == 1:
                    local_ref[2 * row : 2 * (row + tile), :] = total
                else:
                    acc_ref[target, :] = total


def chain_rows(rows, devices):
    unit = 8 * devices
    return -(-(rows + 16) // unit) * unit


def attend_back_call(rows, devices, far, owners, meta, q, grads, bias, logs, levels, scaled, left, right, base, weight, vectors):
    chunks = rows // CHUNK
    _, entries = extended_offsets(rows, far)
    _, slots = slot_layout(far)
    chain = (owners // 2, chain_rows(3 * WIDTH // owners, devices), WIDTH)
    outs = [
        jax.ShapeDtypeStruct((rows, WIDTH), bf16),
        jax.ShapeDtypeStruct((rows, 2 * WIDTH), f32),
        jax.ShapeDtypeStruct((BLOCK * LOCAL, 2 * WIDTH), bf16),
        jax.ShapeDtypeStruct((BLOCK * LOCAL, 2 * WIDTH), bf16),
        jax.ShapeDtypeStruct((8 * devices, WIDTH), bf16),
        jax.ShapeDtypeStruct((8 * devices, WIDTH), bf16),
        jax.ShapeDtypeStruct(chain, bf16),
        jax.ShapeDtypeStruct(chain, bf16),
    ]
    return pl.pallas_call(
        partial(attend_back_kernel, rows, far),
        grid=(chunks,),
        out_shape=outs,
        in_specs=[
            pl.BlockSpec(memory_space=pltpu.SMEM),
            pl.BlockSpec((CHUNK, WIDTH), lambda i: (i, 0)),
            pl.BlockSpec((CHUNK, WIDTH), lambda i: (i, 0)),
            pl.BlockSpec((1, slots, CHUNK), lambda i: (i, 0, 0)),
            pl.BlockSpec((1, 8, 2 * CHUNK), lambda i: (i, 0, 0)),
        ]
        + vmem_specs(2 * LOCAL + 5),
        out_specs=[pl.BlockSpec((CHUNK, WIDTH), lambda i: (i, 0))] + vmem_specs(len(outs) - 1),
        scratch_shapes=[
            pltpu.VMEM((entries, 2 * WIDTH), bf16),
            pltpu.VMEM((8 * devices, 2 * WIDTH), bf16),
            pltpu.VMEM((slots, 2 * WIDTH), bf16),
            pltpu.VMEM((entries, 2 * WIDTH), f32),
            pltpu.VMEM((8 * devices, 2 * WIDTH), f32),
            pltpu.VMEM((entries, WIDTH), bf16),
            pltpu.VMEM((rows, WIDTH), bf16),
        ],
        compiler_params=pltpu.CompilerParams(vmem_limit_bytes=VMEM_LIMIT),
        cost_estimate=pl.CostEstimate(flops=36 << 30, bytes_accessed=24 << 20, transcendentals=4 << 20),
        name="attend_back",
    )(meta, q, grads, bias, logs, *levels, *scaled, left, right, base, weight, vectors)


def normal_parts(values):
    size = jnp.abs(values)
    bell = jnp.exp(-0.5 * values * values)
    t = 1.0 / (1.0 + (0.3275911 / math.sqrt(2.0)) * size)
    poly = t * (
        0.5 * 0.254829592
        + t * (0.5 * -0.284496736 + t * (0.5 * 1.421413741 + t * (0.5 * -1.453152027 + t * (0.5 * 1.061405429))))
    )
    tail = poly * bell
    return jnp.where(values < 0, tail, 1.0 - tail), bell * (1.0 / math.sqrt(2.0 * math.pi))


def feed_kernel(
    hidden_width,
    owners,
    meta_ref,
    x_ref,
    attended_ref,
    cot_ref,
    vec_ref,
    up_bias_ref,
    *refs,
):
    one_refs, two_refs, refs = refs[:owners], refs[owners : 2 * owners], refs[2 * owners :]
    y_ref, grad_middle_ref, grad_attended_ref, keep_ref, send_ref = refs[:5]
    down_w_ref, up_w_ref, out_w_ref, vec_grad_ref, up_bias_grad_ref, down_acc, up_acc, out_acc = refs[5:]
    step = pl.program_id(0)
    rows = WIDTH // owners
    wide_rows = hidden_width // owners
    blocks = hidden_width // WIDTH

    @pl.when(step == 0)
    def _():
        for at, (one, two) in enumerate(zip(one_refs, two_refs)):
            owner = meta_ref[1 + at]
            span = pl.ds(pl.multiple_of(owner * rows, rows), rows)
            for block in range(blocks - 1):
                up_w_ref[span, block * WIDTH : (block + 1) * WIDTH] = one[block * rows : (block + 1) * rows, :]
            up_w_ref[span, (blocks - 1) * WIDTH :] = two[0:rows, :]
            out_w_ref[span, :] = two[rows : 2 * rows, :]
            down_w_ref[pl.ds(pl.multiple_of(owner * wide_rows, wide_rows), wide_rows), :] = two[2 * rows :, :]
        down_acc[...] = jnp.zeros_like(down_acc)
        up_acc[...] = jnp.zeros_like(up_acc)
        out_acc[...] = jnp.zeros_like(out_acc)
        vec_grad_ref[...] = jnp.zeros_like(vec_grad_ref)
        up_bias_grad_ref[...] = jnp.zeros_like(up_bias_grad_ref)

    out_bias, gain, shift, down_bias = (vec_ref[4 + at : 5 + at, :] for at in range(4))
    attended = attended_ref[...]
    middle = x_ref[...].astype(f32) + dot_nn(attended, out_w_ref[...]) + out_bias
    scaled, inverse = norm_rows(middle)
    normed = (scaled * gain + shift).astype(bf16)
    cot = cot_ref[...]
    wide = cot.astype(f32)
    lowered = jnp.zeros_like(middle)
    grad_normed = jnp.zeros_like(middle)
    for block in range(blocks):
        columns = slice(block * WIDTH, (block + 1) * WIDTH)
        down = down_w_ref[columns, :]
        pre = dot_nn(normed, up_w_ref[:, columns]) + up_bias_ref[:, columns]
        phi, bell = normal_parts(pre)
        hidden = (pre * phi).astype(bf16)
        lowered += dot_nn(hidden, down)
        grad_pre = (dot_nt(cot, down) * (phi + pre * bell)).astype(bf16)
        up_bias_grad_ref[:, columns] += column_sum(grad_pre.astype(f32))
        grad_normed += dot_nt(grad_pre, up_w_ref[:, columns])
        down_acc[columns, :] += dot_tn(hidden, cot)
        up_acc[:, columns] += dot_tn(normed, grad_pre)
    y_ref[...] = (middle + lowered + down_bias).astype(bf16)
    grad_middle = wide + norm_back(grad_normed, scaled, inverse, gain)
    grad_middle_ref[...] = grad_middle
    grad_proj = grad_middle.astype(bf16)
    grad_attended_ref[...] = dot_nt(grad_proj, out_w_ref[...]).astype(bf16)
    out_acc[...] += dot_tn(attended, grad_proj)
    vec_grad_ref[0:1, :] += column_sum(grad_proj.astype(f32))
    vec_grad_ref[1:2, :] += column_sum(grad_normed * scaled)
    vec_grad_ref[2:3, :] += column_sum(grad_normed)
    vec_grad_ref[3:4, :] += column_sum(wide)

    @pl.when(step == pl.num_programs(0) - 1)
    def _():
        extra = keep_ref.shape[1] - wide_rows - (blocks + 1) * rows
        row_at = lax.broadcasted_iota(jnp.int32, (extra, 1), 0)
        low_bit = meta_ref[1] & 1

        def put(high, at, count, source):
            mine, other = choose(low_bit, source(2 * high), source(2 * high + 1))
            keep_ref[high, at : at + count, :] = mine.astype(bf16)
            send_ref[high, at : at + count, :] = other.astype(bf16)

        def small(owner):
            first = [vec_grad_ref[i : i + 1, owner * rows : (owner + 1) * rows] for i in range(4)]
            second = up_bias_grad_ref[:, owner * wide_rows : (owner + 1) * wide_rows]
            return jnp.where(row_at == 0, jnp.concatenate(first, axis=1), jnp.where(row_at == 1, second, 0.0))

        for high in range(owners // 2):
            put(high, 0, wide_rows, lambda owner: down_acc[owner * wide_rows : (owner + 1) * wide_rows, :])
            at = wide_rows
            for block in range(blocks):
                columns = slice(block * WIDTH, (block + 1) * WIDTH)
                put(high, at, rows, lambda owner: up_acc[owner * rows : (owner + 1) * rows, columns])
                at += rows
            put(high, at, rows, lambda owner: out_acc[owner * rows : (owner + 1) * rows, :])
            put(high, at + rows, extra, small)


def feed_call(hidden_width, devices, meta, x, attended, cot, vectors, up_bias, ones, twos):
    rows, owners = x.shape[0], len(ones)
    tile = 256
    row_spec = pl.BlockSpec((tile, WIDTH), lambda i: (i, 0))
    chain = chain_rows(2 * (hidden_width // owners) + WIDTH // owners, devices)
    split = jax.ShapeDtypeStruct((owners // 2, chain, WIDTH), bf16)
    return pl.pallas_call(
        partial(feed_kernel, hidden_width, owners),
        grid=(rows // tile,),
        out_shape=[
            jax.ShapeDtypeStruct((rows, WIDTH), bf16),
            jax.ShapeDtypeStruct((rows, WIDTH), f32),
            jax.ShapeDtypeStruct((rows, WIDTH), bf16),
            split,
            split,
        ],
        in_specs=[pl.BlockSpec(memory_space=pltpu.SMEM), row_spec, row_spec, row_spec] + vmem_specs(2 + 2 * owners),
        out_specs=[row_spec, row_spec, row_spec] + vmem_specs(2),
        scratch_shapes=[
            pltpu.VMEM((hidden_width, WIDTH), bf16),
            pltpu.VMEM((WIDTH, hidden_width), bf16),
            pltpu.VMEM((WIDTH, WIDTH), bf16),
            pltpu.VMEM((8, WIDTH), f32),
            pltpu.VMEM((1, hidden_width), f32),
            pltpu.VMEM((hidden_width, WIDTH), f32),
            pltpu.VMEM((WIDTH, hidden_width), f32),
            pltpu.VMEM((WIDTH, WIDTH), f32),
        ],
        compiler_params=pltpu.CompilerParams(vmem_limit_bytes=VMEM_LIMIT),
        cost_estimate=pl.CostEstimate(flops=32 << 30, bytes_accessed=20 << 20, transcendentals=4 << 20),
        name="feed_forward",
    )(meta, x, attended, cot, vectors, up_bias, *ones, *twos)


def input_grad_kernel(
    x_ref,
    dq_refs,
    local_refs,
    grad_middle_ref,
    from_right_ref,
    from_left_ref,
    far_keep_ref,
    far_got_ref,
    w_ref,
    vec_ref,
    out_ref,
    tree_ref,
):
    rows = tree_ref.shape[0]
    step = pl.program_id(0)
    tile = x_ref.shape[0]

    @pl.when(step == 0)
    def _():
        folded = far_keep_ref[...].astype(f32) + far_got_ref[...].astype(f32)
        carry = spread(jnp.concatenate([folded[:8], folded[8:]], axis=1))
        for level in range(LOCAL - 1, -1, -1):
            count = level_rows(rows, level)
            edge = slice(BLOCK * level, BLOCK * (level + 1))
            if level == LOCAL - 1:
                tree_ref[0:count, :] = carry
            tree_ref[0:BLOCK, :] += from_left_ref[edge, :].astype(f32)
            tree_ref[count - BLOCK : count, :] += from_right_ref[edge, :].astype(f32)
            if level:
                part = min(count, 128)
                for row in range(count - part, -1, -part):
                    tree_ref[2 * row : 2 * (row + part), :] = spread(tree_ref[row : row + part, :])

    span = pl.ds(pl.multiple_of(step * tile, tile), tile)
    scaled, inverse = norm_rows(x_ref[...].astype(f32))
    grad = jnp.zeros((tile, WIDTH), f32)
    half = dq_refs[0].shape[1]
    for index, (dq_ref, local_ref) in enumerate(zip(dq_refs, local_refs)):
        lane = index * half
        grad += dot_nt(dq_ref[...], w_ref[:, lane : lane + half])
        for block in range(2):
            column = block * WIDTH + lane
            dkv = (local_ref[:, block * half : (block + 1) * half] + tree_ref[span, column : column + half]).astype(bf16)
            grad += dot_nt(dkv, w_ref[:, WIDTH + column : WIDTH + column + half])
    out_ref[...] = grad_middle_ref[...] + norm_back(grad, scaled, inverse, vec_ref[0:1, :])


def input_grad_call(x, dqs, locals_, grad_middle, from_right, from_left, far_keep, far_got, weight, vectors):
    rows = x.shape[0]
    tile = 256
    count = len(dqs)
    tiled = lambda width: pl.BlockSpec((tile, width), lambda i: (i, 0))

    def kernel(x_ref, *refs):
        input_grad_kernel(x_ref, refs[:count], refs[count : 2 * count], *refs[2 * count :])

    return pl.pallas_call(
        kernel,
        grid=(rows // tile,),
        out_shape=jax.ShapeDtypeStruct((rows, WIDTH), f32),
        in_specs=[tiled(WIDTH)]
        + [tiled(d.shape[1]) for d in dqs]
        + [tiled(d.shape[1]) for d in locals_]
        + [tiled(WIDTH)]
        + vmem_specs(6),
        out_specs=tiled(WIDTH),
        scratch_shapes=[pltpu.VMEM((rows, 2 * WIDTH), f32)],
        compiler_params=pltpu.CompilerParams(vmem_limit_bytes=VMEM_LIMIT),
        cost_estimate=pl.CostEstimate(flops=8 << 30, bytes_accessed=14 << 20, transcendentals=0),
        name="input_grad",
    )(x, *dqs, *locals_, grad_middle, from_right, from_left, far_keep, far_got, weight, vectors)


def shifted(block, axis, distance):
    devices = range(lax.axis_size(axis))
    route = [(i - distance, i) for i in devices if i - distance in devices]
    return lax.ppermute(block, axis, route)


def swap(block, axis, bit):
    return lax.ppermute(block, axis, [(i, i ^ bit) for i in range(lax.axis_size(axis))])


def gather_step(part, axis, bit):
    mine = (lax.axis_index(axis) // bit) % 2
    other = swap(part, axis, bit)
    first = jnp.where(mine == 0, part, other)
    second = jnp.where(mine == 0, other, part)
    return jnp.concatenate([first, second], axis=0)


def together(*values):
    return lax.optimization_barrier(values)


def bits_of(axis):
    size = lax.axis_size(axis)
    return [1 << at for at in range(size.bit_length() - 1)]


def step_call(name, function, meta, arrays, shapes, dtype=bf16):
    def kernel(meta_ref, *refs):
        values = [ref[...].astype(f32) for ref in refs[: len(arrays)]]
        for ref, value in zip(refs[len(arrays) :], function(meta_ref[0], meta_ref[1], *values), strict=True):
            ref[...] = value.astype(dtype)

    size = sum(math.prod(a.shape) for a in arrays)
    return pl.pallas_call(
        kernel,
        out_shape=[jax.ShapeDtypeStruct(shape, dtype) for shape in shapes],
        in_specs=[pl.BlockSpec(memory_space=pltpu.SMEM)] + vmem_specs(len(arrays)),
        out_specs=vmem_specs(len(shapes)),
        compiler_params=pltpu.CompilerParams(vmem_limit_bytes=VMEM_LIMIT),
        cost_estimate=pl.CostEstimate(flops=1 << 20, bytes_accessed=4 * size, transcendentals=0),
        name=name,
    )(meta, *arrays)


def halves(values, axis=0):
    return jnp.split(values, 2, axis=axis)


class Reduction:
    def __init__(self, meta, keep, send, far=None):
        self.meta, self.rows, self.far = meta, keep.shape[1], far
        self.bits = bits_of("ctx")[1:]
        self.keep, self.got = keep, [swap(send, "fsdp", 1)]

    def call(self, name, function, arrays, *shapes):
        return step_call(name, function, self.meta, arrays, [(*shape, WIDTH) for shape in shapes])

    def cross(self):
        far = [self.far[1]] if self.far else []
        extra = far[0].shape[0] if far else 0
        half = self.rows // 2

        def function(here, owner, keep, got, *far):
            mine, other = choose(owner >> 1, *(keep + got))
            keep, near = choose(here & 1, *halves(mine))
            high, both = choose(here & 1, *halves(other))
            return keep, jnp.concatenate([near, *far], axis=0), high, both

        shapes = [(half,), (half + extra,), (half,), (half,)]
        self.keep, near, high, both = self.call("cross", function, [self.keep, *self.got, *far], *shapes)
        count = lax.axis_size("fsdp")
        route = [(i, i ^ count ^ 2) for i in range(count * lax.axis_size("ctx"))]
        self.got = [swap(near, "ctx", 1), swap(high, "fsdp", 2), lax.ppermute(both, ("ctx", "fsdp"), route)]

    def scatter(self, at):
        bit, last = self.bits[at], at == len(self.bits) - 1
        rows = self.keep.shape[0]
        far = [self.far[0]] if self.far else []
        extra = far[0].shape[0] // 2 if far else 0

        def function(here, owner, keep, *got):
            far_keep = got[-1]
            got = got[: len(got) - len(far)]
            total = keep + got[0][:rows]
            for other in got[1:]:
                total = total + other
            flag = (here // bit) & 1
            keep, send = (total, total) if last else choose(flag, *halves(total))
            if not far:
                return [keep] if last else [keep, send]
            far_keep, far_send = choose_groups(flag, far_keep + got[0][rows:])
            return keep, jnp.concatenate([send, far_send], axis=0), far_keep

        count = rows if last else rows // 2
        shapes = [(count,)] if last and not far else [(count,), (count + extra,)]
        out = self.call("scatter", function, [self.keep, *self.got, *far], *shapes, *([(extra,)] if far else []))
        self.keep, send = out[0], out[1] if len(out) > 1 else out[0]
        self.got = [swap(send, "ctx", bit)]
        if far:
            self.far = (out[2], None)

    def gather(self, at):
        rows = self.keep.shape[0]
        bit = self.bits[at]
        last = at == len(self.bits) - 1
        if last and self.far:
            self.far = (self.far[0], self.got[0][rows:])

        def function(here, owner, keep, got):
            if last:
                return [keep + got[:rows]]
            return [jnp.concatenate(choose((here // bit) & 1, keep, got), axis=0)]

        (self.keep,) = self.call("gather", function, [self.keep, *self.got], (rows if last else 2 * rows,))
        self.got = [swap(self.keep, "ctx", self.bits[at - 1] if at else 1)]

    def steps(self):
        count = len(self.bits)
        return (
            [self.cross]
            + [partial(self.scatter, at) for at in range(count)]
            + [partial(self.gather, at) for at in range(count - 1, -1, -1)]
        )

    def finish(self, shapes, unpack):
        def function(here, owner, keep, got):
            return unpack(jnp.concatenate(choose(here & 1, keep, got), axis=0))

        return step_call("finish", function, self.meta, [self.keep, *self.got], shapes, f32)


def shards(
    layer_input,
    doc_lengths,
    ln1_gain,
    ln1_bias,
    qkv_weight,
    query_bias,
    value_bias,
    out_weight,
    out_bias,
    ln2_gain,
    ln2_bias,
    up_weight,
    up_bias,
    down_weight,
    down_bias,
    cotangent,
):
    owners = lax.axis_size("fsdp")
    devices = lax.axis_size("ctx")
    x, cot = layer_input[0], cotangent[0]
    rows = x.shape[0]
    total = rows * devices
    far = far_levels(total)
    here, owner = lax.axis_index("ctx"), lax.axis_index("fsdp")
    part = WIDTH // owners
    hidden_width = up_weight.shape[1]
    meta = jnp.stack([here] + [owner ^ at for at in range(owners)]).astype(jnp.int32)

    vectors = [ln1_gain, ln1_bias, query_bias, value_bias, out_bias, ln2_gain, ln2_bias, down_bias, up_bias]
    own = pack_call(qkv_weight, vectors)
    across = swap(own, "fsdp", 2)
    beside = swap(own, "fsdp", 1)
    one, two = pack_rest_call(down_weight, up_weight, out_weight)
    bias = mask_call(rows, total, far, meta, doc_lengths)
    across, beside, one, two, bias = together(across, beside, one, two, bias)
    pieces = [own, beside, across, swap(across, "fsdp", 1)]
    one_across = swap(one, "fsdp", 2)
    *made, one_across = together(*qkv_call(rows, hidden_width, meta, x, pieces, bias), one_across)
    qkv_full, vec, up_shift, queries = made[:4]
    levels, scaled, (tail, head, base) = made[4 : 4 + LOCAL], made[4 + LOCAL : 4 + 2 * LOCAL], made[4 + 2 * LOCAL :]

    two, one, tail, head, base = together(two, one, tail, head, base)
    two_across = swap(two, "fsdp", 2)
    one_beside, one_both = swap(one, "fsdp", 1), swap(one_across, "fsdp", 1)
    left = shifted(tail, "ctx", 1)
    right = shifted(head, "ctx", -1)
    for at, bit in enumerate(bits_of("ctx")):
        base = gather_step(base, "ctx", bit)
        if at == 0:
            base, left, right = together(base, left, right)
    base, one_beside, one_both, two_across = together(base, one_beside, one_both, two_across)

    two_beside, two_both = swap(two, "fsdp", 1), swap(two_across, "fsdp", 1)
    attended, logs = attend_call(rows, devices, far, meta, queries, bias, levels, left, right, base)
    attended, logs, two_beside, two_both = together(attended, logs, two_beside, two_both)
    output, grad_middle, grad_attended, keep, send = feed_call(
        hidden_width,
        devices,
        meta,
        x,
        attended,
        cot,
        vec,
        up_shift,
        [one, one_beside, one_across, one_both],
        [two, two_beside, two_across, two_both],
    )
    feed = Reduction(meta, keep, send)
    todo = feed.steps()
    todo.pop(0)()
    grad_attended, feed.keep = together(grad_attended, feed.keep)
    made = attend_back_call(
        rows, devices, far, owners, meta, queries, grad_attended, bias, logs, levels, scaled, left, right, base, qkv_full, vec
    )
    count = len(made)
    made = together(*made, *feed.got)
    feed.got = list(made[count:])
    dq, local, to_left, to_right, far_keep, far_send, keep, send = made[:count]
    first = Reduction(meta, keep, send, (far_keep, far_send))
    back_right = shifted(to_left, "ctx", -1)
    back_left = shifted(to_right, "ctx", 1)
    for one, two in zip(first.steps(), todo + [None]):
        if two:
            two()
        one()
    input_grad = input_grad_call(
        x, [dq], [local], grad_middle, back_right, back_left, *first.far, qkv_full, vec
    )

    wide_rows = hidden_width // owners

    def unpack_first(total):
        blocks = [total[at * part : (at + 1) * part] for at in range(3)]
        return [jnp.concatenate(blocks, axis=1), total[3 * part : 3 * part + 1]]

    def unpack_feed(total):
        at = wide_rows
        blocks = []
        for _ in range(hidden_width // WIDTH):
            blocks.append(total[at : at + part])
            at += part
        return [
            total[:wide_rows],
            jnp.concatenate(blocks, axis=1),
            total[at : at + part],
            total[at + part : at + part + 1],
            total[at + part + 1 : at + part + 2],
        ]

    qkv_grad, first_row = first.finish([(part, 3 * WIDTH), (1, WIDTH)], unpack_first)
    down_grad, up_grad, out_grad, feed_row, up_row = feed.finish(
        [(wide_rows, WIDTH), (part, hidden_width), (part, WIDTH), (1, WIDTH), (1, WIDTH)], unpack_feed
    )
    pick = lambda row, at: row[0, at * part : (at + 1) * part]
    return (
        output[None],
        input_grad[None],
        pick(first_row, 0),
        pick(first_row, 1),
        qkv_grad,
        pick(first_row, 2),
        pick(first_row, 3),
        out_grad,
        pick(feed_row, 0),
        pick(feed_row, 1),
        pick(feed_row, 2),
        up_grad,
        up_row[0],
        down_grad,
        pick(feed_row, 3),
    )


def solution(mesh):
    row, vector = P("fsdp", None), P("fsdp")
    tokens = P("fsdp", "ctx", None)
    return jax.shard_map(
        shards,
        mesh=mesh,
        in_specs=(
            tokens,
            row,
            vector,
            vector,
            row,
            vector,
            vector,
            row,
            vector,
            vector,
            vector,
            row,
            vector,
            row,
            vector,
            tokens,
        ),
        out_specs=(
            tokens,
            tokens,
            vector,
            vector,
            row,
            vector,
            vector,
            row,
            vector,
            vector,
            vector,
            row,
            vector,
            row,
            vector,
        ),
        check_vma=False,
    )
```

```python
from functools import partial
import math

import jax
import jax.numpy as jnp
from jax import lax
from jax.experimental import pallas as pl
from jax.experimental.pallas import tpu as pltpu
from jax.sharding import PartitionSpec as P

HEADS = 8
BLOCK = 16
LEVELS = 10
NEAR = 4
LOCAL = 7
CHUNK = 128
WIDTH = 512
PAIRS = HEADS // 2
ENTRY = 3 * WIDTH
SMALL = 16
MASKED = -1e30
EPSILON = 1e-05

f32 = jnp.float32
bf16 = jnp.bfloat16


def level_rows(rows, level):
    return rows // 2**level


def level_offsets(rows):
    offsets = [0]
    for level in range(LOCAL):
        offsets.append(offsets[-1] + level_rows(rows, level))
    return offsets[:-1], offsets[-1]


def far_levels(total):
    return [l for l in range(LOCAL, LEVELS) if total // (BLOCK * 2**l) >= 2]


def extended_offsets(rows, far):
    offsets, cursor = [], 0
    for level in range(LOCAL):
        offsets.append(cursor)
        cursor += level_rows(rows, level) + 2 * BLOCK
    for _ in far:
        offsets.append(cursor)
        cursor += 2 * BLOCK
    return offsets, cursor


def slot_layout(far):
    parts = [(level, CHUNK // 2**level + 2 * BLOCK) for level in range(NEAR)]
    parts += [(level, BLOCK) for level in list(range(NEAR, LOCAL)) + far for _ in range(2)]
    return parts, sum(count for _, count in parts)


def slot_sources(rows, far, chunk):
    offsets, _ = extended_offsets(rows, far)
    sources = []
    for level in range(NEAR):
        sources.append((offsets[level] + chunk * (CHUNK // 2**level), CHUNK // 2**level + 2 * BLOCK))
    for level in range(NEAR, LOCAL):
        block = chunk // (BLOCK * 2**level // CHUNK)
        sources.append((offsets[level] + block * BLOCK, BLOCK))
        sources.append((offsets[level] + block * BLOCK + 2 * BLOCK, BLOCK))
    for at in range(len(far)):
        sources.append((offsets[LOCAL + at], BLOCK))
        sources.append((offsets[LOCAL + at] + BLOCK, BLOCK))
    return sources


def mask_kernel(rows, total, far, here_ref, lengths_ref, bias_ref):
    base = here_ref[0] * rows + pl.program_id(0) * CHUNK
    query = base + lax.broadcasted_iota(jnp.int32, (1, CHUNK), 1)
    first_token = jnp.zeros((1, CHUNK), jnp.int32)
    end_token = jnp.full((1, CHUNK), total, jnp.int32)
    start = jnp.int32(0)
    for at in range(lengths_ref.shape[1]):
        first_token = jnp.where(start <= query, start, first_token)
        start = start + lengths_ref[0, at]
        end_token = jnp.where(start > query, jnp.minimum(end_token, start), end_token)

    def part(at, count, first_row, level):
        span = 2**level
        shift = level + 4
        first = first_row + span * lax.broadcasted_iota(jnp.int32, (count, CHUNK), 0)
        gap = jnp.abs((first >> shift) - (query >> shift))
        if level == 0:
            seen = gap <= 1
        else:
            seen = (gap == 1) & (jnp.abs((first >> (shift - 1)) - (query >> (shift - 1))) > 1)
        seen = seen & (first >= first_token) & (first + (span - 1) < end_token)
        bias_ref[0, at : at + count, :] = jnp.where(seen, level * math.log(2.0), MASKED)

    at = 0
    for level in range(NEAR):
        count = CHUNK // 2**level + 2 * BLOCK
        part(at, count, base - BLOCK * 2**level, level)
        at += count
    for level in list(range(NEAR, LOCAL)) + far:
        block = base >> (level + 4)
        for side in (-1, 1):
            part(at, BLOCK, (block + side) * (BLOCK * 2**level), level)
            at += BLOCK


def mask_call(rows, total, far, meta, lengths):
    chunks = rows // CHUNK
    _, slots = slot_layout(far)
    return pl.pallas_call(
        partial(mask_kernel, rows, total, far),
        grid=(chunks,),
        out_shape=jax.ShapeDtypeStruct((chunks, slots, CHUNK), f32),
        in_specs=[pl.BlockSpec(memory_space=pltpu.SMEM)] * 2,
        out_specs=pl.BlockSpec((1, slots, CHUNK), lambda i: (i, 0, 0)),
        compiler_params=pltpu.CompilerParams(vmem_limit_bytes=8 << 20),
        cost_estimate=pl.CostEstimate(flops=4 << 30, bytes_accessed=3 << 20, transcendentals=0),
        name="mask",
    )(meta, lengths)


def dot_nt(left, right):
    return lax.dot_general(left, right, (((1,), (1,)), ((), ())), preferred_element_type=f32)


def dot_tn(left, right):
    return lax.dot_general(left, right, (((0,), (0,)), ((), ())), preferred_element_type=f32)


def dot_nn(left, right):
    return jnp.dot(left, right, preferred_element_type=f32)


def pool_matrix(count):
    row = lax.broadcasted_iota(jnp.int32, (count // 2, count), 0)
    column = lax.broadcasted_iota(jnp.int32, (count // 2, count), 1)
    return jnp.where((column >> 1) == row, 0.5, 0.0).astype(bf16)


def spread_matrix(count):
    row = lax.broadcasted_iota(jnp.int32, (2 * count, count), 0)
    column = lax.broadcasted_iota(jnp.int32, (2 * count, count), 1)
    return jnp.where((row >> 1) == column, 0.5, 0.0).astype(bf16)


def spread(values):
    count = values.shape[0]
    tile = min(count, 128)
    matrix = spread_matrix(tile)
    high = values.astype(bf16)
    low = (values - high.astype(f32)).astype(bf16)
    parts = [
        dot_nn(matrix, high[at : at + tile]) + dot_nn(matrix, low[at : at + tile])
        for at in range(0, count, tile)
    ]
    return parts[0] if len(parts) == 1 else jnp.concatenate(parts, axis=0)


def norm_rows(values):
    mean = jnp.mean(values, axis=-1, keepdims=True)
    centred = values - mean
    variance = jnp.mean(centred * centred, axis=-1, keepdims=True)
    inverse = lax.rsqrt(variance + EPSILON)
    return centred * inverse, inverse


def norm_back(grad_out, scaled, inverse, gain):
    grad_scaled = grad_out * gain
    first = jnp.mean(grad_scaled, axis=-1, keepdims=True)
    second = jnp.mean(grad_scaled * scaled, axis=-1, keepdims=True)
    return inverse * (grad_scaled - first - scaled * second)


def split_heads(pair):
    lane = lax.broadcasted_iota(jnp.int32, pair.shape, 1)
    zero = jnp.zeros_like(pair)
    return jnp.concatenate([jnp.where(lane < 64, pair, zero), jnp.where(lane < 64, zero, pair)], axis=0)


def join_heads(stacked):
    rows = stacked.shape[0] // 2
    lane = lax.broadcasted_iota(jnp.int32, (rows, stacked.shape[1]), 1)
    return jnp.where(lane < 64, stacked[:rows], stacked[rows:])


def pack_kernel(w_ref, *refs):
    out_ref = refs[-1]
    part = w_ref.shape[0]
    out_ref[0:part, :] = w_ref[...]
    row = jnp.concatenate([ref[...].reshape(1, -1) for ref in refs[:-1]], axis=1)
    out_ref[part : part + SMALL, :] = jnp.broadcast_to(row.astype(f32), (SMALL, row.shape[1])).astype(bf16)


def pack_call(weight, vectors):
    return pl.pallas_call(
        pack_kernel,
        out_shape=jax.ShapeDtypeStruct((weight.shape[0] + SMALL, weight.shape[1]), bf16),
        in_specs=vmem_specs(1 + len(vectors)),
        out_specs=vmem_specs(1)[0],
        compiler_params=pltpu.CompilerParams(vmem_limit_bytes=56 << 20),
        name="pack",
    )(weight, *vectors)


def pack_rest_kernel(down_ref, up_ref, out_w_ref, one_ref, two_ref):
    rows = up_ref.shape[0]
    blocks = up_ref.shape[1] // WIDTH
    for block in range(blocks - 1):
        one_ref[block * rows : (block + 1) * rows, :] = up_ref[:, block * WIDTH : (block + 1) * WIDTH]
    two_ref[0:rows, :] = up_ref[:, (blocks - 1) * WIDTH :]
    two_ref[rows : 2 * rows, :] = out_w_ref[...]
    two_ref[2 * rows :, :] = down_ref[...]


def pack_rest_call(down, up, out_w):
    rows, blocks = up.shape[0], up.shape[1] // WIDTH
    return pl.pallas_call(
        pack_rest_kernel,
        out_shape=[
            jax.ShapeDtypeStruct(((blocks - 1) * rows, WIDTH), bf16),
            jax.ShapeDtypeStruct((2 * rows + down.shape[0], WIDTH), bf16),
        ],
        in_specs=vmem_specs(3),
        out_specs=vmem_specs(2),
        compiler_params=pltpu.CompilerParams(vmem_limit_bytes=56 << 20),
        name="pack_rest",
    )(down, up, out_w)


def vmem_specs(count):
    return [pl.BlockSpec(memory_space=pltpu.VMEM)] * count


def qkv_kernel(rows, owners, meta_ref, x_ref, *refs):
    shard_refs, refs = refs[:owners], refs[owners + 2 :]
    w_ref, vec_ref, up_bias_ref, q_ref = refs[:4]
    kv_ref, scaled_ref, tail_ref, head_ref, top_ref, keep_ref = refs[4:]
    places, _ = level_offsets(rows)
    part = WIDTH // owners
    step = pl.program_id(0)

    @pl.when(step == 0)
    def _():
        for at, ref in enumerate(shard_refs):
            owner = meta_ref[1 + at]
            w_ref[pl.ds(pl.multiple_of(owner * part, part), part), :] = ref[0:part, :]
            row = ref[part : part + 1, :].astype(f32)
            for vector in range(8):
                vec_ref[vector : vector + 1, pl.ds(pl.multiple_of(owner * part, part), part)] = row[
                    :, vector * part : (vector + 1) * part
                ]
            wide = row.shape[1] - 8 * part
            up_bias_ref[:, pl.ds(pl.multiple_of(owner * wide, wide), wide)] = row[:, 8 * part :]

    tile = x_ref.shape[0]
    scaled, _ = norm_rows(x_ref[...].astype(f32))
    normed = (scaled * vec_ref[0:1, :] + vec_ref[1:2, :]).astype(bf16)
    queries = (dot_nn(normed, w_ref[:, :WIDTH]) + vec_ref[2:3, :]).astype(bf16)
    q_ref[...] = queries * jnp.asarray(0.125, bf16)
    keys = dot_nn(normed, w_ref[:, WIDTH : 2 * WIDTH]).astype(bf16)
    values = (dot_nn(normed, w_ref[:, 2 * WIDTH :]) + vec_ref[3:4, :]).astype(bf16)
    current = jnp.concatenate([keys, values, scaled.astype(bf16)], axis=1)

    def edges(level, block):
        @pl.when(step == 0)
        def _():
            head_ref[BLOCK * level : BLOCK * (level + 1), :] = block[:BLOCK]

        @pl.when(step == pl.num_programs(0) - 1)
        def _():
            tail_ref[BLOCK * level : BLOCK * (level + 1), :] = block[block.shape[0] - BLOCK :]

    for level in range(5):
        if level:
            current = dot_nn(pool_matrix(current.shape[0]), current).astype(bf16)
        count = tile // 2**level
        span = pl.ds(pl.multiple_of(places[level] + step * count, count), count)
        kv_ref[span, :] = current[:, : 2 * WIDTH]
        scaled_ref[span, :] = current[:, 2 * WIDTH :]
        edges(level, current)
    keep_ref[pl.ds(pl.multiple_of(step * count, count), count), :] = current

    @pl.when(step == pl.num_programs(0) - 1)
    def _():
        current = keep_ref[...]
        for level in range(5, LOCAL):
            current = dot_nn(pool_matrix(current.shape[0]), current).astype(bf16)
            span = slice(places[level], places[level] + current.shape[0])
            kv_ref[span, :] = current[:, : 2 * WIDTH]
            scaled_ref[span, :] = current[:, 2 * WIDTH :]
            tail_ref[BLOCK * level : BLOCK * (level + 1), :] = current[current.shape[0] - BLOCK :]
            head_ref[BLOCK * level : BLOCK * (level + 1), :] = current[:BLOCK]
        top_ref[...] = dot_nn(pool_matrix(BLOCK), current).astype(bf16)


def qkv_call(rows, hidden_width, meta, x, pieces, earlier):
    owners = len(pieces)
    tile = 256

    def tiled(count, width):
        return pl.BlockSpec((count, width), lambda i: (i, 0))

    _, entries = level_offsets(rows)
    edge = jax.ShapeDtypeStruct((BLOCK * LOCAL, ENTRY), bf16)
    outs = pl.pallas_call(
        partial(qkv_kernel, rows, owners),
        grid=(rows // tile,),
        out_shape=[
            jax.ShapeDtypeStruct((WIDTH, 3 * WIDTH), bf16),
            jax.ShapeDtypeStruct((8, WIDTH), f32),
            jax.ShapeDtypeStruct((1, hidden_width), f32),
            jax.ShapeDtypeStruct((rows, WIDTH), bf16),
        ]
        + [jax.ShapeDtypeStruct((entries, 2 * WIDTH), bf16), jax.ShapeDtypeStruct((entries, WIDTH), bf16)]
        + [edge, edge, jax.ShapeDtypeStruct((BLOCK // 2, ENTRY), bf16)],
        in_specs=[pl.BlockSpec(memory_space=pltpu.SMEM), tiled(tile, WIDTH)]
        + vmem_specs(owners)
        + [pl.BlockSpec(memory_space=pl.ANY)] * 2,
        out_specs=vmem_specs(3) + [tiled(tile, WIDTH)] + vmem_specs(5),
        scratch_shapes=[pltpu.VMEM((level_rows(rows, 4), ENTRY), bf16)],
        compiler_params=pltpu.CompilerParams(vmem_limit_bytes=56 << 20),
        cost_estimate=pl.CostEstimate(flops=9 << 30, bytes_accessed=12 << 20, transcendentals=0),
        name="qkv_levels",
    )(meta, x, *pieces, *earlier)
    return outs


def far_level(entries):
    return dot_nn(pool_matrix(entries.shape[0]), entries).astype(bf16)


def assemble(rows, far, here, columns, own_ref, left_ref, right_ref, base_ref, ext_ref, far_ref):
    offsets, _ = extended_offsets(rows, far)
    places, _ = level_offsets(rows)
    for inner, outer, target, width in columns:
        lanes, edge_lanes = slice(target, target + width), slice(outer, outer + width)
        for level in range(LOCAL):
            at, count = offsets[level], level_rows(rows, level)
            edge = slice(BLOCK * level, BLOCK * (level + 1))
            ext_ref[at : at + BLOCK, lanes] = left_ref[edge, edge_lanes]
            ext_ref[at + BLOCK : at + BLOCK + count, lanes] = own_ref[
                places[level] : places[level] + count, inner : inner + width
            ]
            ext_ref[at + BLOCK + count : at + 2 * BLOCK + count, lanes] = right_ref[edge, edge_lanes]
        current = base_ref[:, edge_lanes]
        for index, level in enumerate(far):
            if index:
                current = far_level(current)
            count = current.shape[0]
            far_ref[0:count, 0:width] = current
            for side, start in enumerate(far_starts(here, level, count)):
                at = offsets[LOCAL + index] + side * BLOCK
                ext_ref[at : at + BLOCK, lanes] = far_ref[pl.ds(start, BLOCK), 0:width]


def far_starts(here, level, count):
    block = here >> (level - 6)
    last = count // BLOCK - 1
    return [pl.multiple_of(jnp.clip(at, 0, last) * BLOCK, BLOCK) for at in (block - 1, block + 1)]


def load_slots(rows, far, chunk, ext_ref, slots_ref):
    at = 0
    for start, count in slot_sources(rows, far, chunk):
        if not isinstance(start, int):
            start = pl.multiple_of(start, BLOCK)
        slots_ref[at : at + count, :] = ext_ref[pl.ds(start, count), :]
        at += count


def attend_kernel(rows, far, meta_ref, q_ref, bias_ref, *refs):
    own_ref, left_ref, right_ref, base_ref, out_ref, log_ref, ext_ref, far_ref, slots_ref = refs
    chunk = pl.program_id(0)

    @pl.when(chunk == 0)
    def _():
        columns = [(0, 0, 0, 2 * WIDTH)]
        assemble(rows, far, meta_ref[0], columns, own_ref, left_ref, right_ref, base_ref, ext_ref, far_ref)

    load_slots(rows, far, chunk, ext_ref, slots_ref)
    bias = bias_ref[0]
    bias = jnp.concatenate([bias, bias], axis=1)
    for pair in range(PAIRS):
        lanes = slice(128 * pair, 128 * (pair + 1))
        values = slots_ref[:, WIDTH + 128 * pair : WIDTH + 128 * (pair + 1)]
        scores = dot_nt(slots_ref[:, lanes], split_heads(q_ref[:, lanes])) + bias
        top = jnp.max(scores, axis=0, keepdims=True)
        exponent = jnp.exp(scores - top)
        total = jnp.sum(exponent, axis=0, keepdims=True)
        probs = (exponent * (1.0 / total)).astype(bf16)
        out_ref[:, lanes] = join_heads(dot_tn(probs, values)).astype(bf16)
        log_ref[0, pair : pair + 1, :] = top + jnp.log(total)


def attend_call(rows, devices, far, meta, q, bias, kv, left, right, base):
    chunks = rows // CHUNK
    _, entries = extended_offsets(rows, far)
    _, slots = slot_layout(far)
    return pl.pallas_call(
        partial(attend_kernel, rows, far),
        grid=(chunks,),
        out_shape=[
            jax.ShapeDtypeStruct((rows, WIDTH), bf16),
            jax.ShapeDtypeStruct((chunks, 8, 2 * CHUNK), f32),
        ],
        in_specs=[
            pl.BlockSpec(memory_space=pltpu.SMEM),
            pl.BlockSpec((CHUNK, WIDTH), lambda i: (i, 0)),
            pl.BlockSpec((1, slots, CHUNK), lambda i: (i, 0, 0)),
        ]
        + vmem_specs(4),
        out_specs=[
            pl.BlockSpec((CHUNK, WIDTH), lambda i: (i, 0)),
            pl.BlockSpec((1, 8, 2 * CHUNK), lambda i: (i, 0, 0)),
        ],
        scratch_shapes=[
            pltpu.VMEM((entries, 2 * WIDTH), bf16),
            pltpu.VMEM((8 * devices, 2 * WIDTH), bf16),
            pltpu.VMEM((slots, 2 * WIDTH), bf16),
        ],
        compiler_params=pltpu.CompilerParams(vmem_limit_bytes=56 << 20),
        cost_estimate=pl.CostEstimate(flops=20 << 30, bytes_accessed=12 << 20, transcendentals=4 << 20),
        name="attend",
    )(meta, q, bias, kv, left, right, base)


def column_sum(values):
    return jnp.sum(values, axis=0, keepdims=True)


def matrix_row(left, right):
    total = None
    for a in two_parts(left):
        for b in two_parts(right):
            term = dot_nt(a, b)
            total = term if total is None else total + term
    return total[0:1]


def two_parts(values):
    if values.dtype == bf16:
        return [values]
    high = values.astype(bf16)
    return [high, (values - high.astype(f32)).astype(bf16)]


def choose(flag, zero, one):
    return jnp.where(flag == 0, zero, one), jnp.where(flag == 0, one, zero)


def choose_groups(flag, folded):
    groups = folded.reshape(-1, 2, 8, folded.shape[1])
    return [part.reshape(-1, folded.shape[1]) for part in choose(flag, groups[:, 0], groups[:, 1])]


def attend_back_kernel(rows, far, *refs):
    refs = list(refs)
    take = lambda count: [refs.pop(0) for _ in range(count)]
    meta_ref, q_ref, grad_ref, bias_ref, log_ref = take(5)
    own_ref, own_scaled_ref = take(2)
    left_ref, right_ref, base_ref, w_ref, vec_ref = take(5)
    dq_ref, local_ref, to_left_ref, to_right_ref, far_keep_ref, far_send_ref, keep_ref, send_ref = take(8)
    ext_ref, far_ref, slots_ref, acc_ref, tree_ref, scaled_ref, dq_keep_ref = take(7)
    chunk = pl.program_id(0)
    offsets, entries = extended_offsets(rows, far)

    @pl.when(chunk == 0)
    def _():
        common = (left_ref, right_ref, base_ref)
        assemble(rows, far, meta_ref[0], [(0, 0, 0, 2 * WIDTH)], own_ref, *common, ext_ref, far_ref)
        assemble(rows, far, meta_ref[0], [(0, 2 * WIDTH, 0, WIDTH)], own_scaled_ref, *common, scaled_ref, far_ref)
        acc_ref[...] = jnp.zeros_like(acc_ref)

    load_slots(rows, far, chunk, ext_ref, slots_ref)
    bias = bias_ref[0]
    bias = jnp.concatenate([bias, bias], axis=1)
    sources = slot_sources(rows, far, chunk)
    for pair in range(PAIRS):
        lanes = slice(128 * pair, 128 * (pair + 1))
        value_lanes = slice(WIDTH + 128 * pair, WIDTH + 128 * (pair + 1))
        keys, values = slots_ref[:, lanes], slots_ref[:, value_lanes]
        queries, grads = split_heads(q_ref[:, lanes]), split_heads(grad_ref[:, lanes])
        probs = jnp.exp(dot_nt(keys, queries) + bias - log_ref[0, pair : pair + 1, :])
        grad_probs = dot_nt(values, grads)
        delta = jnp.sum(probs * grad_probs, axis=0, keepdims=True)
        grad_scores = (probs * (grad_probs - delta)).astype(bf16)
        dq = (join_heads(dot_tn(grad_scores, keys)) * 0.125).astype(bf16)
        dq_ref[:, lanes] = dq
        dq_keep_ref[pl.ds(pl.multiple_of(chunk * CHUNK, CHUNK), CHUNK), lanes] = dq
        grad_keys = dot_nn(grad_scores, queries)
        grad_values = dot_nn(probs.astype(bf16), grads)
        at = 0
        for start, count in sources:
            if not isinstance(start, int):
                start = pl.multiple_of(start, BLOCK)
            acc_ref[pl.ds(start, count), lanes] += grad_keys[at : at + count]
            acc_ref[pl.ds(start, count), value_lanes] += grad_values[at : at + count]
            at += count

    @pl.when(chunk == pl.num_programs(0) - 1)
    def _():
        dq = dq_keep_ref[...]
        sums = [column_sum(dq.astype(f32)), column_sum(acc_ref[:, :WIDTH]), column_sum(acc_ref[:, WIDTH:])]
        both = dot_tn(scaled_ref[...], acc_ref[...].astype(bf16))
        parts = [dot_tn(own_scaled_ref[0:rows, :], dq), both[:, :WIDTH], both[:, WIDTH:]]
        first_row = lax.broadcasted_iota(jnp.int32, (16, 1), 0) == 0
        ones = jnp.where(first_row, jnp.ones((16, WIDTH), f32), 0.0).astype(bf16)
        as_column = lambda row: dot_tn(jnp.where(first_row, row, 0.0).astype(bf16), ones)
        gain, shift = as_column(vec_ref[0:1, :]), as_column(vec_ref[1:2, :])
        gain_grad, shift_grad = jnp.zeros((1, WIDTH), f32), jnp.zeros((1, WIDTH), f32)
        owners = 2 * keep_ref.shape[0]
        part = WIDTH // owners
        low_bit = meta_ref[1] & 1
        for block in range(3):
            weight = w_ref[:, block * WIDTH : (block + 1) * WIDTH]
            gain_grad += matrix_row(jnp.ones((16, WIDTH), bf16), weight.astype(f32) * parts[block])
            shift_grad += matrix_row(jnp.broadcast_to(sums[block], (16, WIDTH)), weight)
            grad = gain * parts[block] + shift * sums[block]
            for high in range(owners // 2):
                at = 2 * high * part
                mine, other = choose(low_bit, grad[at : at + part], grad[at + part : at + 2 * part])
                keep_ref[high, block * part : (block + 1) * part, :] = mine.astype(bf16)
                send_ref[high, block * part : (block + 1) * part, :] = other.astype(bf16)
        extra = keep_ref.shape[1] - 3 * part
        top_row = lax.broadcasted_iota(jnp.int32, (extra, 1), 0) == 0
        vectors = [gain_grad, shift_grad, sums[0], sums[2]]
        owner_row = lambda owner: jnp.concatenate([v[:, owner * part : (owner + 1) * part] for v in vectors], axis=1)
        for high in range(owners // 2):
            mine, other = choose(low_bit, owner_row(2 * high), owner_row(2 * high + 1))
            keep_ref[high, 3 * part :, :] = jnp.where(top_row, mine, 0.0).astype(bf16)
            send_ref[high, 3 * part :, :] = jnp.where(top_row, other, 0.0).astype(bf16)

        for level in range(LOCAL):
            at, count = offsets[level], level_rows(rows, level)
            edge = slice(BLOCK * level, BLOCK * (level + 1))
            to_left_ref[edge, :] = acc_ref[at : at + BLOCK, :].astype(bf16)
            to_right_ref[edge, :] = acc_ref[at + BLOCK + count : at + 2 * BLOCK + count, :].astype(bf16)
        carry = None
        for index in range(len(far) - 1, -1, -1):
            level = far[index]
            count = base_ref.shape[0] // 2 ** (level - LOCAL)
            tree_ref[0:count, :] = jnp.zeros((count, 2 * WIDTH), f32) if carry is None else spread(carry)
            for side, start in enumerate(far_starts(meta_ref[0], level, count)):
                at = offsets[LOCAL + index] + side * BLOCK
                tree_ref[pl.ds(start, BLOCK), :] += acc_ref[at : at + BLOCK, :]
            carry = tree_ref[0:count, :]
        mine, other = choose_groups(meta_ref[0] & 1, jnp.concatenate([carry[:, :WIDTH], carry[:, WIDTH:]], axis=0))
        far_keep_ref[...] = mine.astype(bf16)
        far_send_ref[...] = other.astype(bf16)
        tile = 256
        counts = [tile >> level for level in range(1, LOCAL - 1)]
        token = lax.broadcasted_iota(jnp.int32, (tile, counts[0]), 0)
        entry = lax.broadcasted_iota(jnp.int32, (tile, counts[0]), 1)
        member = jnp.concatenate(
            [
                jnp.where((token >> level) == entry, 0.5**level, 0.0)[:, :count]
                for level, count in enumerate(counts, 1)
            ],
            axis=1,
        ).astype(bf16)
        for at in range(0, rows, tile):
            coarse = [
                acc_ref[offsets[level] + BLOCK + (at >> level) : offsets[level] + BLOCK + ((at + tile) >> level), :]
                for level in range(1, LOCAL - 1)
            ]
            total = acc_ref[BLOCK + at : BLOCK + at + tile, :]
            for half in two_parts(jnp.concatenate(coarse, axis=0)):
                total = total + dot_nn(member, half)
            local_ref[at : at + tile, :] = total.astype(bf16)


def chain_rows(rows, devices):
    unit = 8 * devices
    return -(-(rows + 16) // unit) * unit


def attend_back_call(rows, devices, far, owners, meta, q, grads, bias, logs, kv, scaled, left, right, base, weight, vectors):
    chunks = rows // CHUNK
    _, entries = extended_offsets(rows, far)
    _, slots = slot_layout(far)
    chain = (owners // 2, chain_rows(3 * WIDTH // owners, devices), WIDTH)
    outs = [
        jax.ShapeDtypeStruct((rows, WIDTH), bf16),
        jax.ShapeDtypeStruct((rows, 2 * WIDTH), bf16),
        jax.ShapeDtypeStruct((BLOCK * LOCAL, 2 * WIDTH), bf16),
        jax.ShapeDtypeStruct((BLOCK * LOCAL, 2 * WIDTH), bf16),
        jax.ShapeDtypeStruct((8 * devices, WIDTH), bf16),
        jax.ShapeDtypeStruct((8 * devices, WIDTH), bf16),
        jax.ShapeDtypeStruct(chain, bf16),
        jax.ShapeDtypeStruct(chain, bf16),
    ]
    return pl.pallas_call(
        partial(attend_back_kernel, rows, far),
        grid=(chunks,),
        out_shape=outs,
        in_specs=[
            pl.BlockSpec(memory_space=pltpu.SMEM),
            pl.BlockSpec((CHUNK, WIDTH), lambda i: (i, 0)),
            pl.BlockSpec((CHUNK, WIDTH), lambda i: (i, 0)),
            pl.BlockSpec((1, slots, CHUNK), lambda i: (i, 0, 0)),
            pl.BlockSpec((1, 8, 2 * CHUNK), lambda i: (i, 0, 0)),
        ]
        + vmem_specs(7),
        out_specs=[pl.BlockSpec((CHUNK, WIDTH), lambda i: (i, 0))] + vmem_specs(len(outs) - 1),
        scratch_shapes=[
            pltpu.VMEM((entries, 2 * WIDTH), bf16),
            pltpu.VMEM((8 * devices, 2 * WIDTH), bf16),
            pltpu.VMEM((slots, 2 * WIDTH), bf16),
            pltpu.VMEM((entries, 2 * WIDTH), f32),
            pltpu.VMEM((8 * devices, 2 * WIDTH), f32),
            pltpu.VMEM((entries, WIDTH), bf16),
            pltpu.VMEM((rows, WIDTH), bf16),
        ],
        compiler_params=pltpu.CompilerParams(vmem_limit_bytes=40 << 20),
        cost_estimate=pl.CostEstimate(flops=36 << 30, bytes_accessed=24 << 20, transcendentals=4 << 20),
        name="attend_back",
    )(meta, q, grads, bias, logs, kv, scaled, left, right, base, weight, vectors)


def normal_parts(values):
    size = jnp.abs(values)
    bell = jnp.exp(-0.5 * values * values)
    t = 1.0 / (1.0 + (0.3275911 / math.sqrt(2.0)) * size)
    poly = t * (
        0.5 * 0.254829592
        + t * (0.5 * -0.284496736 + t * (0.5 * 1.421413741 + t * (0.5 * -1.453152027 + t * (0.5 * 1.061405429))))
    )
    tail = poly * bell
    return jnp.where(values < 0, tail, 1.0 - tail), bell * (1.0 / math.sqrt(2.0 * math.pi))


def feed_kernel(
    hidden_width,
    owners,
    meta_ref,
    x_ref,
    attended_ref,
    cot_ref,
    vec_ref,
    up_bias_ref,
    *refs,
):
    one_refs, two_refs, refs = refs[:owners], refs[owners : 2 * owners], refs[2 * owners :]
    y_ref, grad_middle_ref, grad_attended_ref, keep_ref, send_ref = refs[:5]
    down_w_ref, up_w_ref, out_w_ref, vec_grad_ref, up_bias_grad_ref, down_acc, up_acc, out_acc = refs[5:]
    rows = WIDTH // owners
    wide_rows = hidden_width // owners
    blocks = hidden_width // WIDTH

    for at, (one, two) in enumerate(zip(one_refs, two_refs)):
        owner = meta_ref[1 + at]
        span = pl.ds(pl.multiple_of(owner * rows, rows), rows)
        for block in range(blocks - 1):
            up_w_ref[span, block * WIDTH : (block + 1) * WIDTH] = one[block * rows : (block + 1) * rows, :]
        up_w_ref[span, (blocks - 1) * WIDTH :] = two[0:rows, :]
        out_w_ref[span, :] = two[rows : 2 * rows, :]
        down_w_ref[pl.ds(pl.multiple_of(owner * wide_rows, wide_rows), wide_rows), :] = two[2 * rows :, :]

    out_bias, gain, shift, down_bias = (vec_ref[4 + at : 5 + at, :] for at in range(4))
    attended = attended_ref[...]
    middle = x_ref[...].astype(f32) + dot_nn(attended, out_w_ref[...]) + out_bias
    scaled, inverse = norm_rows(middle)
    normed = (scaled * gain + shift).astype(bf16)
    cot = cot_ref[...]
    wide = cot.astype(f32)
    lowered = jnp.zeros_like(middle)
    grad_normed = jnp.zeros_like(middle)
    for block in range(blocks):
        columns = slice(block * WIDTH, (block + 1) * WIDTH)
        down = down_w_ref[columns, :]
        pre = dot_nn(normed, up_w_ref[:, columns]) + up_bias_ref[:, columns]
        phi, bell = normal_parts(pre)
        hidden = (pre * phi).astype(bf16)
        lowered += dot_nn(hidden, down)
        grad_pre = (dot_nt(cot, down) * (phi + pre * bell)).astype(bf16)
        up_bias_grad_ref[:, columns] = column_sum(grad_pre.astype(f32))
        grad_normed += dot_nt(grad_pre, up_w_ref[:, columns])
        down_acc[columns, :] = dot_tn(hidden, cot)
        up_acc[:, columns] = dot_tn(normed, grad_pre)
    y_ref[...] = (middle + lowered + down_bias).astype(bf16)
    grad_middle = wide + norm_back(grad_normed, scaled, inverse, gain)
    grad_middle_ref[...] = grad_middle
    grad_proj = grad_middle.astype(bf16)
    grad_attended_ref[...] = dot_nt(grad_proj, out_w_ref[...]).astype(bf16)
    out_acc[...] = dot_tn(attended, grad_proj)
    vec_grad_ref[0:1, :] = column_sum(grad_proj.astype(f32))
    vec_grad_ref[1:2, :] = column_sum(grad_normed * scaled)
    vec_grad_ref[2:3, :] = column_sum(grad_normed)
    vec_grad_ref[3:4, :] = column_sum(wide)

    extra = keep_ref.shape[1] - wide_rows - (blocks + 1) * rows
    row_at = lax.broadcasted_iota(jnp.int32, (extra, 1), 0)
    low_bit = meta_ref[1] & 1

    def put(high, at, count, source):
        mine, other = choose(low_bit, source(2 * high), source(2 * high + 1))
        keep_ref[high, at : at + count, :] = mine.astype(bf16)
        send_ref[high, at : at + count, :] = other.astype(bf16)

    def small(owner):
        first = [vec_grad_ref[i : i + 1, owner * rows : (owner + 1) * rows] for i in range(4)]
        second = up_bias_grad_ref[:, owner * wide_rows : (owner + 1) * wide_rows]
        return jnp.where(row_at == 0, jnp.concatenate(first, axis=1), jnp.where(row_at == 1, second, 0.0))

    for high in range(owners // 2):
        put(high, 0, wide_rows, lambda owner: down_acc[owner * wide_rows : (owner + 1) * wide_rows, :])
        at = wide_rows
        for block in range(blocks):
            columns = slice(block * WIDTH, (block + 1) * WIDTH)
            put(high, at, rows, lambda owner: up_acc[owner * rows : (owner + 1) * rows, columns])
            at += rows
        put(high, at, rows, lambda owner: out_acc[owner * rows : (owner + 1) * rows, :])
        put(high, at + rows, extra, small)


def feed_call(hidden_width, devices, meta, x, attended, cot, vectors, up_bias, ones, twos):
    rows, owners = x.shape[0], len(ones)
    chain = chain_rows(2 * (hidden_width // owners) + WIDTH // owners, devices)
    split = jax.ShapeDtypeStruct((owners // 2, chain, WIDTH), bf16)
    return pl.pallas_call(
        partial(feed_kernel, hidden_width, owners),
        out_shape=[
            jax.ShapeDtypeStruct((rows, WIDTH), bf16),
            jax.ShapeDtypeStruct((rows, WIDTH), f32),
            jax.ShapeDtypeStruct((rows, WIDTH), bf16),
            split,
            split,
        ],
        in_specs=[pl.BlockSpec(memory_space=pltpu.SMEM)] + vmem_specs(5 + 2 * owners),
        out_specs=vmem_specs(5),
        scratch_shapes=[
            pltpu.VMEM((hidden_width, WIDTH), bf16),
            pltpu.VMEM((WIDTH, hidden_width), bf16),
            pltpu.VMEM((WIDTH, WIDTH), bf16),
            pltpu.VMEM((8, WIDTH), f32),
            pltpu.VMEM((1, hidden_width), f32),
            pltpu.VMEM((hidden_width, WIDTH), f32),
            pltpu.VMEM((WIDTH, hidden_width), f32),
            pltpu.VMEM((WIDTH, WIDTH), f32),
        ],
        compiler_params=pltpu.CompilerParams(vmem_limit_bytes=46 << 20),
        cost_estimate=pl.CostEstimate(flops=32 << 30, bytes_accessed=20 << 20, transcendentals=4 << 20),
        name="feed_forward",
    )(meta, x, attended, cot, vectors, up_bias, *ones, *twos)


def input_grad_kernel(
    rows,
    x_ref,
    dq_ref,
    local_ref,
    grad_middle_ref,
    from_right_ref,
    from_left_ref,
    far_keep_ref,
    far_got_ref,
    w_ref,
    vec_ref,
    out_ref,
    got_ref,
):
    step = pl.program_id(0)
    tile = x_ref.shape[0]
    edge = BLOCK * LOCAL

    @pl.when(step == 0)
    def _():
        folded = far_keep_ref[...].astype(f32) + far_got_ref[...].astype(f32)
        high, low = two_parts(jnp.concatenate([folded[:8], folded[8:]], axis=1))
        got_ref[0:edge, :] = from_left_ref[...]
        got_ref[edge : 2 * edge, :] = from_right_ref[...]
        far = jnp.concatenate([high.astype(f32), low.astype(f32)], axis=0).astype(bf16)
        got_ref[2 * edge : 2 * edge + BLOCK, :] = far
        got_ref[2 * edge + BLOCK :, :] = jnp.zeros((BLOCK, 2 * WIDTH), bf16)

    shape = (1, got_ref.shape[0])
    column = lax.broadcasted_iota(jnp.int32, shape, 1)
    within = jnp.where(column < edge, column, column - edge)
    level = jnp.where(column < 2 * edge, within >> 4, LOCAL)
    last = jnp.where((column >= edge) & (column < 2 * edge), (rows >> level) - BLOCK, 0)
    entry = jnp.where(column < 2 * edge, last + (within & 15), (column - 2 * edge) & 7)
    entry = jnp.where(column < 2 * edge + BLOCK, entry, -1)
    scale = 1.0 / (1 << level).astype(f32)
    token = step * tile + lax.broadcasted_iota(jnp.int32, (tile, shape[1]), 0)
    member = jnp.where((token >> level) == entry, scale, 0.0).astype(bf16)

    scaled, inverse = norm_rows(x_ref[...].astype(f32))
    dkv = (local_ref[...].astype(f32) + dot_nn(member, got_ref[...])).astype(bf16)
    grad = dot_nt(dq_ref[...], w_ref[:, :WIDTH]) + dot_nt(dkv, w_ref[:, WIDTH:])
    out_ref[...] = grad_middle_ref[...] + norm_back(grad, scaled, inverse, vec_ref[0:1, :])


def input_grad_call(x, dq, local, grad_middle, from_right, from_left, far_keep, far_got, weight, vectors):
    rows = x.shape[0]
    tile = 512
    tiled = lambda width: pl.BlockSpec((tile, width), lambda i: (i, 0))
    return pl.pallas_call(
        partial(input_grad_kernel, rows),
        grid=(rows // tile,),
        out_shape=jax.ShapeDtypeStruct((rows, WIDTH), f32),
        in_specs=[tiled(WIDTH), tiled(WIDTH), tiled(2 * WIDTH), tiled(WIDTH)] + vmem_specs(6),
        out_specs=tiled(WIDTH),
        scratch_shapes=[pltpu.VMEM((2 * BLOCK * (LOCAL + 1), 2 * WIDTH), bf16)],
        compiler_params=pltpu.CompilerParams(vmem_limit_bytes=24 << 20),
        cost_estimate=pl.CostEstimate(flops=6 << 30, bytes_accessed=12 << 20, transcendentals=0),
        name="input_grad",
    )(x, dq, local, grad_middle, from_right, from_left, far_keep, far_got, weight, vectors)


def shifted(block, axis, distance):
    devices = range(lax.axis_size(axis))
    route = [(i - distance, i) for i in devices if i - distance in devices]
    return lax.ppermute(block, axis, route)


def swap(block, axis, bit):
    return lax.ppermute(block, axis, [(i, i ^ bit) for i in range(lax.axis_size(axis))])


def gather_step(part, axis, bit):
    mine = (lax.axis_index(axis) // bit) % 2
    other = swap(part, axis, bit)
    first = jnp.where(mine == 0, part, other)
    second = jnp.where(mine == 0, other, part)
    return jnp.stack([first, second], axis=-3)


def together(*values):
    return lax.optimization_barrier(values)


def bits_of(axis):
    size = lax.axis_size(axis)
    return [1 << at for at in range(size.bit_length() - 1)]


def step_call(name, function, meta, arrays, shapes, dtype=bf16):
    def kernel(meta_ref, *refs):
        values = [ref[...].astype(f32) for ref in refs[: len(arrays)]]
        for ref, value in zip(refs[len(arrays) :], function(meta_ref[0], meta_ref[1], *values), strict=True):
            ref[...] = value.astype(dtype)

    size = sum(math.prod(a.shape) for a in arrays)
    return pl.pallas_call(
        kernel,
        out_shape=[jax.ShapeDtypeStruct(shape, dtype) for shape in shapes],
        in_specs=[pl.BlockSpec(memory_space=pltpu.SMEM)] + vmem_specs(len(arrays)),
        out_specs=vmem_specs(len(shapes)),
        compiler_params=pltpu.CompilerParams(vmem_limit_bytes=(4 << 20) + 16 * size),
        cost_estimate=pl.CostEstimate(flops=1 << 20, bytes_accessed=4 * size, transcendentals=0),
        name=name,
    )(meta, *arrays)


def halves(values, axis=0):
    return jnp.split(values, 2, axis=axis)


class Reduction:
    def __init__(self, meta, keep, send, far=None):
        self.meta, self.rows, self.far = meta, keep.shape[1], far
        self.bits = bits_of("ctx")[1:]
        self.keep, self.got = keep, [swap(send, "fsdp", 1)]

    def call(self, name, function, arrays, *shapes):
        return step_call(name, function, self.meta, arrays, [(*shape, WIDTH) for shape in shapes])

    def cross(self):
        far = [self.far[1]] if self.far else []
        extra = far[0].shape[0] if far else 0
        half = self.rows // 2

        def function(here, owner, keep, got, *far):
            mine, other = choose(owner >> 1, *(keep + got))
            keep, near = choose(here & 1, *halves(mine))
            high, both = choose(here & 1, *halves(other))
            return keep, jnp.concatenate([near, *far], axis=0), high, both

        shapes = [(half,), (half + extra,), (half,), (half,)]
        self.keep, near, high, both = self.call("cross", function, [self.keep, *self.got, *far], *shapes)
        count = lax.axis_size("fsdp")
        route = [(i, i ^ count ^ 2) for i in range(count * lax.axis_size("ctx"))]
        self.got = [swap(near, "ctx", 1), swap(high, "fsdp", 2), lax.ppermute(both, ("ctx", "fsdp"), route)]

    def scatter(self, at):
        bit, last = self.bits[at], at == len(self.bits) - 1
        rows = self.keep.shape[0]
        far = [self.far[0]] if self.far else []
        extra = far[0].shape[0] // 2 if far else 0

        def function(here, owner, keep, *got):
            far_keep = got[-1]
            got = got[: len(got) - len(far)]
            total = keep + got[0][:rows]
            for other in got[1:]:
                total = total + other
            flag = (here // bit) & 1
            keep, send = (total, total) if last else choose(flag, *halves(total))
            if not far:
                return [keep] if last else [keep, send]
            far_keep, far_send = choose_groups(flag, far_keep + got[0][rows:])
            return keep, jnp.concatenate([send, far_send], axis=0), far_keep

        count = rows if last else rows // 2
        shapes = [(count,)] if last and not far else [(count,), (count + extra,)]
        out = self.call("scatter", function, [self.keep, *self.got, *far], *shapes, *([(extra,)] if far else []))
        self.keep, send = out[0], out[1] if len(out) > 1 else out[0]
        self.got = [swap(send, "ctx", bit)]
        if far:
            self.far = (out[2], None)


    def order(self):
        high = list(reversed(self.bits[:-1]))
        return list(zip(high + [1], [1] + high))

    def collect(self):
        rows = self.keep.shape[0]
        if self.far:
            self.far = (self.far[0], self.got[0][rows:])
        function = lambda here, owner, keep, got: halves(keep + got[:rows])
        self.send_gather(0, self.call("collect", function, [self.keep, *self.got], (rows // 2,), (rows // 2,)))

    def send_gather(self, at, keep):
        self.keep = keep
        self.got = [swap(part, "ctx", bit) for part, bit in zip(keep, self.order()[at])]

    def gather(self, at):
        bits = self.order()[at]
        rows = 2 * self.keep[0].shape[0]
        function = lambda here, owner, *arrays: self.paired(here, bits, *arrays)
        self.send_gather(at + 1, self.call("gather", function, [*self.keep, *self.got], (rows,), (rows,)))

    def paired(self, here, bits, keep_one, keep_two, got_one, got_two):
        one = jnp.concatenate(choose((here // bits[0]) & 1, keep_one, got_one), axis=0)
        two = jnp.concatenate(choose((here // bits[1]) & 1, keep_two, got_two), axis=0)
        return one, two

    def scatters(self):
        return [self.cross] + [partial(self.scatter, at) for at in range(len(self.bits))]

    def gathers(self):
        return [self.collect] + [partial(self.gather, at) for at in range(len(self.order()) - 1)]

    def finish(self, shapes, unpack):
        bits = self.order()[-1]
        outer = lax.axis_size("ctx") // 4
        rows = self.rows // (4 * outer)

        def function(here, owner, *arrays):
            one, two = self.paired(here, bits, *arrays)
            parts = []
            for low in range(2):
                for high in range(outer):
                    a, b = low * outer + high, 2 * high + low
                    parts += [one[a * rows : (a + 1) * rows], two[b * rows : (b + 1) * rows]]
            return unpack(jnp.concatenate(parts, axis=0))

        return step_call("finish", function, self.meta, [*self.keep, *self.got], shapes, f32)


def shards(
    layer_input,
    doc_lengths,
    ln1_gain,
    ln1_bias,
    qkv_weight,
    query_bias,
    value_bias,
    out_weight,
    out_bias,
    ln2_gain,
    ln2_bias,
    up_weight,
    up_bias,
    down_weight,
    down_bias,
    cotangent,
):
    owners = lax.axis_size("fsdp")
    devices = lax.axis_size("ctx")
    x, cot = layer_input[0], cotangent[0]
    rows = x.shape[0]
    total = rows * devices
    far = far_levels(total)
    here, owner = lax.axis_index("ctx"), lax.axis_index("fsdp")
    part = WIDTH // owners
    hidden_width = up_weight.shape[1]
    meta = jnp.stack([here] + [owner ^ at for at in range(owners)]).astype(jnp.int32)

    vectors = [ln1_gain, ln1_bias, query_bias, value_bias, out_bias, ln2_gain, ln2_bias, down_bias, up_bias]
    own = pack_call(qkv_weight, vectors)
    across = swap(own, "fsdp", 2)
    beside = swap(own, "fsdp", 1)
    one, two = pack_rest_call(down_weight, up_weight, out_weight)
    bias = mask_call(rows, total, far, meta, doc_lengths)
    across, beside, one, two, bias = together(across, beside, one, two, bias)
    pieces = [own, beside, across, swap(across, "fsdp", 1)]
    one_across = swap(one, "fsdp", 2)
    qkv_full, vec, up_shift, queries, kv, scaled, tail, head, base = qkv_call(
        rows, hidden_width, meta, x, pieces, [bias, two]
    )
    vec, tail, head, base, one_across = together(vec, tail, head, base, one_across)

    one_beside, one_both = swap(one, "fsdp", 1), swap(one_across, "fsdp", 1)
    left = shifted(tail, "ctx", 1)
    right = shifted(head, "ctx", -1)
    for at, bit in enumerate(reversed(bits_of("ctx"))):
        base = gather_step(base, "ctx", bit)
        if bit == 1:
            base, left, right = together(base, left, right)
    base = base.reshape(-1, ENTRY)
    base, two = together(base, two)
    two_across, two_beside = swap(two, "fsdp", 2), swap(two, "fsdp", 1)
    attended, logs = attend_call(rows, devices, far, meta, queries, bias, kv, left, right, base)
    logs, two_across, two_beside = together(logs, two_across, two_beside)
    two_both = swap(two_across, "fsdp", 1)
    output, grad_middle, grad_attended, keep, send = feed_call(
        hidden_width,
        devices,
        meta,
        x,
        attended,
        cot,
        vec,
        up_shift,
        [one, one_beside, one_across, one_both],
        [two, two_beside, two_across, two_both],
    )
    feed = Reduction(meta, keep, send)
    feed.cross()
    made = attend_back_call(
        rows, devices, far, owners, meta, queries, grad_attended, bias, logs, kv, scaled, left, right, base, qkv_full, vec
    )
    dq, local, to_left, to_right, far_keep, far_send, keep, send = made
    to_left, to_right, far_keep, far_send, send, *feed.got = together(
        to_left, to_right, far_keep, far_send, send, *feed.got
    )
    first = Reduction(meta, keep, send, (far_keep, far_send))
    back_right = shifted(to_left, "ctx", -1)
    back_left = shifted(to_right, "ctx", 1)
    pending = feed.scatters()[1:]
    pending.pop(0)()
    first.cross()
    tied = together(*first.got, *feed.got)
    first.got, feed.got = list(tied[: len(first.got)]), list(tied[len(first.got) :])
    for one in first.scatters()[1:]:
        one()
        if pending:
            pending.pop(0)()
    for one, two in zip(first.gathers(), feed.gathers()):
        one()
        two()
    input_grad = input_grad_call(
        x, dq, local, grad_middle, back_right, back_left, *first.far, qkv_full, vec
    )

    wide_rows = hidden_width // owners

    def split(row):
        return [row[:, at * part : (at + 1) * part] for at in range(row.shape[1] // part)]

    def unpack_first(total):
        blocks = [total[at * part : (at + 1) * part] for at in range(3)]
        return [jnp.concatenate(blocks, axis=1), *split(total[3 * part : 3 * part + 1])]

    def unpack_feed(total):
        at = wide_rows
        blocks = []
        for _ in range(hidden_width // WIDTH):
            blocks.append(total[at : at + part])
            at += part
        vectors = [*split(total[at + part : at + part + 1]), total[at + part + 1 : at + part + 2]]
        return [total[:wide_rows], jnp.concatenate(blocks, axis=1), total[at : at + part], *vectors]

    vector = (1, part)
    qkv_grad, *firsts = first.finish([(part, 3 * WIDTH)] + [vector] * owners, unpack_first)
    down_grad, up_grad, out_grad, *feeds = feed.finish(
        [(wide_rows, WIDTH), (part, hidden_width), (part, WIDTH)] + [vector] * owners + [(1, wide_rows)], unpack_feed
    )
    gain_first, shift_first, query_grad, value_grad = (v.reshape(-1) for v in firsts)
    out_shift, gain_second, shift_second, down_shift, up_shift_grad = (v.reshape(-1) for v in feeds)
    return (
        output[None],
        input_grad[None],
        gain_first,
        shift_first,
        qkv_grad,
        query_grad,
        value_grad,
        out_grad,
        out_shift,
        gain_second,
        shift_second,
        up_grad,
        up_shift_grad,
        down_grad,
        down_shift,
    )


def solution(mesh):
    row, vector = P("fsdp", None), P("fsdp")
    tokens = P("fsdp", "ctx", None)
    return jax.shard_map(
        shards,
        mesh=mesh,
        in_specs=(
            tokens,
            row,
            vector,
            vector,
            row,
            vector,
            vector,
            row,
            vector,
            vector,
            vector,
            row,
            vector,
            row,
            vector,
            tokens,
        ),
        out_specs=(
            tokens,
            tokens,
            vector,
            vector,
            row,
            vector,
            vector,
            row,
            vector,
            vector,
            vector,
            row,
            vector,
            row,
            vector,
        ),
        check_vma=False,
    )
```

```python
from functools import partial
import math

import jax
import jax.numpy as jnp
from jax import lax
from jax.experimental import pallas as pl
from jax.experimental.pallas import tpu as pltpu
from jax.sharding import PartitionSpec as P

HEADS = 8
BLOCK = 16
LEVELS = 10
NEAR = 4
LOCAL = 7
CHUNK = 128
STEP = 2
WIDTH = 512
PAIRS = HEADS // 2
ENTRY = 3 * WIDTH
SMALL = 16
MASKED = -1e30
EPSILON = 1e-05

f32 = jnp.float32
bf16 = jnp.bfloat16


def level_rows(rows, level):
    return rows // 2**level


def level_offsets(rows):
    offsets = [0]
    for level in range(LOCAL):
        offsets.append(offsets[-1] + level_rows(rows, level))
    return offsets[:-1], offsets[-1]


def far_levels(total):
    return [l for l in range(LOCAL, LEVELS) if total // (BLOCK * 2**l) >= 2]


def extended_offsets(rows, far):
    offsets, cursor = [], 0
    for level in range(LOCAL):
        offsets.append(cursor)
        cursor += level_rows(rows, level) + 2 * BLOCK
    for _ in far:
        offsets.append(cursor)
        cursor += 2 * BLOCK
    return offsets, cursor


def slot_layout(far):
    parts = [(level, CHUNK // 2**level + 2 * BLOCK) for level in range(NEAR)]
    parts += [(level, BLOCK) for level in list(range(NEAR, LOCAL)) + far for _ in range(2)]
    return parts, sum(count for _, count in parts)


def slot_sources(rows, far, chunk):
    offsets, _ = extended_offsets(rows, far)
    sources = []
    for level in range(NEAR):
        sources.append((offsets[level] + chunk * (CHUNK // 2**level), CHUNK // 2**level + 2 * BLOCK))
    for level in range(NEAR, LOCAL):
        block = chunk // (BLOCK * 2**level // CHUNK)
        sources.append((offsets[level] + block * BLOCK, BLOCK))
        sources.append((offsets[level] + block * BLOCK + 2 * BLOCK, BLOCK))
    for at in range(len(far)):
        sources.append((offsets[LOCAL + at], BLOCK))
        sources.append((offsets[LOCAL + at] + BLOCK, BLOCK))
    return sources


def mask_kernel(rows, total, far, here_ref, lengths_ref, bias_ref):
    base = here_ref[0] * rows + pl.program_id(0) * CHUNK
    query = base + lax.broadcasted_iota(jnp.int32, (1, CHUNK), 1)
    first_token = jnp.zeros((1, CHUNK), jnp.int32)
    end_token = jnp.full((1, CHUNK), total, jnp.int32)
    start = jnp.int32(0)
    for at in range(lengths_ref.shape[1]):
        first_token = jnp.where(start <= query, start, first_token)
        start = start + lengths_ref[0, at]
        end_token = jnp.where(start > query, jnp.minimum(end_token, start), end_token)

    def part(at, count, first_row, level):
        span = 2**level
        shift = level + 4
        first = first_row + span * lax.broadcasted_iota(jnp.int32, (count, CHUNK), 0)
        gap = jnp.abs((first >> shift) - (query >> shift))
        if level == 0:
            seen = gap <= 1
        else:
            seen = (gap == 1) & (jnp.abs((first >> (shift - 1)) - (query >> (shift - 1))) > 1)
        seen = seen & (first >= first_token) & (first + (span - 1) < end_token)
        bias_ref[0, at : at + count, :] = jnp.where(seen, level * math.log(2.0), MASKED)

    at = 0
    for level in range(NEAR):
        count = CHUNK // 2**level + 2 * BLOCK
        part(at, count, base - BLOCK * 2**level, level)
        at += count
    for level in list(range(NEAR, LOCAL)) + far:
        block = base >> (level + 4)
        for side in (-1, 1):
            part(at, BLOCK, (block + side) * (BLOCK * 2**level), level)
            at += BLOCK


def mask_call(rows, total, far, meta, lengths):
    chunks = rows // CHUNK
    _, slots = slot_layout(far)
    return pl.pallas_call(
        partial(mask_kernel, rows, total, far),
        grid=(chunks,),
        out_shape=jax.ShapeDtypeStruct((chunks, slots, CHUNK), f32),
        in_specs=[pl.BlockSpec(memory_space=pltpu.SMEM)] * 2,
        out_specs=pl.BlockSpec((1, slots, CHUNK), lambda i: (i, 0, 0)),
        compiler_params=pltpu.CompilerParams(vmem_limit_bytes=8 << 20),
        cost_estimate=pl.CostEstimate(flops=4 << 30, bytes_accessed=3 << 20, transcendentals=0),
        name="mask",
    )(meta, lengths)


def dot_nt(left, right):
    return lax.dot_general(left, right, (((1,), (1,)), ((), ())), preferred_element_type=f32)


def dot_tn(left, right):
    return lax.dot_general(left, right, (((0,), (0,)), ((), ())), preferred_element_type=f32)


def dot_nn(left, right):
    return jnp.dot(left, right, preferred_element_type=f32)


def pool_matrix(count):
    row = lax.broadcasted_iota(jnp.int32, (count // 2, count), 0)
    column = lax.broadcasted_iota(jnp.int32, (count // 2, count), 1)
    return jnp.where((column >> 1) == row, 0.5, 0.0).astype(bf16)


def spread_matrix(count):
    row = lax.broadcasted_iota(jnp.int32, (2 * count, count), 0)
    column = lax.broadcasted_iota(jnp.int32, (2 * count, count), 1)
    return jnp.where((row >> 1) == column, 0.5, 0.0).astype(bf16)


def spread(values):
    count = values.shape[0]
    tile = min(count, 128)
    matrix = spread_matrix(tile)
    high = values.astype(bf16)
    low = (values - high.astype(f32)).astype(bf16)
    parts = [
        dot_nn(matrix, high[at : at + tile]) + dot_nn(matrix, low[at : at + tile])
        for at in range(0, count, tile)
    ]
    return parts[0] if len(parts) == 1 else jnp.concatenate(parts, axis=0)


def norm_rows(values):
    mean = jnp.mean(values, axis=-1, keepdims=True)
    centred = values - mean
    variance = jnp.mean(centred * centred, axis=-1, keepdims=True)
    inverse = lax.rsqrt(variance + EPSILON)
    return centred * inverse, inverse


def norm_back(grad_out, scaled, inverse, gain):
    grad_scaled = grad_out * gain
    first = jnp.mean(grad_scaled, axis=-1, keepdims=True)
    second = jnp.mean(grad_scaled * scaled, axis=-1, keepdims=True)
    return inverse * (grad_scaled - first - scaled * second)


def split_heads(pair):
    lane = lax.broadcasted_iota(jnp.int32, pair.shape, 1)
    zero = jnp.zeros_like(pair)
    return jnp.concatenate([jnp.where(lane < 64, pair, zero), jnp.where(lane < 64, zero, pair)], axis=0)


def join_heads(stacked):
    rows = stacked.shape[0] // 2
    lane = lax.broadcasted_iota(jnp.int32, (rows, stacked.shape[1]), 1)
    return jnp.where(lane < 64, stacked[:rows], stacked[rows:])


def pack_kernel(w_ref, *refs):
    out_ref = refs[-1]
    part = w_ref.shape[0]
    out_ref[0:part, :] = w_ref[...]
    row = jnp.concatenate([ref[...].reshape(1, -1) for ref in refs[:-1]], axis=1)
    out_ref[part : part + SMALL, :] = jnp.broadcast_to(row.astype(f32), (SMALL, row.shape[1])).astype(bf16)


def pack_call(weight, vectors):
    return pl.pallas_call(
        pack_kernel,
        out_shape=jax.ShapeDtypeStruct((weight.shape[0] + SMALL, weight.shape[1]), bf16),
        in_specs=vmem_specs(1 + len(vectors)),
        out_specs=vmem_specs(1)[0],
        compiler_params=pltpu.CompilerParams(vmem_limit_bytes=56 << 20),
        name="pack",
    )(weight, *vectors)


def pack_rest_kernel(down_ref, up_ref, out_w_ref, one_ref, two_ref):
    rows = up_ref.shape[0]
    blocks = up_ref.shape[1] // WIDTH
    for block in range(blocks - 1):
        one_ref[block * rows : (block + 1) * rows, :] = up_ref[:, block * WIDTH : (block + 1) * WIDTH]
    two_ref[0:rows, :] = up_ref[:, (blocks - 1) * WIDTH :]
    two_ref[rows : 2 * rows, :] = out_w_ref[...]
    two_ref[2 * rows :, :] = down_ref[...]


def pack_rest_call(down, up, out_w):
    rows, blocks = up.shape[0], up.shape[1] // WIDTH
    return pl.pallas_call(
        pack_rest_kernel,
        out_shape=[
            jax.ShapeDtypeStruct(((blocks - 1) * rows, WIDTH), bf16),
            jax.ShapeDtypeStruct((2 * rows + down.shape[0], WIDTH), bf16),
        ],
        in_specs=vmem_specs(3),
        out_specs=vmem_specs(2),
        compiler_params=pltpu.CompilerParams(vmem_limit_bytes=56 << 20),
        name="pack_rest",
    )(down, up, out_w)


def vmem_specs(count):
    return [pl.BlockSpec(memory_space=pltpu.VMEM)] * count


def qkv_kernel(rows, owners, meta_ref, x_ref, *refs):
    shard_refs, refs = refs[:owners], refs[owners + 2 :]
    w_ref, vec_ref, up_bias_ref, q_ref = refs[:4]
    kv_ref, scaled_ref, tail_ref, head_ref, top_ref, keep_ref = refs[4:]
    places, _ = level_offsets(rows)
    part = WIDTH // owners
    step = pl.program_id(0)

    @pl.when(step == 0)
    def _():
        for at, ref in enumerate(shard_refs):
            owner = meta_ref[1 + at]
            w_ref[pl.ds(pl.multiple_of(owner * part, part), part), :] = ref[0:part, :]
            row = ref[part : part + 1, :].astype(f32)
            for vector in range(8):
                vec_ref[vector : vector + 1, pl.ds(pl.multiple_of(owner * part, part), part)] = row[
                    :, vector * part : (vector + 1) * part
                ]
            wide = row.shape[1] - 8 * part
            up_bias_ref[:, pl.ds(pl.multiple_of(owner * wide, wide), wide)] = row[:, 8 * part :]

    tile = x_ref.shape[0]
    scaled, _ = norm_rows(x_ref[...].astype(f32))
    normed = (scaled * vec_ref[0:1, :] + vec_ref[1:2, :]).astype(bf16)
    queries = (dot_nn(normed, w_ref[:, :WIDTH]) + vec_ref[2:3, :]).astype(bf16)
    q_ref[...] = queries * jnp.asarray(0.125, bf16)
    keys = dot_nn(normed, w_ref[:, WIDTH : 2 * WIDTH]).astype(bf16)
    values = (dot_nn(normed, w_ref[:, 2 * WIDTH :]) + vec_ref[3:4, :]).astype(bf16)
    current = jnp.concatenate([keys, values, scaled.astype(bf16)], axis=1)

    def edges(level, block):
        @pl.when(step == 0)
        def _():
            head_ref[BLOCK * level : BLOCK * (level + 1), :] = block[:BLOCK]

        @pl.when(step == pl.num_programs(0) - 1)
        def _():
            tail_ref[BLOCK * level : BLOCK * (level + 1), :] = block[block.shape[0] - BLOCK :]

    for level in range(5):
        if level:
            current = dot_nn(pool_matrix(current.shape[0]), current).astype(bf16)
        count = tile // 2**level
        span = pl.ds(pl.multiple_of(places[level] + step * count, count), count)
        kv_ref[span, :] = current[:, : 2 * WIDTH]
        scaled_ref[span, :] = current[:, 2 * WIDTH :]
        edges(level, current)
    keep_ref[pl.ds(pl.multiple_of(step * count, count), count), :] = current

    @pl.when(step == pl.num_programs(0) - 1)
    def _():
        current = keep_ref[...]
        for level in range(5, LOCAL):
            current = dot_nn(pool_matrix(current.shape[0]), current).astype(bf16)
            span = slice(places[level], places[level] + current.shape[0])
            kv_ref[span, :] = current[:, : 2 * WIDTH]
            scaled_ref[span, :] = current[:, 2 * WIDTH :]
            tail_ref[BLOCK * level : BLOCK * (level + 1), :] = current[current.shape[0] - BLOCK :]
            head_ref[BLOCK * level : BLOCK * (level + 1), :] = current[:BLOCK]
        top_ref[...] = dot_nn(pool_matrix(BLOCK), current).astype(bf16)


def qkv_call(rows, hidden_width, meta, x, pieces, earlier):
    owners = len(pieces)
    tile = 256

    def tiled(count, width):
        return pl.BlockSpec((count, width), lambda i: (i, 0))

    _, entries = level_offsets(rows)
    edge = jax.ShapeDtypeStruct((BLOCK * LOCAL, ENTRY), bf16)
    outs = pl.pallas_call(
        partial(qkv_kernel, rows, owners),
        grid=(rows // tile,),
        out_shape=[
            jax.ShapeDtypeStruct((WIDTH, 3 * WIDTH), bf16),
            jax.ShapeDtypeStruct((8, WIDTH), f32),
            jax.ShapeDtypeStruct((1, hidden_width), f32),
            jax.ShapeDtypeStruct((rows, WIDTH), bf16),
        ]
        + [jax.ShapeDtypeStruct((entries, 2 * WIDTH), bf16), jax.ShapeDtypeStruct((entries, WIDTH), bf16)]
        + [edge, edge, jax.ShapeDtypeStruct((BLOCK // 2, ENTRY), bf16)],
        in_specs=[pl.BlockSpec(memory_space=pltpu.SMEM), tiled(tile, WIDTH)]
        + vmem_specs(owners)
        + [pl.BlockSpec(memory_space=pl.ANY)] * 2,
        out_specs=vmem_specs(3) + [tiled(tile, WIDTH)] + vmem_specs(5),
        scratch_shapes=[pltpu.VMEM((level_rows(rows, 4), ENTRY), bf16)],
        compiler_params=pltpu.CompilerParams(vmem_limit_bytes=56 << 20),
        cost_estimate=pl.CostEstimate(flops=9 << 30, bytes_accessed=12 << 20, transcendentals=0),
        name="qkv_levels",
    )(meta, x, *pieces, *earlier)
    return outs


def far_level(entries):
    return dot_nn(pool_matrix(entries.shape[0]), entries).astype(bf16)


def assemble(rows, far, here, columns, own_ref, left_ref, right_ref, base_ref, ext_ref, far_ref):
    offsets, _ = extended_offsets(rows, far)
    places, _ = level_offsets(rows)
    for inner, outer, target, width in columns:
        lanes, edge_lanes = slice(target, target + width), slice(outer, outer + width)
        for level in range(LOCAL):
            at, count = offsets[level], level_rows(rows, level)
            edge = slice(BLOCK * level, BLOCK * (level + 1))
            ext_ref[at : at + BLOCK, lanes] = left_ref[edge, edge_lanes]
            ext_ref[at + BLOCK : at + BLOCK + count, lanes] = own_ref[
                places[level] : places[level] + count, inner : inner + width
            ]
            ext_ref[at + BLOCK + count : at + 2 * BLOCK + count, lanes] = right_ref[edge, edge_lanes]
        current = base_ref[:, edge_lanes]
        for index, level in enumerate(far):
            if index:
                current = far_level(current)
            count = current.shape[0]
            far_ref[0:count, 0:width] = current
            for side, start in enumerate(far_starts(here, level, count)):
                at = offsets[LOCAL + index] + side * BLOCK
                ext_ref[at : at + BLOCK, lanes] = far_ref[pl.ds(start, BLOCK), 0:width]


def far_starts(here, level, count):
    block = here >> (level - 6)
    last = count // BLOCK - 1
    return [pl.multiple_of(jnp.clip(at, 0, last) * BLOCK, BLOCK) for at in (block - 1, block + 1)]


def load_slots(rows, far, chunk, ext_ref, slots_ref):
    at = 0
    for start, count in slot_sources(rows, far, chunk):
        if not isinstance(start, int):
            start = pl.multiple_of(start, BLOCK)
        slots_ref[at : at + count, :] = ext_ref[pl.ds(start, count), :]
        at += count


def attend_kernel(rows, far, meta_ref, q_ref, bias_ref, *refs):
    own_ref, left_ref, right_ref, base_ref, out_ref, exp_ref, inverse_ref, ext_ref, far_ref, slots_ref = refs
    step = pl.program_id(0)

    @pl.when(step == 0)
    def _():
        columns = [(0, 0, 0, 2 * WIDTH)]
        assemble(rows, far, meta_ref[0], columns, own_ref, left_ref, right_ref, base_ref, ext_ref, far_ref)

    ones = jnp.ones((slots_ref.shape[0], 128), bf16)
    for sub in range(STEP):
        span = slice(sub * CHUNK, (sub + 1) * CHUNK)
        load_slots(rows, far, step * STEP + sub, ext_ref, slots_ref)
        bias = bias_ref[sub]
        bias = jnp.concatenate([bias, bias], axis=1)
        for pair in range(PAIRS):
            lanes = slice(128 * pair, 128 * (pair + 1))
            values = slots_ref[:, WIDTH + 128 * pair : WIDTH + 128 * (pair + 1)]
            scores = dot_nt(slots_ref[:, lanes], split_heads(q_ref[span, lanes])) + bias
            exponent = jnp.exp(scores - jnp.max(scores, axis=0, keepdims=True))
            low = exponent.astype(bf16)
            exp_ref[sub, pair] = low
            inverse_ref[sub, pair : pair + 1, :] = 1.0 / jnp.sum(exponent, axis=0, keepdims=True)
            both = dot_tn(low, jnp.concatenate([values, ones], axis=1))
            out_ref[span, lanes] = join_heads(both[:, :128] / both[:, 128:]).astype(bf16)


def attend_call(rows, devices, far, meta, q, bias, kv, left, right, base):
    chunks = rows // CHUNK
    _, entries = extended_offsets(rows, far)
    _, slots = slot_layout(far)
    return pl.pallas_call(
        partial(attend_kernel, rows, far),
        grid=(chunks // STEP,),
        out_shape=[
            jax.ShapeDtypeStruct((rows, WIDTH), bf16),
            jax.ShapeDtypeStruct((chunks, PAIRS, slots, 2 * CHUNK), bf16),
            jax.ShapeDtypeStruct((chunks, 8, 2 * CHUNK), f32),
        ],
        in_specs=[
            pl.BlockSpec(memory_space=pltpu.SMEM),
            pl.BlockSpec((STEP * CHUNK, WIDTH), lambda i: (i, 0)),
            pl.BlockSpec((STEP, slots, CHUNK), lambda i: (i, 0, 0)),
        ]
        + vmem_specs(4),
        out_specs=[
            pl.BlockSpec((STEP * CHUNK, WIDTH), lambda i: (i, 0)),
            pl.BlockSpec((STEP, PAIRS, slots, 2 * CHUNK), lambda i: (i, 0, 0, 0)),
            pl.BlockSpec((STEP, 8, 2 * CHUNK), lambda i: (i, 0, 0)),
        ],
        scratch_shapes=[
            pltpu.VMEM((entries, 2 * WIDTH), bf16),
            pltpu.VMEM((8 * devices, 2 * WIDTH), bf16),
            pltpu.VMEM((slots, 2 * WIDTH), bf16),
        ],
        compiler_params=pltpu.CompilerParams(vmem_limit_bytes=56 << 20),
        cost_estimate=pl.CostEstimate(flops=20 << 30, bytes_accessed=20 << 20, transcendentals=4 << 20),
        name="attend",
    )(meta, q, bias, kv, left, right, base)


def column_sum(values):
    return jnp.sum(values, axis=0, keepdims=True)


def matrix_row(left, right):
    total = None
    for a in two_parts(left):
        for b in two_parts(right):
            term = dot_nt(a, b)
            total = term if total is None else total + term
    return total[0:1]


def two_parts(values):
    if values.dtype == bf16:
        return [values]
    high = values.astype(bf16)
    return [high, (values - high.astype(f32)).astype(bf16)]


def choose(flag, zero, one):
    return jnp.where(flag == 0, zero, one), jnp.where(flag == 0, one, zero)


def choose_groups(flag, folded):
    groups = folded.reshape(-1, 2, 8, folded.shape[1])
    return [part.reshape(-1, folded.shape[1]) for part in choose(flag, groups[:, 0], groups[:, 1])]


def attend_back_kernel(rows, far, *refs):
    refs = list(refs)
    take = lambda count: [refs.pop(0) for _ in range(count)]
    meta_ref, q_ref, grad_ref, exp_ref, inverse_ref = take(5)
    own_ref, own_scaled_ref = take(2)
    left_ref, right_ref, base_ref, w_ref, vec_ref = take(5)
    dq_ref, local_ref, to_left_ref, to_right_ref, far_keep_ref, far_send_ref, keep_ref, send_ref = take(8)
    ext_ref, far_ref, slots_ref, acc_ref, tree_ref, scaled_ref, dq_keep_ref = take(7)
    step = pl.program_id(0)
    offsets, entries = extended_offsets(rows, far)

    @pl.when(step == 0)
    def _():
        common = (left_ref, right_ref, base_ref)
        assemble(rows, far, meta_ref[0], [(0, 0, 0, 2 * WIDTH)], own_ref, *common, ext_ref, far_ref)
        assemble(rows, far, meta_ref[0], [(0, 2 * WIDTH, 0, WIDTH)], own_scaled_ref, *common, scaled_ref, far_ref)
        acc_ref[...] = jnp.zeros_like(acc_ref)

    for sub in range(STEP):
        chunk = step * STEP + sub
        span = slice(sub * CHUNK, (sub + 1) * CHUNK)
        load_slots(rows, far, chunk, ext_ref, slots_ref)
        sources = slot_sources(rows, far, chunk)
        for pair in range(PAIRS):
            lanes = slice(128 * pair, 128 * (pair + 1))
            value_lanes = slice(WIDTH + 128 * pair, WIDTH + 128 * (pair + 1))
            keys, values = slots_ref[:, lanes], slots_ref[:, value_lanes]
            queries, grads = split_heads(q_ref[span, lanes]), split_heads(grad_ref[span, lanes])
            probs = exp_ref[sub, pair].astype(f32) * inverse_ref[sub, pair : pair + 1, :]
            grad_probs = dot_nt(values, grads)
            delta = jnp.sum(probs * grad_probs, axis=0, keepdims=True)
            grad_scores = (probs * (grad_probs - delta)).astype(bf16)
            dq = (join_heads(dot_tn(grad_scores, keys)) * 0.125).astype(bf16)
            dq_ref[span, lanes] = dq
            dq_keep_ref[pl.ds(pl.multiple_of(chunk * CHUNK, CHUNK), CHUNK), lanes] = dq
            grad_keys = dot_nn(grad_scores, queries)
            grad_values = dot_nn(probs.astype(bf16), grads)
            at = 0
            for start, count in sources:
                if not isinstance(start, int):
                    start = pl.multiple_of(start, BLOCK)
                acc_ref[pl.ds(start, count), lanes] += grad_keys[at : at + count]
                acc_ref[pl.ds(start, count), value_lanes] += grad_values[at : at + count]
                at += count

    @pl.when(step == pl.num_programs(0) - 1)
    def _():
        dq = dq_keep_ref[...]
        sums = [column_sum(dq.astype(f32)), column_sum(acc_ref[:, :WIDTH]), column_sum(acc_ref[:, WIDTH:])]
        both = dot_tn(scaled_ref[...], acc_ref[...].astype(bf16))
        parts = [dot_tn(own_scaled_ref[0:rows, :], dq), both[:, :WIDTH], both[:, WIDTH:]]
        first_row = lax.broadcasted_iota(jnp.int32, (16, 1), 0) == 0
        ones = jnp.where(first_row, jnp.ones((16, WIDTH), f32), 0.0).astype(bf16)
        as_column = lambda row: dot_tn(jnp.where(first_row, row, 0.0).astype(bf16), ones)
        gain, shift = as_column(vec_ref[0:1, :]), as_column(vec_ref[1:2, :])
        gain_grad, shift_grad = jnp.zeros((1, WIDTH), f32), jnp.zeros((1, WIDTH), f32)
        owners = 2 * keep_ref.shape[0]
        part = WIDTH // owners
        low_bit = meta_ref[1] & 1
        for block in range(3):
            weight = w_ref[:, block * WIDTH : (block + 1) * WIDTH]
            gain_grad += matrix_row(jnp.ones((16, WIDTH), bf16), weight.astype(f32) * parts[block])
            shift_grad += matrix_row(jnp.broadcast_to(sums[block], (16, WIDTH)), weight)
            grad = gain * parts[block] + shift * sums[block]
            for high in range(owners // 2):
                at = 2 * high * part
                mine, other = choose(low_bit, grad[at : at + part], grad[at + part : at + 2 * part])
                keep_ref[high, block * part : (block + 1) * part, :] = mine.astype(bf16)
                send_ref[high, block * part : (block + 1) * part, :] = other.astype(bf16)
        extra = keep_ref.shape[1] - 3 * part
        top_row = lax.broadcasted_iota(jnp.int32, (extra, 1), 0) == 0
        vectors = [gain_grad, shift_grad, sums[0], sums[2]]
        owner_row = lambda owner: jnp.concatenate([v[:, owner * part : (owner + 1) * part] for v in vectors], axis=1)
        for high in range(owners // 2):
            mine, other = choose(low_bit, owner_row(2 * high), owner_row(2 * high + 1))
            keep_ref[high, 3 * part :, :] = jnp.where(top_row, mine, 0.0).astype(bf16)
            send_ref[high, 3 * part :, :] = jnp.where(top_row, other, 0.0).astype(bf16)

        for level in range(LOCAL):
            at, count = offsets[level], level_rows(rows, level)
            edge = slice(BLOCK * level, BLOCK * (level + 1))
            to_left_ref[edge, :] = acc_ref[at : at + BLOCK, :].astype(bf16)
            to_right_ref[edge, :] = acc_ref[at + BLOCK + count : at + 2 * BLOCK + count, :].astype(bf16)
        carry = None
        for index in range(len(far) - 1, -1, -1):
            level = far[index]
            count = base_ref.shape[0] // 2 ** (level - LOCAL)
            tree_ref[0:count, :] = jnp.zeros((count, 2 * WIDTH), f32) if carry is None else spread(carry)
            for side, start in enumerate(far_starts(meta_ref[0], level, count)):
                at = offsets[LOCAL + index] + side * BLOCK
                tree_ref[pl.ds(start, BLOCK), :] += acc_ref[at : at + BLOCK, :]
            carry = tree_ref[0:count, :]
        mine, other = choose_groups(meta_ref[0] & 1, jnp.concatenate([carry[:, :WIDTH], carry[:, WIDTH:]], axis=0))
        far_keep_ref[...] = mine.astype(bf16)
        far_send_ref[...] = other.astype(bf16)
        tile = 256
        counts = [tile >> level for level in range(1, LOCAL - 1)]
        token = lax.broadcasted_iota(jnp.int32, (tile, counts[0]), 0)
        entry = lax.broadcasted_iota(jnp.int32, (tile, counts[0]), 1)
        member = jnp.concatenate(
            [
                jnp.where((token >> level) == entry, 0.5**level, 0.0)[:, :count]
                for level, count in enumerate(counts, 1)
            ],
            axis=1,
        ).astype(bf16)
        for at in range(0, rows, tile):
            coarse = [
                acc_ref[offsets[level] + BLOCK + (at >> level) : offsets[level] + BLOCK + ((at + tile) >> level), :]
                for level in range(1, LOCAL - 1)
            ]
            total = acc_ref[BLOCK + at : BLOCK + at + tile, :]
            for half in two_parts(jnp.concatenate(coarse, axis=0)):
                total = total + dot_nn(member, half)
            local_ref[at : at + tile, :] = total.astype(bf16)


def chain_rows(rows, devices):
    unit = 8 * devices
    return -(-(rows + 16) // unit) * unit


def attend_back_call(rows, devices, far, owners, meta, q, grads, exps, inverses, kv, scaled, left, right, base, weight, vectors):
    chunks = rows // CHUNK
    _, entries = extended_offsets(rows, far)
    _, slots = slot_layout(far)
    chain = (owners // 2, chain_rows(3 * WIDTH // owners, devices), WIDTH)
    outs = [
        jax.ShapeDtypeStruct((rows, WIDTH), bf16),
        jax.ShapeDtypeStruct((rows, 2 * WIDTH), bf16),
        jax.ShapeDtypeStruct((BLOCK * LOCAL, 2 * WIDTH), bf16),
        jax.ShapeDtypeStruct((BLOCK * LOCAL, 2 * WIDTH), bf16),
        jax.ShapeDtypeStruct((8 * devices, WIDTH), bf16),
        jax.ShapeDtypeStruct((8 * devices, WIDTH), bf16),
        jax.ShapeDtypeStruct(chain, bf16),
        jax.ShapeDtypeStruct(chain, bf16),
    ]
    return pl.pallas_call(
        partial(attend_back_kernel, rows, far),
        grid=(chunks // STEP,),
        out_shape=outs,
        in_specs=[
            pl.BlockSpec(memory_space=pltpu.SMEM),
            pl.BlockSpec((STEP * CHUNK, WIDTH), lambda i: (i, 0)),
            pl.BlockSpec((STEP * CHUNK, WIDTH), lambda i: (i, 0)),
            pl.BlockSpec((STEP, PAIRS, slots, 2 * CHUNK), lambda i: (i, 0, 0, 0)),
            pl.BlockSpec((STEP, 8, 2 * CHUNK), lambda i: (i, 0, 0)),
        ]
        + vmem_specs(7),
        out_specs=[pl.BlockSpec((STEP * CHUNK, WIDTH), lambda i: (i, 0))] + vmem_specs(len(outs) - 1),
        scratch_shapes=[
            pltpu.VMEM((entries, 2 * WIDTH), bf16),
            pltpu.VMEM((8 * devices, 2 * WIDTH), bf16),
            pltpu.VMEM((slots, 2 * WIDTH), bf16),
            pltpu.VMEM((entries, 2 * WIDTH), f32),
            pltpu.VMEM((8 * devices, 2 * WIDTH), f32),
            pltpu.VMEM((entries, WIDTH), bf16),
            pltpu.VMEM((rows, WIDTH), bf16),
        ],
        compiler_params=pltpu.CompilerParams(vmem_limit_bytes=40 << 20),
        cost_estimate=pl.CostEstimate(flops=36 << 30, bytes_accessed=24 << 20, transcendentals=4 << 20),
        name="attend_back",
    )(meta, q, grads, exps, inverses, kv, scaled, left, right, base, weight, vectors)


def normal_parts(values):
    size = jnp.abs(values)
    bell = jnp.exp(-0.5 * values * values)
    t = 1.0 / (1.0 + (0.3275911 / math.sqrt(2.0)) * size)
    poly = t * (
        0.5 * 0.254829592
        + t * (0.5 * -0.284496736 + t * (0.5 * 1.421413741 + t * (0.5 * -1.453152027 + t * (0.5 * 1.061405429))))
    )
    tail = poly * bell
    return jnp.where(values < 0, tail, 1.0 - tail), bell * (1.0 / math.sqrt(2.0 * math.pi))


def feed_kernel(
    hidden_width,
    owners,
    meta_ref,
    x_ref,
    attended_ref,
    cot_ref,
    vec_ref,
    up_bias_ref,
    *refs,
):
    one_refs, two_refs, refs = refs[:owners], refs[owners : 2 * owners], refs[2 * owners :]
    y_ref, grad_middle_ref, grad_attended_ref, keep_ref, send_ref = refs[:5]
    down_w_ref, up_w_ref, out_w_ref, vec_grad_ref, up_bias_grad_ref, down_acc, up_acc, out_acc = refs[5:]
    rows = WIDTH // owners
    wide_rows = hidden_width // owners
    blocks = hidden_width // WIDTH

    for at, (one, two) in enumerate(zip(one_refs, two_refs)):
        owner = meta_ref[1 + at]
        span = pl.ds(pl.multiple_of(owner * rows, rows), rows)
        for block in range(blocks - 1):
            up_w_ref[span, block * WIDTH : (block + 1) * WIDTH] = one[block * rows : (block + 1) * rows, :]
        up_w_ref[span, (blocks - 1) * WIDTH :] = two[0:rows, :]
        out_w_ref[span, :] = two[rows : 2 * rows, :]
        down_w_ref[pl.ds(pl.multiple_of(owner * wide_rows, wide_rows), wide_rows), :] = two[2 * rows :, :]

    out_bias, gain, shift, down_bias = (vec_ref[4 + at : 5 + at, :] for at in range(4))
    attended = attended_ref[...]
    middle = x_ref[...].astype(f32) + dot_nn(attended, out_w_ref[...]) + out_bias
    scaled, inverse = norm_rows(middle)
    normed = (scaled * gain + shift).astype(bf16)
    cot = cot_ref[...]
    wide = cot.astype(f32)
    lowered = jnp.zeros_like(middle)
    grad_normed = jnp.zeros_like(middle)
    for block in range(blocks):
        columns = slice(block * WIDTH, (block + 1) * WIDTH)
        down = down_w_ref[columns, :]
        pre = dot_nn(normed, up_w_ref[:, columns]) + up_bias_ref[:, columns]
        phi, bell = normal_parts(pre)
        hidden = (pre * phi).astype(bf16)
        lowered += dot_nn(hidden, down)
        grad_pre = (dot_nt(cot, down) * (phi + pre * bell)).astype(bf16)
        up_bias_grad_ref[:, columns] = column_sum(grad_pre.astype(f32))
        grad_normed += dot_nt(grad_pre, up_w_ref[:, columns])
        down_acc[columns, :] = dot_tn(hidden, cot)
        up_acc[:, columns] = dot_tn(normed, grad_pre)
    y_ref[...] = (middle + lowered + down_bias).astype(bf16)
    grad_middle = wide + norm_back(grad_normed, scaled, inverse, gain)
    grad_middle_ref[...] = grad_middle
    grad_proj = grad_middle.astype(bf16)
    grad_attended_ref[...] = dot_nt(grad_proj, out_w_ref[...]).astype(bf16)
    out_acc[...] = dot_tn(attended, grad_proj)
    vec_grad_ref[0:1, :] = column_sum(grad_proj.astype(f32))
    vec_grad_ref[1:2, :] = column_sum(grad_normed * scaled)
    vec_grad_ref[2:3, :] = column_sum(grad_normed)
    vec_grad_ref[3:4, :] = column_sum(wide)

    extra = keep_ref.shape[1] - wide_rows - (blocks + 1) * rows
    row_at = lax.broadcasted_iota(jnp.int32, (extra, 1), 0)
    low_bit = meta_ref[1] & 1

    def put(high, at, count, source):
        mine, other = choose(low_bit, source(2 * high), source(2 * high + 1))
        keep_ref[high, at : at + count, :] = mine.astype(bf16)
        send_ref[high, at : at + count, :] = other.astype(bf16)

    def small(owner):
        first = [vec_grad_ref[i : i + 1, owner * rows : (owner + 1) * rows] for i in range(4)]
        second = up_bias_grad_ref[:, owner * wide_rows : (owner + 1) * wide_rows]
        return jnp.where(row_at == 0, jnp.concatenate(first, axis=1), jnp.where(row_at == 1, second, 0.0))

    for high in range(owners // 2):
        put(high, 0, wide_rows, lambda owner: down_acc[owner * wide_rows : (owner + 1) * wide_rows, :])
        at = wide_rows
        for block in range(blocks):
            columns = slice(block * WIDTH, (block + 1) * WIDTH)
            put(high, at, rows, lambda owner: up_acc[owner * rows : (owner + 1) * rows, columns])
            at += rows
        put(high, at, rows, lambda owner: out_acc[owner * rows : (owner + 1) * rows, :])
        put(high, at + rows, extra, small)


def feed_call(hidden_width, devices, meta, x, attended, cot, vectors, up_bias, ones, twos):
    rows, owners = x.shape[0], len(ones)
    chain = chain_rows(2 * (hidden_width // owners) + WIDTH // owners, devices)
    split = jax.ShapeDtypeStruct((owners // 2, chain, WIDTH), bf16)
    return pl.pallas_call(
        partial(feed_kernel, hidden_width, owners),
        out_shape=[
            jax.ShapeDtypeStruct((rows, WIDTH), bf16),
            jax.ShapeDtypeStruct((rows, WIDTH), f32),
            jax.ShapeDtypeStruct((rows, WIDTH), bf16),
            split,
            split,
        ],
        in_specs=[pl.BlockSpec(memory_space=pltpu.SMEM)] + vmem_specs(5 + 2 * owners),
        out_specs=vmem_specs(5),
        scratch_shapes=[
            pltpu.VMEM((hidden_width, WIDTH), bf16),
            pltpu.VMEM((WIDTH, hidden_width), bf16),
            pltpu.VMEM((WIDTH, WIDTH), bf16),
            pltpu.VMEM((8, WIDTH), f32),
            pltpu.VMEM((1, hidden_width), f32),
            pltpu.VMEM((hidden_width, WIDTH), f32),
            pltpu.VMEM((WIDTH, hidden_width), f32),
            pltpu.VMEM((WIDTH, WIDTH), f32),
        ],
        compiler_params=pltpu.CompilerParams(vmem_limit_bytes=46 << 20),
        cost_estimate=pl.CostEstimate(flops=32 << 30, bytes_accessed=20 << 20, transcendentals=4 << 20),
        name="feed_forward",
    )(meta, x, attended, cot, vectors, up_bias, *ones, *twos)


def input_grad_kernel(
    rows,
    x_ref,
    dq_ref,
    local_ref,
    grad_middle_ref,
    from_right_ref,
    from_left_ref,
    far_keep_ref,
    far_got_ref,
    w_ref,
    vec_ref,
    out_ref,
    got_ref,
):
    step = pl.program_id(0)
    tile = x_ref.shape[0]
    edge = BLOCK * LOCAL

    @pl.when(step == 0)
    def _():
        folded = far_keep_ref[...].astype(f32) + far_got_ref[...].astype(f32)
        high, low = two_parts(jnp.concatenate([folded[:8], folded[8:]], axis=1))
        got_ref[0:edge, :] = from_left_ref[...]
        got_ref[edge : 2 * edge, :] = from_right_ref[...]
        far = jnp.concatenate([high.astype(f32), low.astype(f32)], axis=0).astype(bf16)
        got_ref[2 * edge : 2 * edge + BLOCK, :] = far
        got_ref[2 * edge + BLOCK :, :] = jnp.zeros((BLOCK, 2 * WIDTH), bf16)

    shape = (1, got_ref.shape[0])
    column = lax.broadcasted_iota(jnp.int32, shape, 1)
    within = jnp.where(column < edge, column, column - edge)
    level = jnp.where(column < 2 * edge, within >> 4, LOCAL)
    last = jnp.where((column >= edge) & (column < 2 * edge), (rows >> level) - BLOCK, 0)
    entry = jnp.where(column < 2 * edge, last + (within & 15), (column - 2 * edge) & 7)
    entry = jnp.where(column < 2 * edge + BLOCK, entry, -1)
    scale = 1.0 / (1 << level).astype(f32)
    token = step * tile + lax.broadcasted_iota(jnp.int32, (tile, shape[1]), 0)
    member = jnp.where((token >> level) == entry, scale, 0.0).astype(bf16)

    scaled, inverse = norm_rows(x_ref[...].astype(f32))
    dkv = (local_ref[...].astype(f32) + dot_nn(member, got_ref[...])).astype(bf16)
    grad = dot_nt(dq_ref[...], w_ref[:, :WIDTH]) + dot_nt(dkv, w_ref[:, WIDTH:])
    out_ref[...] = grad_middle_ref[...] + norm_back(grad, scaled, inverse, vec_ref[0:1, :])


def input_grad_call(x, dq, local, grad_middle, from_right, from_left, far_keep, far_got, weight, vectors):
    rows = x.shape[0]
    tile = 512
    tiled = lambda width: pl.BlockSpec((tile, width), lambda i: (i, 0))
    return pl.pallas_call(
        partial(input_grad_kernel, rows),
        grid=(rows // tile,),
        out_shape=jax.ShapeDtypeStruct((rows, WIDTH), f32),
        in_specs=[tiled(WIDTH), tiled(WIDTH), tiled(2 * WIDTH), tiled(WIDTH)] + vmem_specs(6),
        out_specs=tiled(WIDTH),
        scratch_shapes=[pltpu.VMEM((2 * BLOCK * (LOCAL + 1), 2 * WIDTH), bf16)],
        compiler_params=pltpu.CompilerParams(vmem_limit_bytes=24 << 20),
        cost_estimate=pl.CostEstimate(flops=6 << 30, bytes_accessed=12 << 20, transcendentals=0),
        name="input_grad",
    )(x, dq, local, grad_middle, from_right, from_left, far_keep, far_got, weight, vectors)


def shifted(block, axis, distance):
    devices = range(lax.axis_size(axis))
    route = [(i - distance, i) for i in devices if i - distance in devices]
    return lax.ppermute(block, axis, route)


def swap(block, axis, bit):
    return lax.ppermute(block, axis, [(i, i ^ bit) for i in range(lax.axis_size(axis))])


def gather_step(part, axis, bit):
    mine = (lax.axis_index(axis) // bit) % 2
    other = swap(part, axis, bit)
    first = jnp.where(mine == 0, part, other)
    second = jnp.where(mine == 0, other, part)
    return jnp.stack([first, second], axis=-3)


def together(*values):
    return lax.optimization_barrier(values)


def bits_of(axis):
    size = lax.axis_size(axis)
    return [1 << at for at in range(size.bit_length() - 1)]


def step_call(name, function, meta, arrays, shapes, dtype=bf16):
    def kernel(meta_ref, *refs):
        values = [ref[...].astype(f32) for ref in refs[: len(arrays)]]
        for ref, value in zip(refs[len(arrays) :], function(meta_ref[0], meta_ref[1], *values), strict=True):
            ref[...] = value.astype(dtype)

    size = sum(math.prod(a.shape) for a in arrays)
    return pl.pallas_call(
        kernel,
        out_shape=[jax.ShapeDtypeStruct(shape, dtype) for shape in shapes],
        in_specs=[pl.BlockSpec(memory_space=pltpu.SMEM)] + vmem_specs(len(arrays)),
        out_specs=vmem_specs(len(shapes)),
        compiler_params=pltpu.CompilerParams(vmem_limit_bytes=(4 << 20) + 16 * size),
        cost_estimate=pl.CostEstimate(flops=1 << 20, bytes_accessed=4 * size, transcendentals=0),
        name=name,
    )(meta, *arrays)


def halves(values, axis=0):
    return jnp.split(values, 2, axis=axis)


class Reduction:
    def __init__(self, meta, keep, send, far=None):
        self.meta, self.rows, self.far = meta, keep.shape[1], far
        self.bits = bits_of("ctx")[1:]
        self.keep, self.got = keep, [swap(send, "fsdp", 1)]

    def call(self, name, function, arrays, *shapes):
        return step_call(name, function, self.meta, arrays, [(*shape, WIDTH) for shape in shapes])

    def cross(self):
        far = [self.far[1]] if self.far else []
        extra = far[0].shape[0] if far else 0
        half = self.rows // 2

        def function(here, owner, keep, got, *far):
            mine, other = choose(owner >> 1, *(keep + got))
            keep, near = choose(here & 1, *halves(mine))
            high, both = choose(here & 1, *halves(other))
            return keep, jnp.concatenate([near, *far], axis=0), high, both

        shapes = [(half,), (half + extra,), (half,), (half,)]
        self.keep, near, high, both = self.call("cross", function, [self.keep, *self.got, *far], *shapes)
        count = lax.axis_size("fsdp")
        route = [(i, i ^ count ^ 2) for i in range(count * lax.axis_size("ctx"))]
        self.got = [swap(near, "ctx", 1), swap(high, "fsdp", 2), lax.ppermute(both, ("ctx", "fsdp"), route)]

    def scatter(self, at):
        bit, last = self.bits[at], at == len(self.bits) - 1
        rows = self.keep.shape[0]
        far = [self.far[0]] if self.far else []
        extra = far[0].shape[0] // 2 if far else 0

        def function(here, owner, keep, *got):
            far_keep = got[-1]
            got = got[: len(got) - len(far)]
            total = keep + got[0][:rows]
            for other in got[1:]:
                total = total + other
            flag = (here // bit) & 1
            keep, send = (total, total) if last else choose(flag, *halves(total))
            if not far:
                return [keep] if last else [keep, send]
            far_keep, far_send = choose_groups(flag, far_keep + got[0][rows:])
            return keep, jnp.concatenate([send, far_send], axis=0), far_keep

        count = rows if last else rows // 2
        shapes = [(count,)] if last and not far else [(count,), (count + extra,)]
        out = self.call("scatter", function, [self.keep, *self.got, *far], *shapes, *([(extra,)] if far else []))
        self.keep, send = out[0], out[1] if len(out) > 1 else out[0]
        self.got = [swap(send, "ctx", bit)]
        if far:
            self.far = (out[2], None)


    def order(self):
        high = list(reversed(self.bits[:-1]))
        return list(zip(high + [1], [1] + high))

    def collect(self):
        rows = self.keep.shape[0]
        if self.far:
            self.far = (self.far[0], self.got[0][rows:])
        function = lambda here, owner, keep, got: halves(keep + got[:rows])
        self.send_gather(0, self.call("collect", function, [self.keep, *self.got], (rows // 2,), (rows // 2,)))

    def send_gather(self, at, keep):
        self.keep = keep
        self.got = [swap(part, "ctx", bit) for part, bit in zip(keep, self.order()[at])]

    def gather(self, at):
        bits = self.order()[at]
        rows = 2 * self.keep[0].shape[0]
        function = lambda here, owner, *arrays: self.paired(here, bits, *arrays)
        self.send_gather(at + 1, self.call("gather", function, [*self.keep, *self.got], (rows,), (rows,)))

    def paired(self, here, bits, keep_one, keep_two, got_one, got_two):
        one = jnp.concatenate(choose((here // bits[0]) & 1, keep_one, got_one), axis=0)
        two = jnp.concatenate(choose((here // bits[1]) & 1, keep_two, got_two), axis=0)
        return one, two

    def scatters(self):
        return [self.cross] + [partial(self.scatter, at) for at in range(len(self.bits))]

    def gathers(self):
        return [self.collect] + [partial(self.gather, at) for at in range(len(self.order()) - 1)]

    def finish(self, shapes, unpack):
        bits = self.order()[-1]
        outer = lax.axis_size("ctx") // 4
        rows = self.rows // (4 * outer)

        def function(here, owner, *arrays):
            one, two = self.paired(here, bits, *arrays)
            parts = []
            for low in range(2):
                for high in range(outer):
                    a, b = low * outer + high, 2 * high + low
                    parts += [one[a * rows : (a + 1) * rows], two[b * rows : (b + 1) * rows]]
            return unpack(jnp.concatenate(parts, axis=0))

        return step_call("finish", function, self.meta, [*self.keep, *self.got], shapes, f32)


def shards(
    layer_input,
    doc_lengths,
    ln1_gain,
    ln1_bias,
    qkv_weight,
    query_bias,
    value_bias,
    out_weight,
    out_bias,
    ln2_gain,
    ln2_bias,
    up_weight,
    up_bias,
    down_weight,
    down_bias,
    cotangent,
):
    owners = lax.axis_size("fsdp")
    devices = lax.axis_size("ctx")
    x, cot = layer_input[0], cotangent[0]
    rows = x.shape[0]
    total = rows * devices
    far = far_levels(total)
    here, owner = lax.axis_index("ctx"), lax.axis_index("fsdp")
    part = WIDTH // owners
    hidden_width = up_weight.shape[1]
    meta = jnp.stack([here] + [owner ^ at for at in range(owners)]).astype(jnp.int32)

    vectors = [ln1_gain, ln1_bias, query_bias, value_bias, out_bias, ln2_gain, ln2_bias, down_bias, up_bias]
    own = pack_call(qkv_weight, vectors)
    across = swap(own, "fsdp", 2)
    beside = swap(own, "fsdp", 1)
    one, two = pack_rest_call(down_weight, up_weight, out_weight)
    bias = mask_call(rows, total, far, meta, doc_lengths)
    across, beside, one, two, bias = together(across, beside, one, two, bias)
    pieces = [own, beside, across, swap(across, "fsdp", 1)]
    one_across = swap(one, "fsdp", 2)
    qkv_full, vec, up_shift, queries, kv, scaled, tail, head, base = qkv_call(
        rows, hidden_width, meta, x, pieces, [bias, two]
    )
    vec, tail, head, base, one_across = together(vec, tail, head, base, one_across)

    one_beside, one_both = swap(one, "fsdp", 1), swap(one_across, "fsdp", 1)
    two_across = swap(two, "fsdp", 2)
    left = shifted(tail, "ctx", 1)
    right = shifted(head, "ctx", -1)
    for bit in reversed(bits_of("ctx")):
        base = gather_step(base, "ctx", bit)
        if bit == 1:
            base, left, right, one_beside, one_both, two_across = together(
                base, left, right, one_beside, one_both, two_across
            )
    base = base.reshape(-1, ENTRY)
    two_beside, two_both = swap(two, "fsdp", 1), swap(two_across, "fsdp", 1)
    attended, exps, inverses = attend_call(rows, devices, far, meta, queries, bias, kv, left, right, base)
    inverses, two_beside, two_both = together(inverses, two_beside, two_both)
    output, grad_middle, grad_attended, keep, send = feed_call(
        hidden_width,
        devices,
        meta,
        x,
        attended,
        cot,
        vec,
        up_shift,
        [one, one_beside, one_across, one_both],
        [two, two_beside, two_across, two_both],
    )
    feed = Reduction(meta, keep, send)
    feed.cross()
    made = attend_back_call(
        rows, devices, far, owners, meta, queries, grad_attended, exps, inverses, kv, scaled, left, right, base, qkv_full, vec
    )
    dq, local, to_left, to_right, far_keep, far_send, keep, send = made
    to_left, to_right, far_keep, far_send, send, *feed.got = together(
        to_left, to_right, far_keep, far_send, send, *feed.got
    )
    first = Reduction(meta, keep, send, (far_keep, far_send))
    back_right = shifted(to_left, "ctx", -1)
    back_left = shifted(to_right, "ctx", 1)
    pending = feed.scatters()[1:]
    pending.pop(0)()
    first.cross()
    tied = together(*first.got, *feed.got)
    first.got, feed.got = list(tied[: len(first.got)]), list(tied[len(first.got) :])
    for one in first.scatters()[1:]:
        one()
        if pending:
            pending.pop(0)()
    for one, two in zip(first.gathers(), feed.gathers()):
        one()
        two()
    input_grad = input_grad_call(
        x, dq, local, grad_middle, back_right, back_left, *first.far, qkv_full, vec
    )

    wide_rows = hidden_width // owners

    def split(row):
        return [row[:, at * part : (at + 1) * part] for at in range(row.shape[1] // part)]

    def unpack_first(total):
        blocks = [total[at * part : (at + 1) * part] for at in range(3)]
        return [jnp.concatenate(blocks, axis=1), *split(total[3 * part : 3 * part + 1])]

    def unpack_feed(total):
        at = wide_rows
        blocks = []
        for _ in range(hidden_width // WIDTH):
            blocks.append(total[at : at + part])
            at += part
        vectors = [*split(total[at + part : at + part + 1]), total[at + part + 1 : at + part + 2]]
        return [total[:wide_rows], jnp.concatenate(blocks, axis=1), total[at : at + part], *vectors]

    vector = (1, part)
    qkv_grad, *firsts = first.finish([(part, 3 * WIDTH)] + [vector] * owners, unpack_first)
    down_grad, up_grad, out_grad, *feeds = feed.finish(
        [(wide_rows, WIDTH), (part, hidden_width), (part, WIDTH)] + [vector] * owners + [(1, wide_rows)], unpack_feed
    )
    gain_first, shift_first, query_grad, value_grad = (v.reshape(-1) for v in firsts)
    out_shift, gain_second, shift_second, down_shift, up_shift_grad = (v.reshape(-1) for v in feeds)
    return (
        output[None],
        input_grad[None],
        gain_first,
        shift_first,
        qkv_grad,
        query_grad,
        value_grad,
        out_grad,
        out_shift,
        gain_second,
        shift_second,
        up_grad,
        up_shift_grad,
        down_grad,
        down_shift,
    )


def solution(mesh):
    row, vector = P("fsdp", None), P("fsdp")
    tokens = P("fsdp", "ctx", None)
    return jax.shard_map(
        shards,
        mesh=mesh,
        in_specs=(
            tokens,
            row,
            vector,
            vector,
            row,
            vector,
            vector,
            row,
            vector,
            vector,
            vector,
            row,
            vector,
            row,
            vector,
            tokens,
        ),
        out_specs=(
            tokens,
            tokens,
            vector,
            vector,
            row,
            vector,
            vector,
            row,
            vector,
            vector,
            vector,
            row,
            vector,
            row,
            vector,
        ),
        check_vma=False,
    )
```

```python
from functools import partial
import math

import jax
import jax.numpy as jnp
from jax import lax
from jax.experimental import pallas as pl
from jax.experimental.pallas import tpu as pltpu
from jax.sharding import PartitionSpec as P

HEADS = 8
BLOCK = 16
LEVELS = 10
NEAR = 3
LOCAL = 7
CHUNK = 64
STEP = 4
WIDTH = 512
GROUP = 4
GROUPS = HEADS // GROUP
LANES = WIDTH // GROUPS
ENTRY = 3 * WIDTH
SMALL = 16
MASKED = -1e30
EPSILON = 1e-05

f32 = jnp.float32
bf16 = jnp.bfloat16


def level_rows(rows, level):
    return rows // 2**level


def level_offsets(rows):
    offsets = [0]
    for level in range(LOCAL):
        offsets.append(offsets[-1] + level_rows(rows, level))
    return offsets[:-1], offsets[-1]


def far_levels(total):
    return [l for l in range(LOCAL, LEVELS) if total // (BLOCK * 2**l) >= 2]


def extended_offsets(rows, far):
    offsets, cursor = [], 0
    for level in range(LOCAL):
        offsets.append(cursor)
        cursor += level_rows(rows, level) + 2 * BLOCK
    for _ in far:
        offsets.append(cursor)
        cursor += 2 * BLOCK
    return offsets, cursor


def slot_layout(far):
    parts = [(level, CHUNK // 2**level + 2 * BLOCK) for level in range(NEAR)]
    parts += [(level, BLOCK) for level in list(range(NEAR, LOCAL)) + far for _ in range(2)]
    return parts, sum(count for _, count in parts)


def slot_sources(rows, far, chunk):
    offsets, _ = extended_offsets(rows, far)
    sources = []
    for level in range(NEAR):
        sources.append((offsets[level] + chunk * (CHUNK // 2**level), CHUNK // 2**level + 2 * BLOCK))
    for level in range(NEAR, LOCAL):
        block = chunk // (BLOCK * 2**level // CHUNK)
        sources.append((offsets[level] + block * BLOCK, BLOCK))
        sources.append((offsets[level] + block * BLOCK + 2 * BLOCK, BLOCK))
    for at in range(len(far)):
        sources.append((offsets[LOCAL + at], BLOCK))
        sources.append((offsets[LOCAL + at] + BLOCK, BLOCK))
    return sources


def mask_kernel(rows, total, far, here_ref, lengths_ref, bias_ref):
    for sub in range(STEP):
        base = here_ref[0] * rows + (pl.program_id(0) * STEP + sub) * CHUNK
        query = base + (lax.broadcasted_iota(jnp.int32, (1, 128), 1) & (CHUNK - 1))
        first_token = jnp.zeros((1, 128), jnp.int32)
        end_token = jnp.full((1, 128), total, jnp.int32)
        start = jnp.int32(0)
        for at in range(lengths_ref.shape[1]):
            first_token = jnp.where(start <= query, start, first_token)
            start = start + lengths_ref[0, at]
            end_token = jnp.where(start > query, jnp.minimum(end_token, start), end_token)

        def part(at, count, first_row, level):
            span = 2**level
            shift = level + 4
            first = first_row + span * lax.broadcasted_iota(jnp.int32, (count, 128), 0)
            gap = jnp.abs((first >> shift) - (query >> shift))
            if level == 0:
                seen = gap <= 1
            else:
                seen = (gap == 1) & (jnp.abs((first >> (shift - 1)) - (query >> (shift - 1))) > 1)
            seen = seen & (first >= first_token) & (first + (span - 1) < end_token)
            bias_ref[sub, at : at + count, :] = jnp.where(seen, level * math.log(2.0), MASKED)

        at = 0
        for level in range(NEAR):
            count = CHUNK // 2**level + 2 * BLOCK
            part(at, count, base - BLOCK * 2**level, level)
            at += count
        for level in list(range(NEAR, LOCAL)) + far:
            block = base >> (level + 4)
            for side in (-1, 1):
                part(at, BLOCK, (block + side) * (BLOCK * 2**level), level)
                at += BLOCK


def mask_call(rows, total, far, meta, lengths):
    chunks = rows // CHUNK
    _, slots = slot_layout(far)
    return pl.pallas_call(
        partial(mask_kernel, rows, total, far),
        grid=(chunks // STEP,),
        out_shape=jax.ShapeDtypeStruct((chunks, slots, 128), f32),
        in_specs=[pl.BlockSpec(memory_space=pltpu.SMEM)] * 2,
        out_specs=pl.BlockSpec((STEP, slots, 128), lambda i: (i, 0, 0)),
        compiler_params=pltpu.CompilerParams(vmem_limit_bytes=8 << 20),
        cost_estimate=pl.CostEstimate(flops=4 << 30, bytes_accessed=3 << 20, transcendentals=0),
        name="mask",
    )(meta, lengths)


def dot_nt(left, right):
    return lax.dot_general(left, right, (((1,), (1,)), ((), ())), preferred_element_type=f32)


def dot_tn(left, right):
    return lax.dot_general(left, right, (((0,), (0,)), ((), ())), preferred_element_type=f32)


def dot_nn(left, right):
    return jnp.dot(left, right, preferred_element_type=f32)


def pool_matrix(count):
    row = lax.broadcasted_iota(jnp.int32, (count // 2, count), 0)
    column = lax.broadcasted_iota(jnp.int32, (count // 2, count), 1)
    return jnp.where((column >> 1) == row, 0.5, 0.0).astype(bf16)


def spread_matrix(count):
    row = lax.broadcasted_iota(jnp.int32, (2 * count, count), 0)
    column = lax.broadcasted_iota(jnp.int32, (2 * count, count), 1)
    return jnp.where((row >> 1) == column, 0.5, 0.0).astype(bf16)


def spread(values):
    count = values.shape[0]
    tile = min(count, 128)
    matrix = spread_matrix(tile)
    high = values.astype(bf16)
    low = (values - high.astype(f32)).astype(bf16)
    parts = [
        dot_nn(matrix, high[at : at + tile]) + dot_nn(matrix, low[at : at + tile])
        for at in range(0, count, tile)
    ]
    return parts[0] if len(parts) == 1 else jnp.concatenate(parts, axis=0)


def norm_rows(values):
    mean = jnp.mean(values, axis=-1, keepdims=True)
    centred = values - mean
    variance = jnp.mean(centred * centred, axis=-1, keepdims=True)
    inverse = lax.rsqrt(variance + EPSILON)
    return centred * inverse, inverse


def norm_back(grad_out, scaled, inverse, gain):
    grad_scaled = grad_out * gain
    first = jnp.mean(grad_scaled, axis=-1, keepdims=True)
    second = jnp.mean(grad_scaled * scaled, axis=-1, keepdims=True)
    return inverse * (grad_scaled - first - scaled * second)


def head_of(shape):
    return lax.broadcasted_iota(jnp.int32, shape, 1) // (WIDTH // HEADS)


def split_heads(group):
    head, zero = head_of(group.shape), jnp.zeros_like(group)
    return jnp.concatenate([jnp.where(head == at, group, zero) for at in range(GROUP)], axis=0)


def join_heads(stacked):
    rows = stacked.shape[0] // GROUP
    head = head_of((rows, stacked.shape[1]))
    out = stacked[:rows]
    for at in range(1, GROUP):
        out = jnp.where(head == at, stacked[at * rows : (at + 1) * rows], out)
    return out


def pack_kernel(*refs):
    out_ref = refs[-1]
    row = jnp.concatenate([ref[...].reshape(1, -1) for ref in refs[:-1]], axis=1)
    out_ref[...] = jnp.broadcast_to(row.astype(f32), out_ref.shape).astype(bf16)


def pack_call(vectors):
    return pl.pallas_call(
        pack_kernel,
        out_shape=jax.ShapeDtypeStruct((SMALL, sum(v.shape[0] for v in vectors)), bf16),
        in_specs=vmem_specs(len(vectors)),
        out_specs=vmem_specs(1)[0],
        compiler_params=pltpu.CompilerParams(vmem_limit_bytes=56 << 20),
        name="pack",
    )(*vectors)


def pack_rest_kernel(down_ref, up_ref, out_w_ref, one_ref, two_ref):
    rows = up_ref.shape[0]
    blocks = up_ref.shape[1] // WIDTH
    for block in range(blocks - 1):
        one_ref[block * rows : (block + 1) * rows, :] = up_ref[:, block * WIDTH : (block + 1) * WIDTH]
    two_ref[0:rows, :] = up_ref[:, (blocks - 1) * WIDTH :]
    two_ref[rows : 2 * rows, :] = out_w_ref[...]
    two_ref[2 * rows :, :] = down_ref[...]


def pack_rest_call(down, up, out_w):
    rows, blocks = up.shape[0], up.shape[1] // WIDTH
    return pl.pallas_call(
        pack_rest_kernel,
        out_shape=[
            jax.ShapeDtypeStruct(((blocks - 1) * rows, WIDTH), bf16),
            jax.ShapeDtypeStruct((2 * rows + down.shape[0], WIDTH), bf16),
        ],
        in_specs=vmem_specs(3),
        out_specs=vmem_specs(2),
        compiler_params=pltpu.CompilerParams(vmem_limit_bytes=56 << 20),
        name="pack_rest",
    )(down, up, out_w)


def vmem_specs(count):
    return [pl.BlockSpec(memory_space=pltpu.VMEM)] * count


def qkv_kernel(rows, owners, meta_ref, x_ref, *refs):
    shard_refs, small_refs, refs = refs[:owners], refs[owners : 2 * owners], refs[2 * owners + 2 :]
    w_ref, vec_ref, up_bias_ref, q_ref = refs[:4]
    kv_ref, scaled_ref, tail_ref, head_ref, top_ref, keep_ref = refs[4:]
    places, _ = level_offsets(rows)
    part = WIDTH // owners
    step = pl.program_id(0)

    @pl.when(step == 0)
    def _():
        for at, (ref, small_ref) in enumerate(zip(shard_refs, small_refs)):
            owner = meta_ref[1 + at]
            w_ref[pl.ds(pl.multiple_of(owner * part, part), part), :] = ref[...]
            row = small_ref[0:1, :].astype(f32)
            for vector in range(8):
                vec_ref[vector : vector + 1, pl.ds(pl.multiple_of(owner * part, part), part)] = row[
                    :, vector * part : (vector + 1) * part
                ]
            wide = row.shape[1] - 8 * part
            up_bias_ref[:, pl.ds(pl.multiple_of(owner * wide, wide), wide)] = row[:, 8 * part :]

    tile = x_ref.shape[0]
    scaled, _ = norm_rows(x_ref[...].astype(f32))
    normed = (scaled * vec_ref[0:1, :] + vec_ref[1:2, :]).astype(bf16)
    queries = (dot_nn(normed, w_ref[:, :WIDTH]) + vec_ref[2:3, :]).astype(bf16)
    q_ref[...] = queries * jnp.asarray(0.125, bf16)
    keys = dot_nn(normed, w_ref[:, WIDTH : 2 * WIDTH]).astype(bf16)
    values = (dot_nn(normed, w_ref[:, 2 * WIDTH :]) + vec_ref[3:4, :]).astype(bf16)
    current = jnp.concatenate([keys, values, scaled.astype(bf16)], axis=1)

    def edges(level, block):
        @pl.when(step == 0)
        def _():
            head_ref[BLOCK * level : BLOCK * (level + 1), :] = block[:BLOCK]

        @pl.when(step == pl.num_programs(0) - 1)
        def _():
            tail_ref[BLOCK * level : BLOCK * (level + 1), :] = block[block.shape[0] - BLOCK :]

    for level in range(5):
        if level:
            current = dot_nn(pool_matrix(current.shape[0]), current).astype(bf16)
        count = tile // 2**level
        span = pl.ds(pl.multiple_of(places[level] + step * count, count), count)
        kv_ref[span, :] = current[:, : 2 * WIDTH]
        scaled_ref[span, :] = current[:, 2 * WIDTH :]
        edges(level, current)
    keep_ref[pl.ds(pl.multiple_of(step * count, count), count), :] = current

    @pl.when(step == pl.num_programs(0) - 1)
    def _():
        current = keep_ref[...]
        for level in range(5, LOCAL):
            current = dot_nn(pool_matrix(current.shape[0]), current).astype(bf16)
            span = slice(places[level], places[level] + current.shape[0])
            kv_ref[span, :] = current[:, : 2 * WIDTH]
            scaled_ref[span, :] = current[:, 2 * WIDTH :]
            tail_ref[BLOCK * level : BLOCK * (level + 1), :] = current[current.shape[0] - BLOCK :]
            head_ref[BLOCK * level : BLOCK * (level + 1), :] = current[:BLOCK]
        top_ref[...] = dot_nn(pool_matrix(BLOCK), current).astype(bf16)


def qkv_call(rows, hidden_width, meta, x, pieces, smalls, earlier):
    owners = len(pieces)
    tile = 512

    def tiled(count, width):
        return pl.BlockSpec((count, width), lambda i: (i, 0))

    _, entries = level_offsets(rows)
    edge = jax.ShapeDtypeStruct((BLOCK * LOCAL, ENTRY), bf16)
    outs = pl.pallas_call(
        partial(qkv_kernel, rows, owners),
        grid=(rows // tile,),
        out_shape=[
            jax.ShapeDtypeStruct((WIDTH, 3 * WIDTH), bf16),
            jax.ShapeDtypeStruct((8, WIDTH), f32),
            jax.ShapeDtypeStruct((1, hidden_width), f32),
            jax.ShapeDtypeStruct((rows, WIDTH), bf16),
        ]
        + [jax.ShapeDtypeStruct((entries, 2 * WIDTH), bf16), jax.ShapeDtypeStruct((entries, WIDTH), bf16)]
        + [edge, edge, jax.ShapeDtypeStruct((BLOCK // 2, ENTRY), bf16)],
        in_specs=[pl.BlockSpec(memory_space=pltpu.SMEM), tiled(tile, WIDTH)]
        + vmem_specs(2 * owners)
        + [pl.BlockSpec(memory_space=pl.ANY)] * 2,
        out_specs=vmem_specs(3) + [tiled(tile, WIDTH)] + vmem_specs(5),
        scratch_shapes=[pltpu.VMEM((level_rows(rows, 4), ENTRY), bf16)],
        compiler_params=pltpu.CompilerParams(vmem_limit_bytes=56 << 20),
        cost_estimate=pl.CostEstimate(flops=9 << 30, bytes_accessed=12 << 20, transcendentals=0),
        name="qkv_levels",
    )(meta, x, *pieces, *smalls, *earlier)
    return outs


def far_level(entries):
    return dot_nn(pool_matrix(entries.shape[0]), entries).astype(bf16)


def assemble(rows, far, here, columns, own_ref, left_ref, right_ref, base_ref, ext_ref, far_ref):
    offsets, _ = extended_offsets(rows, far)
    places, _ = level_offsets(rows)
    for inner, outer, target, width in columns:
        lanes, edge_lanes = slice(target, target + width), slice(outer, outer + width)
        for level in range(LOCAL):
            at, count = offsets[level], level_rows(rows, level)
            edge = slice(BLOCK * level, BLOCK * (level + 1))
            ext_ref[at : at + BLOCK, lanes] = left_ref[edge, edge_lanes]
            ext_ref[at + BLOCK : at + BLOCK + count, lanes] = own_ref[
                places[level] : places[level] + count, inner : inner + width
            ]
            ext_ref[at + BLOCK + count : at + 2 * BLOCK + count, lanes] = right_ref[edge, edge_lanes]
        current = base_ref[:, edge_lanes]
        for index, level in enumerate(far):
            if index:
                current = far_level(current)
            count = current.shape[0]
            far_ref[0:count, 0:width] = current
            for side, start in enumerate(far_starts(here, level, count)):
                at = offsets[LOCAL + index] + side * BLOCK
                ext_ref[at : at + BLOCK, lanes] = far_ref[pl.ds(start, BLOCK), 0:width]


def far_starts(here, level, count):
    block = here >> (level - 6)
    last = count // BLOCK - 1
    return [pl.multiple_of(jnp.clip(at, 0, last) * BLOCK, BLOCK) for at in (block - 1, block + 1)]


def load_slots(rows, far, chunk, ext_ref, slots_ref):
    at = 0
    for start, count in slot_sources(rows, far, chunk):
        if not isinstance(start, int):
            start = pl.multiple_of(start, BLOCK)
        slots_ref[at : at + count, :] = ext_ref[pl.ds(start, count), :]
        at += count


def attend_kernel(rows, far, meta_ref, q_ref, bias_ref, *refs):
    own_ref, left_ref, right_ref, base_ref, out_ref, exp_ref, inverse_ref, ext_ref, far_ref, slots_ref = refs
    step = pl.program_id(0)

    @pl.when(step == 0)
    def _():
        columns = [(0, 0, 0, 2 * WIDTH)]
        assemble(rows, far, meta_ref[0], columns, own_ref, left_ref, right_ref, base_ref, ext_ref, far_ref)

    ones = jnp.ones((slots_ref.shape[0], 128), bf16)
    second_head = (head_of((CHUNK, 256)) & 1) == 1
    for sub in range(STEP):
        span = slice(sub * CHUNK, (sub + 1) * CHUNK)
        load_slots(rows, far, step * STEP + sub, ext_ref, slots_ref)
        bias = bias_ref[sub]
        bias = jnp.concatenate([bias, bias], axis=1)
        for group in range(GROUPS):
            lanes = slice(LANES * group, LANES * (group + 1))
            values = slots_ref[:, WIDTH + LANES * group : WIDTH + LANES * (group + 1)]
            scores = dot_nt(slots_ref[:, lanes], split_heads(q_ref[span, lanes])) + bias
            exponent = jnp.exp(scores - jnp.max(scores, axis=0, keepdims=True))
            low = exponent.astype(bf16)
            exp_ref[sub, group] = low
            inverse = 1.0 / jnp.sum(exponent, axis=0, keepdims=True)
            inverse_ref[sub, group : group + 1, :] = inverse
            for half in range(LANES // 128):
                columns = slice(128 * half, 128 * (half + 1))
                both = dot_tn(low[:, columns], jnp.concatenate([values[:, columns], ones], axis=1))
                pair = jnp.where(second_head, both[CHUNK:], both[:CHUNK])
                at = LANES * group + 128 * half
                out_ref[span, at : at + 128] = (pair[:, :128] / pair[:, 128:]).astype(bf16)


def attend_call(rows, devices, far, meta, q, bias, kv, left, right, base):
    chunks = rows // CHUNK
    _, entries = extended_offsets(rows, far)
    _, slots = slot_layout(far)
    return pl.pallas_call(
        partial(attend_kernel, rows, far),
        grid=(chunks // STEP,),
        out_shape=[
            jax.ShapeDtypeStruct((rows, WIDTH), bf16),
            jax.ShapeDtypeStruct((chunks, GROUPS, slots, LANES), bf16),
            jax.ShapeDtypeStruct((chunks, 8, LANES), f32),
        ],
        in_specs=[
            pl.BlockSpec(memory_space=pltpu.SMEM),
            pl.BlockSpec((STEP * CHUNK, WIDTH), lambda i: (i, 0)),
            pl.BlockSpec((STEP, slots, 128), lambda i: (i, 0, 0)),
        ]
        + vmem_specs(4),
        out_specs=[
            pl.BlockSpec((STEP * CHUNK, WIDTH), lambda i: (i, 0)),
            pl.BlockSpec((STEP, GROUPS, slots, LANES), lambda i: (i, 0, 0, 0)),
            pl.BlockSpec((STEP, 8, LANES), lambda i: (i, 0, 0)),
        ],
        scratch_shapes=[
            pltpu.VMEM((entries, 2 * WIDTH), bf16),
            pltpu.VMEM((8 * devices, 2 * WIDTH), bf16),
            pltpu.VMEM((slots, 2 * WIDTH), bf16),
        ],
        compiler_params=pltpu.CompilerParams(vmem_limit_bytes=56 << 20),
        cost_estimate=pl.CostEstimate(flops=20 << 30, bytes_accessed=20 << 20, transcendentals=4 << 20),
        name="attend",
    )(meta, q, bias, kv, left, right, base)


def column_sum(values):
    return jnp.sum(values, axis=0, keepdims=True)


def matrix_row(left, right):
    total = None
    for a in two_parts(left):
        for b in two_parts(right):
            term = dot_nt(a, b)
            total = term if total is None else total + term
    return total[0:1]


def two_parts(values):
    if values.dtype == bf16:
        return [values]
    high = values.astype(bf16)
    return [high, (values - high.astype(f32)).astype(bf16)]


def choose(flag, zero, one):
    return jnp.where(flag == 0, zero, one), jnp.where(flag == 0, one, zero)


def choose_groups(flag, folded):
    groups = folded.reshape(-1, 2, 8, folded.shape[1])
    return [part.reshape(-1, folded.shape[1]) for part in choose(flag, groups[:, 0], groups[:, 1])]


def attend_back_kernel(rows, far, *refs):
    refs = list(refs)
    take = lambda count: [refs.pop(0) for _ in range(count)]
    meta_ref, q_ref, grad_ref, exp_ref, inverse_ref = take(5)
    own_ref, own_scaled_ref = take(2)
    left_ref, right_ref, base_ref, w_ref, vec_ref = take(5)
    dq_ref, local_ref, to_left_ref, to_right_ref, far_keep_ref, far_send_ref, keep_ref, send_ref = take(8)
    ext_ref, far_ref, slots_ref, acc_ref, tree_ref, scaled_ref, dq_keep_ref = take(7)
    step = pl.program_id(0)
    offsets, entries = extended_offsets(rows, far)

    @pl.when(step == 0)
    def _():
        common = (left_ref, right_ref, base_ref)
        assemble(rows, far, meta_ref[0], [(0, 0, 0, 2 * WIDTH)], own_ref, *common, ext_ref, far_ref)
        assemble(rows, far, meta_ref[0], [(0, 2 * WIDTH, 0, WIDTH)], own_scaled_ref, *common, scaled_ref, far_ref)
        acc_ref[...] = jnp.zeros_like(acc_ref)

    for sub in range(STEP):
        chunk = step * STEP + sub
        span = slice(sub * CHUNK, (sub + 1) * CHUNK)
        load_slots(rows, far, chunk, ext_ref, slots_ref)
        sources = slot_sources(rows, far, chunk)
        for group in range(GROUPS):
            lanes = slice(LANES * group, LANES * (group + 1))
            value_lanes = slice(WIDTH + LANES * group, WIDTH + LANES * (group + 1))
            keys, values = slots_ref[:, lanes], slots_ref[:, value_lanes]
            queries, grads = split_heads(q_ref[span, lanes]), split_heads(grad_ref[span, lanes])
            probs = exp_ref[sub, group].astype(f32) * inverse_ref[sub, group : group + 1, :]
            grad_probs = dot_nt(values, grads)
            delta = jnp.sum(probs * grad_probs, axis=0, keepdims=True)
            grad_scores = (probs * (grad_probs - delta)).astype(bf16)
            dq = (join_heads(dot_tn(grad_scores, keys)) * 0.125).astype(bf16)
            dq_ref[span, lanes] = dq
            dq_keep_ref[pl.ds(pl.multiple_of(chunk * CHUNK, CHUNK), CHUNK), lanes] = dq
            grad_keys = dot_nn(grad_scores, queries)
            grad_values = dot_nn(probs.astype(bf16), grads)
            at = 0
            for start, count in sources:
                if not isinstance(start, int):
                    start = pl.multiple_of(start, BLOCK)
                acc_ref[pl.ds(start, count), lanes] += grad_keys[at : at + count]
                acc_ref[pl.ds(start, count), value_lanes] += grad_values[at : at + count]
                at += count

    @pl.when(step == pl.num_programs(0) - 1)
    def _():
        dq = dq_keep_ref[...]
        sums = [column_sum(dq.astype(f32)), column_sum(acc_ref[:, :WIDTH]), column_sum(acc_ref[:, WIDTH:])]
        both = dot_tn(scaled_ref[...], acc_ref[...].astype(bf16))
        parts = [dot_tn(own_scaled_ref[0:rows, :], dq), both[:, :WIDTH], both[:, WIDTH:]]
        first_row = lax.broadcasted_iota(jnp.int32, (16, 1), 0) == 0
        ones = jnp.where(first_row, jnp.ones((16, WIDTH), f32), 0.0).astype(bf16)
        as_column = lambda row: dot_tn(jnp.where(first_row, row, 0.0).astype(bf16), ones)
        gain, shift = as_column(vec_ref[0:1, :]), as_column(vec_ref[1:2, :])
        gain_grad, shift_grad = jnp.zeros((1, WIDTH), f32), jnp.zeros((1, WIDTH), f32)
        owners = 2 * keep_ref.shape[0]
        part = WIDTH // owners
        low_bit = meta_ref[1] & 1
        for block in range(3):
            weight = w_ref[:, block * WIDTH : (block + 1) * WIDTH]
            gain_grad += matrix_row(jnp.ones((16, WIDTH), bf16), weight.astype(f32) * parts[block])
            shift_grad += matrix_row(jnp.broadcast_to(sums[block], (16, WIDTH)), weight)
            grad = gain * parts[block] + shift * sums[block]
            for high in range(owners // 2):
                at = 2 * high * part
                mine, other = choose(low_bit, grad[at : at + part], grad[at + part : at + 2 * part])
                keep_ref[high, block * part : (block + 1) * part, :] = mine.astype(bf16)
                send_ref[high, block * part : (block + 1) * part, :] = other.astype(bf16)
        extra = keep_ref.shape[1] - 3 * part
        top_row = lax.broadcasted_iota(jnp.int32, (extra, 1), 0) == 0
        vectors = [gain_grad, shift_grad, sums[0], sums[2]]
        owner_row = lambda owner: jnp.concatenate([v[:, owner * part : (owner + 1) * part] for v in vectors], axis=1)
        for high in range(owners // 2):
            mine, other = choose(low_bit, owner_row(2 * high), owner_row(2 * high + 1))
            keep_ref[high, 3 * part :, :] = jnp.where(top_row, mine, 0.0).astype(bf16)
            send_ref[high, 3 * part :, :] = jnp.where(top_row, other, 0.0).astype(bf16)

        for level in range(LOCAL):
            at, count = offsets[level], level_rows(rows, level)
            edge = slice(BLOCK * level, BLOCK * (level + 1))
            to_left_ref[edge, :] = acc_ref[at : at + BLOCK, :].astype(bf16)
            to_right_ref[edge, :] = acc_ref[at + BLOCK + count : at + 2 * BLOCK + count, :].astype(bf16)
        carry = None
        for index in range(len(far) - 1, -1, -1):
            level = far[index]
            count = base_ref.shape[0] // 2 ** (level - LOCAL)
            tree_ref[0:count, :] = jnp.zeros((count, 2 * WIDTH), f32) if carry is None else spread(carry)
            for side, start in enumerate(far_starts(meta_ref[0], level, count)):
                at = offsets[LOCAL + index] + side * BLOCK
                tree_ref[pl.ds(start, BLOCK), :] += acc_ref[at : at + BLOCK, :]
            carry = tree_ref[0:count, :]
        mine, other = choose_groups(meta_ref[0] & 1, jnp.concatenate([carry[:, :WIDTH], carry[:, WIDTH:]], axis=0))
        far_keep_ref[...] = mine.astype(bf16)
        far_send_ref[...] = other.astype(bf16)
        tile = 256
        counts = [tile >> level for level in range(1, LOCAL - 1)]
        token = lax.broadcasted_iota(jnp.int32, (tile, counts[0]), 0)
        entry = lax.broadcasted_iota(jnp.int32, (tile, counts[0]), 1)
        member = jnp.concatenate(
            [
                jnp.where((token >> level) == entry, 0.5**level, 0.0)[:, :count]
                for level, count in enumerate(counts, 1)
            ],
            axis=1,
        ).astype(bf16)
        for at in range(0, rows, tile):
            coarse = [
                acc_ref[offsets[level] + BLOCK + (at >> level) : offsets[level] + BLOCK + ((at + tile) >> level), :]
                for level in range(1, LOCAL - 1)
            ]
            total = acc_ref[BLOCK + at : BLOCK + at + tile, :]
            for half in two_parts(jnp.concatenate(coarse, axis=0)):
                total = total + dot_nn(member, half)
            local_ref[at : at + tile, :] = total.astype(bf16)


def chain_rows(rows, devices):
    unit = 8 * devices
    return -(-(rows + 16) // unit) * unit


def attend_back_call(rows, devices, far, owners, meta, q, grads, exps, inverses, kv, scaled, left, right, base, weight, vectors):
    chunks = rows // CHUNK
    _, entries = extended_offsets(rows, far)
    _, slots = slot_layout(far)
    chain = (owners // 2, chain_rows(3 * WIDTH // owners, devices), WIDTH)
    outs = [
        jax.ShapeDtypeStruct((rows, WIDTH), bf16),
        jax.ShapeDtypeStruct((rows, 2 * WIDTH), bf16),
        jax.ShapeDtypeStruct((BLOCK * LOCAL, 2 * WIDTH), bf16),
        jax.ShapeDtypeStruct((BLOCK * LOCAL, 2 * WIDTH), bf16),
        jax.ShapeDtypeStruct((8 * devices, WIDTH), bf16),
        jax.ShapeDtypeStruct((8 * devices, WIDTH), bf16),
        jax.ShapeDtypeStruct(chain, bf16),
        jax.ShapeDtypeStruct(chain, bf16),
    ]
    return pl.pallas_call(
        partial(attend_back_kernel, rows, far),
        grid=(chunks // STEP,),
        out_shape=outs,
        in_specs=[
            pl.BlockSpec(memory_space=pltpu.SMEM),
            pl.BlockSpec((STEP * CHUNK, WIDTH), lambda i: (i, 0)),
            pl.BlockSpec((STEP * CHUNK, WIDTH), lambda i: (i, 0)),
            pl.BlockSpec((STEP, GROUPS, slots, LANES), lambda i: (i, 0, 0, 0)),
            pl.BlockSpec((STEP, 8, LANES), lambda i: (i, 0, 0)),
        ]
        + vmem_specs(7),
        out_specs=[pl.BlockSpec((STEP * CHUNK, WIDTH), lambda i: (i, 0))] + vmem_specs(len(outs) - 1),
        scratch_shapes=[
            pltpu.VMEM((entries, 2 * WIDTH), bf16),
            pltpu.VMEM((8 * devices, 2 * WIDTH), bf16),
            pltpu.VMEM((slots, 2 * WIDTH), bf16),
            pltpu.VMEM((entries, 2 * WIDTH), f32),
            pltpu.VMEM((8 * devices, 2 * WIDTH), f32),
            pltpu.VMEM((entries, WIDTH), bf16),
            pltpu.VMEM((rows, WIDTH), bf16),
        ],
        compiler_params=pltpu.CompilerParams(vmem_limit_bytes=40 << 20),
        cost_estimate=pl.CostEstimate(flops=36 << 30, bytes_accessed=24 << 20, transcendentals=4 << 20),
        name="attend_back",
    )(meta, q, grads, exps, inverses, kv, scaled, left, right, base, weight, vectors)


def normal_parts(values):
    size = jnp.abs(values)
    bell = jnp.exp(-0.5 * values * values)
    t = 1.0 / (1.0 + (0.3275911 / math.sqrt(2.0)) * size)
    poly = t * (
        0.5 * 0.254829592
        + t * (0.5 * -0.284496736 + t * (0.5 * 1.421413741 + t * (0.5 * -1.453152027 + t * (0.5 * 1.061405429))))
    )
    tail = poly * bell
    return jnp.where(values < 0, tail, 1.0 - tail), bell * (1.0 / math.sqrt(2.0 * math.pi))


def feed_kernel(
    hidden_width,
    owners,
    meta_ref,
    x_ref,
    attended_ref,
    cot_ref,
    vec_ref,
    up_bias_ref,
    *refs,
):
    one_refs, two_refs, refs = refs[:owners], refs[owners : 2 * owners], refs[2 * owners :]
    y_ref, grad_middle_ref, grad_attended_ref, keep_ref, send_ref = refs[:5]
    down_w_ref, up_w_ref, out_w_ref, vec_grad_ref, up_bias_grad_ref, down_acc, up_acc, out_acc = refs[5:]
    rows = WIDTH // owners
    wide_rows = hidden_width // owners
    blocks = hidden_width // WIDTH

    for at, (one, two) in enumerate(zip(one_refs, two_refs)):
        owner = meta_ref[1 + at]
        span = pl.ds(pl.multiple_of(owner * rows, rows), rows)
        for block in range(blocks - 1):
            up_w_ref[span, block * WIDTH : (block + 1) * WIDTH] = one[block * rows : (block + 1) * rows, :]
        up_w_ref[span, (blocks - 1) * WIDTH :] = two[0:rows, :]
        out_w_ref[span, :] = two[rows : 2 * rows, :]
        down_w_ref[pl.ds(pl.multiple_of(owner * wide_rows, wide_rows), wide_rows), :] = two[2 * rows :, :]

    out_bias, gain, shift, down_bias = (vec_ref[4 + at : 5 + at, :] for at in range(4))
    attended = attended_ref[...]
    middle = x_ref[...].astype(f32) + dot_nn(attended, out_w_ref[...]) + out_bias
    scaled, inverse = norm_rows(middle)
    normed = (scaled * gain + shift).astype(bf16)
    cot = cot_ref[...]
    wide = cot.astype(f32)
    lowered = jnp.zeros_like(middle)
    grad_normed = jnp.zeros_like(middle)
    for block in range(blocks):
        columns = slice(block * WIDTH, (block + 1) * WIDTH)
        down = down_w_ref[columns, :]
        pre = dot_nn(normed, up_w_ref[:, columns]) + up_bias_ref[:, columns]
        phi, bell = normal_parts(pre)
        hidden = (pre * phi).astype(bf16)
        lowered += dot_nn(hidden, down)
        grad_pre = (dot_nt(cot, down) * (phi + pre * bell)).astype(bf16)
        up_bias_grad_ref[:, columns] = column_sum(grad_pre.astype(f32))
        grad_normed += dot_nt(grad_pre, up_w_ref[:, columns])
        down_acc[columns, :] = dot_tn(hidden, cot)
        up_acc[:, columns] = dot_tn(normed, grad_pre)
    y_ref[...] = (middle + lowered + down_bias).astype(bf16)
    grad_middle = wide + norm_back(grad_normed, scaled, inverse, gain)
    grad_middle_ref[...] = grad_middle
    grad_proj = grad_middle.astype(bf16)
    grad_attended_ref[...] = dot_nt(grad_proj, out_w_ref[...]).astype(bf16)
    out_acc[...] = dot_tn(attended, grad_proj)
    vec_grad_ref[0:1, :] = column_sum(grad_proj.astype(f32))
    vec_grad_ref[1:2, :] = column_sum(grad_normed * scaled)
    vec_grad_ref[2:3, :] = column_sum(grad_normed)
    vec_grad_ref[3:4, :] = column_sum(wide)

    extra = keep_ref.shape[1] - wide_rows - (blocks + 1) * rows
    row_at = lax.broadcasted_iota(jnp.int32, (extra, 1), 0)
    low_bit = meta_ref[1] & 1

    def put(high, at, count, source):
        mine, other = choose(low_bit, source(2 * high), source(2 * high + 1))
        keep_ref[high, at : at + count, :] = mine.astype(bf16)
        send_ref[high, at : at + count, :] = other.astype(bf16)

    def small(owner):
        first = [vec_grad_ref[i : i + 1, owner * rows : (owner + 1) * rows] for i in range(4)]
        second = up_bias_grad_ref[:, owner * wide_rows : (owner + 1) * wide_rows]
        return jnp.where(row_at == 0, jnp.concatenate(first, axis=1), jnp.where(row_at == 1, second, 0.0))

    for high in range(owners // 2):
        put(high, 0, wide_rows, lambda owner: down_acc[owner * wide_rows : (owner + 1) * wide_rows, :])
        at = wide_rows
        for block in range(blocks):
            columns = slice(block * WIDTH, (block + 1) * WIDTH)
            put(high, at, rows, lambda owner: up_acc[owner * rows : (owner + 1) * rows, columns])
            at += rows
        put(high, at, rows, lambda owner: out_acc[owner * rows : (owner + 1) * rows, :])
        put(high, at + rows, extra, small)


def feed_call(hidden_width, devices, meta, x, attended, cot, vectors, up_bias, ones, twos):
    rows, owners = x.shape[0], len(ones)
    chain = chain_rows(2 * (hidden_width // owners) + WIDTH // owners, devices)
    split = jax.ShapeDtypeStruct((owners // 2, chain, WIDTH), bf16)
    return pl.pallas_call(
        partial(feed_kernel, hidden_width, owners),
        out_shape=[
            jax.ShapeDtypeStruct((rows, WIDTH), bf16),
            jax.ShapeDtypeStruct((rows, WIDTH), f32),
            jax.ShapeDtypeStruct((rows, WIDTH), bf16),
            split,
            split,
        ],
        in_specs=[pl.BlockSpec(memory_space=pltpu.SMEM)] + vmem_specs(5 + 2 * owners),
        out_specs=vmem_specs(5),
        scratch_shapes=[
            pltpu.VMEM((hidden_width, WIDTH), bf16),
            pltpu.VMEM((WIDTH, hidden_width), bf16),
            pltpu.VMEM((WIDTH, WIDTH), bf16),
            pltpu.VMEM((8, WIDTH), f32),
            pltpu.VMEM((1, hidden_width), f32),
            pltpu.VMEM((hidden_width, WIDTH), f32),
            pltpu.VMEM((WIDTH, hidden_width), f32),
            pltpu.VMEM((WIDTH, WIDTH), f32),
        ],
        compiler_params=pltpu.CompilerParams(vmem_limit_bytes=46 << 20),
        cost_estimate=pl.CostEstimate(flops=32 << 30, bytes_accessed=20 << 20, transcendentals=4 << 20),
        name="feed_forward",
    )(meta, x, attended, cot, vectors, up_bias, *ones, *twos)


def input_grad_kernel(
    rows,
    x_ref,
    dq_ref,
    local_ref,
    grad_middle_ref,
    from_right_ref,
    from_left_ref,
    far_keep_ref,
    far_got_ref,
    w_ref,
    vec_ref,
    out_ref,
    got_ref,
):
    step = pl.program_id(0)
    tile = x_ref.shape[0]
    edge = BLOCK * LOCAL

    @pl.when(step == 0)
    def _():
        folded = far_keep_ref[...].astype(f32) + far_got_ref[...].astype(f32)
        high, low = two_parts(jnp.concatenate([folded[:8], folded[8:]], axis=1))
        got_ref[0:edge, :] = from_left_ref[...]
        got_ref[edge : 2 * edge, :] = from_right_ref[...]
        far = jnp.concatenate([high.astype(f32), low.astype(f32)], axis=0).astype(bf16)
        got_ref[2 * edge : 2 * edge + BLOCK, :] = far
        got_ref[2 * edge + BLOCK :, :] = jnp.zeros((BLOCK, 2 * WIDTH), bf16)

    shape = (1, got_ref.shape[0])
    column = lax.broadcasted_iota(jnp.int32, shape, 1)
    within = jnp.where(column < edge, column, column - edge)
    level = jnp.where(column < 2 * edge, within >> 4, LOCAL)
    last = jnp.where((column >= edge) & (column < 2 * edge), (rows >> level) - BLOCK, 0)
    entry = jnp.where(column < 2 * edge, last + (within & 15), (column - 2 * edge) & 7)
    entry = jnp.where(column < 2 * edge + BLOCK, entry, -1)
    scale = 1.0 / (1 << level).astype(f32)
    token = step * tile + lax.broadcasted_iota(jnp.int32, (tile, shape[1]), 0)
    member = jnp.where((token >> level) == entry, scale, 0.0).astype(bf16)

    scaled, inverse = norm_rows(x_ref[...].astype(f32))
    dkv = (local_ref[...].astype(f32) + dot_nn(member, got_ref[...])).astype(bf16)
    grad = dot_nt(dq_ref[...], w_ref[:, :WIDTH]) + dot_nt(dkv, w_ref[:, WIDTH:])
    out_ref[...] = grad_middle_ref[...] + norm_back(grad, scaled, inverse, vec_ref[0:1, :])


def input_grad_call(x, dq, local, grad_middle, from_right, from_left, far_keep, far_got, weight, vectors):
    rows = x.shape[0]
    tile = 512
    tiled = lambda width: pl.BlockSpec((tile, width), lambda i: (i, 0))
    return pl.pallas_call(
        partial(input_grad_kernel, rows),
        grid=(rows // tile,),
        out_shape=jax.ShapeDtypeStruct((rows, WIDTH), f32),
        in_specs=[tiled(WIDTH), tiled(WIDTH), tiled(2 * WIDTH), tiled(WIDTH)] + vmem_specs(6),
        out_specs=tiled(WIDTH),
        scratch_shapes=[pltpu.VMEM((2 * BLOCK * (LOCAL + 1), 2 * WIDTH), bf16)],
        compiler_params=pltpu.CompilerParams(vmem_limit_bytes=24 << 20),
        cost_estimate=pl.CostEstimate(flops=6 << 30, bytes_accessed=12 << 20, transcendentals=0),
        name="input_grad",
    )(x, dq, local, grad_middle, from_right, from_left, far_keep, far_got, weight, vectors)


def shifted(block, axis, distance):
    devices = range(lax.axis_size(axis))
    route = [(i - distance, i) for i in devices if i - distance in devices]
    return lax.ppermute(block, axis, route)


def swap(block, axis, bit):
    return lax.ppermute(block, axis, [(i, i ^ bit) for i in range(lax.axis_size(axis))])


def gather_step(part, axis, bit):
    mine = (lax.axis_index(axis) // bit) % 2
    other = swap(part, axis, bit)
    first = jnp.where(mine == 0, part, other)
    second = jnp.where(mine == 0, other, part)
    return jnp.stack([first, second], axis=-3)


def together(*values):
    return lax.optimization_barrier(values)


def bits_of(axis):
    size = lax.axis_size(axis)
    return [1 << at for at in range(size.bit_length() - 1)]


def step_call(name, function, meta, arrays, shapes, dtype=bf16):
    def kernel(meta_ref, *refs):
        values = [ref[...].astype(f32) for ref in refs[: len(arrays)]]
        for ref, value in zip(refs[len(arrays) :], function(meta_ref[0], meta_ref[1], *values), strict=True):
            ref[...] = value.astype(dtype)

    size = sum(math.prod(a.shape) for a in arrays)
    return pl.pallas_call(
        kernel,
        out_shape=[jax.ShapeDtypeStruct(shape, dtype) for shape in shapes],
        in_specs=[pl.BlockSpec(memory_space=pltpu.SMEM)] + vmem_specs(len(arrays)),
        out_specs=vmem_specs(len(shapes)),
        compiler_params=pltpu.CompilerParams(vmem_limit_bytes=(4 << 20) + 16 * size),
        cost_estimate=pl.CostEstimate(flops=1 << 20, bytes_accessed=4 * size, transcendentals=0),
        name=name,
    )(meta, *arrays)


def halves(values, axis=0):
    return jnp.split(values, 2, axis=axis)


class Reduction:
    def __init__(self, meta, keep, send, far=None):
        self.meta, self.rows, self.far = meta, keep.shape[1], far
        self.bits = bits_of("ctx")[1:]
        self.keep, self.got = keep, [swap(send, "fsdp", 1)]

    def call(self, name, function, arrays, *shapes):
        return step_call(name, function, self.meta, arrays, [(*shape, WIDTH) for shape in shapes])

    def cross(self):
        far = [self.far[1]] if self.far else []
        extra = far[0].shape[0] if far else 0
        half = self.rows // 2

        def function(here, owner, keep, got, *far):
            mine, other = choose(owner >> 1, *(keep + got))
            keep, near = choose(here & 1, *halves(mine))
            high, both = choose(here & 1, *halves(other))
            return keep, jnp.concatenate([near, *far], axis=0), high, both

        shapes = [(half,), (half + extra,), (half,), (half,)]
        self.keep, near, high, both = self.call("cross", function, [self.keep, *self.got, *far], *shapes)
        count = lax.axis_size("fsdp")
        route = [(i, i ^ count ^ 2) for i in range(count * lax.axis_size("ctx"))]
        self.got = [swap(near, "ctx", 1), swap(high, "fsdp", 2), lax.ppermute(both, ("ctx", "fsdp"), route)]

    def scatter(self, at):
        bit, last = self.bits[at], at == len(self.bits) - 1
        rows = self.keep.shape[0]
        far = [self.far[0]] if self.far else []
        extra = far[0].shape[0] // 2 if far else 0

        def function(here, owner, keep, *got):
            far_keep = got[-1]
            got = got[: len(got) - len(far)]
            total = keep + got[0][:rows]
            for other in got[1:]:
                total = total + other
            flag = (here // bit) & 1
            keep, send = (total, total) if last else choose(flag, *halves(total))
            if not far:
                return [keep] if last else [keep, send]
            far_keep, far_send = choose_groups(flag, far_keep + got[0][rows:])
            return keep, jnp.concatenate([send, far_send], axis=0), far_keep

        count = rows if last else rows // 2
        shapes = [(count,)] if last and not far else [(count,), (count + extra,)]
        out = self.call("scatter", function, [self.keep, *self.got, *far], *shapes, *([(extra,)] if far else []))
        self.keep, send = out[0], out[1] if len(out) > 1 else out[0]
        self.got = [swap(send, "ctx", bit)]
        if far:
            self.far = (out[2], None)


    def order(self):
        high = list(reversed(self.bits[:-1]))
        return list(zip(high + [1], [1] + high))

    def collect(self):
        rows = self.keep.shape[0]
        if self.far:
            self.far = (self.far[0], self.got[0][rows:])
        function = lambda here, owner, keep, got: halves(keep + got[:rows])
        self.send_gather(0, self.call("collect", function, [self.keep, *self.got], (rows // 2,), (rows // 2,)))

    def send_gather(self, at, keep):
        self.keep = keep
        self.got = [swap(part, "ctx", bit) for part, bit in zip(keep, self.order()[at])]

    def gather(self, at):
        bits = self.order()[at]
        rows = 2 * self.keep[0].shape[0]
        function = lambda here, owner, *arrays: self.paired(here, bits, *arrays)
        self.send_gather(at + 1, self.call("gather", function, [*self.keep, *self.got], (rows,), (rows,)))

    def paired(self, here, bits, keep_one, keep_two, got_one, got_two):
        one = jnp.concatenate(choose((here // bits[0]) & 1, keep_one, got_one), axis=0)
        two = jnp.concatenate(choose((here // bits[1]) & 1, keep_two, got_two), axis=0)
        return one, two

    def scatters(self):
        return [self.cross] + [partial(self.scatter, at) for at in range(len(self.bits))]

    def gathers(self):
        return [self.collect] + [partial(self.gather, at) for at in range(len(self.order()) - 1)]

    def finish(self, shapes, unpack):
        bits = self.order()[-1]
        outer = lax.axis_size("ctx") // 4
        rows = self.rows // (4 * outer)

        def function(here, owner, *arrays):
            one, two = self.paired(here, bits, *arrays)
            parts = []
            for low in range(2):
                for high in range(outer):
                    a, b = low * outer + high, 2 * high + low
                    parts += [one[a * rows : (a + 1) * rows], two[b * rows : (b + 1) * rows]]
            return unpack(jnp.concatenate(parts, axis=0))

        return step_call("finish", function, self.meta, [*self.keep, *self.got], shapes, f32)


def shards(
    layer_input,
    doc_lengths,
    ln1_gain,
    ln1_bias,
    qkv_weight,
    query_bias,
    value_bias,
    out_weight,
    out_bias,
    ln2_gain,
    ln2_bias,
    up_weight,
    up_bias,
    down_weight,
    down_bias,
    cotangent,
):
    owners = lax.axis_size("fsdp")
    devices = lax.axis_size("ctx")
    x, cot = layer_input[0], cotangent[0]
    rows = x.shape[0]
    total = rows * devices
    far = far_levels(total)
    here, owner = lax.axis_index("ctx"), lax.axis_index("fsdp")
    part = WIDTH // owners
    hidden_width = up_weight.shape[1]
    meta = jnp.stack([here] + [owner ^ at for at in range(owners)]).astype(jnp.int32)

    vectors = [ln1_gain, ln1_bias, query_bias, value_bias, out_bias, ln2_gain, ln2_bias, down_bias, up_bias]
    across, beside = swap(qkv_weight, "fsdp", 2), swap(qkv_weight, "fsdp", 1)
    small = pack_call(vectors)
    small_across, small_beside = swap(small, "fsdp", 2), swap(small, "fsdp", 1)
    one, two = pack_rest_call(down_weight, up_weight, out_weight)
    bias = mask_call(rows, total, far, meta, doc_lengths)
    across, beside, small_across, small_beside, one, two, bias = together(
        across, beside, small_across, small_beside, one, two, bias
    )
    pieces = [qkv_weight, beside, across, swap(across, "fsdp", 1)]
    smalls = [small, small_beside, small_across, swap(small_across, "fsdp", 1)]
    one_across = swap(one, "fsdp", 2)
    qkv_full, vec, up_shift, queries, kv, scaled, tail, head, base = qkv_call(
        rows, hidden_width, meta, x, pieces, smalls, [bias, two]
    )
    vec, tail, head, base, one_across = together(vec, tail, head, base, one_across)

    one_beside, one_both = swap(one, "fsdp", 1), swap(one_across, "fsdp", 1)
    two_across = swap(two, "fsdp", 2)
    left = shifted(tail, "ctx", 1)
    right = shifted(head, "ctx", -1)
    for bit in reversed(bits_of("ctx")):
        base = gather_step(base, "ctx", bit)
        if bit == 1:
            base, left, right, one_beside, one_both, two_across = together(
                base, left, right, one_beside, one_both, two_across
            )
    base = base.reshape(-1, ENTRY)
    two_beside, two_both = swap(two, "fsdp", 1), swap(two_across, "fsdp", 1)
    attended, exps, inverses = attend_call(rows, devices, far, meta, queries, bias, kv, left, right, base)
    inverses, two_beside, two_both = together(inverses, two_beside, two_both)
    output, grad_middle, grad_attended, keep, send = feed_call(
        hidden_width,
        devices,
        meta,
        x,
        attended,
        cot,
        vec,
        up_shift,
        [one, one_beside, one_across, one_both],
        [two, two_beside, two_across, two_both],
    )
    feed = Reduction(meta, keep, send)
    feed.cross()
    made = attend_back_call(
        rows, devices, far, owners, meta, queries, grad_attended, exps, inverses, kv, scaled, left, right, base, qkv_full, vec
    )
    dq, local, to_left, to_right, far_keep, far_send, keep, send = made
    to_left, to_right, far_keep, far_send, send, *feed.got = together(
        to_left, to_right, far_keep, far_send, send, *feed.got
    )
    first = Reduction(meta, keep, send, (far_keep, far_send))
    back_right = shifted(to_left, "ctx", -1)
    back_left = shifted(to_right, "ctx", 1)
    pending = feed.scatters()[1:]
    pending.pop(0)()
    first.cross()
    tied = together(*first.got, *feed.got)
    first.got, feed.got = list(tied[: len(first.got)]), list(tied[len(first.got) :])
    for one in first.scatters()[1:]:
        one()
        if pending:
            pending.pop(0)()
    tied = together(*first.got, back_right, back_left)
    first.got, (back_right, back_left) = list(tied[:1]), tied[1:]
    for one, two in zip(first.gathers(), feed.gathers()):
        one()
        two()
    input_grad = input_grad_call(
        x, dq, local, grad_middle, back_right, back_left, *first.far, qkv_full, vec
    )

    wide_rows = hidden_width // owners

    def split(row):
        return [row[:, at * part : (at + 1) * part] for at in range(row.shape[1] // part)]

    def unpack_first(total):
        blocks = [total[at * part : (at + 1) * part] for at in range(3)]
        return [jnp.concatenate(blocks, axis=1), *split(total[3 * part : 3 * part + 1])]

    def unpack_feed(total):
        at = wide_rows
        blocks = []
        for _ in range(hidden_width // WIDTH):
            blocks.append(total[at : at + part])
            at += part
        vectors = [*split(total[at + part : at + part + 1]), total[at + part + 1 : at + part + 2]]
        return [total[:wide_rows], jnp.concatenate(blocks, axis=1), total[at : at + part], *vectors]

    vector = (1, part)
    qkv_grad, *firsts = first.finish([(part, 3 * WIDTH)] + [vector] * owners, unpack_first)
    down_grad, up_grad, out_grad, *feeds = feed.finish(
        [(wide_rows, WIDTH), (part, hidden_width), (part, WIDTH)] + [vector] * owners + [(1, wide_rows)], unpack_feed
    )
    gain_first, shift_first, query_grad, value_grad = (v.reshape(-1) for v in firsts)
    out_shift, gain_second, shift_second, down_shift, up_shift_grad = (v.reshape(-1) for v in feeds)
    return (
        output[None],
        input_grad[None],
        gain_first,
        shift_first,
        qkv_grad,
        query_grad,
        value_grad,
        out_grad,
        out_shift,
        gain_second,
        shift_second,
        up_grad,
        up_shift_grad,
        down_grad,
        down_shift,
    )


def solution(mesh):
    row, vector = P("fsdp", None), P("fsdp")
    tokens = P("fsdp", "ctx", None)
    return jax.shard_map(
        shards,
        mesh=mesh,
        in_specs=(
            tokens,
            row,
            vector,
            vector,
            row,
            vector,
            vector,
            row,
            vector,
            vector,
            vector,
            row,
            vector,
            row,
            vector,
            tokens,
        ),
        out_specs=(
            tokens,
            tokens,
            vector,
            vector,
            row,
            vector,
            vector,
            row,
            vector,
            vector,
            vector,
            row,
            vector,
            row,
            vector,
        ),
        check_vma=False,
    )
```

```python
from functools import partial
import math

import jax
import jax.numpy as jnp
from jax import lax
from jax.experimental import pallas as pl
from jax.experimental.pallas import tpu as pltpu
from jax.sharding import PartitionSpec as P

HEADS = 8
BLOCK = 16
LEVELS = 10
NEAR = 3
LOCAL = 7
CHUNK = 64
STEP = 4
WIDTH = 512
GROUP = 4
GROUPS = HEADS // GROUP
LANES = WIDTH // GROUPS
ENTRY = 3 * WIDTH
SMALL = 16
MASKED = -1e30
EPSILON = 1e-05

f32 = jnp.float32
bf16 = jnp.bfloat16


def level_rows(rows, level):
    return rows // 2**level


def level_offsets(rows):
    offsets = [0]
    for level in range(LOCAL):
        offsets.append(offsets[-1] + level_rows(rows, level))
    return offsets[:-1], offsets[-1]


def far_levels(total):
    return [l for l in range(LOCAL, LEVELS) if total // (BLOCK * 2**l) >= 2]


def extended_offsets(rows, far):
    offsets, cursor = [], 0
    for level in range(LOCAL):
        offsets.append(cursor)
        cursor += level_rows(rows, level) + 2 * BLOCK
    for _ in far:
        offsets.append(cursor)
        cursor += 2 * BLOCK
    return offsets, cursor


def slot_layout(far):
    parts = [(level, CHUNK // 2**level + 2 * BLOCK) for level in range(NEAR)]
    parts += [(level, BLOCK) for level in list(range(NEAR, LOCAL)) + far for _ in range(2)]
    return parts, sum(count for _, count in parts)


def slot_sources(rows, far, chunk):
    offsets, _ = extended_offsets(rows, far)
    sources = []
    for level in range(NEAR):
        sources.append((offsets[level] + chunk * (CHUNK // 2**level), CHUNK // 2**level + 2 * BLOCK))
    for level in range(NEAR, LOCAL):
        block = chunk // (BLOCK * 2**level // CHUNK)
        sources.append((offsets[level] + block * BLOCK, BLOCK))
        sources.append((offsets[level] + block * BLOCK + 2 * BLOCK, BLOCK))
    for at in range(len(far)):
        sources.append((offsets[LOCAL + at], BLOCK))
        sources.append((offsets[LOCAL + at] + BLOCK, BLOCK))
    return sources


def mask_kernel(rows, total, far, here_ref, lengths_ref, bias_ref):
    for sub in range(STEP):
        base = here_ref[0] * rows + (pl.program_id(0) * STEP + sub) * CHUNK
        query = base + (lax.broadcasted_iota(jnp.int32, (1, 128), 1) & (CHUNK - 1))
        first_token = jnp.zeros((1, 128), jnp.int32)
        end_token = jnp.full((1, 128), total, jnp.int32)
        start = jnp.int32(0)
        for at in range(lengths_ref.shape[1]):
            first_token = jnp.where(start <= query, start, first_token)
            start = start + lengths_ref[0, at]
            end_token = jnp.where(start > query, jnp.minimum(end_token, start), end_token)

        def part(at, count, first_row, level):
            span = 2**level
            shift = level + 4
            first = first_row + span * lax.broadcasted_iota(jnp.int32, (count, 128), 0)
            gap = jnp.abs((first >> shift) - (query >> shift))
            if level == 0:
                seen = gap <= 1
            else:
                seen = (gap == 1) & (jnp.abs((first >> (shift - 1)) - (query >> (shift - 1))) > 1)
            seen = seen & (first >= first_token) & (first + (span - 1) < end_token)
            bias_ref[sub, at : at + count, :] = jnp.where(seen, level * math.log(2.0), MASKED)

        at = 0
        for level in range(NEAR):
            count = CHUNK // 2**level + 2 * BLOCK
            part(at, count, base - BLOCK * 2**level, level)
            at += count
        for level in list(range(NEAR, LOCAL)) + far:
            block = base >> (level + 4)
            for side in (-1, 1):
                part(at, BLOCK, (block + side) * (BLOCK * 2**level), level)
                at += BLOCK


def mask_call(rows, total, far, meta, lengths):
    chunks = rows // CHUNK
    _, slots = slot_layout(far)
    return pl.pallas_call(
        partial(mask_kernel, rows, total, far),
        grid=(chunks // STEP,),
        out_shape=jax.ShapeDtypeStruct((chunks, slots, 128), f32),
        in_specs=[pl.BlockSpec(memory_space=pltpu.SMEM)] * 2,
        out_specs=pl.BlockSpec((STEP, slots, 128), lambda i: (i, 0, 0)),
        compiler_params=pltpu.CompilerParams(vmem_limit_bytes=8 << 20),
        cost_estimate=pl.CostEstimate(flops=4 << 30, bytes_accessed=3 << 20, transcendentals=0),
        name="mask",
    )(meta, lengths)


def dot_nt(left, right):
    return lax.dot_general(left, right, (((1,), (1,)), ((), ())), preferred_element_type=f32)


def dot_tn(left, right):
    return lax.dot_general(left, right, (((0,), (0,)), ((), ())), preferred_element_type=f32)


def dot_nn(left, right):
    return jnp.dot(left, right, preferred_element_type=f32)


def pool_matrix(count):
    row = lax.broadcasted_iota(jnp.int32, (count // 2, count), 0)
    column = lax.broadcasted_iota(jnp.int32, (count // 2, count), 1)
    return jnp.where((column >> 1) == row, 0.5, 0.0).astype(bf16)


def spread_matrix(count):
    row = lax.broadcasted_iota(jnp.int32, (2 * count, count), 0)
    column = lax.broadcasted_iota(jnp.int32, (2 * count, count), 1)
    return jnp.where((row >> 1) == column, 0.5, 0.0).astype(bf16)


def spread(values):
    count = values.shape[0]
    tile = min(count, 128)
    matrix = spread_matrix(tile)
    high = values.astype(bf16)
    low = (values - high.astype(f32)).astype(bf16)
    parts = [
        dot_nn(matrix, high[at : at + tile]) + dot_nn(matrix, low[at : at + tile])
        for at in range(0, count, tile)
    ]
    return parts[0] if len(parts) == 1 else jnp.concatenate(parts, axis=0)


def norm_rows(values):
    mean = jnp.mean(values, axis=-1, keepdims=True)
    centred = values - mean
    variance = jnp.mean(centred * centred, axis=-1, keepdims=True)
    inverse = lax.rsqrt(variance + EPSILON)
    return centred * inverse, inverse


def norm_back(grad_out, scaled, inverse, gain):
    grad_scaled = grad_out * gain
    first = jnp.mean(grad_scaled, axis=-1, keepdims=True)
    second = jnp.mean(grad_scaled * scaled, axis=-1, keepdims=True)
    return inverse * (grad_scaled - first - scaled * second)


def head_of(shape):
    return lax.broadcasted_iota(jnp.int32, shape, 1) // (WIDTH // HEADS)


def split_heads(group):
    head, zero = head_of(group.shape), jnp.zeros_like(group)
    return jnp.concatenate([jnp.where(head == at, group, zero) for at in range(GROUP)], axis=0)


def join_heads(stacked):
    rows = stacked.shape[0] // GROUP
    head = head_of((rows, stacked.shape[1]))
    out = stacked[:rows]
    for at in range(1, GROUP):
        out = jnp.where(head == at, stacked[at * rows : (at + 1) * rows], out)
    return out


def pack_kernel(*refs):
    out_ref = refs[-1]
    row = jnp.concatenate([ref[...].reshape(1, -1) for ref in refs[:-2]], axis=1)
    out_ref[...] = jnp.broadcast_to(row.astype(f32), out_ref.shape).astype(bf16)


def pack_call(vectors, earlier):
    return pl.pallas_call(
        pack_kernel,
        out_shape=jax.ShapeDtypeStruct((SMALL, sum(v.shape[0] for v in vectors)), bf16),
        in_specs=vmem_specs(len(vectors)) + [pl.BlockSpec(memory_space=pl.ANY)],
        out_specs=vmem_specs(1)[0],
        compiler_params=pltpu.CompilerParams(vmem_limit_bytes=56 << 20),
        name="pack",
    )(*vectors, earlier)


def pack_rest_kernel(down_ref, up_ref, out_w_ref, one_ref, two_ref):
    rows = up_ref.shape[0]
    blocks = up_ref.shape[1] // WIDTH
    for block in range(blocks - 1):
        one_ref[block * rows : (block + 1) * rows, :] = up_ref[:, block * WIDTH : (block + 1) * WIDTH]
    two_ref[0:rows, :] = up_ref[:, (blocks - 1) * WIDTH :]
    two_ref[rows : 2 * rows, :] = out_w_ref[...]
    two_ref[2 * rows :, :] = down_ref[...]


def pack_rest_call(down, up, out_w):
    rows, blocks = up.shape[0], up.shape[1] // WIDTH
    return pl.pallas_call(
        pack_rest_kernel,
        out_shape=[
            jax.ShapeDtypeStruct(((blocks - 1) * rows, WIDTH), bf16),
            jax.ShapeDtypeStruct((2 * rows + down.shape[0], WIDTH), bf16),
        ],
        in_specs=vmem_specs(3),
        out_specs=vmem_specs(2),
        compiler_params=pltpu.CompilerParams(vmem_limit_bytes=56 << 20),
        name="pack_rest",
    )(down, up, out_w)


def vmem_specs(count):
    return [pl.BlockSpec(memory_space=pltpu.VMEM)] * count


def qkv_kernel(rows, owners, meta_ref, x_ref, *refs):
    shard_refs, small_refs, refs = refs[:owners], refs[owners : 2 * owners], refs[2 * owners + 2 :]
    w_ref, vec_ref, up_bias_ref, q_ref = refs[:4]
    kv_ref, scaled_ref, tail_ref, head_ref, top_ref, keep_ref = refs[4:]
    places, _ = level_offsets(rows)
    part = WIDTH // owners
    step = pl.program_id(0)

    @pl.when(step == 0)
    def _():
        for at, (ref, small_ref) in enumerate(zip(shard_refs, small_refs)):
            owner = meta_ref[1 + at]
            w_ref[pl.ds(pl.multiple_of(owner * part, part), part), :] = ref[...]
            row = small_ref[0:1, :].astype(f32)
            for vector in range(8):
                vec_ref[vector : vector + 1, pl.ds(pl.multiple_of(owner * part, part), part)] = row[
                    :, vector * part : (vector + 1) * part
                ]
            wide = row.shape[1] - 8 * part
            up_bias_ref[:, pl.ds(pl.multiple_of(owner * wide, wide), wide)] = row[:, 8 * part :]

    tile = x_ref.shape[0]
    scaled, _ = norm_rows(x_ref[...].astype(f32))
    normed = (scaled * vec_ref[0:1, :] + vec_ref[1:2, :]).astype(bf16)
    queries = (dot_nn(normed, w_ref[:, :WIDTH]) + vec_ref[2:3, :]).astype(bf16)
    q_ref[...] = queries * jnp.asarray(0.125, bf16)
    keys = dot_nn(normed, w_ref[:, WIDTH : 2 * WIDTH]).astype(bf16)
    values = (dot_nn(normed, w_ref[:, 2 * WIDTH :]) + vec_ref[3:4, :]).astype(bf16)
    current = jnp.concatenate([keys, values, scaled.astype(bf16)], axis=1)

    def edges(level, block):
        @pl.when(step == 0)
        def _():
            head_ref[BLOCK * level : BLOCK * (level + 1), :] = block[:BLOCK]

        @pl.when(step == pl.num_programs(0) - 1)
        def _():
            tail_ref[BLOCK * level : BLOCK * (level + 1), :] = block[block.shape[0] - BLOCK :]

    for level in range(5):
        if level:
            current = dot_nn(pool_matrix(current.shape[0]), current).astype(bf16)
        count = tile // 2**level
        span = pl.ds(pl.multiple_of(places[level] + step * count, count), count)
        kv_ref[span, :] = current[:, : 2 * WIDTH]
        scaled_ref[span, :] = current[:, 2 * WIDTH :]
        edges(level, current)
    keep_ref[pl.ds(pl.multiple_of(step * count, count), count), :] = current

    @pl.when(step == pl.num_programs(0) - 1)
    def _():
        current = keep_ref[...]
        for level in range(5, LOCAL):
            current = dot_nn(pool_matrix(current.shape[0]), current).astype(bf16)
            span = slice(places[level], places[level] + current.shape[0])
            kv_ref[span, :] = current[:, : 2 * WIDTH]
            scaled_ref[span, :] = current[:, 2 * WIDTH :]
            tail_ref[BLOCK * level : BLOCK * (level + 1), :] = current[current.shape[0] - BLOCK :]
            head_ref[BLOCK * level : BLOCK * (level + 1), :] = current[:BLOCK]
        top_ref[...] = dot_nn(pool_matrix(BLOCK), current).astype(bf16)


def qkv_call(rows, hidden_width, meta, x, pieces, smalls, earlier):
    owners = len(pieces)
    tile = 512

    def tiled(count, width):
        return pl.BlockSpec((count, width), lambda i: (i, 0))

    _, entries = level_offsets(rows)
    edge = jax.ShapeDtypeStruct((BLOCK * LOCAL, ENTRY), bf16)
    outs = pl.pallas_call(
        partial(qkv_kernel, rows, owners),
        grid=(rows // tile,),
        out_shape=[
            jax.ShapeDtypeStruct((WIDTH, 3 * WIDTH), bf16),
            jax.ShapeDtypeStruct((8, WIDTH), f32),
            jax.ShapeDtypeStruct((1, hidden_width), f32),
            jax.ShapeDtypeStruct((rows, WIDTH), bf16),
        ]
        + [jax.ShapeDtypeStruct((entries, 2 * WIDTH), bf16), jax.ShapeDtypeStruct((entries, WIDTH), bf16)]
        + [edge, edge, jax.ShapeDtypeStruct((BLOCK // 2, ENTRY), bf16)],
        in_specs=[pl.BlockSpec(memory_space=pltpu.SMEM), tiled(tile, WIDTH)]
        + vmem_specs(2 * owners)
        + [pl.BlockSpec(memory_space=pl.ANY)] * 2,
        out_specs=vmem_specs(3) + [tiled(tile, WIDTH)] + vmem_specs(5),
        scratch_shapes=[pltpu.VMEM((level_rows(rows, 4), ENTRY), bf16)],
        compiler_params=pltpu.CompilerParams(vmem_limit_bytes=56 << 20),
        cost_estimate=pl.CostEstimate(flops=9 << 30, bytes_accessed=12 << 20, transcendentals=0),
        name="qkv_levels",
    )(meta, x, *pieces, *smalls, *earlier)
    return outs


def far_level(entries):
    return dot_nn(pool_matrix(entries.shape[0]), entries).astype(bf16)


def assemble(rows, far, here, columns, own_ref, left_ref, right_ref, base_ref, ext_ref, far_ref):
    offsets, _ = extended_offsets(rows, far)
    places, _ = level_offsets(rows)
    for inner, outer, target, width in columns:
        lanes, edge_lanes = slice(target, target + width), slice(outer, outer + width)
        for level in range(LOCAL):
            at, count = offsets[level], level_rows(rows, level)
            edge = slice(BLOCK * level, BLOCK * (level + 1))
            ext_ref[at : at + BLOCK, lanes] = left_ref[edge, edge_lanes]
            ext_ref[at + BLOCK : at + BLOCK + count, lanes] = own_ref[
                places[level] : places[level] + count, inner : inner + width
            ]
            ext_ref[at + BLOCK + count : at + 2 * BLOCK + count, lanes] = right_ref[edge, edge_lanes]
        current = base_ref[:, edge_lanes]
        for index, level in enumerate(far):
            if index:
                current = far_level(current)
            count = current.shape[0]
            far_ref[0:count, 0:width] = current
            for side, start in enumerate(far_starts(here, level, count)):
                at = offsets[LOCAL + index] + side * BLOCK
                ext_ref[at : at + BLOCK, lanes] = far_ref[pl.ds(start, BLOCK), 0:width]


def far_starts(here, level, count):
    block = here >> (level - 6)
    last = count // BLOCK - 1
    return [pl.multiple_of(jnp.clip(at, 0, last) * BLOCK, BLOCK) for at in (block - 1, block + 1)]


def load_slots(rows, far, chunk, ext_ref, slots_ref):
    at = 0
    for start, count in slot_sources(rows, far, chunk):
        if not isinstance(start, int):
            start = pl.multiple_of(start, BLOCK)
        slots_ref[at : at + count, :] = ext_ref[pl.ds(start, count), :]
        at += count


def attend_kernel(rows, far, meta_ref, q_ref, bias_ref, *refs):
    own_ref, left_ref, right_ref, base_ref, out_ref, exp_ref, inverse_ref, ext_ref, far_ref, slots_ref = refs
    step = pl.program_id(0)

    @pl.when(step == 0)
    def _():
        columns = [(0, 0, 0, 2 * WIDTH)]
        assemble(rows, far, meta_ref[0], columns, own_ref, left_ref, right_ref, base_ref, ext_ref, far_ref)

    ones = jnp.ones((slots_ref.shape[0], 128), bf16)
    second_head = (head_of((CHUNK, 256)) & 1) == 1
    for sub in range(STEP):
        span = slice(sub * CHUNK, (sub + 1) * CHUNK)
        load_slots(rows, far, step * STEP + sub, ext_ref, slots_ref)
        bias = bias_ref[sub]
        bias = jnp.concatenate([bias, bias], axis=1)
        for group in range(GROUPS):
            lanes = slice(LANES * group, LANES * (group + 1))
            values = slots_ref[:, WIDTH + LANES * group : WIDTH + LANES * (group + 1)]
            scores = dot_nt(slots_ref[:, lanes], split_heads(q_ref[span, lanes])) + bias
            exponent = jnp.exp(scores - jnp.max(scores, axis=0, keepdims=True))
            low = exponent.astype(bf16)
            exp_ref[sub, group] = low
            inverse = 1.0 / jnp.sum(exponent, axis=0, keepdims=True)
            inverse_ref[sub, group : group + 1, :] = inverse
            for half in range(LANES // 128):
                columns = slice(128 * half, 128 * (half + 1))
                both = dot_tn(low[:, columns], jnp.concatenate([values[:, columns], ones], axis=1))
                pair = jnp.where(second_head, both[CHUNK:], both[:CHUNK])
                at = LANES * group + 128 * half
                out_ref[span, at : at + 128] = (pair[:, :128] / pair[:, 128:]).astype(bf16)


def attend_call(rows, devices, far, meta, q, bias, kv, left, right, base):
    chunks = rows // CHUNK
    _, entries = extended_offsets(rows, far)
    _, slots = slot_layout(far)
    return pl.pallas_call(
        partial(attend_kernel, rows, far),
        grid=(chunks // STEP,),
        out_shape=[
            jax.ShapeDtypeStruct((rows, WIDTH), bf16),
            jax.ShapeDtypeStruct((chunks, GROUPS, slots, LANES), bf16),
            jax.ShapeDtypeStruct((chunks, 8, LANES), f32),
        ],
        in_specs=[
            pl.BlockSpec(memory_space=pltpu.SMEM),
            pl.BlockSpec((STEP * CHUNK, WIDTH), lambda i: (i, 0)),
            pl.BlockSpec((STEP, slots, 128), lambda i: (i, 0, 0)),
        ]
        + vmem_specs(4),
        out_specs=[
            pl.BlockSpec((STEP * CHUNK, WIDTH), lambda i: (i, 0)),
            pl.BlockSpec((STEP, GROUPS, slots, LANES), lambda i: (i, 0, 0, 0)),
            pl.BlockSpec((STEP, 8, LANES), lambda i: (i, 0, 0)),
        ],
        scratch_shapes=[
            pltpu.VMEM((entries, 2 * WIDTH), bf16),
            pltpu.VMEM((8 * devices, 2 * WIDTH), bf16),
            pltpu.VMEM((slots, 2 * WIDTH), bf16),
        ],
        compiler_params=pltpu.CompilerParams(vmem_limit_bytes=56 << 20),
        cost_estimate=pl.CostEstimate(flops=20 << 30, bytes_accessed=20 << 20, transcendentals=4 << 20),
        name="attend",
    )(meta, q, bias, kv, left, right, base)


def column_sum(values):
    return jnp.sum(values, axis=0, keepdims=True)


def matrix_row(left, right):
    total = None
    for a in two_parts(left):
        for b in two_parts(right):
            term = dot_nt(a, b)
            total = term if total is None else total + term
    return total[0:1]


def two_parts(values):
    if values.dtype == bf16:
        return [values]
    high = values.astype(bf16)
    return [high, (values - high.astype(f32)).astype(bf16)]


def choose(flag, zero, one):
    return jnp.where(flag == 0, zero, one), jnp.where(flag == 0, one, zero)


def choose_groups(flag, folded):
    groups = folded.reshape(-1, 2, 8, folded.shape[1])
    return [part.reshape(-1, folded.shape[1]) for part in choose(flag, groups[:, 0], groups[:, 1])]


def attend_back_kernel(rows, far, *refs):
    refs = list(refs)
    take = lambda count: [refs.pop(0) for _ in range(count)]
    meta_ref, q_ref, grad_ref, exp_ref, inverse_ref = take(5)
    own_ref, own_scaled_ref = take(2)
    left_ref, right_ref, base_ref, w_ref, vec_ref = take(5)
    dq_ref, local_ref, to_left_ref, to_right_ref, far_keep_ref, far_send_ref, keep_ref, send_ref = take(8)
    ext_ref, far_ref, slots_ref, acc_ref, tree_ref, scaled_ref, dq_keep_ref = take(7)
    step = pl.program_id(0)
    offsets, entries = extended_offsets(rows, far)

    @pl.when(step == 0)
    def _():
        common = (left_ref, right_ref, base_ref)
        assemble(rows, far, meta_ref[0], [(0, 0, 0, 2 * WIDTH)], own_ref, *common, ext_ref, far_ref)
        assemble(rows, far, meta_ref[0], [(0, 2 * WIDTH, 0, WIDTH)], own_scaled_ref, *common, scaled_ref, far_ref)
        acc_ref[...] = jnp.zeros_like(acc_ref)

    for sub in range(STEP):
        chunk = step * STEP + sub
        span = slice(sub * CHUNK, (sub + 1) * CHUNK)
        load_slots(rows, far, chunk, ext_ref, slots_ref)
        sources = slot_sources(rows, far, chunk)
        for group in range(GROUPS):
            lanes = slice(LANES * group, LANES * (group + 1))
            value_lanes = slice(WIDTH + LANES * group, WIDTH + LANES * (group + 1))
            keys, values = slots_ref[:, lanes], slots_ref[:, value_lanes]
            queries, grads = split_heads(q_ref[span, lanes]), split_heads(grad_ref[span, lanes])
            probs = exp_ref[sub, group].astype(f32) * inverse_ref[sub, group : group + 1, :]
            grad_probs = dot_nt(values, grads)
            delta = jnp.sum(probs * grad_probs, axis=0, keepdims=True)
            grad_scores = (probs * (grad_probs - delta)).astype(bf16)
            dq = (join_heads(dot_tn(grad_scores, keys)) * 0.125).astype(bf16)
            dq_ref[span, lanes] = dq
            dq_keep_ref[pl.ds(pl.multiple_of(chunk * CHUNK, CHUNK), CHUNK), lanes] = dq
            grad_keys = dot_nn(grad_scores, queries)
            grad_values = dot_nn(probs.astype(bf16), grads)
            at = 0
            for start, count in sources:
                if not isinstance(start, int):
                    start = pl.multiple_of(start, BLOCK)
                acc_ref[pl.ds(start, count), lanes] += grad_keys[at : at + count]
                acc_ref[pl.ds(start, count), value_lanes] += grad_values[at : at + count]
                at += count

    @pl.when(step == pl.num_programs(0) - 1)
    def _():
        dq = dq_keep_ref[...]
        sums = [column_sum(dq.astype(f32)), column_sum(acc_ref[:, :WIDTH]), column_sum(acc_ref[:, WIDTH:])]
        both = dot_tn(scaled_ref[...], acc_ref[...].astype(bf16))
        parts = [dot_tn(own_scaled_ref[0:rows, :], dq), both[:, :WIDTH], both[:, WIDTH:]]
        first_row = lax.broadcasted_iota(jnp.int32, (16, 1), 0) == 0
        ones = jnp.where(first_row, jnp.ones((16, WIDTH), f32), 0.0).astype(bf16)
        as_column = lambda row: dot_tn(jnp.where(first_row, row, 0.0).astype(bf16), ones)
        gain, shift = as_column(vec_ref[0:1, :]), as_column(vec_ref[1:2, :])
        gain_grad, shift_grad = jnp.zeros((1, WIDTH), f32), jnp.zeros((1, WIDTH), f32)
        owners = 2 * keep_ref.shape[0]
        part = WIDTH // owners
        low_bit = meta_ref[1] & 1
        for block in range(3):
            weight = w_ref[:, block * WIDTH : (block + 1) * WIDTH]
            gain_grad += matrix_row(jnp.ones((16, WIDTH), bf16), weight.astype(f32) * parts[block])
            shift_grad += matrix_row(jnp.broadcast_to(sums[block], (16, WIDTH)), weight)
            grad = gain * parts[block] + shift * sums[block]
            for high in range(owners // 2):
                at = 2 * high * part
                mine, other = choose(low_bit, grad[at : at + part], grad[at + part : at + 2 * part])
                keep_ref[high, block * part : (block + 1) * part, :] = mine.astype(bf16)
                send_ref[high, block * part : (block + 1) * part, :] = other.astype(bf16)
        extra = keep_ref.shape[1] - 3 * part
        top_row = lax.broadcasted_iota(jnp.int32, (extra, 1), 0) == 0
        vectors = [gain_grad, shift_grad, sums[0], sums[2]]
        owner_row = lambda owner: jnp.concatenate([v[:, owner * part : (owner + 1) * part] for v in vectors], axis=1)
        for high in range(owners // 2):
            mine, other = choose(low_bit, owner_row(2 * high), owner_row(2 * high + 1))
            keep_ref[high, 3 * part :, :] = jnp.where(top_row, mine, 0.0).astype(bf16)
            send_ref[high, 3 * part :, :] = jnp.where(top_row, other, 0.0).astype(bf16)

        for level in range(LOCAL):
            at, count = offsets[level], level_rows(rows, level)
            edge = slice(BLOCK * level, BLOCK * (level + 1))
            to_left_ref[edge, :] = acc_ref[at : at + BLOCK, :].astype(bf16)
            to_right_ref[edge, :] = acc_ref[at + BLOCK + count : at + 2 * BLOCK + count, :].astype(bf16)
        carry = None
        for index in range(len(far) - 1, -1, -1):
            level = far[index]
            count = base_ref.shape[0] // 2 ** (level - LOCAL)
            tree_ref[0:count, :] = jnp.zeros((count, 2 * WIDTH), f32) if carry is None else spread(carry)
            for side, start in enumerate(far_starts(meta_ref[0], level, count)):
                at = offsets[LOCAL + index] + side * BLOCK
                tree_ref[pl.ds(start, BLOCK), :] += acc_ref[at : at + BLOCK, :]
            carry = tree_ref[0:count, :]
        mine, other = choose_groups(meta_ref[0] & 1, jnp.concatenate([carry[:, :WIDTH], carry[:, WIDTH:]], axis=0))
        far_keep_ref[...] = mine.astype(bf16)
        far_send_ref[...] = other.astype(bf16)
        tile = 256
        counts = [tile >> level for level in range(1, LOCAL - 1)]
        token = lax.broadcasted_iota(jnp.int32, (tile, counts[0]), 0)
        entry = lax.broadcasted_iota(jnp.int32, (tile, counts[0]), 1)
        member = jnp.concatenate(
            [
                jnp.where((token >> level) == entry, 0.5**level, 0.0)[:, :count]
                for level, count in enumerate(counts, 1)
            ],
            axis=1,
        ).astype(bf16)
        for at in range(0, rows, tile):
            coarse = [
                acc_ref[offsets[level] + BLOCK + (at >> level) : offsets[level] + BLOCK + ((at + tile) >> level), :]
                for level in range(1, LOCAL - 1)
            ]
            total = acc_ref[BLOCK + at : BLOCK + at + tile, :]
            for half in two_parts(jnp.concatenate(coarse, axis=0)):
                total = total + dot_nn(member, half)
            local_ref[at : at + tile, :] = total.astype(bf16)


def chain_rows(rows, devices):
    unit = 8 * devices
    return -(-(rows + 16) // unit) * unit


def attend_back_call(rows, devices, far, owners, meta, q, grads, exps, inverses, kv, scaled, left, right, base, weight, vectors):
    chunks = rows // CHUNK
    _, entries = extended_offsets(rows, far)
    _, slots = slot_layout(far)
    chain = (owners // 2, chain_rows(3 * WIDTH // owners, devices), WIDTH)
    outs = [
        jax.ShapeDtypeStruct((rows, WIDTH), bf16),
        jax.ShapeDtypeStruct((rows, 2 * WIDTH), bf16),
        jax.ShapeDtypeStruct((BLOCK * LOCAL, 2 * WIDTH), bf16),
        jax.ShapeDtypeStruct((BLOCK * LOCAL, 2 * WIDTH), bf16),
        jax.ShapeDtypeStruct((8 * devices, WIDTH), bf16),
        jax.ShapeDtypeStruct((8 * devices, WIDTH), bf16),
        jax.ShapeDtypeStruct(chain, bf16),
        jax.ShapeDtypeStruct(chain, bf16),
    ]
    return pl.pallas_call(
        partial(attend_back_kernel, rows, far),
        grid=(chunks // STEP,),
        out_shape=outs,
        in_specs=[
            pl.BlockSpec(memory_space=pltpu.SMEM),
            pl.BlockSpec((STEP * CHUNK, WIDTH), lambda i: (i, 0)),
            pl.BlockSpec((STEP * CHUNK, WIDTH), lambda i: (i, 0)),
            pl.BlockSpec((STEP, GROUPS, slots, LANES), lambda i: (i, 0, 0, 0)),
            pl.BlockSpec((STEP, 8, LANES), lambda i: (i, 0, 0)),
        ]
        + vmem_specs(7),
        out_specs=[pl.BlockSpec((STEP * CHUNK, WIDTH), lambda i: (i, 0))] + vmem_specs(len(outs) - 1),
        scratch_shapes=[
            pltpu.VMEM((entries, 2 * WIDTH), bf16),
            pltpu.VMEM((8 * devices, 2 * WIDTH), bf16),
            pltpu.VMEM((slots, 2 * WIDTH), bf16),
            pltpu.VMEM((entries, 2 * WIDTH), f32),
            pltpu.VMEM((8 * devices, 2 * WIDTH), f32),
            pltpu.VMEM((entries, WIDTH), bf16),
            pltpu.VMEM((rows, WIDTH), bf16),
        ],
        compiler_params=pltpu.CompilerParams(vmem_limit_bytes=40 << 20),
        cost_estimate=pl.CostEstimate(flops=36 << 30, bytes_accessed=24 << 20, transcendentals=4 << 20),
        name="attend_back",
    )(meta, q, grads, exps, inverses, kv, scaled, left, right, base, weight, vectors)


def normal_parts(values):
    size = jnp.abs(values)
    bell = jnp.exp(-0.5 * values * values)
    t = 1.0 / (1.0 + (0.3275911 / math.sqrt(2.0)) * size)
    poly = t * (
        0.5 * 0.254829592
        + t * (0.5 * -0.284496736 + t * (0.5 * 1.421413741 + t * (0.5 * -1.453152027 + t * (0.5 * 1.061405429))))
    )
    tail = poly * bell
    return jnp.where(values < 0, tail, 1.0 - tail), bell * (1.0 / math.sqrt(2.0 * math.pi))


def feed_kernel(
    hidden_width,
    owners,
    meta_ref,
    x_ref,
    attended_ref,
    cot_ref,
    vec_ref,
    up_bias_ref,
    *refs,
):
    one_refs, two_refs, refs = refs[:owners], refs[owners : 2 * owners], refs[2 * owners :]
    y_ref, grad_middle_ref, grad_attended_ref, keep_ref, send_ref = refs[:5]
    down_w_ref, up_w_ref, out_w_ref, vec_grad_ref, up_bias_grad_ref, down_acc, up_acc, out_acc = refs[5:]
    rows = WIDTH // owners
    wide_rows = hidden_width // owners
    blocks = hidden_width // WIDTH

    for at, (one, two) in enumerate(zip(one_refs, two_refs)):
        owner = meta_ref[1 + at]
        span = pl.ds(pl.multiple_of(owner * rows, rows), rows)
        for block in range(blocks - 1):
            up_w_ref[span, block * WIDTH : (block + 1) * WIDTH] = one[block * rows : (block + 1) * rows, :]
        up_w_ref[span, (blocks - 1) * WIDTH :] = two[0:rows, :]
        out_w_ref[span, :] = two[rows : 2 * rows, :]
        down_w_ref[pl.ds(pl.multiple_of(owner * wide_rows, wide_rows), wide_rows), :] = two[2 * rows :, :]

    out_bias, gain, shift, down_bias = (vec_ref[4 + at : 5 + at, :] for at in range(4))
    attended = attended_ref[...]
    middle = x_ref[...].astype(f32) + dot_nn(attended, out_w_ref[...]) + out_bias
    scaled, inverse = norm_rows(middle)
    normed = (scaled * gain + shift).astype(bf16)
    cot = cot_ref[...]
    wide = cot.astype(f32)
    lowered = jnp.zeros_like(middle)
    grad_normed = jnp.zeros_like(middle)
    for block in range(blocks):
        columns = slice(block * WIDTH, (block + 1) * WIDTH)
        down = down_w_ref[columns, :]
        pre = dot_nn(normed, up_w_ref[:, columns]) + up_bias_ref[:, columns]
        phi, bell = normal_parts(pre)
        hidden = (pre * phi).astype(bf16)
        lowered += dot_nn(hidden, down)
        grad_pre = (dot_nt(cot, down) * (phi + pre * bell)).astype(bf16)
        up_bias_grad_ref[:, columns] = column_sum(grad_pre.astype(f32))
        grad_normed += dot_nt(grad_pre, up_w_ref[:, columns])
        down_acc[columns, :] = dot_tn(hidden, cot)
        up_acc[:, columns] = dot_tn(normed, grad_pre)
    y_ref[...] = (middle + lowered + down_bias).astype(bf16)
    grad_middle = wide + norm_back(grad_normed, scaled, inverse, gain)
    grad_middle_ref[...] = grad_middle
    grad_proj = grad_middle.astype(bf16)
    grad_attended_ref[...] = dot_nt(grad_proj, out_w_ref[...]).astype(bf16)
    out_acc[...] = dot_tn(attended, grad_proj)
    vec_grad_ref[0:1, :] = column_sum(grad_proj.astype(f32))
    vec_grad_ref[1:2, :] = column_sum(grad_normed * scaled)
    vec_grad_ref[2:3, :] = column_sum(grad_normed)
    vec_grad_ref[3:4, :] = column_sum(wide)

    extra = keep_ref.shape[1] - wide_rows - (blocks + 1) * rows
    row_at = lax.broadcasted_iota(jnp.int32, (extra, 1), 0)
    low_bit = meta_ref[1] & 1

    def put(high, at, count, source):
        mine, other = choose(low_bit, source(2 * high), source(2 * high + 1))
        keep_ref[high, at : at + count, :] = mine.astype(bf16)
        send_ref[high, at : at + count, :] = other.astype(bf16)

    def small(owner):
        first = [vec_grad_ref[i : i + 1, owner * rows : (owner + 1) * rows] for i in range(4)]
        second = up_bias_grad_ref[:, owner * wide_rows : (owner + 1) * wide_rows]
        return jnp.where(row_at == 0, jnp.concatenate(first, axis=1), jnp.where(row_at == 1, second, 0.0))

    for high in range(owners // 2):
        put(high, 0, wide_rows, lambda owner: down_acc[owner * wide_rows : (owner + 1) * wide_rows, :])
        at = wide_rows
        for block in range(blocks):
            columns = slice(block * WIDTH, (block + 1) * WIDTH)
            put(high, at, rows, lambda owner: up_acc[owner * rows : (owner + 1) * rows, columns])
            at += rows
        put(high, at, rows, lambda owner: out_acc[owner * rows : (owner + 1) * rows, :])
        put(high, at + rows, extra, small)


def feed_call(hidden_width, devices, meta, x, attended, cot, vectors, up_bias, ones, twos):
    rows, owners = x.shape[0], len(ones)
    chain = chain_rows(2 * (hidden_width // owners) + WIDTH // owners, devices)
    split = jax.ShapeDtypeStruct((owners // 2, chain, WIDTH), bf16)
    return pl.pallas_call(
        partial(feed_kernel, hidden_width, owners),
        out_shape=[
            jax.ShapeDtypeStruct((rows, WIDTH), bf16),
            jax.ShapeDtypeStruct((rows, WIDTH), f32),
            jax.ShapeDtypeStruct((rows, WIDTH), bf16),
            split,
            split,
        ],
        in_specs=[pl.BlockSpec(memory_space=pltpu.SMEM)] + vmem_specs(5 + 2 * owners),
        out_specs=vmem_specs(5),
        scratch_shapes=[
            pltpu.VMEM((hidden_width, WIDTH), bf16),
            pltpu.VMEM((WIDTH, hidden_width), bf16),
            pltpu.VMEM((WIDTH, WIDTH), bf16),
            pltpu.VMEM((8, WIDTH), f32),
            pltpu.VMEM((1, hidden_width), f32),
            pltpu.VMEM((hidden_width, WIDTH), f32),
            pltpu.VMEM((WIDTH, hidden_width), f32),
            pltpu.VMEM((WIDTH, WIDTH), f32),
        ],
        compiler_params=pltpu.CompilerParams(vmem_limit_bytes=46 << 20),
        cost_estimate=pl.CostEstimate(flops=32 << 30, bytes_accessed=20 << 20, transcendentals=4 << 20),
        name="feed_forward",
    )(meta, x, attended, cot, vectors, up_bias, *ones, *twos)


def input_grad_kernel(
    rows,
    x_ref,
    dq_ref,
    local_ref,
    grad_middle_ref,
    from_right_ref,
    from_left_ref,
    far_keep_ref,
    far_got_ref,
    w_ref,
    vec_ref,
    out_ref,
    got_ref,
):
    step = pl.program_id(0)
    tile = x_ref.shape[0]
    edge = BLOCK * LOCAL

    @pl.when(step == 0)
    def _():
        folded = far_keep_ref[...].astype(f32) + far_got_ref[...].astype(f32)
        high, low = two_parts(jnp.concatenate([folded[:8], folded[8:]], axis=1))
        got_ref[0:edge, :] = from_left_ref[...]
        got_ref[edge : 2 * edge, :] = from_right_ref[...]
        far = jnp.concatenate([high.astype(f32), low.astype(f32)], axis=0).astype(bf16)
        got_ref[2 * edge : 2 * edge + BLOCK, :] = far
        got_ref[2 * edge + BLOCK :, :] = jnp.zeros((BLOCK, 2 * WIDTH), bf16)

    shape = (1, got_ref.shape[0])
    column = lax.broadcasted_iota(jnp.int32, shape, 1)
    within = jnp.where(column < edge, column, column - edge)
    level = jnp.where(column < 2 * edge, within >> 4, LOCAL)
    last = jnp.where((column >= edge) & (column < 2 * edge), (rows >> level) - BLOCK, 0)
    entry = jnp.where(column < 2 * edge, last + (within & 15), (column - 2 * edge) & 7)
    entry = jnp.where(column < 2 * edge + BLOCK, entry, -1)
    scale = 1.0 / (1 << level).astype(f32)
    token = step * tile + lax.broadcasted_iota(jnp.int32, (tile, shape[1]), 0)
    member = jnp.where((token >> level) == entry, scale, 0.0).astype(bf16)

    scaled, inverse = norm_rows(x_ref[...].astype(f32))
    dkv = (local_ref[...].astype(f32) + dot_nn(member, got_ref[...])).astype(bf16)
    grad = dot_nt(dq_ref[...], w_ref[:, :WIDTH]) + dot_nt(dkv, w_ref[:, WIDTH:])
    out_ref[...] = grad_middle_ref[...] + norm_back(grad, scaled, inverse, vec_ref[0:1, :])


def input_grad_call(x, dq, local, grad_middle, from_right, from_left, far_keep, far_got, weight, vectors):
    rows = x.shape[0]
    tile = 512
    tiled = lambda width: pl.BlockSpec((tile, width), lambda i: (i, 0))
    return pl.pallas_call(
        partial(input_grad_kernel, rows),
        grid=(rows // tile,),
        out_shape=jax.ShapeDtypeStruct((rows, WIDTH), f32),
        in_specs=[tiled(WIDTH), tiled(WIDTH), tiled(2 * WIDTH), tiled(WIDTH)] + vmem_specs(6),
        out_specs=tiled(WIDTH),
        scratch_shapes=[pltpu.VMEM((2 * BLOCK * (LOCAL + 1), 2 * WIDTH), bf16)],
        compiler_params=pltpu.CompilerParams(vmem_limit_bytes=24 << 20),
        cost_estimate=pl.CostEstimate(flops=6 << 30, bytes_accessed=12 << 20, transcendentals=0),
        name="input_grad",
    )(x, dq, local, grad_middle, from_right, from_left, far_keep, far_got, weight, vectors)


def shifted(block, axis, distance):
    devices = range(lax.axis_size(axis))
    route = [(i - distance, i) for i in devices if i - distance in devices]
    return lax.ppermute(block, axis, route)


def swap(block, axis, bit):
    return lax.ppermute(block, axis, [(i, i ^ bit) for i in range(lax.axis_size(axis))])


def gather_step(part, axis, bit):
    mine = (lax.axis_index(axis) // bit) % 2
    other = swap(part, axis, bit)
    first = jnp.where(mine == 0, part, other)
    second = jnp.where(mine == 0, other, part)
    return jnp.stack([first, second], axis=-3)


def together(*values):
    return lax.optimization_barrier(values)


def bits_of(axis):
    size = lax.axis_size(axis)
    return [1 << at for at in range(size.bit_length() - 1)]


def step_call(name, function, meta, arrays, shapes, dtype=bf16):
    def kernel(meta_ref, *refs):
        values = [ref[...].astype(f32) for ref in refs[: len(arrays)]]
        for ref, value in zip(refs[len(arrays) :], function(meta_ref[0], meta_ref[1], *values), strict=True):
            ref[...] = value.astype(dtype)

    size = sum(math.prod(a.shape) for a in arrays)
    return pl.pallas_call(
        kernel,
        out_shape=[jax.ShapeDtypeStruct(shape, dtype) for shape in shapes],
        in_specs=[pl.BlockSpec(memory_space=pltpu.SMEM)] + vmem_specs(len(arrays)),
        out_specs=vmem_specs(len(shapes)),
        compiler_params=pltpu.CompilerParams(vmem_limit_bytes=(4 << 20) + 16 * size),
        cost_estimate=pl.CostEstimate(flops=1 << 20, bytes_accessed=4 * size, transcendentals=0),
        name=name,
    )(meta, *arrays)


def halves(values, axis=0):
    return jnp.split(values, 2, axis=axis)


class Reduction:
    def __init__(self, meta, keep, send, far=None):
        self.meta, self.rows, self.far = meta, keep.shape[1], far
        self.bits = bits_of("ctx")[1:]
        self.keep, self.got = keep, [swap(send, "fsdp", 1)]

    def call(self, name, function, arrays, *shapes):
        return step_call(name, function, self.meta, arrays, [(*shape, WIDTH) for shape in shapes])

    def cross(self):
        far = [self.far[1]] if self.far else []
        extra = far[0].shape[0] if far else 0
        half = self.rows // 2

        def function(here, owner, keep, got, *far):
            mine, other = choose(owner >> 1, *(keep + got))
            keep, near = choose(here & 1, *halves(mine))
            high, both = choose(here & 1, *halves(other))
            return keep, jnp.concatenate([near, *far], axis=0), high, both

        shapes = [(half,), (half + extra,), (half,), (half,)]
        self.keep, near, high, both = self.call("cross", function, [self.keep, *self.got, *far], *shapes)
        count = lax.axis_size("fsdp")
        route = [(i, i ^ count ^ 2) for i in range(count * lax.axis_size("ctx"))]
        self.got = [swap(near, "ctx", 1), swap(high, "fsdp", 2), lax.ppermute(both, ("ctx", "fsdp"), route)]

    def scatter(self, at):
        bit, last = self.bits[at], at == len(self.bits) - 1
        rows = self.keep.shape[0]
        far = [self.far[0]] if self.far else []
        extra = far[0].shape[0] // 2 if far else 0

        def function(here, owner, keep, *got):
            far_keep = got[-1]
            got = got[: len(got) - len(far)]
            total = keep + got[0][:rows]
            for other in got[1:]:
                total = total + other
            flag = (here // bit) & 1
            keep, send = (total, total) if last else choose(flag, *halves(total))
            if not far:
                return [keep] if last else [keep, send]
            far_keep, far_send = choose_groups(flag, far_keep + got[0][rows:])
            return keep, jnp.concatenate([send, far_send], axis=0), far_keep

        count = rows if last else rows // 2
        shapes = [(count,)] if last and not far else [(count,), (count + extra,)]
        out = self.call("scatter", function, [self.keep, *self.got, *far], *shapes, *([(extra,)] if far else []))
        self.keep, send = out[0], out[1] if len(out) > 1 else out[0]
        self.got = [swap(send, "ctx", bit)]
        if far:
            self.far = (out[2], None)


    def order(self):
        high = list(reversed(self.bits[:-1]))
        return list(zip(high + [1], [1] + high))

    def collect(self):
        rows = self.keep.shape[0]
        if self.far:
            self.far = (self.far[0], self.got[0][rows:])
        function = lambda here, owner, keep, got: halves(keep + got[:rows])
        self.send_gather(0, self.call("collect", function, [self.keep, *self.got], (rows // 2,), (rows // 2,)))

    def send_gather(self, at, keep):
        self.keep = keep
        self.got = [swap(part, "ctx", bit) for part, bit in zip(keep, self.order()[at])]

    def gather(self, at):
        bits = self.order()[at]
        rows = 2 * self.keep[0].shape[0]
        function = lambda here, owner, *arrays: self.paired(here, bits, *arrays)
        self.send_gather(at + 1, self.call("gather", function, [*self.keep, *self.got], (rows,), (rows,)))

    def paired(self, here, bits, keep_one, keep_two, got_one, got_two):
        one = jnp.concatenate(choose((here // bits[0]) & 1, keep_one, got_one), axis=0)
        two = jnp.concatenate(choose((here // bits[1]) & 1, keep_two, got_two), axis=0)
        return one, two

    def scatters(self):
        return [self.cross] + [partial(self.scatter, at) for at in range(len(self.bits))]

    def gathers(self):
        return [self.collect] + [partial(self.gather, at) for at in range(len(self.order()) - 1)]

    def finish(self, shapes, unpack):
        bits = self.order()[-1]
        outer = lax.axis_size("ctx") // 4
        rows = self.rows // (4 * outer)

        def function(here, owner, *arrays):
            one, two = self.paired(here, bits, *arrays)
            parts = []
            for low in range(2):
                for high in range(outer):
                    a, b = low * outer + high, 2 * high + low
                    parts += [one[a * rows : (a + 1) * rows], two[b * rows : (b + 1) * rows]]
            return unpack(jnp.concatenate(parts, axis=0))

        return step_call("finish", function, self.meta, [*self.keep, *self.got], shapes, f32)


def shards(
    layer_input,
    doc_lengths,
    ln1_gain,
    ln1_bias,
    qkv_weight,
    query_bias,
    value_bias,
    out_weight,
    out_bias,
    ln2_gain,
    ln2_bias,
    up_weight,
    up_bias,
    down_weight,
    down_bias,
    cotangent,
):
    owners = lax.axis_size("fsdp")
    devices = lax.axis_size("ctx")
    x, cot = layer_input[0], cotangent[0]
    rows = x.shape[0]
    total = rows * devices
    far = far_levels(total)
    here, owner = lax.axis_index("ctx"), lax.axis_index("fsdp")
    part = WIDTH // owners
    hidden_width = up_weight.shape[1]
    meta = jnp.stack([here] + [owner ^ at for at in range(owners)]).astype(jnp.int32)

    vectors = [ln1_gain, ln1_bias, query_bias, value_bias, out_bias, ln2_gain, ln2_bias, down_bias, up_bias]
    across, beside = swap(qkv_weight, "fsdp", 2), swap(qkv_weight, "fsdp", 1)
    small = pack_call(vectors, beside)
    small_across, small_beside = swap(small, "fsdp", 2), swap(small, "fsdp", 1)
    one, two = pack_rest_call(down_weight, up_weight, out_weight)
    bias = mask_call(rows, total, far, meta, doc_lengths)
    across, beside, small_across, small_beside, one, two, bias = together(
        across, beside, small_across, small_beside, one, two, bias
    )
    pieces = [qkv_weight, beside, across, swap(across, "fsdp", 1)]
    smalls = [small, small_beside, small_across, swap(small_across, "fsdp", 1)]
    one_across = swap(one, "fsdp", 2)
    qkv_full, vec, up_shift, queries, kv, scaled, tail, head, base = qkv_call(
        rows, hidden_width, meta, x, pieces, smalls, [bias, two]
    )
    vec, tail, head, base, one_across = together(vec, tail, head, base, one_across)

    one_beside, one_both = swap(one, "fsdp", 1), swap(one_across, "fsdp", 1)
    two_across = swap(two, "fsdp", 2)
    left = shifted(tail, "ctx", 1)
    right = shifted(head, "ctx", -1)
    for bit in reversed(bits_of("ctx")):
        base = gather_step(base, "ctx", bit)
        if bit == 1:
            base, left, right, one_beside, one_both, two_across = together(
                base, left, right, one_beside, one_both, two_across
            )
    base = base.reshape(-1, ENTRY)
    two_beside, two_both = swap(two, "fsdp", 1), swap(two_across, "fsdp", 1)
    attended, exps, inverses = attend_call(rows, devices, far, meta, queries, bias, kv, left, right, base)
    inverses, two_beside, two_both = together(inverses, two_beside, two_both)
    output, grad_middle, grad_attended, keep, send = feed_call(
        hidden_width,
        devices,
        meta,
        x,
        attended,
        cot,
        vec,
        up_shift,
        [one, one_beside, one_across, one_both],
        [two, two_beside, two_across, two_both],
    )
    feed = Reduction(meta, keep, send)
    feed.cross()
    made = attend_back_call(
        rows, devices, far, owners, meta, queries, grad_attended, exps, inverses, kv, scaled, left, right, base, qkv_full, vec
    )
    dq, local, to_left, to_right, far_keep, far_send, keep, send = made
    to_left, to_right, far_keep, far_send, send, *feed.got = together(
        to_left, to_right, far_keep, far_send, send, *feed.got
    )
    first = Reduction(meta, keep, send, (far_keep, far_send))
    back_right = shifted(to_left, "ctx", -1)
    back_left = shifted(to_right, "ctx", 1)
    pending = feed.scatters()[1:]
    pending.pop(0)()
    first.cross()
    tied = together(*first.got, *feed.got)
    first.got, feed.got = list(tied[: len(first.got)]), list(tied[len(first.got) :])
    for one in first.scatters()[1:]:
        one()
        if pending:
            pending.pop(0)()
    tied = together(*first.got, back_right, back_left)
    first.got, (back_right, back_left) = list(tied[:1]), tied[1:]
    for at, (one, two) in enumerate(zip(first.gathers(), feed.gathers())):
        if at == 1:
            tied = together(*feed.got, *first.got)
            feed.got, first.got = list(tied[:2]), list(tied[2:])
        two()
        one()
    input_grad = input_grad_call(
        x, dq, local, grad_middle, back_right, back_left, *first.far, qkv_full, vec
    )

    wide_rows = hidden_width // owners

    def split(row):
        return [row[:, at * part : (at + 1) * part] for at in range(row.shape[1] // part)]

    def unpack_first(total):
        blocks = [total[at * part : (at + 1) * part] for at in range(3)]
        return [jnp.concatenate(blocks, axis=1), *split(total[3 * part : 3 * part + 1])]

    def unpack_feed(total):
        at = wide_rows
        blocks = []
        for _ in range(hidden_width // WIDTH):
            blocks.append(total[at : at + part])
            at += part
        vectors = [*split(total[at + part : at + part + 1]), total[at + part + 1 : at + part + 2]]
        return [total[:wide_rows], jnp.concatenate(blocks, axis=1), total[at : at + part], *vectors]

    vector = (1, part)
    qkv_grad, *firsts = first.finish([(part, 3 * WIDTH)] + [vector] * owners, unpack_first)
    down_grad, up_grad, out_grad, *feeds = feed.finish(
        [(wide_rows, WIDTH), (part, hidden_width), (part, WIDTH)] + [vector] * owners + [(1, wide_rows)], unpack_feed
    )
    gain_first, shift_first, query_grad, value_grad = (v.reshape(-1) for v in firsts)
    out_shift, gain_second, shift_second, down_shift, up_shift_grad = (v.reshape(-1) for v in feeds)
    return (
        output[None],
        input_grad[None],
        gain_first,
        shift_first,
        qkv_grad,
        query_grad,
        value_grad,
        out_grad,
        out_shift,
        gain_second,
        shift_second,
        up_grad,
        up_shift_grad,
        down_grad,
        down_shift,
    )


def solution(mesh):
    row, vector = P("fsdp", None), P("fsdp")
    tokens = P("fsdp", "ctx", None)
    return jax.shard_map(
        shards,
        mesh=mesh,
        in_specs=(
            tokens,
            row,
            vector,
            vector,
            row,
            vector,
            vector,
            row,
            vector,
            vector,
            vector,
            row,
            vector,
            row,
            vector,
            tokens,
        ),
        out_specs=(
            tokens,
            tokens,
            vector,
            vector,
            row,
            vector,
            vector,
            row,
            vector,
            vector,
            vector,
            row,
            vector,
            row,
            vector,
        ),
        check_vma=False,
    )
```

```python
from functools import partial
import math

import jax
import jax.numpy as jnp
from jax import lax
from jax.experimental import pallas as pl
from jax.experimental.pallas import tpu as pltpu
from jax.sharding import PartitionSpec as P

HEADS = 8
BLOCK = 16
LEVELS = 10
NEAR = 3
LOCAL = 7
CHUNK = 64
STEP = 4
WIDTH = 512
GROUP = 4
GROUPS = HEADS // GROUP
LANES = WIDTH // GROUPS
ENTRY = 3 * WIDTH
SMALL = 16
MASKED = -1e30
EPSILON = 1e-05

f32 = jnp.float32
bf16 = jnp.bfloat16


def level_rows(rows, level):
    return rows // 2**level


def level_offsets(rows):
    offsets = [0]
    for level in range(LOCAL):
        offsets.append(offsets[-1] + level_rows(rows, level))
    return offsets[:-1], offsets[-1]


def far_levels(total):
    return [l for l in range(LOCAL, LEVELS) if total // (BLOCK * 2**l) >= 2]


def extended_offsets(rows, far):
    offsets, cursor = [], 0
    for level in range(LOCAL):
        offsets.append(cursor)
        cursor += level_rows(rows, level) + 2 * BLOCK
    for _ in far:
        offsets.append(cursor)
        cursor += 2 * BLOCK
    return offsets, cursor


def slot_layout(far):
    parts = [(level, CHUNK // 2**level + 2 * BLOCK) for level in range(NEAR)]
    parts += [(level, BLOCK) for level in list(range(NEAR, LOCAL)) + far for _ in range(2)]
    return parts, sum(count for _, count in parts)


def slot_sources(rows, far, chunk):
    offsets, _ = extended_offsets(rows, far)
    sources = []
    for level in range(NEAR):
        sources.append((offsets[level] + chunk * (CHUNK // 2**level), CHUNK // 2**level + 2 * BLOCK))
    for level in range(NEAR, LOCAL):
        block = chunk // (BLOCK * 2**level // CHUNK)
        sources.append((offsets[level] + block * BLOCK, BLOCK))
        sources.append((offsets[level] + block * BLOCK + 2 * BLOCK, BLOCK))
    for at in range(len(far)):
        sources.append((offsets[LOCAL + at], BLOCK))
        sources.append((offsets[LOCAL + at] + BLOCK, BLOCK))
    return sources


def mask_kernel(rows, total, far, here_ref, lengths_ref, bias_ref):
    for sub in range(STEP):
        base = here_ref[0] * rows + (pl.program_id(0) * STEP + sub) * CHUNK
        query = base + (lax.broadcasted_iota(jnp.int32, (1, 128), 1) & (CHUNK - 1))
        first_token = jnp.zeros((1, 128), jnp.int32)
        end_token = jnp.full((1, 128), total, jnp.int32)
        start = jnp.int32(0)
        for at in range(lengths_ref.shape[1]):
            first_token = jnp.where(start <= query, start, first_token)
            start = start + lengths_ref[0, at]
            end_token = jnp.where(start > query, jnp.minimum(end_token, start), end_token)

        def part(at, count, first_row, level):
            span = 2**level
            shift = level + 4
            first = first_row + span * lax.broadcasted_iota(jnp.int32, (count, 128), 0)
            gap = jnp.abs((first >> shift) - (query >> shift))
            if level == 0:
                seen = gap <= 1
            else:
                seen = (gap == 1) & (jnp.abs((first >> (shift - 1)) - (query >> (shift - 1))) > 1)
            seen = seen & (first >= first_token) & (first + (span - 1) < end_token)
            bias_ref[sub, at : at + count, :] = jnp.where(seen, level * math.log(2.0), MASKED)

        at = 0
        for level in range(NEAR):
            count = CHUNK // 2**level + 2 * BLOCK
            part(at, count, base - BLOCK * 2**level, level)
            at += count
        for level in list(range(NEAR, LOCAL)) + far:
            block = base >> (level + 4)
            for side in (-1, 1):
                part(at, BLOCK, (block + side) * (BLOCK * 2**level), level)
                at += BLOCK


def mask_call(rows, total, far, meta, lengths):
    chunks = rows // CHUNK
    _, slots = slot_layout(far)
    return pl.pallas_call(
        partial(mask_kernel, rows, total, far),
        grid=(chunks // STEP,),
        out_shape=jax.ShapeDtypeStruct((chunks, slots, 128), f32),
        in_specs=[pl.BlockSpec(memory_space=pltpu.SMEM)] * 2,
        out_specs=pl.BlockSpec((STEP, slots, 128), lambda i: (i, 0, 0)),
        compiler_params=pltpu.CompilerParams(vmem_limit_bytes=8 << 20),
        cost_estimate=pl.CostEstimate(flops=4 << 30, bytes_accessed=3 << 20, transcendentals=0),
        name="mask",
    )(meta, lengths)


def dot_nt(left, right):
    return lax.dot_general(left, right, (((1,), (1,)), ((), ())), preferred_element_type=f32)


def dot_tn(left, right):
    return lax.dot_general(left, right, (((0,), (0,)), ((), ())), preferred_element_type=f32)


def dot_nn(left, right):
    return jnp.dot(left, right, preferred_element_type=f32)


def pool_matrix(count):
    row = lax.broadcasted_iota(jnp.int32, (count // 2, count), 0)
    column = lax.broadcasted_iota(jnp.int32, (count // 2, count), 1)
    return jnp.where((column >> 1) == row, 0.5, 0.0).astype(bf16)


def spread_matrix(count):
    row = lax.broadcasted_iota(jnp.int32, (2 * count, count), 0)
    column = lax.broadcasted_iota(jnp.int32, (2 * count, count), 1)
    return jnp.where((row >> 1) == column, 0.5, 0.0).astype(bf16)


def spread(values):
    count = values.shape[0]
    tile = min(count, 128)
    matrix = spread_matrix(tile)
    high = values.astype(bf16)
    low = (values - high.astype(f32)).astype(bf16)
    parts = [
        dot_nn(matrix, high[at : at + tile]) + dot_nn(matrix, low[at : at + tile])
        for at in range(0, count, tile)
    ]
    return parts[0] if len(parts) == 1 else jnp.concatenate(parts, axis=0)


def norm_rows(values):
    mean = jnp.mean(values, axis=-1, keepdims=True)
    centred = values - mean
    variance = jnp.mean(centred * centred, axis=-1, keepdims=True)
    inverse = lax.rsqrt(variance + EPSILON)
    return centred * inverse, inverse


def norm_back(grad_out, scaled, inverse, gain):
    grad_scaled = grad_out * gain
    first = jnp.mean(grad_scaled, axis=-1, keepdims=True)
    second = jnp.mean(grad_scaled * scaled, axis=-1, keepdims=True)
    return inverse * (grad_scaled - first - scaled * second)


def head_of(shape):
    return lax.broadcasted_iota(jnp.int32, shape, 1) // (WIDTH // HEADS)


def split_heads(group):
    head, zero = head_of(group.shape), jnp.zeros_like(group)
    return jnp.concatenate([jnp.where(head == at, group, zero) for at in range(GROUP)], axis=0)


def join_heads(stacked):
    rows = stacked.shape[0] // GROUP
    head = head_of((rows, stacked.shape[1]))
    out = stacked[:rows]
    for at in range(1, GROUP):
        out = jnp.where(head == at, stacked[at * rows : (at + 1) * rows], out)
    return out


def pack_kernel(*refs):
    out_ref = refs[-1]
    row = jnp.concatenate([ref[...].reshape(1, -1) for ref in refs[:-2]], axis=1)
    out_ref[...] = jnp.broadcast_to(row.astype(f32), out_ref.shape).astype(bf16)


def pack_call(vectors, earlier):
    return pl.pallas_call(
        pack_kernel,
        out_shape=jax.ShapeDtypeStruct((SMALL, sum(v.shape[0] for v in vectors)), bf16),
        in_specs=vmem_specs(len(vectors)) + [pl.BlockSpec(memory_space=pl.ANY)],
        out_specs=vmem_specs(1)[0],
        compiler_params=pltpu.CompilerParams(vmem_limit_bytes=56 << 20),
        name="pack",
    )(*vectors, earlier)


def pack_rest_kernel(down_ref, up_ref, out_w_ref, one_ref, two_ref):
    rows = up_ref.shape[0]
    blocks = up_ref.shape[1] // WIDTH
    for block in range(blocks - 1):
        one_ref[block * rows : (block + 1) * rows, :] = up_ref[:, block * WIDTH : (block + 1) * WIDTH]
    two_ref[0:rows, :] = up_ref[:, (blocks - 1) * WIDTH :]
    two_ref[rows : 2 * rows, :] = out_w_ref[...]
    two_ref[2 * rows :, :] = down_ref[...]


def pack_rest_call(down, up, out_w):
    rows, blocks = up.shape[0], up.shape[1] // WIDTH
    return pl.pallas_call(
        pack_rest_kernel,
        out_shape=[
            jax.ShapeDtypeStruct(((blocks - 1) * rows, WIDTH), bf16),
            jax.ShapeDtypeStruct((2 * rows + down.shape[0], WIDTH), bf16),
        ],
        in_specs=vmem_specs(3),
        out_specs=vmem_specs(2),
        compiler_params=pltpu.CompilerParams(vmem_limit_bytes=56 << 20),
        name="pack_rest",
    )(down, up, out_w)


def vmem_specs(count):
    return [pl.BlockSpec(memory_space=pltpu.VMEM)] * count


def qkv_kernel(rows, owners, meta_ref, x_ref, *refs):
    shard_refs, small_refs, refs = refs[:owners], refs[owners : 2 * owners], refs[2 * owners + 2 :]
    w_ref, vec_ref, up_bias_ref, q_ref = refs[:4]
    kv_ref, scaled_ref, tail_ref, head_ref, top_ref, keep_ref = refs[4:]
    places, _ = level_offsets(rows)
    part = WIDTH // owners
    step = pl.program_id(0)

    @pl.when(step == 0)
    def _():
        for at, (ref, small_ref) in enumerate(zip(shard_refs, small_refs)):
            owner = meta_ref[1 + at]
            w_ref[pl.ds(pl.multiple_of(owner * part, part), part), :] = ref[...]
            row = small_ref[0:1, :].astype(f32)
            for vector in range(8):
                vec_ref[vector : vector + 1, pl.ds(pl.multiple_of(owner * part, part), part)] = row[
                    :, vector * part : (vector + 1) * part
                ]
            wide = row.shape[1] - 8 * part
            up_bias_ref[:, pl.ds(pl.multiple_of(owner * wide, wide), wide)] = row[:, 8 * part :]

    tile = x_ref.shape[0]
    scaled, _ = norm_rows(x_ref[...].astype(f32))
    normed = (scaled * vec_ref[0:1, :] + vec_ref[1:2, :]).astype(bf16)
    queries = (dot_nn(normed, w_ref[:, :WIDTH]) + vec_ref[2:3, :]).astype(bf16)
    q_ref[...] = queries * jnp.asarray(0.125, bf16)
    keys = dot_nn(normed, w_ref[:, WIDTH : 2 * WIDTH]).astype(bf16)
    values = (dot_nn(normed, w_ref[:, 2 * WIDTH :]) + vec_ref[3:4, :]).astype(bf16)
    current = jnp.concatenate([keys, values, scaled.astype(bf16)], axis=1)

    def edges(level, block):
        @pl.when(step == 0)
        def _():
            head_ref[BLOCK * level : BLOCK * (level + 1), :] = block[:BLOCK]

        @pl.when(step == pl.num_programs(0) - 1)
        def _():
            tail_ref[BLOCK * level : BLOCK * (level + 1), :] = block[block.shape[0] - BLOCK :]

    for level in range(5):
        if level:
            current = dot_nn(pool_matrix(current.shape[0]), current).astype(bf16)
        count = tile // 2**level
        span = pl.ds(pl.multiple_of(places[level] + step * count, count), count)
        kv_ref[span, :] = current[:, : 2 * WIDTH]
        scaled_ref[span, :] = current[:, 2 * WIDTH :]
        edges(level, current)
    keep_ref[pl.ds(pl.multiple_of(step * count, count), count), :] = current

    @pl.when(step == pl.num_programs(0) - 1)
    def _():
        current = keep_ref[...]
        for level in range(5, LOCAL):
            current = dot_nn(pool_matrix(current.shape[0]), current).astype(bf16)
            span = slice(places[level], places[level] + current.shape[0])
            kv_ref[span, :] = current[:, : 2 * WIDTH]
            scaled_ref[span, :] = current[:, 2 * WIDTH :]
            tail_ref[BLOCK * level : BLOCK * (level + 1), :] = current[current.shape[0] - BLOCK :]
            head_ref[BLOCK * level : BLOCK * (level + 1), :] = current[:BLOCK]
        top_ref[...] = dot_nn(pool_matrix(BLOCK), current).astype(bf16)


def qkv_call(rows, hidden_width, meta, x, pieces, smalls, earlier):
    owners = len(pieces)
    tile = 512

    def tiled(count, width):
        return pl.BlockSpec((count, width), lambda i: (i, 0))

    _, entries = level_offsets(rows)
    edge = jax.ShapeDtypeStruct((BLOCK * LOCAL, ENTRY), bf16)
    outs = pl.pallas_call(
        partial(qkv_kernel, rows, owners),
        grid=(rows // tile,),
        out_shape=[
            jax.ShapeDtypeStruct((WIDTH, 3 * WIDTH), bf16),
            jax.ShapeDtypeStruct((8, WIDTH), f32),
            jax.ShapeDtypeStruct((1, hidden_width), f32),
            jax.ShapeDtypeStruct((rows, WIDTH), bf16),
        ]
        + [jax.ShapeDtypeStruct((entries, 2 * WIDTH), bf16), jax.ShapeDtypeStruct((entries, WIDTH), bf16)]
        + [edge, edge, jax.ShapeDtypeStruct((BLOCK // 2, ENTRY), bf16)],
        in_specs=[pl.BlockSpec(memory_space=pltpu.SMEM), tiled(tile, WIDTH)]
        + vmem_specs(2 * owners)
        + [pl.BlockSpec(memory_space=pl.ANY)] * 2,
        out_specs=vmem_specs(3) + [tiled(tile, WIDTH)] + vmem_specs(5),
        scratch_shapes=[pltpu.VMEM((level_rows(rows, 4), ENTRY), bf16)],
        compiler_params=pltpu.CompilerParams(vmem_limit_bytes=56 << 20),
        cost_estimate=pl.CostEstimate(flops=9 << 30, bytes_accessed=12 << 20, transcendentals=0),
        name="qkv_levels",
    )(meta, x, *pieces, *smalls, *earlier)
    return outs


def far_level(entries):
    return dot_nn(pool_matrix(entries.shape[0]), entries).astype(bf16)


def assemble(rows, far, here, columns, own_ref, left_ref, right_ref, base_ref, ext_ref, far_ref):
    offsets, _ = extended_offsets(rows, far)
    places, _ = level_offsets(rows)
    for inner, outer, target, width in columns:
        lanes, edge_lanes = slice(target, target + width), slice(outer, outer + width)
        for level in range(LOCAL):
            at, count = offsets[level], level_rows(rows, level)
            edge = slice(BLOCK * level, BLOCK * (level + 1))
            ext_ref[at : at + BLOCK, lanes] = left_ref[edge, edge_lanes]
            ext_ref[at + BLOCK : at + BLOCK + count, lanes] = own_ref[
                places[level] : places[level] + count, inner : inner + width
            ]
            ext_ref[at + BLOCK + count : at + 2 * BLOCK + count, lanes] = right_ref[edge, edge_lanes]
        current = base_ref[:, edge_lanes]
        for index, level in enumerate(far):
            if index:
                current = far_level(current)
            count = current.shape[0]
            far_ref[0:count, 0:width] = current
            for side, start in enumerate(far_starts(here, level, count)):
                at = offsets[LOCAL + index] + side * BLOCK
                ext_ref[at : at + BLOCK, lanes] = far_ref[pl.ds(start, BLOCK), 0:width]


def far_starts(here, level, count):
    block = here >> (level - 6)
    last = count // BLOCK - 1
    return [pl.multiple_of(jnp.clip(at, 0, last) * BLOCK, BLOCK) for at in (block - 1, block + 1)]


def load_slots(rows, far, chunk, ext_ref, slots_ref):
    at = 0
    for start, count in slot_sources(rows, far, chunk):
        if not isinstance(start, int):
            start = pl.multiple_of(start, BLOCK)
        slots_ref[at : at + count, :] = ext_ref[pl.ds(start, count), :]
        at += count


def attend_kernel(rows, far, meta_ref, q_ref, bias_ref, *refs):
    own_ref, left_ref, right_ref, base_ref, out_ref, exp_ref, inverse_ref, ext_ref, far_ref, slots_ref = refs
    step = pl.program_id(0)

    @pl.when(step == 0)
    def _():
        columns = [(0, 0, 0, 2 * WIDTH)]
        assemble(rows, far, meta_ref[0], columns, own_ref, left_ref, right_ref, base_ref, ext_ref, far_ref)

    ones = jnp.ones((slots_ref.shape[0], 128), bf16)
    second_head = (head_of((CHUNK, 256)) & 1) == 1
    for sub in range(STEP):
        span = slice(sub * CHUNK, (sub + 1) * CHUNK)
        load_slots(rows, far, step * STEP + sub, ext_ref, slots_ref)
        bias = bias_ref[sub]
        bias = jnp.concatenate([bias, bias], axis=1)
        for group in range(GROUPS):
            lanes = slice(LANES * group, LANES * (group + 1))
            values = slots_ref[:, WIDTH + LANES * group : WIDTH + LANES * (group + 1)]
            scores = dot_nt(slots_ref[:, lanes], split_heads(q_ref[span, lanes])) + bias
            exponent = jnp.exp(scores - jnp.max(scores, axis=0, keepdims=True))
            low = exponent.astype(bf16)
            exp_ref[sub, group] = low
            inverse = 1.0 / jnp.sum(exponent, axis=0, keepdims=True)
            inverse_ref[sub, group : group + 1, :] = inverse
            for half in range(LANES // 128):
                columns = slice(128 * half, 128 * (half + 1))
                both = dot_tn(low[:, columns], jnp.concatenate([values[:, columns], ones], axis=1))
                pair = jnp.where(second_head, both[CHUNK:], both[:CHUNK])
                at = LANES * group + 128 * half
                out_ref[span, at : at + 128] = (pair[:, :128] / pair[:, 128:]).astype(bf16)


def attend_call(rows, devices, far, meta, q, bias, kv, left, right, base):
    chunks = rows // CHUNK
    _, entries = extended_offsets(rows, far)
    _, slots = slot_layout(far)
    return pl.pallas_call(
        partial(attend_kernel, rows, far),
        grid=(chunks // STEP,),
        out_shape=[
            jax.ShapeDtypeStruct((rows, WIDTH), bf16),
            jax.ShapeDtypeStruct((chunks, GROUPS, slots, LANES), bf16),
            jax.ShapeDtypeStruct((chunks, 8, LANES), f32),
        ],
        in_specs=[
            pl.BlockSpec(memory_space=pltpu.SMEM),
            pl.BlockSpec((STEP * CHUNK, WIDTH), lambda i: (i, 0)),
            pl.BlockSpec((STEP, slots, 128), lambda i: (i, 0, 0)),
        ]
        + vmem_specs(4),
        out_specs=[
            pl.BlockSpec((STEP * CHUNK, WIDTH), lambda i: (i, 0)),
            pl.BlockSpec((STEP, GROUPS, slots, LANES), lambda i: (i, 0, 0, 0)),
            pl.BlockSpec((STEP, 8, LANES), lambda i: (i, 0, 0)),
        ],
        scratch_shapes=[
            pltpu.VMEM((entries, 2 * WIDTH), bf16),
            pltpu.VMEM((8 * devices, 2 * WIDTH), bf16),
            pltpu.VMEM((slots, 2 * WIDTH), bf16),
        ],
        compiler_params=pltpu.CompilerParams(vmem_limit_bytes=56 << 20),
        cost_estimate=pl.CostEstimate(flops=20 << 30, bytes_accessed=20 << 20, transcendentals=4 << 20),
        name="attend",
    )(meta, q, bias, kv, left, right, base)


def column_sum(values):
    return jnp.sum(values, axis=0, keepdims=True)


def matrix_row(left, right):
    total = None
    for a in two_parts(left):
        for b in two_parts(right):
            term = dot_nt(a, b)
            total = term if total is None else total + term
    return total[0:1]


def two_parts(values):
    if values.dtype == bf16:
        return [values]
    high = values.astype(bf16)
    return [high, (values - high.astype(f32)).astype(bf16)]


def choose(flag, zero, one):
    return jnp.where(flag == 0, zero, one), jnp.where(flag == 0, one, zero)


CROSS = 2


def choose_groups(flag, folded, inner):
    groups = folded.reshape(-1, 2, 8 * inner, folded.shape[1])
    return [part.reshape(-1, folded.shape[1]) for part in choose(flag, groups[:, 0], groups[:, 1])]


def attend_back_kernel(rows, far, *refs):
    refs = list(refs)
    take = lambda count: [refs.pop(0) for _ in range(count)]
    meta_ref, q_ref, grad_ref, exp_ref, inverse_ref = take(5)
    own_ref, own_scaled_ref = take(2)
    left_ref, right_ref, base_ref, w_ref, vec_ref = take(5)
    dq_ref, local_ref, to_left_ref, to_right_ref, far_keep_ref, far_send_ref, keep_ref, send_ref = take(8)
    ext_ref, far_ref, slots_ref, acc_ref, tree_ref, scaled_ref, dq_keep_ref = take(7)
    step = pl.program_id(0)
    offsets, entries = extended_offsets(rows, far)

    @pl.when(step == 0)
    def _():
        common = (left_ref, right_ref, base_ref)
        assemble(rows, far, meta_ref[0], [(0, 0, 0, 2 * WIDTH)], own_ref, *common, ext_ref, far_ref)
        assemble(rows, far, meta_ref[0], [(0, 2 * WIDTH, 0, WIDTH)], own_scaled_ref, *common, scaled_ref, far_ref)
        acc_ref[...] = jnp.zeros_like(acc_ref)

    for sub in range(STEP):
        chunk = step * STEP + sub
        span = slice(sub * CHUNK, (sub + 1) * CHUNK)
        load_slots(rows, far, chunk, ext_ref, slots_ref)
        sources = slot_sources(rows, far, chunk)
        for group in range(GROUPS):
            lanes = slice(LANES * group, LANES * (group + 1))
            value_lanes = slice(WIDTH + LANES * group, WIDTH + LANES * (group + 1))
            keys, values = slots_ref[:, lanes], slots_ref[:, value_lanes]
            queries, grads = split_heads(q_ref[span, lanes]), split_heads(grad_ref[span, lanes])
            probs = exp_ref[sub, group].astype(f32) * inverse_ref[sub, group : group + 1, :]
            grad_probs = dot_nt(values, grads)
            delta = jnp.sum(probs * grad_probs, axis=0, keepdims=True)
            grad_scores = (probs * (grad_probs - delta)).astype(bf16)
            dq = (join_heads(dot_tn(grad_scores, keys)) * 0.125).astype(bf16)
            dq_ref[span, lanes] = dq
            dq_keep_ref[pl.ds(pl.multiple_of(chunk * CHUNK, CHUNK), CHUNK), lanes] = dq
            grad_keys = dot_nn(grad_scores, queries)
            grad_values = dot_nn(probs.astype(bf16), grads)
            at = 0
            for start, count in sources:
                if not isinstance(start, int):
                    start = pl.multiple_of(start, BLOCK)
                acc_ref[pl.ds(start, count), lanes] += grad_keys[at : at + count]
                acc_ref[pl.ds(start, count), value_lanes] += grad_values[at : at + count]
                at += count

    @pl.when(step == pl.num_programs(0) - 1)
    def _():
        dq = dq_keep_ref[...]
        sums = [column_sum(dq.astype(f32)), column_sum(acc_ref[:, :WIDTH]), column_sum(acc_ref[:, WIDTH:])]
        both = dot_tn(scaled_ref[...], acc_ref[...].astype(bf16))
        parts = [dot_tn(own_scaled_ref[0:rows, :], dq), both[:, :WIDTH], both[:, WIDTH:]]
        first_row = lax.broadcasted_iota(jnp.int32, (16, 1), 0) == 0
        ones = jnp.where(first_row, jnp.ones((16, WIDTH), f32), 0.0).astype(bf16)
        as_column = lambda row: dot_tn(jnp.where(first_row, row, 0.0).astype(bf16), ones)
        gain, shift = as_column(vec_ref[0:1, :]), as_column(vec_ref[1:2, :])
        gain_grad, shift_grad = jnp.zeros((1, WIDTH), f32), jnp.zeros((1, WIDTH), f32)
        owners = 2 * keep_ref.shape[0]
        part = WIDTH // owners
        low_bit = meta_ref[1] & 1
        for block in range(3):
            weight = w_ref[:, block * WIDTH : (block + 1) * WIDTH]
            gain_grad += matrix_row(jnp.ones((16, WIDTH), bf16), weight.astype(f32) * parts[block])
            shift_grad += matrix_row(jnp.broadcast_to(sums[block], (16, WIDTH)), weight)
            grad = gain * parts[block] + shift * sums[block]
            for high in range(owners // 2):
                at = 2 * high * part
                mine, other = choose(low_bit, grad[at : at + part], grad[at + part : at + 2 * part])
                keep_ref[high, block * part : (block + 1) * part, :] = mine.astype(bf16)
                send_ref[high, block * part : (block + 1) * part, :] = other.astype(bf16)
        extra = keep_ref.shape[1] - 3 * part
        top_row = lax.broadcasted_iota(jnp.int32, (extra, 1), 0) == 0
        vectors = [gain_grad, shift_grad, sums[0], sums[2]]
        owner_row = lambda owner: jnp.concatenate([v[:, owner * part : (owner + 1) * part] for v in vectors], axis=1)
        for high in range(owners // 2):
            mine, other = choose(low_bit, owner_row(2 * high), owner_row(2 * high + 1))
            keep_ref[high, 3 * part :, :] = jnp.where(top_row, mine, 0.0).astype(bf16)
            send_ref[high, 3 * part :, :] = jnp.where(top_row, other, 0.0).astype(bf16)

        for level in range(LOCAL):
            at, count = offsets[level], level_rows(rows, level)
            edge = slice(BLOCK * level, BLOCK * (level + 1))
            to_left_ref[edge, :] = acc_ref[at : at + BLOCK, :].astype(bf16)
            to_right_ref[edge, :] = acc_ref[at + BLOCK + count : at + 2 * BLOCK + count, :].astype(bf16)
        carry = None
        for index in range(len(far) - 1, -1, -1):
            level = far[index]
            count = base_ref.shape[0] // 2 ** (level - LOCAL)
            tree_ref[0:count, :] = jnp.zeros((count, 2 * WIDTH), f32) if carry is None else spread(carry)
            for side, start in enumerate(far_starts(meta_ref[0], level, count)):
                at = offsets[LOCAL + index] + side * BLOCK
                tree_ref[pl.ds(start, BLOCK), :] += acc_ref[at : at + BLOCK, :]
            carry = tree_ref[0:count, :]
        mine, other = choose_groups(
            (meta_ref[0] // CROSS) & 1, jnp.concatenate([carry[:, :WIDTH], carry[:, WIDTH:]], axis=0), CROSS
        )
        far_keep_ref[...] = mine.astype(bf16)
        far_send_ref[...] = other.astype(bf16)
        tile = 256
        counts = [tile >> level for level in range(1, LOCAL - 1)]
        token = lax.broadcasted_iota(jnp.int32, (tile, counts[0]), 0)
        entry = lax.broadcasted_iota(jnp.int32, (tile, counts[0]), 1)
        member = jnp.concatenate(
            [
                jnp.where((token >> level) == entry, 0.5**level, 0.0)[:, :count]
                for level, count in enumerate(counts, 1)
            ],
            axis=1,
        ).astype(bf16)
        for at in range(0, rows, tile):
            coarse = [
                acc_ref[offsets[level] + BLOCK + (at >> level) : offsets[level] + BLOCK + ((at + tile) >> level), :]
                for level in range(1, LOCAL - 1)
            ]
            total = acc_ref[BLOCK + at : BLOCK + at + tile, :]
            for half in two_parts(jnp.concatenate(coarse, axis=0)):
                total = total + dot_nn(member, half)
            local_ref[at : at + tile, :] = total.astype(bf16)


def chain_rows(rows, devices):
    unit = 8 * devices
    return -(-(rows + 16) // unit) * unit


def attend_back_call(rows, devices, far, owners, meta, q, grads, exps, inverses, kv, scaled, left, right, base, weight, vectors):
    chunks = rows // CHUNK
    _, entries = extended_offsets(rows, far)
    _, slots = slot_layout(far)
    chain = (owners // 2, chain_rows(3 * WIDTH // owners, devices), WIDTH)
    outs = [
        jax.ShapeDtypeStruct((rows, WIDTH), bf16),
        jax.ShapeDtypeStruct((rows, 2 * WIDTH), bf16),
        jax.ShapeDtypeStruct((BLOCK * LOCAL, 2 * WIDTH), bf16),
        jax.ShapeDtypeStruct((BLOCK * LOCAL, 2 * WIDTH), bf16),
        jax.ShapeDtypeStruct((8 * devices, WIDTH), bf16),
        jax.ShapeDtypeStruct((8 * devices, WIDTH), bf16),
        jax.ShapeDtypeStruct(chain, bf16),
        jax.ShapeDtypeStruct(chain, bf16),
    ]
    return pl.pallas_call(
        partial(attend_back_kernel, rows, far),
        grid=(chunks // STEP,),
        out_shape=outs,
        in_specs=[
            pl.BlockSpec(memory_space=pltpu.SMEM),
            pl.BlockSpec((STEP * CHUNK, WIDTH), lambda i: (i, 0)),
            pl.BlockSpec((STEP * CHUNK, WIDTH), lambda i: (i, 0)),
            pl.BlockSpec((STEP, GROUPS, slots, LANES), lambda i: (i, 0, 0, 0)),
            pl.BlockSpec((STEP, 8, LANES), lambda i: (i, 0, 0)),
        ]
        + vmem_specs(7),
        out_specs=[pl.BlockSpec((STEP * CHUNK, WIDTH), lambda i: (i, 0))] + vmem_specs(len(outs) - 1),
        scratch_shapes=[
            pltpu.VMEM((entries, 2 * WIDTH), bf16),
            pltpu.VMEM((8 * devices, 2 * WIDTH), bf16),
            pltpu.VMEM((slots, 2 * WIDTH), bf16),
            pltpu.VMEM((entries, 2 * WIDTH), f32),
            pltpu.VMEM((8 * devices, 2 * WIDTH), f32),
            pltpu.VMEM((entries, WIDTH), bf16),
            pltpu.VMEM((rows, WIDTH), bf16),
        ],
        compiler_params=pltpu.CompilerParams(vmem_limit_bytes=40 << 20),
        cost_estimate=pl.CostEstimate(flops=36 << 30, bytes_accessed=24 << 20, transcendentals=4 << 20),
        name="attend_back",
    )(meta, q, grads, exps, inverses, kv, scaled, left, right, base, weight, vectors)


def normal_parts(values):
    size = jnp.abs(values)
    bell = jnp.exp(-0.5 * values * values)
    t = 1.0 / (1.0 + (0.3275911 / math.sqrt(2.0)) * size)
    poly = t * (
        0.5 * 0.254829592
        + t * (0.5 * -0.284496736 + t * (0.5 * 1.421413741 + t * (0.5 * -1.453152027 + t * (0.5 * 1.061405429))))
    )
    tail = poly * bell
    return jnp.where(values < 0, tail, 1.0 - tail), bell * (1.0 / math.sqrt(2.0 * math.pi))


def feed_kernel(
    hidden_width,
    owners,
    meta_ref,
    x_ref,
    attended_ref,
    cot_ref,
    vec_ref,
    up_bias_ref,
    *refs,
):
    one_refs, two_refs, refs = refs[:owners], refs[owners : 2 * owners], refs[2 * owners :]
    y_ref, grad_middle_ref, grad_attended_ref, keep_ref, send_ref = refs[:5]
    down_w_ref, up_w_ref, out_w_ref, vec_grad_ref, up_bias_grad_ref, down_acc, up_acc, out_acc = refs[5:]
    rows = WIDTH // owners
    wide_rows = hidden_width // owners
    blocks = hidden_width // WIDTH

    for at, (one, two) in enumerate(zip(one_refs, two_refs)):
        owner = meta_ref[1 + at]
        span = pl.ds(pl.multiple_of(owner * rows, rows), rows)
        for block in range(blocks - 1):
            up_w_ref[span, block * WIDTH : (block + 1) * WIDTH] = one[block * rows : (block + 1) * rows, :]
        up_w_ref[span, (blocks - 1) * WIDTH :] = two[0:rows, :]
        out_w_ref[span, :] = two[rows : 2 * rows, :]
        down_w_ref[pl.ds(pl.multiple_of(owner * wide_rows, wide_rows), wide_rows), :] = two[2 * rows :, :]

    out_bias, gain, shift, down_bias = (vec_ref[4 + at : 5 + at, :] for at in range(4))
    attended = attended_ref[...]
    middle = x_ref[...].astype(f32) + dot_nn(attended, out_w_ref[...]) + out_bias
    scaled, inverse = norm_rows(middle)
    normed = (scaled * gain + shift).astype(bf16)
    cot = cot_ref[...]
    wide = cot.astype(f32)
    lowered = jnp.zeros_like(middle)
    grad_normed = jnp.zeros_like(middle)
    for block in range(blocks):
        columns = slice(block * WIDTH, (block + 1) * WIDTH)
        down = down_w_ref[columns, :]
        pre = dot_nn(normed, up_w_ref[:, columns]) + up_bias_ref[:, columns]
        phi, bell = normal_parts(pre)
        hidden = (pre * phi).astype(bf16)
        lowered += dot_nn(hidden, down)
        grad_pre = (dot_nt(cot, down) * (phi + pre * bell)).astype(bf16)
        up_bias_grad_ref[:, columns] = column_sum(grad_pre.astype(f32))
        grad_normed += dot_nt(grad_pre, up_w_ref[:, columns])
        down_acc[columns, :] = dot_tn(hidden, cot)
        up_acc[:, columns] = dot_tn(normed, grad_pre)
    y_ref[...] = (middle + lowered + down_bias).astype(bf16)
    grad_middle = wide + norm_back(grad_normed, scaled, inverse, gain)
    grad_middle_ref[...] = grad_middle
    grad_proj = grad_middle.astype(bf16)
    grad_attended_ref[...] = dot_nt(grad_proj, out_w_ref[...]).astype(bf16)
    out_acc[...] = dot_tn(attended, grad_proj)
    vec_grad_ref[0:1, :] = column_sum(grad_proj.astype(f32))
    vec_grad_ref[1:2, :] = column_sum(grad_normed * scaled)
    vec_grad_ref[2:3, :] = column_sum(grad_normed)
    vec_grad_ref[3:4, :] = column_sum(wide)

    extra = keep_ref.shape[1] - wide_rows - (blocks + 1) * rows
    row_at = lax.broadcasted_iota(jnp.int32, (extra, 1), 0)
    low_bit = meta_ref[1] & 1

    def put(high, at, count, source):
        mine, other = choose(low_bit, source(2 * high), source(2 * high + 1))
        keep_ref[high, at : at + count, :] = mine.astype(bf16)
        send_ref[high, at : at + count, :] = other.astype(bf16)

    def small(owner):
        first = [vec_grad_ref[i : i + 1, owner * rows : (owner + 1) * rows] for i in range(4)]
        second = up_bias_grad_ref[:, owner * wide_rows : (owner + 1) * wide_rows]
        return jnp.where(row_at == 0, jnp.concatenate(first, axis=1), jnp.where(row_at == 1, second, 0.0))

    for high in range(owners // 2):
        put(high, 0, wide_rows, lambda owner: down_acc[owner * wide_rows : (owner + 1) * wide_rows, :])
        at = wide_rows
        for block in range(blocks):
            columns = slice(block * WIDTH, (block + 1) * WIDTH)
            put(high, at, rows, lambda owner: up_acc[owner * rows : (owner + 1) * rows, columns])
            at += rows
        put(high, at, rows, lambda owner: out_acc[owner * rows : (owner + 1) * rows, :])
        put(high, at + rows, extra, small)


def feed_call(hidden_width, devices, meta, x, attended, cot, vectors, up_bias, ones, twos):
    rows, owners = x.shape[0], len(ones)
    chain = chain_rows(2 * (hidden_width // owners) + WIDTH // owners, devices)
    split = jax.ShapeDtypeStruct((owners // 2, chain, WIDTH), bf16)
    return pl.pallas_call(
        partial(feed_kernel, hidden_width, owners),
        out_shape=[
            jax.ShapeDtypeStruct((rows, WIDTH), bf16),
            jax.ShapeDtypeStruct((rows, WIDTH), f32),
            jax.ShapeDtypeStruct((rows, WIDTH), bf16),
            split,
            split,
        ],
        in_specs=[pl.BlockSpec(memory_space=pltpu.SMEM)] + vmem_specs(5 + 2 * owners),
        out_specs=vmem_specs(5),
        scratch_shapes=[
            pltpu.VMEM((hidden_width, WIDTH), bf16),
            pltpu.VMEM((WIDTH, hidden_width), bf16),
            pltpu.VMEM((WIDTH, WIDTH), bf16),
            pltpu.VMEM((8, WIDTH), f32),
            pltpu.VMEM((1, hidden_width), f32),
            pltpu.VMEM((hidden_width, WIDTH), f32),
            pltpu.VMEM((WIDTH, hidden_width), f32),
            pltpu.VMEM((WIDTH, WIDTH), f32),
        ],
        compiler_params=pltpu.CompilerParams(vmem_limit_bytes=46 << 20),
        cost_estimate=pl.CostEstimate(flops=32 << 30, bytes_accessed=20 << 20, transcendentals=4 << 20),
        name="feed_forward",
    )(meta, x, attended, cot, vectors, up_bias, *ones, *twos)


def input_grad_kernel(
    rows,
    x_ref,
    dq_ref,
    local_ref,
    grad_middle_ref,
    from_right_ref,
    from_left_ref,
    far_keep_ref,
    far_got_ref,
    w_ref,
    vec_ref,
    out_ref,
    got_ref,
):
    step = pl.program_id(0)
    tile = x_ref.shape[0]
    edge = BLOCK * LOCAL

    @pl.when(step == 0)
    def _():
        folded = far_keep_ref[...].astype(f32) + far_got_ref[...].astype(f32)
        high, low = two_parts(jnp.concatenate([folded[:8], folded[8:]], axis=1))
        got_ref[0:edge, :] = from_left_ref[...]
        got_ref[edge : 2 * edge, :] = from_right_ref[...]
        far = jnp.concatenate([high.astype(f32), low.astype(f32)], axis=0).astype(bf16)
        got_ref[2 * edge : 2 * edge + BLOCK, :] = far
        got_ref[2 * edge + BLOCK :, :] = jnp.zeros((BLOCK, 2 * WIDTH), bf16)

    shape = (1, got_ref.shape[0])
    column = lax.broadcasted_iota(jnp.int32, shape, 1)
    within = jnp.where(column < edge, column, column - edge)
    level = jnp.where(column < 2 * edge, within >> 4, LOCAL)
    last = jnp.where((column >= edge) & (column < 2 * edge), (rows >> level) - BLOCK, 0)
    entry = jnp.where(column < 2 * edge, last + (within & 15), (column - 2 * edge) & 7)
    entry = jnp.where(column < 2 * edge + BLOCK, entry, -1)
    scale = 1.0 / (1 << level).astype(f32)
    token = step * tile + lax.broadcasted_iota(jnp.int32, (tile, shape[1]), 0)
    member = jnp.where((token >> level) == entry, scale, 0.0).astype(bf16)

    scaled, inverse = norm_rows(x_ref[...].astype(f32))
    dkv = (local_ref[...].astype(f32) + dot_nn(member, got_ref[...])).astype(bf16)
    grad = dot_nt(dq_ref[...], w_ref[:, :WIDTH]) + dot_nt(dkv, w_ref[:, WIDTH:])
    out_ref[...] = grad_middle_ref[...] + norm_back(grad, scaled, inverse, vec_ref[0:1, :])


def input_grad_call(x, dq, local, grad_middle, from_right, from_left, far_keep, far_got, weight, vectors):
    rows = x.shape[0]
    tile = 512
    tiled = lambda width: pl.BlockSpec((tile, width), lambda i: (i, 0))
    return pl.pallas_call(
        partial(input_grad_kernel, rows),
        grid=(rows // tile,),
        out_shape=jax.ShapeDtypeStruct((rows, WIDTH), f32),
        in_specs=[tiled(WIDTH), tiled(WIDTH), tiled(2 * WIDTH), tiled(WIDTH)] + vmem_specs(6),
        out_specs=tiled(WIDTH),
        scratch_shapes=[pltpu.VMEM((2 * BLOCK * (LOCAL + 1), 2 * WIDTH), bf16)],
        compiler_params=pltpu.CompilerParams(vmem_limit_bytes=24 << 20),
        cost_estimate=pl.CostEstimate(flops=6 << 30, bytes_accessed=12 << 20, transcendentals=0),
        name="input_grad",
    )(x, dq, local, grad_middle, from_right, from_left, far_keep, far_got, weight, vectors)


def shifted(block, axis, distance):
    devices = range(lax.axis_size(axis))
    route = [(i - distance, i) for i in devices if i - distance in devices]
    return lax.ppermute(block, axis, route)


def swap(block, axis, bit):
    return lax.ppermute(block, axis, [(i, i ^ bit) for i in range(lax.axis_size(axis))])


def gather_step(part, axis, bit):
    mine = (lax.axis_index(axis) // bit) % 2
    other = swap(part, axis, bit)
    first = jnp.where(mine == 0, part, other)
    second = jnp.where(mine == 0, other, part)
    return jnp.stack([first, second], axis=-3)


def together(*values):
    return lax.optimization_barrier(values)


def bits_of(axis):
    size = lax.axis_size(axis)
    return [1 << at for at in range(size.bit_length() - 1)]


def step_call(name, function, meta, arrays, shapes, dtype=bf16):
    def kernel(meta_ref, *refs):
        values = [ref[...].astype(f32) for ref in refs[: len(arrays)]]
        for ref, value in zip(refs[len(arrays) :], function(meta_ref[0], meta_ref[1], *values), strict=True):
            ref[...] = value.astype(dtype)

    size = sum(math.prod(a.shape) for a in arrays)
    return pl.pallas_call(
        kernel,
        out_shape=[jax.ShapeDtypeStruct(shape, dtype) for shape in shapes],
        in_specs=[pl.BlockSpec(memory_space=pltpu.SMEM)] + vmem_specs(len(arrays)),
        out_specs=vmem_specs(len(shapes)),
        compiler_params=pltpu.CompilerParams(vmem_limit_bytes=(4 << 20) + 16 * size),
        cost_estimate=pl.CostEstimate(flops=1 << 20, bytes_accessed=4 * size, transcendentals=0),
        name=name,
    )(meta, *arrays)


def halves(values, axis=0):
    return jnp.split(values, 2, axis=axis)


class Reduction:
    def __init__(self, meta, keep, send, far=None):
        self.meta, self.rows, self.far = meta, keep.shape[1], far
        self.bits = [bit for bit in bits_of("ctx") if bit != CROSS]
        self.keep, self.got = keep, [swap(send, "fsdp", 1)]

    def call(self, name, function, arrays, *shapes):
        return step_call(name, function, self.meta, arrays, [(*shape, WIDTH) for shape in shapes])

    def cross(self):
        far = [self.far[1]] if self.far else []
        extra = far[0].shape[0] if far else 0
        half = self.rows // 2

        def function(here, owner, keep, got, *far):
            mine, other = choose(owner >> 1, *(keep + got))
            keep, near = choose((here // CROSS) & 1, *halves(mine))
            high, both = choose((here // CROSS) & 1, *halves(other))
            return keep, jnp.concatenate([near, *far], axis=0), high, both

        shapes = [(half,), (half + extra,), (half,), (half,)]
        self.keep, near, high, both = self.call("cross", function, [self.keep, *self.got, *far], *shapes)
        count = lax.axis_size("fsdp")
        route = [(i, i ^ (CROSS * count) ^ 2) for i in range(count * lax.axis_size("ctx"))]
        self.got = [swap(near, "ctx", CROSS), swap(high, "fsdp", 2), lax.ppermute(both, ("ctx", "fsdp"), route)]

    def scatter(self, at):
        bit, last = self.bits[at], at == len(self.bits) - 1
        rows = self.keep.shape[0]
        far = [self.far[0]] if self.far else []
        extra = far[0].shape[0] // 2 if far else 0

        def function(here, owner, keep, *got):
            far_keep = got[-1]
            got = got[: len(got) - len(far)]
            total = keep + got[0][:rows]
            for other in got[1:]:
                total = total + other
            flag = (here // bit) & 1
            keep, send = (total, total) if last else choose(flag, *halves(total))
            if not far:
                return [keep] if last else [keep, send]
            far_keep, far_send = choose_groups(flag, far_keep + got[0][rows:], 1)
            return keep, jnp.concatenate([send, far_send], axis=0), far_keep

        count = rows if last else rows // 2
        shapes = [(count,)] if last and not far else [(count,), (count + extra,)]
        out = self.call("scatter", function, [self.keep, *self.got, *far], *shapes, *([(extra,)] if far else []))
        self.keep, send = out[0], out[1] if len(out) > 1 else out[0]
        self.got = [swap(send, "ctx", bit)]
        if far:
            self.far = (out[2], None)


    def order(self):
        high = list(reversed(self.bits[:-1]))
        return list(zip(high + [CROSS], [CROSS] + high))

    def collect(self):
        rows = self.keep.shape[0]
        if self.far:
            self.far = (self.far[0], self.got[0][rows:])
        function = lambda here, owner, keep, got: halves(keep + got[:rows])
        self.send_gather(0, self.call("collect", function, [self.keep, *self.got], (rows // 2,), (rows // 2,)))

    def send_gather(self, at, keep):
        self.keep = keep
        self.got = [swap(part, "ctx", bit) for part, bit in zip(keep, self.order()[at])]

    def gather(self, at):
        bits = self.order()[at]
        rows = 2 * self.keep[0].shape[0]
        function = lambda here, owner, *arrays: self.paired(here, bits, *arrays)
        self.send_gather(at + 1, self.call("gather", function, [*self.keep, *self.got], (rows,), (rows,)))

    def paired(self, here, bits, keep_one, keep_two, got_one, got_two):
        one = jnp.concatenate(choose((here // bits[0]) & 1, keep_one, got_one), axis=0)
        two = jnp.concatenate(choose((here // bits[1]) & 1, keep_two, got_two), axis=0)
        return one, two

    def scatters(self):
        return [self.cross] + [partial(self.scatter, at) for at in range(len(self.bits))]

    def gathers(self):
        return [self.collect] + [partial(self.gather, at) for at in range(len(self.order()) - 1)]

    def finish(self, shapes, unpack):
        bits = self.order()[-1]
        outer = lax.axis_size("ctx") // 4
        rows = self.rows // (4 * outer)

        def function(here, owner, *arrays):
            one, two = self.paired(here, bits, *arrays)
            parts = []
            for low in range(2):
                for high in range(outer):
                    a, b = low * outer + high, 2 * high + low
                    parts += [one[a * rows : (a + 1) * rows], two[b * rows : (b + 1) * rows]]
            return unpack(jnp.concatenate(parts, axis=0))

        return step_call("finish", function, self.meta, [*self.keep, *self.got], shapes, f32)


def shards(
    layer_input,
    doc_lengths,
    ln1_gain,
    ln1_bias,
    qkv_weight,
    query_bias,
    value_bias,
    out_weight,
    out_bias,
    ln2_gain,
    ln2_bias,
    up_weight,
    up_bias,
    down_weight,
    down_bias,
    cotangent,
):
    owners = lax.axis_size("fsdp")
    devices = lax.axis_size("ctx")
    x, cot = layer_input[0], cotangent[0]
    rows = x.shape[0]
    total = rows * devices
    far = far_levels(total)
    here, owner = lax.axis_index("ctx"), lax.axis_index("fsdp")
    part = WIDTH // owners
    hidden_width = up_weight.shape[1]
    meta = jnp.stack([here] + [owner ^ at for at in range(owners)]).astype(jnp.int32)

    vectors = [ln1_gain, ln1_bias, query_bias, value_bias, out_bias, ln2_gain, ln2_bias, down_bias, up_bias]
    across, beside = swap(qkv_weight, "fsdp", 2), swap(qkv_weight, "fsdp", 1)
    small = pack_call(vectors, beside)
    small_across, small_beside = swap(small, "fsdp", 2), swap(small, "fsdp", 1)
    one, two = pack_rest_call(down_weight, up_weight, out_weight)
    bias = mask_call(rows, total, far, meta, doc_lengths)
    across, beside, small_across, small_beside, one, two, bias = together(
        across, beside, small_across, small_beside, one, two, bias
    )
    pieces = [qkv_weight, beside, across, swap(across, "fsdp", 1)]
    smalls = [small, small_beside, small_across, swap(small_across, "fsdp", 1)]
    one_across = swap(one, "fsdp", 2)
    qkv_full, vec, up_shift, queries, kv, scaled, tail, head, base = qkv_call(
        rows, hidden_width, meta, x, pieces, smalls, [bias, two]
    )
    vec, tail, head, base, one_across = together(vec, tail, head, base, one_across)

    one_beside, one_both = swap(one, "fsdp", 1), swap(one_across, "fsdp", 1)
    two_across = swap(two, "fsdp", 2)
    left = shifted(tail, "ctx", 1)
    right = shifted(head, "ctx", -1)
    for bit in reversed(bits_of("ctx")):
        base = gather_step(base, "ctx", bit)
        if bit == 1:
            base, left, right, one_beside, one_both, two_across = together(
                base, left, right, one_beside, one_both, two_across
            )
    base = base.reshape(-1, ENTRY)
    two_beside, two_both = swap(two, "fsdp", 1), swap(two_across, "fsdp", 1)
    attended, exps, inverses = attend_call(rows, devices, far, meta, queries, bias, kv, left, right, base)
    inverses, two_beside, two_both = together(inverses, two_beside, two_both)
    output, grad_middle, grad_attended, keep, send = feed_call(
        hidden_width,
        devices,
        meta,
        x,
        attended,
        cot,
        vec,
        up_shift,
        [one, one_beside, one_across, one_both],
        [two, two_beside, two_across, two_both],
    )
    feed = Reduction(meta, keep, send)
    feed.cross()
    made = attend_back_call(
        rows, devices, far, owners, meta, queries, grad_attended, exps, inverses, kv, scaled, left, right, base, qkv_full, vec
    )
    dq, local, to_left, to_right, far_keep, far_send, keep, send = made
    to_left, to_right, far_keep, far_send, send, *feed.got = together(
        to_left, to_right, far_keep, far_send, send, *feed.got
    )
    first = Reduction(meta, keep, send, (far_keep, far_send))
    back_right = shifted(to_left, "ctx", -1)
    back_left = shifted(to_right, "ctx", 1)
    pending = feed.scatters()[1:]
    pending.pop(0)()
    first.cross()
    tied = together(*first.got, *feed.got)
    first.got, feed.got = list(tied[: len(first.got)]), list(tied[len(first.got) :])
    for one in first.scatters()[1:]:
        one()
        if pending:
            pending.pop(0)()
    tied = together(*first.got, back_right, back_left)
    first.got, (back_right, back_left) = list(tied[:1]), tied[1:]
    for at, (one, two) in enumerate(zip(first.gathers(), feed.gathers())):
        if at == 1:
            tied = together(*feed.got, *first.got)
            feed.got, first.got = list(tied[:2]), list(tied[2:])
        two()
        one()
    input_grad = input_grad_call(
        x, dq, local, grad_middle, back_right, back_left, *first.far, qkv_full, vec
    )

    wide_rows = hidden_width // owners

    def split(row):
        return [row[:, at * part : (at + 1) * part] for at in range(row.shape[1] // part)]

    def unpack_first(total):
        blocks = [total[at * part : (at + 1) * part] for at in range(3)]
        return [jnp.concatenate(blocks, axis=1), *split(total[3 * part : 3 * part + 1])]

    def unpack_feed(total):
        at = wide_rows
        blocks = []
        for _ in range(hidden_width // WIDTH):
            blocks.append(total[at : at + part])
            at += part
        vectors = [*split(total[at + part : at + part + 1]), total[at + part + 1 : at + part + 2]]
        return [total[:wide_rows], jnp.concatenate(blocks, axis=1), total[at : at + part], *vectors]

    vector = (1, part)
    qkv_grad, *firsts = first.finish([(part, 3 * WIDTH)] + [vector] * owners, unpack_first)
    down_grad, up_grad, out_grad, *feeds = feed.finish(
        [(wide_rows, WIDTH), (part, hidden_width), (part, WIDTH)] + [vector] * owners + [(1, wide_rows)], unpack_feed
    )
    gain_first, shift_first, query_grad, value_grad = (v.reshape(-1) for v in firsts)
    out_shift, gain_second, shift_second, down_shift, up_shift_grad = (v.reshape(-1) for v in feeds)
    return (
        output[None],
        input_grad[None],
        gain_first,
        shift_first,
        qkv_grad,
        query_grad,
        value_grad,
        out_grad,
        out_shift,
        gain_second,
        shift_second,
        up_grad,
        up_shift_grad,
        down_grad,
        down_shift,
    )


def solution(mesh):
    row, vector = P("fsdp", None), P("fsdp")
    tokens = P("fsdp", "ctx", None)
    return jax.shard_map(
        shards,
        mesh=mesh,
        in_specs=(
            tokens,
            row,
            vector,
            vector,
            row,
            vector,
            vector,
            row,
            vector,
            vector,
            vector,
            row,
            vector,
            row,
            vector,
            tokens,
        ),
        out_specs=(
            tokens,
            tokens,
            vector,
            vector,
            row,
            vector,
            vector,
            row,
            vector,
            vector,
            vector,
            row,
            vector,
            row,
            vector,
        ),
        check_vma=False,
    )
```
